32 devices in a mesh: expert: 8 (over z, y), dp: 4 (over x, core).
Axes of the slice: x: 2, y: 2, z: 4, core: 2. Of those that a mesh axis runs over, the one named last changes fastest.
Arguments:
- tokens: bfloat16 [2048, 2048], P(('expert', 'dp')), may hold values from -6 to 6
- grad_out: bfloat16 [2048, 2048], P(('expert', 'dp')), may hold values from -6 to 6
- route_expert: int32 [2048, 4], P(('expert', 'dp')), may hold values from 0 to 7, all different within a row; in each aligned block of 64 rows (0 to 63, 64 to 127, ...) at most 33 rows name the same one
- route_weight: bfloat16 [2048, 4], P(('expert', 'dp')), may hold values from 0.019897461 to 0.5
- gate_up_weight: bfloat16 [8, 2048, 768], P('expert', 'dp'), may hold values from -0.125 to 0.125
- down_weight: bfloat16 [8, 2048, 384], P('expert', 'dp'), may hold values from -0.3125 to 0.3125
Outputs:
- grad_tokens: bfloat16 [2048, 2048], P(('expert', 'dp'))
- grad_route: bfloat16 [2048, 4], P(('expert', 'dp'))
- grad_gate_up: float32 [8, 2048, 768], P('expert', 'dp')
- grad_down: float32 [8, 2048, 384], P('expert', 'dp')
The draws below stay inside these ranges and needn't reach their ends.
Inputs may be any that keep to these rules, and one draw needn't show every extreme that they name: `route_expert`: each row names 4 different experts. In the 64 rows of one device (aligned blocks) no expert is named by more than 33 rows, a bound that some block reaches.
All inputs are finite; a program needn't handle non-finite values.
Results may differ from the reference program's by a relative error of at most 0.01.
Values may be sent and summed in bfloat16 or wider, within the bound.
No kernel may reach another device: no remote copies, remote signals or barrier semaphores. Data moves between devices by JAX's collectives and lax.ppermute only.
A program may use at most 64 MiB of HBM per device.

```python
import math
import jax
import jax.numpy as jnp
import numpy as np
from jax import lax

D = 2048
F = 384
TOP = 4
TOK_DEV = 64
EXPERTS = 8
CAP = 33
TOKENS = 2048
N_EXPERT = 8
N_DP = 4


def block_scale(stream_key, dims, cuts, low, high):
    level, own = 1.0, jax.random.fold_in(stream_key, 6)
    for axis_at, shards_of in cuts:
        draws = jnp.exp(jax.random.uniform(jax.random.fold_in(own, axis_at), (shards_of,), jnp.float32, low / len(cuts), high / len(cuts)))
        level = level * jnp.repeat(draws, dims[axis_at] // shards_of).reshape([-1 if axis == axis_at else 1 for axis in range(len(dims))])
    return level


def shared_out(own_key, own, number, rows, number_of, top, limit, slope):
    ranking = jax.random.permutation(own_key, number_of)
    packed, ordinary = shares(number_of, rows * top, limit, slope, True), shares(number_of, rows * top, limit, slope, False)
    places = jnp.arange(number_of)

    def named(tallies, turn):
        used = int((tallies > 0).sum())
        fixed = max(1, used // 4)
        moved = fixed + (places - fixed + turn * (used - fixed)) % max(1, number_of - fixed)
        return jnp.zeros((number_of,), jnp.int32).at[ranking[jnp.where(places < fixed, places, moved)]].set(jnp.asarray(tallies, jnp.int32))

    tallies = jnp.where(number % 4 == 0, named(packed, number // 4), named(ordinary, number - number // 4 - 1))
    mixed = jax.random.permutation(jax.random.fold_in(own, 3), number_of)
    giver, sink = mixed[0:number_of // 2 * 2:2], mixed[1:number_of // 2 * 2:2]
    room = jnp.minimum(tallies[giver] - 1, limit - tallies[sink]) // 2
    room = jnp.where((giver == ranking[0]) | (sink == ranking[0]) | (tallies[sink] == 0), 0, jnp.maximum(room, 0))
    moved = jax.random.randint(jax.random.fold_in(own, 4), (number_of // 2,), 0, 1 << 20) % (room + 1)
    tallies = tallies.at[giver].add(-moved).at[sink].add(moved)
    members = jnp.searchsorted(jnp.cumsum(tallies), jnp.arange(rows * top), side="right").astype(jnp.int32)
    listing = members.reshape(top, rows).T
    listing = listing[jax.random.permutation(jax.random.fold_in(own, 1), rows)]
    turn = jax.random.randint(jax.random.fold_in(own, 2), (rows, 1), 0, top)
    return jnp.take_along_axis(listing, (jnp.arange(top)[None, :] + turn) % top, axis=1)


def shares(number_of, total, most, lean, full):
    weights = [(1 << 20) // math.isqrt(standing ** lean) + 1 for standing in range(1, number_of + 1)]
    largest = most if full else min(most, max(-(-total // number_of), total * weights[0] // sum(weights)))
    least = 1 if total - largest >= number_of - 1 else 0
    given, spare = [largest] + [least] * (number_of - 1), total - largest - least * (number_of - 1)
    while spare > 0:
        free = [i for i in range(1, number_of) if given[i] < largest] or [i for i in range(1, number_of) if given[i] < most]
        pool, left = sum([weights[i] for i in free]), spare
        for i in free:
            more = min(most - given[i], max(1, left * weights[i] // pool), spare)
            given[i] = given[i] + more
            spare = spare - more
    return np.array(given)


def noise(stream_key, shape, spread, limit, split=(), kind=jnp.bfloat16):
    array = jax.random.normal(stream_key, shape, jnp.float32) * spread
    if len(split) > 0:
        array = block_scale(stream_key, shape, split, -0.22, 0.18) * array
    return jnp.clip(array, min=-limit, max=limit).astype(kind)


def setup_inputs(seed: int = 0) -> dict:
    keys = jax.random.split(jax.random.key(seed), 7)
    tokens = noise(keys[0], (TOKENS, D), 1.0, 6.0, ((0, 32),))
    grad_out = noise(keys[1], (TOKENS, D), 1.0, 6.0, ((0, 32),))
    route_expert_keys = jax.random.split(jax.random.fold_in(keys[2], 1), TOKENS // TOK_DEV)
    route_expert_turns = jax.random.permutation(jax.random.fold_in(keys[2], 3), TOKENS // TOK_DEV)
    route_expert = jax.vmap(lambda own, number: shared_out(jax.random.fold_in(keys[2], 2), own, number, TOK_DEV, EXPERTS, TOP, CAP, 2))(route_expert_keys, route_expert_turns).reshape((TOKENS, TOP))
    route_weight = jnp.clip(jnp.exp(math.log(0.5) - 3.224016 * jax.random.uniform(keys[3], (TOKENS, TOP), jnp.float32) ** block_scale(keys[3], (TOKENS, TOP), ((0, 32),), -0.2, 0.2)), 0.019897461, 0.5).astype(jnp.bfloat16)
    gate_up_weight = noise(keys[4], (EXPERTS, D, 2 * F), D ** -0.5, 0.125, ((0, 8), (1, 4)))
    down_weight = noise(keys[5], (EXPERTS, D, F), F ** -0.5, 0.3125, ((0, 8), (1, 4)))
    return dict(tokens=tokens, grad_out=grad_out, route_expert=route_expert, route_weight=route_weight, gate_up_weight=gate_up_weight, down_weight=down_weight)


def rounded(value):
    return lax.optimization_barrier(value.astype(jnp.bfloat16)).astype(jnp.float32)


def swish(value):
    return value * jax.nn.sigmoid(value)


def reference(tokens, grad_out, route_expert, route_weight, gate_up_weight, down_weight):
    total_rows = tokens.shape[0]
    flat_expert = route_expert.reshape(-1)
    flat_weight = route_weight.reshape(-1).astype(jnp.float32)
    pair_total = flat_expert.shape[0]
    slot_total = CAP * N_EXPERT * N_DP
    high = lax.Precision.HIGHEST

    def per_expert(carry, expert):
        grad_acc, route_acc = carry
        chosen = flat_expert == expert
        position = jnp.cumsum(chosen.astype(jnp.int32)) - 1
        target = jnp.where(chosen, position, slot_total).astype(jnp.int32)
        source = jnp.zeros((slot_total,), jnp.int32).at[target].set(jnp.arange(pair_total, dtype=jnp.int32), mode="drop")
        filled = jnp.zeros((slot_total,), jnp.float32).at[target].set(1.0, mode="drop")
        token_row = source // TOP
        rows_x = tokens[token_row].astype(jnp.float32) * filled[:, None]
        rows_dy = grad_out[token_row].astype(jnp.float32) * filled[:, None]
        rows_w = flat_weight[source] * filled
        in_mat = lax.dynamic_index_in_dim(gate_up_weight, expert, 0, keepdims=False).astype(jnp.float32)
        out_mat = lax.dynamic_index_in_dim(down_weight, expert, 0, keepdims=False).astype(jnp.float32)
        pre = jnp.dot(rows_x, in_mat, precision=high, preferred_element_type=jnp.float32)
        gate_pre = pre[:, :F]
        up_pre = pre[:, F:]
        act = swish(gate_pre)
        hidden = rounded(act * up_pre)
        expert_out = jnp.dot(hidden, out_mat.T, precision=high, preferred_element_type=jnp.float32)
        route_grad = rounded(jnp.sum(rows_dy * expert_out, axis=1))
        scaled = rounded(rows_w[:, None] * rows_dy)
        grad_hidden = jnp.dot(scaled, out_mat, precision=high, preferred_element_type=jnp.float32)
        sig = jax.nn.sigmoid(gate_pre)
        grad_gate = grad_hidden * up_pre * sig * (1.0 + gate_pre * (1.0 - sig))
        grad_up = grad_hidden * act
        grad_pre = rounded(jnp.concatenate([grad_gate, grad_up], axis=1))
        rows_grad = rounded(jnp.dot(grad_pre, in_mat.T, precision=high, preferred_element_type=jnp.float32))
        grad_in = jnp.dot(rows_x.T, grad_pre, precision=high, preferred_element_type=jnp.float32)
        grad_outw = jnp.dot(scaled.T, hidden, precision=high, preferred_element_type=jnp.float32)
        live = filled > 0
        grad_acc = grad_acc.at[jnp.where(live, token_row, total_rows).astype(jnp.int32)].add(rows_grad, mode="drop")
        route_acc = route_acc.at[jnp.where(live, source, pair_total).astype(jnp.int32)].set(route_grad, mode="drop")
        return (grad_acc, route_acc), (grad_in, grad_outw)

    start = (jnp.zeros((total_rows, D), jnp.float32), jnp.zeros((pair_total,), jnp.float32))
    (grad_acc, route_acc), (grad_gate_up, grad_down) = lax.scan(per_expert, start, jnp.arange(EXPERTS, dtype=jnp.int32))
    grad_tokens = grad_acc.astype(jnp.bfloat16)
    grad_route = route_acc.reshape(total_rows, TOP).astype(jnp.bfloat16)
    return (grad_tokens, grad_route, grad_gate_up, grad_down)
```

```python
import functools

import jax
import jax.numpy as jnp
from jax import lax
from jax.experimental import pallas as pl
from jax.experimental.pallas import tpu as pltpu
from jax.sharding import PartitionSpec as P

BF16 = jnp.bfloat16
F32 = jnp.float32


def swish(value):
    return value * jax.nn.sigmoid(value)


def dot(a, b):
    return jnp.dot(a, b, preferred_element_type=F32)


def dot_nt(a, b):
    return lax.dot_general(a, b, (((1,), (1,)), ((), ())), preferred_element_type=F32)


def dot_tn(a, b):
    return lax.dot_general(a, b, (((0,), (0,)), ((), ())), preferred_element_type=F32)


def select_matrix(weight_row, row_total):
    token_total = weight_row.shape[1]
    routed = weight_row != 0.0
    earlier = lax.broadcasted_iota(jnp.int32, (token_total, token_total), 0)
    later = lax.broadcasted_iota(jnp.int32, (token_total, token_total), 1)
    upper = (earlier < later).astype(F32).astype(BF16)
    ones = jnp.broadcast_to(routed.astype(F32), (8, token_total)).astype(BF16)
    rank = dot(ones, upper)[0:1, :]
    rank = jnp.where(routed, rank, -1.0).astype(jnp.int32)
    slots = lax.broadcasted_iota(jnp.int32, (row_total, token_total), 0)
    return (slots == rank).astype(F32).astype(BF16)


def x_kernel(place_ref, w_ref, x_ref, *refs):
    parts = (len(refs) - 2) // 2
    in_refs, slice_refs = refs[:parts], refs[parts : 2 * parts]
    pre_ref, pick_ref = refs[2 * parts :]
    rows, depth = slice_refs[0].shape
    pick_ref[...] = select_matrix(w_ref[...], rows)
    for j in range(parts):
        columns = pl.ds(pl.multiple_of(place_ref[j] * depth, depth), depth)
        slice_refs[j][...] = dot(pick_ref[...], x_ref[:, columns]).astype(BF16)
        term = dot(slice_refs[j][...], in_refs[j][...])
        if j == 0:
            pre_ref[...] = term
        else:
            pre_ref[...] += term


def dy_kernel(place_ref, w_ref, dy_ref, pre_ref, pick_ref, *refs):
    parts = (len(refs) - 3) // 3
    in_refs, out_refs, slice_refs = refs[:parts], refs[parts : 2 * parts], refs[2 * parts : 3 * parts]
    mid_ref, grad_ref, route_ref = refs[3 * parts :]
    rows, depth = slice_refs[0].shape
    hidden_width = out_refs[0].shape[1]
    pick = pick_ref[...]
    back = jnp.zeros((rows, hidden_width), F32)
    for j in range(parts):
        columns = pl.ds(pl.multiple_of(place_ref[j] * depth, depth), depth)
        slice_refs[j][...] = dot(pick, dy_ref[:, columns]).astype(BF16)
        back += dot(slice_refs[j][...], out_refs[j][...])
    weight = jnp.sum(pick.astype(F32) * w_ref[...], axis=1, keepdims=True)
    gate_pre = pre_ref[:, :hidden_width]
    up_pre = pre_ref[:, hidden_width:]
    sig = jax.nn.sigmoid(gate_pre)
    act = gate_pre * sig
    hidden = (act * up_pre).astype(BF16).astype(F32)
    route = jnp.sum(hidden * back, axis=1, keepdims=True)
    grad_hidden = weight * back
    grad_gate = grad_hidden * up_pre * sig * (1.0 + gate_pre * (1.0 - sig))
    mid_ref[:, :hidden_width] = grad_gate.astype(BF16)
    mid_ref[:, hidden_width : 2 * hidden_width] = (grad_hidden * act).astype(BF16)
    mid_ref[:, 2 * hidden_width :] = (weight * hidden).astype(BF16)
    route_ref[...] = jnp.sum(pick.astype(F32) * route, axis=0, keepdims=True)
    spread = dot_tn(pick, mid_ref[:, : 2 * hidden_width]).astype(BF16)
    for j in range(parts):
        columns = pl.ds(pl.multiple_of(place_ref[j] * depth, depth), depth)
        grad_ref[:, columns] = dot_nt(spread, in_refs[j][...]).astype(BF16)


def weight_kernel(*refs):
    parts = (len(refs) - 2) // 3
    x_refs, dy_refs, mid_refs = refs[:parts], refs[parts : 2 * parts], refs[2 * parts : 3 * parts]
    in_ref, out_ref = refs[3 * parts :]
    hidden_width = out_ref.shape[1]
    for j in range(parts):
        in_term = dot_tn(x_refs[j][...], mid_refs[j][:, : 2 * hidden_width])
        out_term = dot_tn(dy_refs[j][...], mid_refs[j][:, 2 * hidden_width :])
        if j == 0:
            in_ref[...] = in_term
            out_ref[...] = out_term
        else:
            in_ref[...] += in_term
            out_ref[...] += out_term


def call(kernel, out_shapes, smem, arrays, flops):
    vmem = pl.BlockSpec(memory_space=pltpu.VMEM)
    specs = [pl.BlockSpec(memory_space=pltpu.SMEM)] * len(smem) + [vmem] * len(arrays)
    moved = sum(a.size * a.dtype.itemsize for a in list(arrays) + list(out_shapes))
    return pl.pallas_call(
        kernel,
        out_shape=tuple(out_shapes),
        in_specs=specs,
        out_specs=tuple([vmem] * len(out_shapes)),
        compiler_params=pltpu.CompilerParams(vmem_limit_bytes=40 * 1024 * 1024),
        cost_estimate=pl.CostEstimate(flops=flops, bytes_accessed=moved, transcendentals=0),
    )(*smem, *arrays)


def swap(value, axis, size, mask):
    return lax.ppermute(value, axis, [(i, i ^ mask) for i in range(size)])


def gather_four(value):
    near = swap(value, "dp", 4, 1)
    far = swap(value, "dp", 4, 2)
    return [value, near, far, swap(far, "dp", 4, 1)]


def spread_four(values):
    return [values[0]] + [swap(values[j], "dp", 4, j) for j in range(1, 4)]


def on_device_gathered(tokens, grad_out, route_expert, route_weight, gate_up_weight, down_weight):
    token_count, model_width = tokens.shape
    route_count = route_expert.shape[1]
    group_count = lax.axis_size("expert")
    part_count = lax.axis_size("dp")
    hidden_width = down_weight.shape[2]
    depth = model_width // part_count
    capacity = min(token_count, (token_count * route_count + group_count - 1) // group_count + 1)
    rows = (group_count * capacity + 15) // 16 * 16
    everyone = group_count * token_count

    places = lax.axis_index("dp") ^ jnp.arange(part_count, dtype=jnp.int32)
    names = route_expert.T[None, :, :] == jnp.arange(group_count, dtype=jnp.int32)[:, None, None]
    dense = jnp.sum(jnp.where(names, route_weight.T[None, :, :], 0), axis=1).astype(BF16)
    weight_row = lax.all_to_all(dense, "expert", split_axis=0, concat_axis=0, tiled=True)
    weight_row = weight_row.reshape(1, everyone).astype(F32)

    all_tokens = lax.all_gather(tokens, "expert", axis=0, tiled=True)
    all_grad = lax.all_gather(grad_out, "expert", axis=0, tiled=True)
    in_parts = gather_four(gate_up_weight[0])
    out_parts = gather_four(down_weight[0])

    sliced = [jax.ShapeDtypeStruct((rows, depth), BF16)] * part_count
    *x_slices, pre, pick = call(
        x_kernel,
        sliced
        + [
            jax.ShapeDtypeStruct((rows, 2 * hidden_width), F32),
            jax.ShapeDtypeStruct((rows, everyone), BF16),
        ],
        [places],
        [weight_row, all_tokens, *in_parts],
        2 * rows * model_width * (everyone + 2 * hidden_width),
    )
    x_slices = spread_four(x_slices)
    *dy_slices, mid, grad_rows, route_row = call(
        dy_kernel,
        sliced
        + [
            jax.ShapeDtypeStruct((rows, 3 * hidden_width), BF16),
            jax.ShapeDtypeStruct((everyone, model_width), BF16),
            jax.ShapeDtypeStruct((1, everyone), F32),
        ],
        [places],
        [weight_row, all_grad, pre, pick, *in_parts, *out_parts],
        2 * rows * model_width * (everyone + hidden_width) + 4 * everyone * hidden_width * model_width,
    )
    dy_slices = spread_four(dy_slices)
    mids = gather_four(mid)
    grad_tokens = lax.psum_scatter(grad_rows, "expert", scatter_dimension=0, tiled=True)
    route_back = lax.all_to_all(
        route_row.reshape(group_count, token_count).astype(BF16),
        "expert",
        split_axis=0,
        concat_axis=0,
        tiled=True,
    )
    grad_route = jnp.sum(jnp.where(names, route_back[:, None, :], 0), axis=0).astype(BF16).T
    grad_gate_up, grad_down = call(
        weight_kernel,
        [
            jax.ShapeDtypeStruct((depth, 2 * hidden_width), F32),
            jax.ShapeDtypeStruct((depth, hidden_width), F32),
        ],
        [],
        [*x_slices, *dy_slices, *mids],
        2 * part_count * rows * depth * 3 * hidden_width,
    )
    return (grad_tokens, grad_route, grad_gate_up[None], grad_down[None])

def to_local(rows, group_count, local_count, capacity):
    tail = rows.shape[2:]
    shaped = rows.reshape((group_count, local_count, capacity) + tail)
    shaped = jnp.swapaxes(shaped, 0, 1)
    return shaped.reshape((local_count, group_count * capacity) + tail)


def to_groups(rows, group_count, local_count, capacity):
    tail = rows.shape[2:]
    shaped = rows.reshape((local_count, group_count, capacity) + tail)
    shaped = jnp.swapaxes(shaped, 0, 1)
    return shaped.reshape((group_count, local_count * capacity) + tail)


def on_device_routed(tokens, grad_out, route_expert, route_weight, gate_up_weight, down_weight):
    token_count, model_width = tokens.shape
    route_count = route_expert.shape[1]
    group_count = lax.axis_size("expert")
    local_count = gate_up_weight.shape[0]
    hidden_width = down_weight.shape[2]
    expert_total = local_count * group_count
    capacity = min(token_count, (token_count * route_count + expert_total - 1) // expert_total + 1)
    slot_total = expert_total * capacity
    flat_expert = route_expert.reshape(-1)
    expert_ids = jnp.arange(expert_total, dtype=jnp.int32)
    onehot = (flat_expert[:, None] == expert_ids[None, :]).astype(jnp.int32)
    before = jnp.cumsum(onehot, axis=0) - onehot
    rank = jnp.sum(before * onehot, axis=1)
    slot_of = flat_expert * capacity + rank
    slot_ids = jnp.arange(slot_total, dtype=jnp.int32)
    placed = slot_ids[:, None] == slot_of[None, :]
    by_token = jnp.any(placed.reshape(slot_total, token_count, route_count), axis=2).astype(
        jnp.bfloat16
    )
    send_x = jnp.dot(by_token, tokens, preferred_element_type=jnp.float32).astype(jnp.bfloat16)
    send_dy = jnp.dot(by_token, grad_out, preferred_element_type=jnp.float32).astype(jnp.bfloat16)
    flat_weight = route_weight.reshape(-1).astype(jnp.float32)
    send_w = jnp.sum(jnp.where(placed, flat_weight[None, :], 0.0), axis=1).astype(jnp.bfloat16)
    recv_x, recv_dy, recv_w = (
        lax.all_to_all(
            send_x.reshape(group_count, local_count * capacity, model_width),
            "expert",
            split_axis=0,
            concat_axis=0,
            tiled=True,
        ),
        lax.all_to_all(
            send_dy.reshape(group_count, local_count * capacity, model_width),
            "expert",
            split_axis=0,
            concat_axis=0,
            tiled=True,
        ),
        lax.all_to_all(
            send_w.reshape(group_count, local_count * capacity),
            "expert",
            split_axis=0,
            concat_axis=0,
            tiled=True,
        ),
    )
    rows_x = to_local(recv_x, group_count, local_count, capacity)
    rows_dy = to_local(recv_dy, group_count, local_count, capacity)
    rows_w = to_local(recv_w, group_count, local_count, capacity)
    full_in, full_out = (
        lax.all_gather(gate_up_weight, "dp", axis=1, tiled=True),
        lax.all_gather(down_weight, "dp", axis=1, tiled=True),
    )
    pre = jnp.einsum("erd,edf->erf", rows_x, full_in, preferred_element_type=jnp.float32)
    gate_pre = pre[:, :, :hidden_width]
    up_pre = pre[:, :, hidden_width:]
    act = swish(gate_pre)
    hidden = (act * up_pre).astype(jnp.bfloat16)
    expert_out = jnp.einsum("erf,edf->erd", hidden, full_out, preferred_element_type=jnp.float32)
    route_grad = jnp.sum(rows_dy.astype(jnp.float32) * expert_out, axis=2).astype(jnp.bfloat16)
    scaled = (rows_w.astype(jnp.float32)[:, :, None] * rows_dy).astype(jnp.bfloat16)
    grad_hidden = jnp.einsum("erd,edf->erf", scaled, full_out, preferred_element_type=jnp.float32)
    sig = jax.nn.sigmoid(gate_pre)
    grad_gate = grad_hidden * up_pre * sig * (1.0 + gate_pre * (1.0 - sig))
    grad_up = grad_hidden * act
    grad_pre = jnp.concatenate([grad_gate, grad_up], axis=2).astype(jnp.bfloat16)
    rows_grad = jnp.einsum(
        "erf,edf->erd", grad_pre, full_in, preferred_element_type=jnp.float32
    ).astype(jnp.bfloat16)
    back_x, back_w = (
        lax.all_to_all(
            to_groups(rows_grad, group_count, local_count, capacity),
            "expert",
            split_axis=0,
            concat_axis=0,
            tiled=True,
        ),
        lax.all_to_all(
            to_groups(route_grad, group_count, local_count, capacity),
            "expert",
            split_axis=0,
            concat_axis=0,
            tiled=True,
        ),
    )
    back_x = back_x.reshape(slot_total, model_width)
    back_w = back_w.reshape(slot_total).astype(jnp.float32)
    grad_tokens = jnp.einsum(
        "st,sd->td", by_token, back_x, preferred_element_type=jnp.float32
    ).astype(jnp.bfloat16)
    grad_route = jnp.sum(jnp.where(placed, back_w[:, None], 0.0), axis=0)
    grad_route = grad_route.reshape(token_count, route_count).astype(jnp.bfloat16)
    all_x = lax.all_to_all(rows_x, "dp", split_axis=2, concat_axis=1, tiled=True)
    grad_gate_up = jnp.einsum(
        "erd,erf->edf",
        all_x,
        lax.all_gather(grad_pre, "dp", axis=1, tiled=True),
        preferred_element_type=jnp.float32,
    )
    summed = lax.psum_scatter(
        jnp.einsum("erd,erf->def", scaled, hidden, preferred_element_type=jnp.float32),
        "dp",
        scatter_dimension=0,
        tiled=True,
    )
    grad_down = jnp.swapaxes(summed, 0, 1)
    return (grad_tokens, grad_route, grad_gate_up, grad_down)


def solution(mesh):
    def on_device(*arrays):
        route_expert, down_weight = arrays[2], arrays[5]
        gathers = (
            down_weight.shape[0] == 1
            and lax.axis_size("dp") == 4
            and lax.axis_size("expert") <= 2 * route_expert.shape[1]
        )
        return (on_device_gathered if gathers else on_device_routed)(*arrays)

    return jax.shard_map(
        on_device,
        mesh=mesh,
        in_specs=(
            P(("expert", "dp"), None),
            P(("expert", "dp"), None),
            P(("expert", "dp"), None),
            P(("expert", "dp"), None),
            P("expert", "dp", None),
            P("expert", "dp", None),
        ),
        out_specs=(
            P(("expert", "dp"), None),
            P(("expert", "dp"), None),
            P("expert", "dp", None),
            P("expert", "dp", None),
        ),
        check_vma=False,
    )
```

```python
import functools

import jax
import jax.numpy as jnp
from jax import lax
from jax.experimental import pallas as pl
from jax.experimental.pallas import tpu as pltpu
from jax.sharding import PartitionSpec as P

BF16 = jnp.bfloat16
F32 = jnp.float32
LANES = 128


def swish(value):
    return value * jax.nn.sigmoid(value)


def dot(a, b):
    return jnp.dot(a, b, preferred_element_type=F32)


def dot_nt(a, b):
    return lax.dot_general(a, b, (((1,), (1,)), ((), ())), preferred_element_type=F32)


def dot_tn(a, b):
    return lax.dot_general(a, b, (((0,), (0,)), ((), ())), preferred_element_type=F32)


def start(source, target, sem):
    copy = pltpu.make_async_copy(source, target, sem)
    copy.start()
    return copy


def picks(weight, main):
    token_count = weight.shape[1]
    routed = weight != 0.0
    first = lax.broadcasted_iota(jnp.int32, (token_count, token_count), 0)
    second = lax.broadcasted_iota(jnp.int32, (token_count, token_count), 1)
    upper = (first < second).astype(F32).astype(BF16)
    rank = dot(routed.astype(F32).astype(BF16), upper)
    rank = jnp.where(routed, rank, -1.0).astype(jnp.int32)
    slots = lax.broadcasted_iota(jnp.int32, (main, token_count), 0)
    mains = [(slots == rank[i : i + 1, :]).astype(F32) for i in range(weight.shape[0])]
    tails = (rank == main).astype(F32)
    return mains, tails


def bounce(pairs, held, target, sems):
    copies = [start(source, place, sems.at[i]) for i, (source, place) in enumerate(pairs)]
    for copy in copies:
        copy.wait()
    start(held, target, sems.at[0]).wait()


def route_kernel(peer_ref, named_ref, given_ref, dy_ref, joint_ref, dense_ref, held, sems):
    count = dy_ref.shape[0]
    copy = start(dy_ref, held.at[pl.ds(0, count)], sems.at[0])
    named = named_ref[...]
    given = given_ref[...].astype(F32)
    experts = dense_ref.shape[0]
    lines = [
        jnp.sum(jnp.where(named == peer_ref[i], given, 0.0), axis=0, keepdims=True) for i in range(experts)
    ]
    dense = jnp.concatenate(lines, axis=0)
    dense_ref[...] = dense
    turned = jnp.concatenate(lines[experts // 2 :] + lines[: experts // 2] + [jnp.zeros_like(dense)], axis=0)
    held[count:, :] = jnp.zeros((held.shape[0] - count, held.shape[1]), BF16)
    held[count:, :count] = turned.astype(BF16)
    copy.wait()
    start(held, joint_ref, sems.at[1]).wait()


def join_kernel(in_ref, out_ref, joint_ref, again_ref, held, sems):
    width = in_ref.shape[1]
    pairs = [
        (in_ref, held.at[:, pl.ds(0, width)]),
        (out_ref, held.at[:, pl.ds(width, out_ref.shape[1])]),
    ]
    copies = [start(source, place, sems.at[i]) for i, (source, place) in enumerate(pairs)]
    for copy in copies:
        copy.wait()
    copies = [start(held, joint_ref, sems.at[0]), start(held, again_ref, sems.at[1])]
    for copy in copies:
        copy.wait()


def after_kernel(*refs):
    pass


def stack_kernel(own_ref, far_ref, after_ref, joint_ref, held, sems):
    count = own_ref.shape[0]
    pairs = [(own_ref, held.at[pl.ds(0, count)]), (far_ref, held.at[pl.ds(count, count)])]
    bounce(pairs, held, joint_ref, sems)


def relay_kernel(near_a, far_a, near_b, far_b, after_ref, mid_ref, joint_ref, mid_out_ref, held, sems):
    count, width = near_a.shape
    pairs = []
    for at, near, far in ((0, near_a, far_a), (count, near_b, far_b)):
        pairs.append((near, held.at[pl.ds(at, count), pl.ds(0, width)]))
        pairs.append((far.at[:, pl.ds(width, width)], held.at[pl.ds(at, count), pl.ds(width, width)]))
    bounce(pairs, held, joint_ref, sems)


def pack_kernel(first, x_ref, joint_ref, *refs):
    count = 4
    x, joint, block, fold, sems = refs[-5:]
    out_refs = refs[-5 - count : -5]
    tokens, width = x.shape
    chunks = width // LANES
    main = block.shape[1] // 2
    copies = [
        start(joint_ref.at[pl.ds(tokens, 16)], joint.at[pl.ds(tokens, 16)], sems.at[count]),
        start(x_ref, x, sems.at[count + 1]),
        start(joint_ref.at[pl.ds(0, tokens)], joint.at[pl.ds(0, tokens)], sems.at[count + 2]),
    ]
    copies.pop(0).wait()
    weight = joint[tokens:, :LANES].astype(F32)[0:8, :tokens]
    mains, tails = picks(weight, main)
    mains = mains[first : first + count]
    pick = jnp.concatenate(mains + [tails, jnp.zeros_like(tails)], axis=0).astype(BF16)
    lane = lax.broadcasted_iota(jnp.int32, (main, LANES), 1)
    for source, base in ((x, 0), (joint, main)):
        copies.pop(0).wait()
        rows = dot(pick, source[0:tokens])
        for j in range(count):
            block[j, base : base + main, :width] = rows[main * j : main * (j + 1)].astype(BF16)
            line = main * count + first + j
            for c in range(chunks):
                fold[c : c + 1, :] = rows[line : line + 1, LANES * c : LANES * (c + 1)]
            low = 0 if base == 0 else chunks
            block[j, low : low + chunks, width:] = fold[...].astype(BF16)
    copies = []
    for j in range(count):
        mine = weight[first + j : first + j + 1, :]
        column = jnp.sum(mains[j] * mine, axis=1, keepdims=True)
        last = jnp.sum(tails[first + j : first + j + 1, :] * mine, axis=1, keepdims=True)
        block[j, main:, width:] = jnp.where(lane < LANES // 2, column, last).astype(BF16)
        copies.append(start(block.at[j], out_refs[j], sems.at[j]))
    for copy in copies:
        copy.wait()


def slice_kernel(place_ref, *refs):
    blocks, parts = 4, 4
    in_refs, (keep_ref, near_ref, far_ref, weight_ref) = refs[:blocks], refs[blocks : blocks + 4]
    held, sliced, fold, sems, out_sems = refs[blocks + 4 :]
    main = held.shape[1] // 2
    depth = sliced.shape[2] // 2
    width = parts * depth
    chunks = width // LANES
    copies = [start(in_refs[i], held.at[i], sems.at[i]) for i in range(blocks)]
    lane = lax.broadcasted_iota(jnp.int32, (1, LANES), 1)
    lasts = []
    for i in range(blocks):
        copies[i].wait()
        for j in range(parts):
            columns = pl.ds(pl.multiple_of(place_ref[j] * depth, depth), depth)
            for side in range(2):
                sliced[j, main * i : main * (i + 1), side * depth : (side + 1) * depth] = held[
                    i, side * main : (side + 1) * main, columns
                ]
        for side in range(2):
            fold[side, chunks * i : chunks * (i + 1), :] = held[
                i, side * chunks : (side + 1) * chunks, width:
            ].astype(F32)
        weights = held[i, main:, width:].astype(F32)
        weight_ref[main * i : main * (i + 1), :] = weights
        last = jnp.sum(jnp.where(lane == LANES - 1, weights[0:1, :], 0.0), axis=1, keepdims=True)
        lasts.append(jnp.broadcast_to(last, (1, LANES)))
    weight_ref[main * blocks :, :] = jnp.concatenate(lasts + [jnp.zeros((16 - blocks, LANES), F32)], axis=0)
    each = chunks // parts
    for j in range(parts):
        for side in range(2):
            for q in range(each):
                tail = fold[side, pl.ds(place_ref[j] * each + q, blocks, stride=chunks), :]
                tail = jnp.concatenate([tail, jnp.zeros((16 - blocks, LANES), F32)], axis=0).astype(BF16)
                at = side * depth + q * LANES
                sliced[j, main * blocks :, at : at + LANES] = tail
    targets = [keep_ref, near_ref, far_ref.at[:, pl.ds(0, 2 * depth)], far_ref.at[:, pl.ds(2 * depth, 2 * depth)]]
    copies = [start(sliced.at[j], targets[j], out_sems.at[j]) for j in range(parts)]
    for copy in copies:
        copy.wait()


def main_kernel(early, place_ref, w_ref, *refs):
    blocks, parts = 4, 4
    weights = refs[:parts]
    keep_ref, near_ref, far_ref = refs[parts : parts + 3]
    x, dy, mid, back, tail, fold, sems, out_sems = refs[-8:]
    mid_ref, back_refs = refs[-9 - blocks], refs[-8 - blocks : -8]
    width = x.shape[1]
    depth = width // parts
    row_refs = [keep_ref, near_ref, far_ref.at[:, pl.ds(0, 2 * depth)], far_ref.at[:, pl.ds(2 * depth, 2 * depth)]]
    hidden_width = mid.shape[1] // 3
    main = back.shape[1]
    chunks = width // LANES
    total = x.shape[0]
    loads = []
    for j in range(parts):
        at = pl.ds(j * depth, depth)
        loads.append(start(row_refs[j].at[:, pl.ds(0, depth)], x.at[:, at], sems.at[0, j]))
        loads.append(start(row_refs[j].at[:, pl.ds(depth, depth)], dy.at[:, at], sems.at[1, j]))
    if early:
        start(refs[parts + 3], mid.at[pl.ds(0, early)], sems.at[2, 0]).wait()
    pre = jnp.zeros((total, 2 * hidden_width), F32)
    grad = jnp.zeros((total, hidden_width), F32)
    for j in range(parts):
        at = slice(j * depth, (j + 1) * depth)
        loads.pop(0).wait()
        pre += dot(x[:, at], weights[j][:, : 2 * hidden_width])
        loads.pop(0).wait()
        grad += dot(dy[:, at], weights[j][:, 2 * hidden_width :])
    weight = w_ref[:, 0:1]
    gate_pre = pre[:, :hidden_width]
    up_pre = pre[:, hidden_width:]
    sig = jax.nn.sigmoid(gate_pre)
    act = gate_pre * sig
    hidden = (act * up_pre).astype(BF16).astype(F32)
    route = jnp.sum(hidden * grad, axis=1, keepdims=True)
    grad_hidden = weight * grad
    grad_gate = grad_hidden * up_pre * sig * (1.0 + gate_pre * (1.0 - sig))
    mid[early:, :hidden_width] = grad_gate.astype(BF16)
    mid[early:, hidden_width : 2 * hidden_width] = (grad_hidden * act).astype(BF16)
    mid[early:, 2 * hidden_width :] = (weight * hidden).astype(BF16)
    copies = [start(mid, mid_ref, out_sems.at[blocks])]
    for j in range(parts):
        columns = pl.ds(pl.multiple_of(place_ref[j] * depth, depth), depth)
        part = dot_nt(mid[early:, : 2 * hidden_width], weights[j][:, : 2 * hidden_width])
        tail[:, columns] = part[main * blocks :]
        part = part.astype(BF16)
        for i in range(blocks):
            back[i, :, columns] = part[main * i : main * (i + 1)]
    row = lax.broadcasted_iota(jnp.int32, (main, LANES), 0)
    lane = lax.broadcasted_iota(jnp.int32, (main, LANES), 1)
    for i in range(blocks):
        for c in range(chunks):
            fold[c : c + 1, :] = tail[i : i + 1, LANES * c : LANES * (c + 1)]
        back[i, :chunks, width:] = fold[...].astype(BF16)
        mine = jnp.where(row == lane, route[main * i : main * (i + 1)], 0.0)
        mine = jnp.sum(mine, axis=0, keepdims=True)
        mine = jnp.where(lane[0:1] == main, route[main * blocks + i : main * blocks + i + 1], mine)
        back[i, chunks:, width:] = jnp.broadcast_to(mine, (main - chunks, LANES)).astype(BF16)
        copies.append(start(back.at[i], back_refs[i], out_sems.at[i]))
    for copy in copies:
        copy.wait()


def unpack_sum(weight, block_refs, held, rows, fold, sems):
    count = len(block_refs)
    main = held.shape[1]
    width = rows.shape[1]
    chunks = width // LANES
    copies = [start(block_refs[j], held.at[j], sems.at[j]) for j in range(count)]
    mains, tails = picks(weight, main)
    mains = mains[:count]
    pick = jnp.concatenate(mains + [tails, jnp.zeros_like(tails)], axis=0).astype(BF16)
    lane = lax.broadcasted_iota(jnp.int32, (1, LANES), 1)
    routes = []
    for j in range(count):
        copies[j].wait()
        rows[main * j : main * (j + 1), :] = held[j, :, :width]
        fold[chunks * j : chunks * (j + 1), :] = held[j, :chunks, width:].astype(F32)
        mine = held[j, chunks:, width:].astype(F32)
        dense = dot(mine[:, :main].astype(BF16), mains[j].astype(BF16))[0:1, :]
        last = jnp.sum(jnp.where(lane == main, mine[0:1, :], 0.0), axis=1, keepdims=True)
        routes.append(dense + last * tails[j : j + 1, :])
    for c in range(chunks):
        tail = fold[pl.ds(c, count, stride=chunks), :]
        tail = jnp.concatenate([tail, jnp.zeros((16 - count, LANES), F32)], axis=0).astype(BF16)
        rows[main * count :, LANES * c : LANES * (c + 1)] = tail
    return dot_tn(pick, rows[...]), routes


def relay_sum_kernel(joint_ref, b0, b1, b2, b3, out_ref, given, held, rows, fold, total, sems):
    tokens, width = total.shape[0], rows.shape[1]
    start(joint_ref.at[pl.ds(tokens, 16), pl.ds(0, LANES)], given, sems.at[4]).wait()
    weight = given[...].astype(F32)[0:8, :tokens]
    summed, routes = unpack_sum(weight, (b0, b1, b2, b3), held, rows, fold, sems)
    total[:, :width] = summed.astype(BF16)
    total[:, width:] = jnp.zeros((tokens, LANES), BF16)
    block = jnp.concatenate(routes + [jnp.zeros((12, tokens), F32)], axis=0).astype(BF16)
    total[0:16, width : width + tokens] = block
    start(total, out_ref, sems.at[4]).wait()


def combine_kernel(peer_ref, w_ref, named_ref, b0, b1, b2, b3, far_ref, grad_ref, route_ref, far, held, rows, fold, sems):
    width = grad_ref.shape[1]
    tokens = grad_ref.shape[0]
    copy = start(far_ref, far, sems.at[4])
    summed, routes = unpack_sum(w_ref[...], (b0, b1, b2, b3), held, rows, fold, sems)
    copy.wait()
    grad_ref[...] = (summed + far[:, :width].astype(F32)).astype(BF16)
    others = far[0:16, width : width + tokens].astype(F32)
    named = named_ref[...]
    route = jnp.zeros(route_ref.shape, F32)
    for j in range(4):
        route = route + jnp.where(named == peer_ref[j], routes[j], 0.0)
        route = route + jnp.where(named == peer_ref[4 + j], others[j : j + 1, :], 0.0)
    route_ref[...] = route.astype(BF16)


def weight_kernel(keep_a, keep_b, near_ref, far_a, far_b, mid_ref, mid_near_ref, mid_far_ref, in_ref, out_ref, rows, mids, sems):
    depth, hidden_width = out_ref.shape
    count = keep_a.shape[0]
    span, other = pl.ds(0, 2 * depth), pl.ds(2 * depth, 2 * depth)
    copies = []
    row_refs = [keep_a, keep_b, near_ref.at[:, span], far_a.at[:, span], far_b.at[:, span], near_ref.at[:, other]]
    at = 0
    for i, ref in enumerate(row_refs):
        copies.append(start(ref, rows.at[pl.ds(at, ref.shape[0])], sems.at[0, i]))
        at += ref.shape[0]
    both = 2 * count
    mid_refs = [mid_ref, mid_near_ref.at[pl.ds(0, both)], mid_far_ref, mid_near_ref.at[pl.ds(both, both)]]
    for j, ref in enumerate(mid_refs):
        copies.append(start(ref, mids.at[pl.ds(both * j, both)], sems.at[1, j]))
    for copy in copies:
        copy.wait()
    in_ref[...] = dot_tn(rows[:, :depth], mids[:, : 2 * hidden_width])
    out_ref[...] = dot_tn(rows[:, depth:], mids[:, 2 * hidden_width :])


def call(kernel, outs, smem, vmem, hbm, scratch, flops, hbm_outs, mib=20, aliases=None):
    on_vmem = pl.BlockSpec(memory_space=pltpu.VMEM)
    on_hbm = pl.BlockSpec(memory_space=pltpu.HBM)
    on_smem = pl.BlockSpec(memory_space=pltpu.SMEM)
    outs = [jax.ShapeDtypeStruct(shape, kind) for shape, kind in outs]
    moved = sum(a.size * a.dtype.itemsize for a in list(vmem) + list(hbm) + outs)
    return pl.pallas_call(
        kernel,
        out_shape=tuple(outs),
        in_specs=[on_smem] * len(smem) + [on_vmem] * len(vmem) + [on_hbm] * len(hbm),
        out_specs=tuple([on_hbm] * hbm_outs + [on_vmem] * (len(outs) - hbm_outs)),
        scratch_shapes=scratch,
        compiler_params=pltpu.CompilerParams(vmem_limit_bytes=mib * 1024 * 1024),
        cost_estimate=pl.CostEstimate(flops=flops, bytes_accessed=moved, transcendentals=0),
        input_output_aliases=aliases or {},
    )(*smem, *vmem, *hbm)


def swap(value, axis, mask):
    return lax.ppermute(value, axis, [(i, i ^ mask) for i in range(lax.axis_size(axis))])


def on_device_packed(tokens, grad_out, route_expert, route_weight, gate_up_weight, down_weight):
    token_count, width = tokens.shape
    blocks, parts, half = 8, 4, 4
    hidden_width = down_weight.shape[2]
    depth = width // parts
    chunks = width // LANES
    main = block_rows(token_count, route_expert.shape[1], blocks) // 16 * 16
    rows = main * half + 16

    peers = lax.axis_index("expert") ^ jnp.arange(blocks, dtype=jnp.int32)
    places = lax.axis_index("dp") ^ jnp.arange(parts, dtype=jnp.int32)
    named = route_expert.T
    far_tokens = swap(tokens, "expert", half)
    joint, dense = call(
        route_kernel,
        [((token_count + 16, width), BF16), ((blocks, token_count), F32)],
        [peers],
        [named, route_weight.T],
        [grad_out],
        [pltpu.VMEM((token_count + 16, width), BF16), pltpu.SemaphoreType.DMA((2,))],
        0,
        1,
    )
    far_joint = swap(joint, "expert", half)

    def stack(own, far, after):
        (joined,) = call(
            stack_kernel,
            [((2 * own.shape[0], own.shape[1]), BF16)],
            [],
            [],
            [own, far, after],
            [pltpu.VMEM((2 * own.shape[0], own.shape[1]), BF16), pltpu.SemaphoreType.DMA((2,))],
            0,
            1,
        )
        return joined

    def pack(first, x, value, after):
        packed = call(
            functools.partial(pack_kernel, first),
            [((2 * main, width + LANES), BF16)] * half,
            [],
            [],
            [x, value, *after],
            [
                pltpu.VMEM((token_count, width), BF16),
                pltpu.VMEM((token_count + 16, width), BF16),
                pltpu.VMEM((half, 2 * main, width + LANES), BF16),
                pltpu.VMEM((chunks, LANES), F32),
                pltpu.SemaphoreType.DMA((half + 3,)),
            ],
            4 * (half * main + 16) * token_count * width,
            half,
        )
        return [packed[0]] + [swap(packed[j], "expert", j) for j in range(1, half)]

    own = pack(half, tokens, joint, [])
    weights, again = call(
        join_kernel,
        [((depth, 3 * hidden_width), BF16)] * 2,
        [],
        [],
        [gate_up_weight[0], down_weight[0]],
        [pltpu.VMEM((depth, 3 * hidden_width), BF16), pltpu.SemaphoreType.DMA((2,))],
        0,
        2,
    )
    far_weights = swap(weights, "dp", 2)
    far = pack(0, far_tokens, far_joint, own[1:])

    again, far_weights = call(
        after_kernel,
        [(again.shape, BF16), (far_weights.shape, BF16)],
        [],
        [],
        [again, far_weights, far[0]],
        [],
        0,
        2,
        aliases={0: 0, 1: 1},
    )
    weight_parts = [again, swap(again, "dp", 1), far_weights, swap(far_weights, "dp", 1)]

    def sliced(packed):
        return call(
            slice_kernel,
            [
                ((rows, 2 * depth), BF16),
                ((rows, 2 * depth), BF16),
                ((rows, 4 * depth), BF16),
                ((rows, LANES), F32),
            ],
            [places],
            [],
            packed,
            [
                pltpu.VMEM((half, 2 * main, width + LANES), BF16),
                pltpu.VMEM((parts, rows, 2 * depth), BF16),
                pltpu.VMEM((2, half * chunks, LANES), F32),
                pltpu.SemaphoreType.DMA((half,)),
                pltpu.SemaphoreType.DMA((parts,)),
            ],
            0,
            3,
        )

    def middle(slices, weight, before):
        early = before[0].shape[0] if before else 0
        return call(
            functools.partial(main_kernel, early),
            [((early + rows, 3 * hidden_width), BF16)] + [((main, width + LANES), BF16)] * half,
            [places],
            [weight, *weight_parts],
            [*slices, *before],
            [
                pltpu.VMEM((rows, width), BF16),
                pltpu.VMEM((rows, width), BF16),
                pltpu.VMEM((early + rows, 3 * hidden_width), BF16),
                pltpu.VMEM((half, main, width + LANES), BF16),
                pltpu.VMEM((16, width), F32),
                pltpu.VMEM((chunks, LANES), F32),
                pltpu.SemaphoreType.DMA((3, parts)),
                pltpu.SemaphoreType.DMA((half + 1,)),
            ],
            2 * rows * width * 5 * hidden_width,
            1 + half,
        )

    *own_slices, own_weight = sliced(own)
    own_far = swap(own_slices[2], "dp", 2)
    own_mid, *near_back = middle(own_slices, own_weight, [])
    *far_slices, far_weight = sliced(far)
    far_far = swap(far_slices[2], "dp", 2)
    mid, *far_back = middle(far_slices, far_weight, [own_mid])
    sum_scratch = [
        pltpu.VMEM((half, main, width + LANES), BF16),
        pltpu.VMEM((half * main + 16, width), BF16),
        pltpu.VMEM((half * chunks, LANES), F32),
    ]
    far_back = far_back[:1] + [swap(far_back[j], "expert", j) for j in range(1, half)]
    (partial,) = call(
        relay_sum_kernel,
        [((token_count, width + LANES), BF16)],
        [],
        [],
        [far_joint, *far_back],
        [pltpu.VMEM((16, LANES), BF16)]
        + sum_scratch
        + [pltpu.VMEM((token_count, width + LANES), BF16), pltpu.SemaphoreType.DMA((half + 1,))],
        2 * (half * main + 16) * width * token_count,
        1,
    )
    far_partial = swap(partial, "expert", half)
    near_back = near_back[:1] + [swap(near_back[j], "expert", j) for j in range(1, half)]
    near_rows, mid = call(
        relay_kernel,
        [((2 * rows, 4 * depth), BF16), (mid.shape, BF16)],
        [],
        [],
        [own_slices[1], own_far, far_slices[1], far_far, partial, mid],
        [pltpu.VMEM((2 * rows, 4 * depth), BF16), pltpu.SemaphoreType.DMA((4,))],
        0,
        2,
        aliases={5: 1},
    )
    mid_far = swap(mid, "dp", 2)
    near_rows = swap(near_rows, "dp", 1)
    grad_tokens, grad_route = call(
        combine_kernel,
        [((token_count, width), BF16), (named.shape, BF16)],
        [peers],
        [dense, named],
        [*near_back, far_partial],
        [pltpu.VMEM((token_count, width + LANES), BF16)] + sum_scratch + [pltpu.SemaphoreType.DMA((half + 1,))],
        2 * (half * main + 16) * width * token_count,
        0,
    )
    mid_near = swap(stack(mid, mid_far, grad_route), "dp", 1)
    grad_gate_up, grad_down = call(
        weight_kernel,
        [((depth, 2 * hidden_width), F32), ((depth, hidden_width), F32)],
        [],
        [],
        [own_slices[0], far_slices[0], near_rows, own_far, far_far, mid, mid_near, mid_far],
        [
            pltpu.VMEM((2 * parts * rows, 2 * depth), BF16),
            pltpu.VMEM((2 * parts * rows, 3 * hidden_width), BF16),
            pltpu.SemaphoreType.DMA((2, 6)),
        ],
        4 * parts * rows * depth * 3 * hidden_width,
        0,
    )
    return (grad_tokens, grad_route.T, grad_gate_up[None], grad_down[None])


def block_rows(token_count, route_count, expert_total):
    return min(token_count, (token_count * route_count + expert_total - 1) // expert_total + 1)


def to_local(rows, group_count, local_count, capacity):
    tail = rows.shape[2:]
    shaped = rows.reshape((group_count, local_count, capacity) + tail)
    shaped = jnp.swapaxes(shaped, 0, 1)
    return shaped.reshape((local_count, group_count * capacity) + tail)


def to_groups(rows, group_count, local_count, capacity):
    tail = rows.shape[2:]
    shaped = rows.reshape((local_count, group_count, capacity) + tail)
    shaped = jnp.swapaxes(shaped, 0, 1)
    return shaped.reshape((group_count, local_count * capacity) + tail)


def on_device_routed(tokens, grad_out, route_expert, route_weight, gate_up_weight, down_weight):
    token_count, model_width = tokens.shape
    route_count = route_expert.shape[1]
    group_count = lax.axis_size("expert")
    local_count = gate_up_weight.shape[0]
    hidden_width = down_weight.shape[2]
    expert_total = local_count * group_count
    capacity = min(token_count, (token_count * route_count + expert_total - 1) // expert_total + 1)
    slot_total = expert_total * capacity
    flat_expert = route_expert.reshape(-1)
    expert_ids = jnp.arange(expert_total, dtype=jnp.int32)
    onehot = (flat_expert[:, None] == expert_ids[None, :]).astype(jnp.int32)
    before = jnp.cumsum(onehot, axis=0) - onehot
    rank = jnp.sum(before * onehot, axis=1)
    slot_of = flat_expert * capacity + rank
    slot_ids = jnp.arange(slot_total, dtype=jnp.int32)
    placed = slot_ids[:, None] == slot_of[None, :]
    by_token = jnp.any(placed.reshape(slot_total, token_count, route_count), axis=2).astype(
        jnp.bfloat16
    )
    send_x = jnp.dot(by_token, tokens, preferred_element_type=jnp.float32).astype(jnp.bfloat16)
    send_dy = jnp.dot(by_token, grad_out, preferred_element_type=jnp.float32).astype(jnp.bfloat16)
    flat_weight = route_weight.reshape(-1).astype(jnp.float32)
    send_w = jnp.sum(jnp.where(placed, flat_weight[None, :], 0.0), axis=1).astype(jnp.bfloat16)
    recv_x, recv_dy, recv_w = (
        lax.all_to_all(
            send_x.reshape(group_count, local_count * capacity, model_width),
            "expert",
            split_axis=0,
            concat_axis=0,
            tiled=True,
        ),
        lax.all_to_all(
            send_dy.reshape(group_count, local_count * capacity, model_width),
            "expert",
            split_axis=0,
            concat_axis=0,
            tiled=True,
        ),
        lax.all_to_all(
            send_w.reshape(group_count, local_count * capacity),
            "expert",
            split_axis=0,
            concat_axis=0,
            tiled=True,
        ),
    )
    rows_x = to_local(recv_x, group_count, local_count, capacity)
    rows_dy = to_local(recv_dy, group_count, local_count, capacity)
    rows_w = to_local(recv_w, group_count, local_count, capacity)
    full_in, full_out = (
        lax.all_gather(gate_up_weight, "dp", axis=1, tiled=True),
        lax.all_gather(down_weight, "dp", axis=1, tiled=True),
    )
    pre = jnp.einsum("erd,edf->erf", rows_x, full_in, preferred_element_type=jnp.float32)
    gate_pre = pre[:, :, :hidden_width]
    up_pre = pre[:, :, hidden_width:]
    act = swish(gate_pre)
    hidden = (act * up_pre).astype(jnp.bfloat16)
    expert_out = jnp.einsum("erf,edf->erd", hidden, full_out, preferred_element_type=jnp.float32)
    route_grad = jnp.sum(rows_dy.astype(jnp.float32) * expert_out, axis=2).astype(jnp.bfloat16)
    scaled = (rows_w.astype(jnp.float32)[:, :, None] * rows_dy).astype(jnp.bfloat16)
    grad_hidden = jnp.einsum("erd,edf->erf", scaled, full_out, preferred_element_type=jnp.float32)
    sig = jax.nn.sigmoid(gate_pre)
    grad_gate = grad_hidden * up_pre * sig * (1.0 + gate_pre * (1.0 - sig))
    grad_up = grad_hidden * act
    grad_pre = jnp.concatenate([grad_gate, grad_up], axis=2).astype(jnp.bfloat16)
    rows_grad = jnp.einsum(
        "erf,edf->erd", grad_pre, full_in, preferred_element_type=jnp.float32
    ).astype(jnp.bfloat16)
    back_x, back_w = (
        lax.all_to_all(
            to_groups(rows_grad, group_count, local_count, capacity),
            "expert",
            split_axis=0,
            concat_axis=0,
            tiled=True,
        ),
        lax.all_to_all(
            to_groups(route_grad, group_count, local_count, capacity),
            "expert",
            split_axis=0,
            concat_axis=0,
            tiled=True,
        ),
    )
    back_x = back_x.reshape(slot_total, model_width)
    back_w = back_w.reshape(slot_total).astype(jnp.float32)
    grad_tokens = jnp.einsum(
        "st,sd->td", by_token, back_x, preferred_element_type=jnp.float32
    ).astype(jnp.bfloat16)
    grad_route = jnp.sum(jnp.where(placed, back_w[:, None], 0.0), axis=0)
    grad_route = grad_route.reshape(token_count, route_count).astype(jnp.bfloat16)
    all_x = lax.all_to_all(rows_x, "dp", split_axis=2, concat_axis=1, tiled=True)
    grad_gate_up = jnp.einsum(
        "erd,erf->edf",
        all_x,
        lax.all_gather(grad_pre, "dp", axis=1, tiled=True),
        preferred_element_type=jnp.float32,
    )
    summed = lax.psum_scatter(
        jnp.einsum("erd,erf->def", scaled, hidden, preferred_element_type=jnp.float32),
        "dp",
        scatter_dimension=0,
        tiled=True,
    )
    grad_down = jnp.swapaxes(summed, 0, 1)
    return (grad_tokens, grad_route, grad_gate_up, grad_down)


def packs(tokens, route_expert, down_weight):
    chunks = tokens.shape[1] // LANES
    capacity = block_rows(tokens.shape[0], route_expert.shape[1], lax.axis_size("expert"))
    return (
        lax.axis_size("expert") == 8
        and lax.axis_size("dp") == 4
        and down_weight.shape[0] == 1
        and capacity % 16 <= 1
        and chunks == 16
        and 2 * chunks <= capacity < LANES // 2
    )


def solution(mesh):
    def on_device(*arrays):
        if packs(arrays[0], arrays[2], arrays[5]):
            return on_device_packed(*arrays)
        return on_device_routed(*arrays)

    return jax.shard_map(
        on_device,
        mesh=mesh,
        in_specs=(
            P(("expert", "dp"), None),
            P(("expert", "dp"), None),
            P(("expert", "dp"), None),
            P(("expert", "dp"), None),
            P("expert", "dp", None),
            P("expert", "dp", None),
        ),
        out_specs=(
            P(("expert", "dp"), None),
            P(("expert", "dp"), None),
            P("expert", "dp", None),
            P("expert", "dp", None),
        ),
        check_vma=False,
    )
```

```python
import functools

import jax
import jax.numpy as jnp
from jax import lax
from jax.experimental import pallas as pl
from jax.experimental.pallas import tpu as pltpu
from jax.sharding import PartitionSpec as P

BF16 = jnp.bfloat16
F32 = jnp.float32
LANES = 128


def swish(value):
    return value * jax.nn.sigmoid(value)


def dot(a, b):
    return jnp.dot(a, b, preferred_element_type=F32)


def dot_nt(a, b):
    return lax.dot_general(a, b, (((1,), (1,)), ((), ())), preferred_element_type=F32)


def dot_tn(a, b):
    return lax.dot_general(a, b, (((0,), (0,)), ((), ())), preferred_element_type=F32)


def picks(weight, main):
    token_count = weight.shape[1]
    routed = weight != 0.0
    first = lax.broadcasted_iota(jnp.int32, (token_count, token_count), 0)
    second = lax.broadcasted_iota(jnp.int32, (token_count, token_count), 1)
    upper = (first < second).astype(F32).astype(BF16)
    rank = dot(routed.astype(F32).astype(BF16), upper)
    rank = jnp.where(routed, rank, -1.0).astype(jnp.int32)
    slots = lax.broadcasted_iota(jnp.int32, (main, token_count), 0)
    mains = [(slots == rank[i : i + 1, :]).astype(F32) for i in range(weight.shape[0])]
    tails = (rank == main).astype(F32)
    return mains, tails


def route_kernel(peer_ref, named_ref, given_ref, x_ref, dy_ref, joint_ref, dense_ref):
    count, width = x_ref.shape
    named = named_ref[...]
    given = given_ref[...].astype(F32)
    experts = dense_ref.shape[0]
    lines = [
        jnp.sum(jnp.where(named == peer_ref[i], given, 0.0), axis=0, keepdims=True) for i in range(experts)
    ]
    dense = jnp.concatenate(lines, axis=0)
    dense_ref[...] = dense
    turned = jnp.concatenate(lines[experts // 2 :] + lines[: experts // 2] + [jnp.zeros_like(dense)], axis=0)
    joint_ref[0:count, :width] = x_ref[...]
    joint_ref[count:, :width] = dy_ref[...]
    joint_ref[:, width:] = jnp.zeros((2 * count, LANES), BF16)
    joint_ref[0:16, width : width + count] = turned.astype(BF16)


def join_kernel(in_ref, out_ref, after_ref, joint_ref, again_ref):
    width = in_ref.shape[1]
    for target in (joint_ref, again_ref):
        target[:, :width] = in_ref[...]
        target[:, width:] = out_ref[...]


def after_kernel(*refs):
    pass


def relay_kernel(near_a, far_a, near_b, far_b, mid_ref, mid_out_ref, joint_ref):
    count, width = near_a.shape
    for at, near, far in ((0, near_a, far_a), (count, near_b, far_b)):
        joint_ref[at : at + count, :width] = near[...]
        joint_ref[at : at + count, width:] = far[:, width:]


def pack_kernel(first, joint_ref, *refs):
    count = 4
    out_refs, fold = refs[-1 - count : -1], refs[-1]
    tokens, width = joint_ref.shape[0] // 2, joint_ref.shape[1] - LANES
    chunks = width // LANES
    main = out_refs[0].shape[0] // 2
    weight = joint_ref[0:16, width:].astype(F32)[0:8, :tokens]
    mains, tails = picks(weight, main)
    mains = mains[first : first + count]
    pick = jnp.concatenate(mains + [tails, jnp.zeros_like(tails)], axis=0).astype(BF16)
    lane = lax.broadcasted_iota(jnp.int32, (main, LANES), 1)
    for at, base, low in ((0, 0, 0), (tokens, main, chunks)):
        rows = dot(pick, joint_ref[at : at + tokens, :width])
        for j in range(count):
            out_refs[j][base : base + main, :width] = rows[main * j : main * (j + 1)].astype(BF16)
            line = main * count + first + j
            for c in range(chunks):
                fold[c : c + 1, :] = rows[line : line + 1, LANES * c : LANES * (c + 1)]
            out_refs[j][low : low + chunks, width:] = fold[...].astype(BF16)
    for j in range(count):
        mine = weight[first + j : first + j + 1, :]
        column = jnp.sum(mains[j] * mine, axis=1, keepdims=True)
        last = jnp.sum(tails[first + j : first + j + 1, :] * mine, axis=1, keepdims=True)
        out_refs[j][main:, width:] = jnp.where(lane < LANES // 2, column, last).astype(BF16)


def slice_kernel(place_ref, *refs):
    blocks, parts = 4, 4
    in_refs, (keep_ref, near_ref, far_ref, weight_ref, fold) = refs[:blocks], refs[-5:]
    main = in_refs[0].shape[0] // 2
    depth = keep_ref.shape[1] // 2
    width = parts * depth
    chunks = width // LANES
    targets = [(keep_ref, 0), (near_ref, 0), (far_ref, 0), (far_ref, 2 * depth)]
    lane = lax.broadcasted_iota(jnp.int32, (1, LANES), 1)
    lasts = []
    for i in range(blocks):
        for j, (target, shift) in enumerate(targets):
            columns = pl.ds(pl.multiple_of(place_ref[j] * depth, depth), depth)
            for side in range(2):
                at = shift + side * depth
                target[main * i : main * (i + 1), at : at + depth] = in_refs[i][
                    side * main : (side + 1) * main, columns
                ]
        for side in range(2):
            fold[side, chunks * i : chunks * (i + 1), :] = in_refs[i][
                side * chunks : (side + 1) * chunks, width:
            ].astype(F32)
        weights = in_refs[i][main:, width:].astype(F32)
        weight_ref[main * i : main * (i + 1), :] = weights
        last = jnp.sum(jnp.where(lane == LANES - 1, weights[0:1, :], 0.0), axis=1, keepdims=True)
        lasts.append(jnp.broadcast_to(last, (1, LANES)))
    weight_ref[main * blocks :, :] = jnp.concatenate(lasts + [jnp.zeros((16 - blocks, LANES), F32)], axis=0)
    each = chunks // parts
    for j, (target, shift) in enumerate(targets):
        for side in range(2):
            for q in range(each):
                tail = fold[side, pl.ds(place_ref[j] * each + q, blocks, stride=chunks), :]
                tail = jnp.concatenate([tail, jnp.zeros((16 - blocks, LANES), F32)], axis=0).astype(BF16)
                at = shift + side * depth + q * LANES
                target[main * blocks :, at : at + LANES] = tail


def main_kernel(early, place_ref, w_ref, *refs):
    blocks, parts = 4, 4
    weights = refs[:parts]
    keep_ref, near_ref, far_ref = refs[parts : parts + 3]
    mid, backs, (tail, fold) = refs[-3 - blocks], refs[-2 - blocks : -2], refs[-2:]
    depth = keep_ref.shape[1] // 2
    width = parts * depth
    hidden_width = mid.shape[1] // 3
    main = backs[0].shape[0]
    chunks = width // LANES
    total = keep_ref.shape[0]
    pre = jnp.zeros((total, 2 * hidden_width), F32)
    grad = jnp.zeros((total, hidden_width), F32)
    for j, (ref, shift) in enumerate([(keep_ref, 0), (near_ref, 0), (far_ref, 0), (far_ref, 2 * depth)]):
        pre += dot(ref[:, shift : shift + depth], weights[j][:, : 2 * hidden_width])
        grad += dot(ref[:, shift + depth : shift + 2 * depth], weights[j][:, 2 * hidden_width :])
    if early:
        mid[0:early, :] = refs[parts + 3][...]
    weight = w_ref[:, 0:1]
    gate_pre = pre[:, :hidden_width]
    up_pre = pre[:, hidden_width:]
    sig = jax.nn.sigmoid(gate_pre)
    act = gate_pre * sig
    hidden = (act * up_pre).astype(BF16).astype(F32)
    route = jnp.sum(hidden * grad, axis=1, keepdims=True)
    grad_hidden = weight * grad
    grad_gate = grad_hidden * up_pre * sig * (1.0 + gate_pre * (1.0 - sig))
    mid[early:, :hidden_width] = grad_gate.astype(BF16)
    mid[early:, hidden_width : 2 * hidden_width] = (grad_hidden * act).astype(BF16)
    mid[early:, 2 * hidden_width :] = (weight * hidden).astype(BF16)
    for j in range(parts):
        columns = pl.ds(pl.multiple_of(place_ref[j] * depth, depth), depth)
        part = dot_nt(mid[early:, : 2 * hidden_width], weights[j][:, : 2 * hidden_width])
        tail[:, columns] = part[main * blocks :]
        part = part.astype(BF16)
        for i in range(blocks):
            backs[i][:, columns] = part[main * i : main * (i + 1)]
    row = lax.broadcasted_iota(jnp.int32, (main, LANES), 0)
    lane = lax.broadcasted_iota(jnp.int32, (main, LANES), 1)
    for i in range(blocks):
        for c in range(chunks):
            fold[c : c + 1, :] = tail[i : i + 1, LANES * c : LANES * (c + 1)]
        backs[i][:chunks, width:] = fold[...].astype(BF16)
        mine = jnp.where(row == lane, route[main * i : main * (i + 1)], 0.0)
        mine = jnp.sum(mine, axis=0, keepdims=True)
        mine = jnp.where(lane[0:1] == main, route[main * blocks + i : main * blocks + i + 1], mine)
        backs[i][chunks:, width:] = jnp.broadcast_to(mine, (main - chunks, LANES)).astype(BF16)


def unpack_sum(weight, block_refs, rows, fold):
    count = len(block_refs)
    main = block_refs[0].shape[0]
    width = rows.shape[1]
    chunks = width // LANES
    mains, tails = picks(weight, main)
    mains = mains[:count]
    pick = jnp.concatenate(mains + [tails, jnp.zeros_like(tails)], axis=0).astype(BF16)
    lane = lax.broadcasted_iota(jnp.int32, (1, LANES), 1)
    routes = []
    for j in range(count):
        rows[main * j : main * (j + 1), :] = block_refs[j][:, :width]
        fold[chunks * j : chunks * (j + 1), :] = block_refs[j][:chunks, width:].astype(F32)
        mine = block_refs[j][chunks:, width:].astype(F32)
        dense = dot(mine[:, :main].astype(BF16), mains[j].astype(BF16))[0:1, :]
        last = jnp.sum(jnp.where(lane == main, mine[0:1, :], 0.0), axis=1, keepdims=True)
        routes.append(dense + last * tails[j : j + 1, :])
    for c in range(chunks):
        tail = fold[pl.ds(c, count, stride=chunks), :]
        tail = jnp.concatenate([tail, jnp.zeros((16 - count, LANES), F32)], axis=0).astype(BF16)
        rows[main * count :, LANES * c : LANES * (c + 1)] = tail
    return dot_tn(pick, rows[...]), routes


def relay_sum_kernel(joint_ref, b0, b1, b2, b3, after_ref, out_ref, rows, fold):
    tokens, width = out_ref.shape[0], rows.shape[1]
    weight = joint_ref[0:16, width:].astype(F32)[0:8, :tokens]
    summed, routes = unpack_sum(weight, (b0, b1, b2, b3), rows, fold)
    out_ref[:, :width] = summed.astype(BF16)
    out_ref[:, width:] = jnp.zeros((tokens, LANES), BF16)
    block = jnp.concatenate(routes + [jnp.zeros((12, tokens), F32)], axis=0).astype(BF16)
    out_ref[0:16, width : width + tokens] = block


def near_sum_kernel(w_ref, b0, b1, b2, b3, grad_ref, route_ref, rows, fold):
    summed, routes = unpack_sum(w_ref[...], (b0, b1, b2, b3), rows, fold)
    grad_ref[...] = summed
    route_ref[...] = jnp.concatenate(routes + [jnp.zeros_like(route) for route in routes], axis=0)


def combine_kernel(peer_ref, named_ref, near_ref, near_route_ref, far_ref, grad_ref, route_ref):
    tokens, width = grad_ref.shape
    grad_ref[...] = (near_ref[...] + far_ref[:, :width].astype(F32)).astype(BF16)
    others = far_ref[0:16, width : width + tokens].astype(F32)
    named = named_ref[...]
    route = jnp.zeros(route_ref.shape, F32)
    for j in range(4):
        route = route + jnp.where(named == peer_ref[j], near_route_ref[j : j + 1, :], 0.0)
        route = route + jnp.where(named == peer_ref[4 + j], others[j : j + 1, :], 0.0)
    route_ref[...] = route.astype(BF16)


def weight_kernel(half, rows_a, rows_b, near_ref, mid_a, mid_b, *refs):
    in_ref, out_ref, rows, mids = refs[-4:]
    before = refs[:-4]
    depth, hidden_width = out_ref.shape
    count = rows_a.shape[0]
    rows[0:count, :] = rows_a[:, : 2 * depth]
    rows[count : 2 * count, :] = rows_b[:, : 2 * depth]
    rows[2 * count :, :] = near_ref[:, 2 * depth * half : 2 * depth * (half + 1)]
    mids[0 : 2 * count, :] = mid_a[...]
    mids[2 * count :, :] = mid_b[...]
    in_part = dot_tn(rows[:, :depth], mids[:, : 2 * hidden_width])
    out_part = dot_tn(rows[:, depth:], mids[:, 2 * hidden_width :])
    if before:
        in_part = in_part + before[0][...]
        out_part = out_part + before[1][...]
    in_ref[...] = in_part
    out_ref[...] = out_part


def call(kernel, outs, smem, vmem, either, scratch, flops, either_outs=0, aliases=None):
    on_vmem = pl.BlockSpec(memory_space=pltpu.VMEM)
    on_either = pl.BlockSpec(memory_space=pl.ANY)
    on_smem = pl.BlockSpec(memory_space=pltpu.SMEM)
    outs = [jax.ShapeDtypeStruct(shape, kind) for shape, kind in outs]
    moved = sum(a.size * a.dtype.itemsize for a in list(vmem) + outs[either_outs:])
    return pl.pallas_call(
        kernel,
        out_shape=tuple(outs),
        in_specs=[on_smem] * len(smem) + [on_vmem] * len(vmem) + [on_either] * len(either),
        out_specs=tuple([on_either] * either_outs + [on_vmem] * (len(outs) - either_outs)),
        scratch_shapes=scratch,
        compiler_params=pltpu.CompilerParams(vmem_limit_bytes=24 * 1024 * 1024),
        cost_estimate=pl.CostEstimate(flops=flops, bytes_accessed=moved, transcendentals=0),
        input_output_aliases=aliases or {},
    )(*smem, *vmem, *either)


def swap(value, axis, mask):
    return lax.ppermute(value, axis, [(i, i ^ mask) for i in range(lax.axis_size(axis))])


def on_device_packed(tokens, grad_out, route_expert, route_weight, gate_up_weight, down_weight):
    token_count, width = tokens.shape
    blocks, parts, half = 8, 4, 4
    hidden_width = down_weight.shape[2]
    depth = width // parts
    chunks = width // LANES
    main = block_rows(token_count, route_expert.shape[1], blocks) // 16 * 16
    rows = main * half + 16

    peers = lax.axis_index("expert") ^ jnp.arange(blocks, dtype=jnp.int32)
    places = lax.axis_index("dp") ^ jnp.arange(parts, dtype=jnp.int32)
    named = route_expert.T
    packed_shape = ((2 * main, width + LANES), BF16)
    back_shape = ((main, width + LANES), BF16)

    joint, dense = call(
        route_kernel,
        [((2 * token_count, width + LANES), BF16), ((blocks, token_count), F32)],
        [peers],
        [named, route_weight.T, tokens, grad_out],
        [],
        [],
        0,
    )
    far_joint = swap(joint, "expert", half)

    weights, again = call(
        join_kernel,
        [((depth, 3 * hidden_width), BF16)] * 2,
        [],
        [gate_up_weight[0], down_weight[0]],
        [dense],
        [],
        0,
    )
    far_weights = swap(weights, "dp", 2)

    def pack(first, value, after):
        packed = call(
            functools.partial(pack_kernel, first),
            [packed_shape] * half,
            [],
            [value],
            after,
            [pltpu.VMEM((chunks, LANES), F32)],
            4 * (half * main + 16) * token_count * width,
        )
        return [packed[0]] + [swap(packed[j], "expert", j) for j in range(1, half)]

    own = pack(half, joint, [])
    again, far_weights = call(
        after_kernel,
        [(again.shape, BF16), (far_weights.shape, BF16)],
        [],
        [],
        [again, far_weights, far_joint],
        [],
        0,
        2,
        {0: 0, 1: 1},
    )
    weight_parts = [again, swap(again, "dp", 1), far_weights, swap(far_weights, "dp", 1)]
    far = pack(0, far_joint, own[1:])

    def sliced(packed, after):
        return call(
            slice_kernel,
            [
                ((rows, 2 * depth), BF16),
                ((rows, 2 * depth), BF16),
                ((rows, 4 * depth), BF16),
                ((rows, LANES), F32),
            ],
            [places],
            packed,
            after,
            [pltpu.VMEM((2, half * chunks, LANES), F32)],
            0,
        )

    def middle(slices, weight, before, after):
        early = before[0].shape[0] if before else 0
        return call(
            functools.partial(main_kernel, early),
            [((early + rows, 3 * hidden_width), BF16)] + [back_shape] * half,
            [places],
            [weight, *weight_parts, *slices, *before],
            after,
            [pltpu.VMEM((16, width), F32), pltpu.VMEM((chunks, LANES), F32)],
            2 * rows * width * 5 * hidden_width,
        )

    *own_slices, own_weight = sliced(own, [])
    own_far = swap(own_slices[2], "dp", 2)
    own_mid, *near_back = middle(own_slices, own_weight, [], [])
    *far_slices, far_weight = sliced(far, [own_mid])
    far_far = swap(far_slices[2], "dp", 2)
    mid, *far_back = middle(far_slices, far_weight, [own_mid], [own_far])

    mid, near_rows = call(
        relay_kernel,
        [(mid.shape, BF16), ((2 * rows, 4 * depth), BF16)],
        [],
        [own_slices[1], own_far, far_slices[1], far_far],
        [mid],
        [],
        0,
        1,
        {4: 0},
    )
    mid_far = swap(mid, "dp", 2)
    mid_near = swap(mid, "dp", 1)

    sum_scratch = [
        pltpu.VMEM((half * main + 16, width), BF16),
        pltpu.VMEM((half * chunks, LANES), F32),
    ]
    sum_flops = 2 * (half * main + 16) * width * token_count
    far_back = far_back[:1] + [swap(far_back[j], "expert", j) for j in range(1, half)]
    (partial,) = call(
        relay_sum_kernel,
        [((token_count, width + LANES), BF16)],
        [],
        [far_joint, *far_back],
        [near_rows],
        sum_scratch,
        sum_flops,
    )
    far_partial = swap(partial, "expert", half)
    near_rows = swap(near_rows, "dp", 1)
    near_back = near_back[:1] + [swap(near_back[j], "expert", j) for j in range(1, half)]
    near_sum, near_route = call(
        near_sum_kernel,
        [((token_count, width), F32), ((blocks, token_count), F32)],
        [],
        [dense, *near_back],
        [],
        sum_scratch,
        sum_flops,
    )
    grad_tokens, grad_route = call(
        combine_kernel,
        [((token_count, width), BF16), (named.shape, BF16)],
        [peers],
        [named, near_sum, near_route, far_partial],
        [],
        [],
        0,
    )

    def weight_part(which, arrays, before):
        return call(
            functools.partial(weight_kernel, which),
            [((depth, 2 * hidden_width), F32), ((depth, hidden_width), F32)],
            [],
            [*arrays, *before],
            [],
            [pltpu.VMEM((4 * rows, 2 * depth), BF16), pltpu.VMEM((4 * rows, 3 * hidden_width), BF16)],
            2 * 4 * rows * depth * 3 * hidden_width,
        )

    first = weight_part(0, [own_slices[0], far_slices[0], near_rows, mid, mid_near], [])
    (mid_far,) = call(
        after_kernel,
        [(mid_far.shape, BF16)],
        [],
        [],
        [mid_far, first[1], far_partial],
        [],
        0,
        1,
        {0: 0},
    )
    grad_gate_up, grad_down = weight_part(
        1, [own_far, far_far, near_rows, mid_far, swap(mid_far, "dp", 1)], first
    )
    return (grad_tokens, grad_route.T, grad_gate_up[None], grad_down[None])


def block_rows(token_count, route_count, expert_total):
    return min(token_count, (token_count * route_count + expert_total - 1) // expert_total + 1)


def to_local(rows, group_count, local_count, capacity):
    tail = rows.shape[2:]
    shaped = rows.reshape((group_count, local_count, capacity) + tail)
    shaped = jnp.swapaxes(shaped, 0, 1)
    return shaped.reshape((local_count, group_count * capacity) + tail)


def to_groups(rows, group_count, local_count, capacity):
    tail = rows.shape[2:]
    shaped = rows.reshape((local_count, group_count, capacity) + tail)
    shaped = jnp.swapaxes(shaped, 0, 1)
    return shaped.reshape((group_count, local_count * capacity) + tail)


def on_device_routed(tokens, grad_out, route_expert, route_weight, gate_up_weight, down_weight):
    token_count, model_width = tokens.shape
    route_count = route_expert.shape[1]
    group_count = lax.axis_size("expert")
    local_count = gate_up_weight.shape[0]
    hidden_width = down_weight.shape[2]
    expert_total = local_count * group_count
    capacity = min(token_count, (token_count * route_count + expert_total - 1) // expert_total + 1)
    slot_total = expert_total * capacity
    flat_expert = route_expert.reshape(-1)
    expert_ids = jnp.arange(expert_total, dtype=jnp.int32)
    onehot = (flat_expert[:, None] == expert_ids[None, :]).astype(jnp.int32)
    before = jnp.cumsum(onehot, axis=0) - onehot
    rank = jnp.sum(before * onehot, axis=1)
    slot_of = flat_expert * capacity + rank
    slot_ids = jnp.arange(slot_total, dtype=jnp.int32)
    placed = slot_ids[:, None] == slot_of[None, :]
    by_token = jnp.any(placed.reshape(slot_total, token_count, route_count), axis=2).astype(
        jnp.bfloat16
    )
    send_x = jnp.dot(by_token, tokens, preferred_element_type=jnp.float32).astype(jnp.bfloat16)
    send_dy = jnp.dot(by_token, grad_out, preferred_element_type=jnp.float32).astype(jnp.bfloat16)
    flat_weight = route_weight.reshape(-1).astype(jnp.float32)
    send_w = jnp.sum(jnp.where(placed, flat_weight[None, :], 0.0), axis=1).astype(jnp.bfloat16)
    recv_x, recv_dy, recv_w = (
        lax.all_to_all(
            send_x.reshape(group_count, local_count * capacity, model_width),
            "expert",
            split_axis=0,
            concat_axis=0,
            tiled=True,
        ),
        lax.all_to_all(
            send_dy.reshape(group_count, local_count * capacity, model_width),
            "expert",
            split_axis=0,
            concat_axis=0,
            tiled=True,
        ),
        lax.all_to_all(
            send_w.reshape(group_count, local_count * capacity),
            "expert",
            split_axis=0,
            concat_axis=0,
            tiled=True,
        ),
    )
    rows_x = to_local(recv_x, group_count, local_count, capacity)
    rows_dy = to_local(recv_dy, group_count, local_count, capacity)
    rows_w = to_local(recv_w, group_count, local_count, capacity)
    full_in, full_out = (
        lax.all_gather(gate_up_weight, "dp", axis=1, tiled=True),
        lax.all_gather(down_weight, "dp", axis=1, tiled=True),
    )
    pre = jnp.einsum("erd,edf->erf", rows_x, full_in, preferred_element_type=jnp.float32)
    gate_pre = pre[:, :, :hidden_width]
    up_pre = pre[:, :, hidden_width:]
    act = swish(gate_pre)
    hidden = (act * up_pre).astype(jnp.bfloat16)
    expert_out = jnp.einsum("erf,edf->erd", hidden, full_out, preferred_element_type=jnp.float32)
    route_grad = jnp.sum(rows_dy.astype(jnp.float32) * expert_out, axis=2).astype(jnp.bfloat16)
    scaled = (rows_w.astype(jnp.float32)[:, :, None] * rows_dy).astype(jnp.bfloat16)
    grad_hidden = jnp.einsum("erd,edf->erf", scaled, full_out, preferred_element_type=jnp.float32)
    sig = jax.nn.sigmoid(gate_pre)
    grad_gate = grad_hidden * up_pre * sig * (1.0 + gate_pre * (1.0 - sig))
    grad_up = grad_hidden * act
    grad_pre = jnp.concatenate([grad_gate, grad_up], axis=2).astype(jnp.bfloat16)
    rows_grad = jnp.einsum(
        "erf,edf->erd", grad_pre, full_in, preferred_element_type=jnp.float32
    ).astype(jnp.bfloat16)
    back_x, back_w = (
        lax.all_to_all(
            to_groups(rows_grad, group_count, local_count, capacity),
            "expert",
            split_axis=0,
            concat_axis=0,
            tiled=True,
        ),
        lax.all_to_all(
            to_groups(route_grad, group_count, local_count, capacity),
            "expert",
            split_axis=0,
            concat_axis=0,
            tiled=True,
        ),
    )
    back_x = back_x.reshape(slot_total, model_width)
    back_w = back_w.reshape(slot_total).astype(jnp.float32)
    grad_tokens = jnp.einsum(
        "st,sd->td", by_token, back_x, preferred_element_type=jnp.float32
    ).astype(jnp.bfloat16)
    grad_route = jnp.sum(jnp.where(placed, back_w[:, None], 0.0), axis=0)
    grad_route = grad_route.reshape(token_count, route_count).astype(jnp.bfloat16)
    all_x = lax.all_to_all(rows_x, "dp", split_axis=2, concat_axis=1, tiled=True)
    grad_gate_up = jnp.einsum(
        "erd,erf->edf",
        all_x,
        lax.all_gather(grad_pre, "dp", axis=1, tiled=True),
        preferred_element_type=jnp.float32,
    )
    summed = lax.psum_scatter(
        jnp.einsum("erd,erf->def", scaled, hidden, preferred_element_type=jnp.float32),
        "dp",
        scatter_dimension=0,
        tiled=True,
    )
    grad_down = jnp.swapaxes(summed, 0, 1)
    return (grad_tokens, grad_route, grad_gate_up, grad_down)


def packs(tokens, route_expert, down_weight):
    chunks = tokens.shape[1] // LANES
    capacity = block_rows(tokens.shape[0], route_expert.shape[1], lax.axis_size("expert"))
    return (
        lax.axis_size("expert") == 8
        and lax.axis_size("dp") == 4
        and down_weight.shape[0] == 1
        and capacity % 16 <= 1
        and chunks == 16
        and 2 * chunks <= capacity < LANES // 2
    )


def solution(mesh):
    def on_device(*arrays):
        if packs(arrays[0], arrays[2], arrays[5]):
            return on_device_packed(*arrays)
        return on_device_routed(*arrays)

    return jax.shard_map(
        on_device,
        mesh=mesh,
        in_specs=(
            P(("expert", "dp"), None),
            P(("expert", "dp"), None),
            P(("expert", "dp"), None),
            P(("expert", "dp"), None),
            P("expert", "dp", None),
            P("expert", "dp", None),
        ),
        out_specs=(
            P(("expert", "dp"), None),
            P(("expert", "dp"), None),
            P("expert", "dp", None),
            P("expert", "dp", None),
        ),
        check_vma=False,
    )
```

```python
import functools

import jax
import jax.numpy as jnp
from jax import lax
from jax.experimental import pallas as pl
from jax.experimental.pallas import tpu as pltpu
from jax.sharding import PartitionSpec as P

BF16 = jnp.bfloat16
F32 = jnp.float32
LANES = 128


def swish(value):
    return value * jax.nn.sigmoid(value)


def dot(a, b):
    return jnp.dot(a, b, preferred_element_type=F32)


def dot_nt(a, b):
    return lax.dot_general(a, b, (((1,), (1,)), ((), ())), preferred_element_type=F32)


def dot_tn(a, b):
    return lax.dot_general(a, b, (((0,), (0,)), ((), ())), preferred_element_type=F32)


def picks(weight, main):
    token_count = weight.shape[1]
    routed = weight != 0.0
    first = lax.broadcasted_iota(jnp.int32, (token_count, token_count), 0)
    second = lax.broadcasted_iota(jnp.int32, (token_count, token_count), 1)
    upper = (first < second).astype(F32).astype(BF16)
    rank = dot(routed.astype(F32).astype(BF16), upper)
    rank = jnp.where(routed, rank, -1.0).astype(jnp.int32)
    slots = lax.broadcasted_iota(jnp.int32, (main, token_count), 0)
    mains = [(slots == rank[i : i + 1, :]).astype(F32) for i in range(weight.shape[0])]
    tails = (rank == main).astype(F32)
    return mains, tails


def route_kernel(peer_ref, named_ref, given_ref, x_ref, dy_ref, joint_ref, dense_ref):
    count, width = x_ref.shape
    named = named_ref[...]
    given = given_ref[...].astype(F32)
    experts = dense_ref.shape[0]
    lines = [
        jnp.sum(jnp.where(named == peer_ref[i], given, 0.0), axis=0, keepdims=True) for i in range(experts)
    ]
    dense = jnp.concatenate(lines, axis=0)
    dense_ref[...] = dense
    turned = jnp.concatenate(lines[experts // 2 :] + lines[: experts // 2] + [jnp.zeros_like(dense)], axis=0)
    joint_ref[0:count, :width] = x_ref[...]
    joint_ref[count:, :width] = dy_ref[...]
    joint_ref[:, width:] = jnp.zeros((2 * count, LANES), BF16)
    joint_ref[0:16, width : width + count] = turned.astype(BF16)


def join_kernel(in_ref, out_ref, joint_ref):
    width = in_ref.shape[1]
    joint_ref[:, :width] = in_ref[...]
    joint_ref[:, width:] = out_ref[...]


def stack_kernel(own_ref, far_ref, after_ref, stacked_ref):
    count = own_ref.shape[0]
    stacked_ref[0:count, :] = own_ref[...]
    stacked_ref[count:, :] = far_ref[...]


def after_kernel(*refs):
    pass


def relay_kernel(near_a, far_a, near_b, far_b, mid_ref, after_ref, joint_ref):
    count, width = near_a.shape
    for at, near, far in ((0, near_a, far_a), (count, near_b, far_b)):
        joint_ref[at : at + count, :width] = near[...]
        joint_ref[at : at + count, width : 2 * width] = far[:, width:]
    joint_ref[:, 2 * width :] = mid_ref[...]


def pack_kernel(first, joint_ref, *refs):
    count = 4
    fold = refs[-1]
    out_refs = refs[-1 - count : -1]
    tokens, width = joint_ref.shape[0] // 2, joint_ref.shape[1] - LANES
    chunks = width // LANES
    main = out_refs[0].shape[0] // 2
    weight = joint_ref[0:16, width:].astype(F32)[0:8, :tokens]
    mains, tails = picks(weight, main)
    mains = mains[first : first + count]
    pick = jnp.concatenate(mains + [tails, jnp.zeros_like(tails)], axis=0).astype(BF16)
    lane = lax.broadcasted_iota(jnp.int32, (main, LANES), 1)
    for at, base, low in ((0, 0, 0), (tokens, main, chunks)):
        rows = dot(pick, joint_ref[at : at + tokens, :width])
        for j in range(count):
            out_refs[j][base : base + main, :width] = rows[main * j : main * (j + 1)].astype(BF16)
            line = main * count + first + j
            for c in range(chunks):
                fold[c : c + 1, :] = rows[line : line + 1, LANES * c : LANES * (c + 1)]
            out_refs[j][low : low + chunks, width:] = fold[...].astype(BF16)
    for j in range(count):
        mine = weight[first + j : first + j + 1, :]
        column = jnp.sum(mains[j] * mine, axis=1, keepdims=True)
        last = jnp.sum(tails[first + j : first + j + 1, :] * mine, axis=1, keepdims=True)
        out_refs[j][main:, width:] = jnp.where(lane < LANES // 2, column, last).astype(BF16)


def slice_kernel(place_ref, *refs):
    blocks, parts = 4, 4
    in_refs, (keep_ref, near_ref, far_ref, weight_ref, fold) = refs[:blocks], refs[-5:]
    main = in_refs[0].shape[0] // 2
    depth = keep_ref.shape[1] // 2
    width = parts * depth
    chunks = width // LANES
    targets = [(keep_ref, 0), (near_ref, 0), (far_ref, 0), (far_ref, 2 * depth)]
    lane = lax.broadcasted_iota(jnp.int32, (1, LANES), 1)
    lasts = []
    for i in range(blocks):
        for j, (target, shift) in enumerate(targets):
            columns = pl.ds(pl.multiple_of(place_ref[j] * depth, depth), depth)
            for side in range(2):
                at = shift + side * depth
                target[main * i : main * (i + 1), at : at + depth] = in_refs[i][
                    side * main : (side + 1) * main, columns
                ]
        for side in range(2):
            fold[side, chunks * i : chunks * (i + 1), :] = in_refs[i][
                side * chunks : (side + 1) * chunks, width:
            ].astype(F32)
        weights = in_refs[i][main:, width:].astype(F32)
        weight_ref[main * i : main * (i + 1), :] = weights
        last = jnp.sum(jnp.where(lane == LANES - 1, weights[0:1, :], 0.0), axis=1, keepdims=True)
        lasts.append(jnp.broadcast_to(last, (1, LANES)))
    weight_ref[main * blocks :, :] = jnp.concatenate(lasts + [jnp.zeros((16 - blocks, LANES), F32)], axis=0)
    each = chunks // parts
    for j, (target, shift) in enumerate(targets):
        for side in range(2):
            for q in range(each):
                tail = fold[side, pl.ds(place_ref[j] * each + q, blocks, stride=chunks), :]
                tail = jnp.concatenate([tail, jnp.zeros((16 - blocks, LANES), F32)], axis=0).astype(BF16)
                at = shift + side * depth + q * LANES
                target[main * blocks :, at : at + LANES] = tail


def main_kernel(early, place_ref, w_ref, *refs):
    blocks, parts = 4, 4
    own_ref, other_ref = refs[:2]
    keep_ref, near_ref, far_ref = refs[2:5]
    mid, backs, (tail, fold) = refs[-3 - blocks], refs[-2 - blocks : -2], refs[-2:]
    depth = keep_ref.shape[1] // 2
    width = parts * depth
    hidden_width = mid.shape[1] // 3
    main = backs[0].shape[0]
    chunks = width // LANES
    total = keep_ref.shape[0]
    first, second = pl.ds(0, depth), pl.ds(depth, depth)
    weights = [own_ref.at[first], other_ref.at[first], own_ref.at[second], other_ref.at[second]]
    pre = jnp.zeros((total, 2 * hidden_width), F32)
    grad = jnp.zeros((total, hidden_width), F32)
    for j, (ref, shift) in enumerate([(keep_ref, 0), (near_ref, 0), (far_ref, 0), (far_ref, 2 * depth)]):
        pre += dot(ref[:, shift : shift + depth], weights[j][:, : 2 * hidden_width])
        grad += dot(ref[:, shift + depth : shift + 2 * depth], weights[j][:, 2 * hidden_width :])
    if early:
        mid[0:early, :] = refs[5][...]
    weight = w_ref[:, 0:1]
    gate_pre = pre[:, :hidden_width]
    up_pre = pre[:, hidden_width:]
    sig = jax.nn.sigmoid(gate_pre)
    act = gate_pre * sig
    hidden = (act * up_pre).astype(BF16).astype(F32)
    route = jnp.sum(hidden * grad, axis=1, keepdims=True)
    grad_hidden = weight * grad
    grad_gate = grad_hidden * up_pre * sig * (1.0 + gate_pre * (1.0 - sig))
    mid[early:, :hidden_width] = grad_gate.astype(BF16)
    mid[early:, hidden_width : 2 * hidden_width] = (grad_hidden * act).astype(BF16)
    mid[early:, 2 * hidden_width :] = (weight * hidden).astype(BF16)
    for j in range(parts):
        columns = pl.ds(pl.multiple_of(place_ref[j] * depth, depth), depth)
        part = dot_nt(mid[early:, : 2 * hidden_width], weights[j][:, : 2 * hidden_width])
        tail[:, columns] = part[main * blocks :]
        part = part.astype(BF16)
        for i in range(blocks):
            backs[i][:, columns] = part[main * i : main * (i + 1)]
    row = lax.broadcasted_iota(jnp.int32, (main, LANES), 0)
    lane = lax.broadcasted_iota(jnp.int32, (main, LANES), 1)
    for i in range(blocks):
        for c in range(chunks):
            fold[c : c + 1, :] = tail[i : i + 1, LANES * c : LANES * (c + 1)]
        backs[i][:chunks, width:] = fold[...].astype(BF16)
        mine = jnp.where(row == lane, route[main * i : main * (i + 1)], 0.0)
        mine = jnp.sum(mine, axis=0, keepdims=True)
        mine = jnp.where(lane[0:1] == main, route[main * blocks + i : main * blocks + i + 1], mine)
        backs[i][chunks:, width:] = jnp.broadcast_to(mine, (main - chunks, LANES)).astype(BF16)


def unpack_sum(weight, block_refs, rows, fold):
    count = len(block_refs)
    main = block_refs[0].shape[0]
    width = rows.shape[1]
    chunks = width // LANES
    mains, tails = picks(weight, main)
    mains = mains[:count]
    pick = jnp.concatenate(mains + [tails, jnp.zeros_like(tails)], axis=0).astype(BF16)
    lane = lax.broadcasted_iota(jnp.int32, (1, LANES), 1)
    routes = []
    for j in range(count):
        rows[main * j : main * (j + 1), :] = block_refs[j][:, :width]
        fold[chunks * j : chunks * (j + 1), :] = block_refs[j][:chunks, width:].astype(F32)
        mine = block_refs[j][chunks:, width:].astype(F32)
        dense = dot(mine[:, :main].astype(BF16), mains[j].astype(BF16))[0:1, :]
        last = jnp.sum(jnp.where(lane == main, mine[0:1, :], 0.0), axis=1, keepdims=True)
        routes.append(dense + last * tails[j : j + 1, :])
    for c in range(chunks):
        tail = fold[pl.ds(c, count, stride=chunks), :]
        tail = jnp.concatenate([tail, jnp.zeros((16 - count, LANES), F32)], axis=0).astype(BF16)
        rows[main * count :, LANES * c : LANES * (c + 1)] = tail
    return dot_tn(pick, rows[...]), routes


def relay_sum_kernel(joint_ref, b0, b1, b2, b3, out_ref, rows, fold):
    tokens, width = out_ref.shape[0], rows.shape[1]
    weight = joint_ref[0:16, width:].astype(F32)[0:8, :tokens]
    summed, routes = unpack_sum(weight, (b0, b1, b2, b3), rows, fold)
    out_ref[:, :width] = summed.astype(BF16)
    out_ref[:, width:] = jnp.zeros((tokens, LANES), BF16)
    block = jnp.concatenate(routes + [jnp.zeros((12, tokens), F32)], axis=0).astype(BF16)
    out_ref[0:16, width : width + tokens] = block


def near_sum_kernel(w_ref, b0, b1, b2, b3, grad_ref, route_ref, rows, fold):
    summed, routes = unpack_sum(w_ref[...], (b0, b1, b2, b3), rows, fold)
    grad_ref[...] = summed
    route_ref[...] = jnp.concatenate(routes + [jnp.zeros_like(route) for route in routes], axis=0)


def combine_kernel(peer_ref, named_ref, near_ref, near_route_ref, far_ref, grad_ref, route_ref):
    tokens, width = grad_ref.shape
    grad_ref[...] = (near_ref[...] + far_ref[:, :width].astype(F32)).astype(BF16)
    others = far_ref[0:16, width : width + tokens].astype(F32)
    named = named_ref[...]
    route = jnp.zeros(route_ref.shape, F32)
    for j in range(4):
        route = route + jnp.where(named == peer_ref[j], near_route_ref[j : j + 1, :], 0.0)
        route = route + jnp.where(named == peer_ref[4 + j], others[j : j + 1, :], 0.0)
    route_ref[...] = route.astype(BF16)


def weight_kernel(half, rows_a, rows_b, near_ref, *refs):
    in_ref, out_ref, rows, mids = refs[-4:]
    if half:
        mid_a, mid_b, before = refs[0][...], refs[1][...], refs[2:4]
    else:
        mid_a, mid_b, before = refs[0][...], near_ref[:, 2 * rows.shape[1] :], ()
    depth, hidden_width = out_ref.shape
    count = rows_a.shape[0]
    rows[0:count, :] = rows_a[:, : 2 * depth]
    rows[count : 2 * count, :] = rows_b[:, : 2 * depth]
    rows[2 * count :, :] = near_ref[:, 2 * depth * half : 2 * depth * (half + 1)]
    mids[0 : 2 * count, :] = mid_a
    mids[2 * count :, :] = mid_b
    in_part = dot_tn(rows[:, :depth], mids[:, : 2 * hidden_width])
    out_part = dot_tn(rows[:, depth:], mids[:, 2 * hidden_width :])
    if before:
        in_part = in_part + before[0][...]
        out_part = out_part + before[1][...]
    in_ref[...] = in_part
    out_ref[...] = out_part


def call(kernel, outs, smem, vmem, either, scratch, flops, either_outs=0, aliases=None):
    on_vmem = pl.BlockSpec(memory_space=pltpu.VMEM)
    on_either = pl.BlockSpec(memory_space=pl.ANY)
    on_smem = pl.BlockSpec(memory_space=pltpu.SMEM)
    outs = [jax.ShapeDtypeStruct(shape, kind) for shape, kind in outs]
    moved = sum(a.size * a.dtype.itemsize for a in list(vmem) + outs[either_outs:])
    return pl.pallas_call(
        kernel,
        out_shape=tuple(outs),
        in_specs=[on_smem] * len(smem) + [on_vmem] * len(vmem) + [on_either] * len(either),
        out_specs=tuple([on_either] * either_outs + [on_vmem] * (len(outs) - either_outs)),
        scratch_shapes=scratch,
        compiler_params=pltpu.CompilerParams(vmem_limit_bytes=16 * 1024 * 1024),
        cost_estimate=pl.CostEstimate(flops=flops, bytes_accessed=moved, transcendentals=0),
        input_output_aliases=aliases or {},
    )(*smem, *vmem, *either)


def swap(value, axis, mask):
    return lax.ppermute(value, axis, [(i, i ^ mask) for i in range(lax.axis_size(axis))])


def on_device_packed(tokens, grad_out, route_expert, route_weight, gate_up_weight, down_weight):
    token_count, width = tokens.shape
    blocks, parts, half = 8, 4, 4
    hidden_width = down_weight.shape[2]
    depth = width // parts
    chunks = width // LANES
    main = block_rows(token_count, route_expert.shape[1], blocks) // 16 * 16
    rows = main * half + 16

    peers = lax.axis_index("expert") ^ jnp.arange(blocks, dtype=jnp.int32)
    places = lax.axis_index("dp") ^ jnp.arange(parts, dtype=jnp.int32)
    named = route_expert.T
    packed_shape = ((2 * main, width + LANES), BF16)
    back_shape = ((main, width + LANES), BF16)

    joint, dense = call(
        route_kernel,
        [((2 * token_count, width + LANES), BF16), ((blocks, token_count), F32)],
        [peers],
        [named, route_weight.T, tokens, grad_out],
        [],
        [],
        0,
    )
    far_joint = swap(joint, "expert", half)

    (weights,) = call(
        join_kernel,
        [((depth, 3 * hidden_width), BF16)],
        [],
        [gate_up_weight[0], down_weight[0]],
        [],
        [],
        0,
    )
    far_weights = swap(weights, "dp", 2)

    def pack(first, value, after):
        packed = call(
            functools.partial(pack_kernel, first),
            [packed_shape] * half,
            [],
            [value],
            after,
            [pltpu.VMEM((chunks, LANES), F32)],
            4 * (half * main + 16) * token_count * width,
        )
        return [packed[0]] + [swap(packed[j], "expert", j) for j in range(1, half)]

    def sliced(packed, after):
        return call(
            slice_kernel,
            [
                ((rows, 2 * depth), BF16),
                ((rows, 2 * depth), BF16),
                ((rows, 4 * depth), BF16),
                ((rows, LANES), F32),
            ],
            [places],
            packed,
            after,
            [pltpu.VMEM((2, half * chunks, LANES), F32)],
            0,
        )

    own = pack(half, joint, [])
    *own_slices, own_weight = sliced(own, [far_joint])
    own_far = swap(own_slices[2], "dp", 2)
    far = pack(0, far_joint, [own_slices[0], far_weights])
    (stacked,) = call(
        stack_kernel,
        [((2 * depth, 3 * hidden_width), BF16)],
        [],
        [weights, far_weights],
        [far[0]],
        [],
        0,
    )
    weight_parts = [stacked, swap(stacked, "dp", 1)]

    def middle(slices, weight, before):
        early = before[0].shape[0] if before else 0
        return call(
            functools.partial(main_kernel, early),
            [((early + rows, 3 * hidden_width), BF16)] + [back_shape] * half,
            [places],
            [weight, *weight_parts, *slices, *before],
            [],
            [pltpu.VMEM((16, width), F32), pltpu.VMEM((chunks, LANES), F32)],
            2 * rows * width * 5 * hidden_width,
        )

    own_mid, *near_back = middle(own_slices, own_weight, [])
    *far_slices, far_weight = sliced(far, [own_mid])
    far_far = swap(far_slices[2], "dp", 2)
    mid, *far_back = middle(far_slices, far_weight, [own_mid])

    sum_scratch = [
        pltpu.VMEM((half * main + 16, width), BF16),
        pltpu.VMEM((half * chunks, LANES), F32),
    ]
    sum_flops = 2 * (half * main + 16) * width * token_count
    far_back = far_back[:1] + [swap(far_back[j], "expert", j) for j in range(1, half)]
    (partial,) = call(
        relay_sum_kernel,
        [((token_count, width + LANES), BF16)],
        [],
        [far_joint, *far_back],
        [],
        sum_scratch,
        sum_flops,
    )
    far_partial = swap(partial, "expert", half)

    mid_far = swap(mid, "dp", 2)
    (near,) = call(
        relay_kernel,
        [((2 * rows, 4 * depth + 3 * hidden_width), BF16)],
        [],
        [own_slices[1], own_far, far_slices[1], far_far, mid],
        [partial],
        [],
        0,
    )
    near = swap(near, "dp", 1)
    near_back = near_back[:1] + [swap(near_back[j], "expert", j) for j in range(1, half)]
    near_sum, near_route = call(
        near_sum_kernel,
        [((token_count, width), F32), ((blocks, token_count), F32)],
        [],
        [dense, *near_back],
        [],
        sum_scratch,
        sum_flops,
    )
    grad_tokens, grad_route = call(
        combine_kernel,
        [((token_count, width), BF16), (named.shape, BF16)],
        [peers],
        [named, near_sum, near_route, far_partial],
        [],
        [],
        0,
    )

    def weight_part(which, arrays, before):
        return call(
            functools.partial(weight_kernel, which),
            [((depth, 2 * hidden_width), F32), ((depth, hidden_width), F32)],
            [],
            [*arrays, *before],
            [],
            [pltpu.VMEM((4 * rows, 2 * depth), BF16), pltpu.VMEM((4 * rows, 3 * hidden_width), BF16)],
            2 * 4 * rows * depth * 3 * hidden_width,
        )

    first = weight_part(0, [own_slices[0], far_slices[0], near, mid], [])
    (mid_far,) = call(
        after_kernel,
        [(mid_far.shape, BF16)],
        [],
        [],
        [mid_far, first[1], far_partial, near_sum],
        [],
        0,
        1,
        {0: 0},
    )
    grad_gate_up, grad_down = weight_part(1, [own_far, far_far, near, mid_far, swap(mid_far, "dp", 1)], first)
    return (grad_tokens, grad_route.T, grad_gate_up[None], grad_down[None])


def block_rows(token_count, route_count, expert_total):
    return min(token_count, (token_count * route_count + expert_total - 1) // expert_total + 1)


def to_local(rows, group_count, local_count, capacity):
    tail = rows.shape[2:]
    shaped = rows.reshape((group_count, local_count, capacity) + tail)
    shaped = jnp.swapaxes(shaped, 0, 1)
    return shaped.reshape((local_count, group_count * capacity) + tail)


def to_groups(rows, group_count, local_count, capacity):
    tail = rows.shape[2:]
    shaped = rows.reshape((local_count, group_count, capacity) + tail)
    shaped = jnp.swapaxes(shaped, 0, 1)
    return shaped.reshape((group_count, local_count * capacity) + tail)


def on_device_routed(tokens, grad_out, route_expert, route_weight, gate_up_weight, down_weight):
    token_count, model_width = tokens.shape
    route_count = route_expert.shape[1]
    group_count = lax.axis_size("expert")
    local_count = gate_up_weight.shape[0]
    hidden_width = down_weight.shape[2]
    expert_total = local_count * group_count
    capacity = min(token_count, (token_count * route_count + expert_total - 1) // expert_total + 1)
    slot_total = expert_total * capacity
    flat_expert = route_expert.reshape(-1)
    expert_ids = jnp.arange(expert_total, dtype=jnp.int32)
    onehot = (flat_expert[:, None] == expert_ids[None, :]).astype(jnp.int32)
    before = jnp.cumsum(onehot, axis=0) - onehot
    rank = jnp.sum(before * onehot, axis=1)
    slot_of = flat_expert * capacity + rank
    slot_ids = jnp.arange(slot_total, dtype=jnp.int32)
    placed = slot_ids[:, None] == slot_of[None, :]
    by_token = jnp.any(placed.reshape(slot_total, token_count, route_count), axis=2).astype(
        jnp.bfloat16
    )
    send_x = jnp.dot(by_token, tokens, preferred_element_type=jnp.float32).astype(jnp.bfloat16)
    send_dy = jnp.dot(by_token, grad_out, preferred_element_type=jnp.float32).astype(jnp.bfloat16)
    flat_weight = route_weight.reshape(-1).astype(jnp.float32)
    send_w = jnp.sum(jnp.where(placed, flat_weight[None, :], 0.0), axis=1).astype(jnp.bfloat16)
    recv_x, recv_dy, recv_w = (
        lax.all_to_all(
            send_x.reshape(group_count, local_count * capacity, model_width),
            "expert",
            split_axis=0,
            concat_axis=0,
            tiled=True,
        ),
        lax.all_to_all(
            send_dy.reshape(group_count, local_count * capacity, model_width),
            "expert",
            split_axis=0,
            concat_axis=0,
            tiled=True,
        ),
        lax.all_to_all(
            send_w.reshape(group_count, local_count * capacity),
            "expert",
            split_axis=0,
            concat_axis=0,
            tiled=True,
        ),
    )
    rows_x = to_local(recv_x, group_count, local_count, capacity)
    rows_dy = to_local(recv_dy, group_count, local_count, capacity)
    rows_w = to_local(recv_w, group_count, local_count, capacity)
    full_in, full_out = (
        lax.all_gather(gate_up_weight, "dp", axis=1, tiled=True),
        lax.all_gather(down_weight, "dp", axis=1, tiled=True),
    )
    pre = jnp.einsum("erd,edf->erf", rows_x, full_in, preferred_element_type=jnp.float32)
    gate_pre = pre[:, :, :hidden_width]
    up_pre = pre[:, :, hidden_width:]
    act = swish(gate_pre)
    hidden = (act * up_pre).astype(jnp.bfloat16)
    expert_out = jnp.einsum("erf,edf->erd", hidden, full_out, preferred_element_type=jnp.float32)
    route_grad = jnp.sum(rows_dy.astype(jnp.float32) * expert_out, axis=2).astype(jnp.bfloat16)
    scaled = (rows_w.astype(jnp.float32)[:, :, None] * rows_dy).astype(jnp.bfloat16)
    grad_hidden = jnp.einsum("erd,edf->erf", scaled, full_out, preferred_element_type=jnp.float32)
    sig = jax.nn.sigmoid(gate_pre)
    grad_gate = grad_hidden * up_pre * sig * (1.0 + gate_pre * (1.0 - sig))
    grad_up = grad_hidden * act
    grad_pre = jnp.concatenate([grad_gate, grad_up], axis=2).astype(jnp.bfloat16)
    rows_grad = jnp.einsum(
        "erf,edf->erd", grad_pre, full_in, preferred_element_type=jnp.float32
    ).astype(jnp.bfloat16)
    back_x, back_w = (
        lax.all_to_all(
            to_groups(rows_grad, group_count, local_count, capacity),
            "expert",
            split_axis=0,
            concat_axis=0,
            tiled=True,
        ),
        lax.all_to_all(
            to_groups(route_grad, group_count, local_count, capacity),
            "expert",
            split_axis=0,
            concat_axis=0,
            tiled=True,
        ),
    )
    back_x = back_x.reshape(slot_total, model_width)
    back_w = back_w.reshape(slot_total).astype(jnp.float32)
    grad_tokens = jnp.einsum(
        "st,sd->td", by_token, back_x, preferred_element_type=jnp.float32
    ).astype(jnp.bfloat16)
    grad_route = jnp.sum(jnp.where(placed, back_w[:, None], 0.0), axis=0)
    grad_route = grad_route.reshape(token_count, route_count).astype(jnp.bfloat16)
    all_x = lax.all_to_all(rows_x, "dp", split_axis=2, concat_axis=1, tiled=True)
    grad_gate_up = jnp.einsum(
        "erd,erf->edf",
        all_x,
        lax.all_gather(grad_pre, "dp", axis=1, tiled=True),
        preferred_element_type=jnp.float32,
    )
    summed = lax.psum_scatter(
        jnp.einsum("erd,erf->def", scaled, hidden, preferred_element_type=jnp.float32),
        "dp",
        scatter_dimension=0,
        tiled=True,
    )
    grad_down = jnp.swapaxes(summed, 0, 1)
    return (grad_tokens, grad_route, grad_gate_up, grad_down)


def packs(tokens, route_expert, down_weight):
    chunks = tokens.shape[1] // LANES
    capacity = block_rows(tokens.shape[0], route_expert.shape[1], lax.axis_size("expert"))
    return (
        lax.axis_size("expert") == 8
        and lax.axis_size("dp") == 4
        and down_weight.shape[0] == 1
        and capacity % 16 <= 1
        and chunks == 16
        and 2 * chunks <= capacity < LANES // 2
    )


def solution(mesh):
    def on_device(*arrays):
        if packs(arrays[0], arrays[2], arrays[5]):
            return on_device_packed(*arrays)
        return on_device_routed(*arrays)

    return jax.shard_map(
        on_device,
        mesh=mesh,
        in_specs=(
            P(("expert", "dp"), None),
            P(("expert", "dp"), None),
            P(("expert", "dp"), None),
            P(("expert", "dp"), None),
            P("expert", "dp", None),
            P("expert", "dp", None),
        ),
        out_specs=(
            P(("expert", "dp"), None),
            P(("expert", "dp"), None),
            P("expert", "dp", None),
            P("expert", "dp", None),
        ),
        check_vma=False,
    )
```

```python
import functools

import jax
import jax.numpy as jnp
from jax import lax
from jax.experimental import pallas as pl
from jax.experimental.pallas import tpu as pltpu
from jax.sharding import PartitionSpec as P

BF16 = jnp.bfloat16
F32 = jnp.float32
LANES = 128


def swish(value):
    return value * jax.nn.sigmoid(value)


def dot(a, b):
    return jnp.dot(a, b, preferred_element_type=F32)


def dot_nt(a, b):
    return lax.dot_general(a, b, (((1,), (1,)), ((), ())), preferred_element_type=F32)


def dot_tn(a, b):
    return lax.dot_general(a, b, (((0,), (0,)), ((), ())), preferred_element_type=F32)


def start(source, target, sem):
    copy = pltpu.make_async_copy(source, target, sem)
    copy.start()
    return copy


def picks(weight, main):
    token_count = weight.shape[1]
    routed = weight != 0.0
    first = lax.broadcasted_iota(jnp.int32, (token_count, token_count), 0)
    second = lax.broadcasted_iota(jnp.int32, (token_count, token_count), 1)
    upper = (first < second).astype(F32).astype(BF16)
    rank = dot(routed.astype(F32).astype(BF16), upper)
    rank = jnp.where(routed, rank, -1.0).astype(jnp.int32)
    slots = lax.broadcasted_iota(jnp.int32, (main, token_count), 0)
    mains = [(slots == rank[i : i + 1, :]).astype(F32) for i in range(weight.shape[0])]
    tails = (rank == main).astype(F32)
    return mains, tails


def route_kernel(peer_ref, named_ref, given_ref, x_ref, dy_ref, joint_ref, dense_ref):
    count, width = x_ref.shape
    named = named_ref[...]
    given = given_ref[...].astype(F32)
    experts = dense_ref.shape[0]
    lines = [
        jnp.sum(jnp.where(named == peer_ref[i], given, 0.0), axis=0, keepdims=True) for i in range(experts)
    ]
    dense = jnp.concatenate(lines, axis=0)
    dense_ref[...] = dense
    turned = jnp.concatenate(lines[experts // 2 :] + lines[: experts // 2] + [jnp.zeros_like(dense)], axis=0)
    joint_ref[0:count, :width] = x_ref[...]
    joint_ref[count:, :width] = dy_ref[...]
    joint_ref[:, width:] = jnp.zeros((2 * count, LANES), BF16)
    joint_ref[0:16, width : width + count] = turned.astype(BF16)


def join_kernel(in_ref, out_ref, joint_ref):
    width = in_ref.shape[1]
    joint_ref[:, :width] = in_ref[...]
    joint_ref[:, width:] = out_ref[...]


def stack_kernel(own_ref, far_ref, after_ref, stacked_ref):
    count = own_ref.shape[0]
    stacked_ref[0:count, :] = own_ref[...]
    stacked_ref[count:, :] = far_ref[...]


def after_kernel(*refs):
    pass


def relay_kernel(near_a, far_a, near_b, far_b, mid_ref, *refs):
    joint_ref = refs[-1]
    count, width = near_a.shape
    for at, near, far in ((0, near_a, far_a), (count, near_b, far_b)):
        joint_ref[at : at + count, :width] = near[...]
        joint_ref[at : at + count, width : 2 * width] = far[:, width:]
    joint_ref[:, 2 * width :] = mid_ref[...]


def pack_kernel(first, joint_ref, *refs):
    count = 4
    kept, fold, sem = refs[-3:]
    kept_ref, *out_refs = refs[-3 - count : -3]
    out_refs = [kept, *out_refs]
    tokens, width = joint_ref.shape[0] // 2, joint_ref.shape[1] - LANES
    chunks = width // LANES
    main = out_refs[0].shape[0] // 2
    weight = joint_ref[0:16, width:].astype(F32)[0:8, :tokens]
    mains, tails = picks(weight, main)
    mains = mains[first : first + count]
    pick = jnp.concatenate(mains + [tails, jnp.zeros_like(tails)], axis=0).astype(BF16)
    lane = lax.broadcasted_iota(jnp.int32, (main, LANES), 1)
    for at, base, low in ((0, 0, 0), (tokens, main, chunks)):
        rows = dot(pick, joint_ref[at : at + tokens, :width])
        for j in range(count):
            out_refs[j][base : base + main, :width] = rows[main * j : main * (j + 1)].astype(BF16)
            line = main * count + first + j
            for c in range(chunks):
                fold[c : c + 1, :] = rows[line : line + 1, LANES * c : LANES * (c + 1)]
            out_refs[j][low : low + chunks, width:] = fold[...].astype(BF16)
    for j in range(count):
        mine = weight[first + j : first + j + 1, :]
        column = jnp.sum(mains[j] * mine, axis=1, keepdims=True)
        last = jnp.sum(tails[first + j : first + j + 1, :] * mine, axis=1, keepdims=True)
        out_refs[j][main:, width:] = jnp.where(lane < LANES // 2, column, last).astype(BF16)
        if j == 0:
            copy = start(kept, kept_ref, sem)
    copy.wait()


def slice_kernel(there, place_ref, *refs):
    blocks, parts = 4, 4
    keep_ref, near_ref, far_ref, weight_ref, fold, held, sems = refs[-7:]
    copies = {i: start(refs[i], held.at[i - there], sems.at[i - there]) for i in range(there, blocks)}
    in_refs = list(refs[:there]) + [held.at[i - there] for i in range(there, blocks)]
    main = in_refs[0].shape[0] // 2
    depth = keep_ref.shape[1] // 2
    width = parts * depth
    chunks = width // LANES
    targets = [(keep_ref, 0), (near_ref, 0), (far_ref, 0), (far_ref, 2 * depth)]
    lane = lax.broadcasted_iota(jnp.int32, (1, LANES), 1)
    lasts = []
    for i in range(blocks):
        if i in copies:
            copies[i].wait()
        for j, (target, shift) in enumerate(targets):
            columns = pl.ds(pl.multiple_of(place_ref[j] * depth, depth), depth)
            for side in range(2):
                at = shift + side * depth
                target[main * i : main * (i + 1), at : at + depth] = in_refs[i][
                    side * main : (side + 1) * main, columns
                ]
        for side in range(2):
            fold[side, chunks * i : chunks * (i + 1), :] = in_refs[i][
                side * chunks : (side + 1) * chunks, width:
            ].astype(F32)
        weights = in_refs[i][main:, width:].astype(F32)
        weight_ref[main * i : main * (i + 1), :] = weights
        last = jnp.sum(jnp.where(lane == LANES - 1, weights[0:1, :], 0.0), axis=1, keepdims=True)
        lasts.append(jnp.broadcast_to(last, (1, LANES)))
    weight_ref[main * blocks :, :] = jnp.concatenate(lasts + [jnp.zeros((16 - blocks, LANES), F32)], axis=0)
    each = chunks // parts
    for j, (target, shift) in enumerate(targets):
        for side in range(2):
            for q in range(each):
                tail = fold[side, pl.ds(place_ref[j] * each + q, blocks, stride=chunks), :]
                tail = jnp.concatenate([tail, jnp.zeros((16 - blocks, LANES), F32)], axis=0).astype(BF16)
                at = shift + side * depth + q * LANES
                target[main * blocks :, at : at + LANES] = tail


def main_kernel(early, place_ref, w_ref, *refs):
    blocks, parts = 4, 4
    own_ref, other_ref = refs[:2]
    keep_ref, near_ref, far_ref = refs[2:5]
    mid, backs, (tail, fold) = refs[-3 - blocks], refs[-2 - blocks : -2], refs[-2:]
    depth = keep_ref.shape[1] // 2
    width = parts * depth
    hidden_width = mid.shape[1] // 3
    main = backs[0].shape[0]
    chunks = width // LANES
    total = keep_ref.shape[0]
    first, second = pl.ds(0, depth), pl.ds(depth, depth)
    weights = [own_ref.at[first], other_ref.at[first], own_ref.at[second], other_ref.at[second]]
    pre = jnp.zeros((total, 2 * hidden_width), F32)
    grad = jnp.zeros((total, hidden_width), F32)
    for j, (ref, shift) in enumerate([(keep_ref, 0), (near_ref, 0), (far_ref, 0), (far_ref, 2 * depth)]):
        pre += dot(ref[:, shift : shift + depth], weights[j][:, : 2 * hidden_width])
        grad += dot(ref[:, shift + depth : shift + 2 * depth], weights[j][:, 2 * hidden_width :])
    if early:
        mid[0:early, :] = refs[5][...]
    weight = w_ref[:, 0:1]
    gate_pre = pre[:, :hidden_width]
    up_pre = pre[:, hidden_width:]
    sig = jax.nn.sigmoid(gate_pre)
    act = gate_pre * sig
    hidden = (act * up_pre).astype(BF16).astype(F32)
    route = jnp.sum(hidden * grad, axis=1, keepdims=True)
    grad_hidden = weight * grad
    grad_gate = grad_hidden * up_pre * sig * (1.0 + gate_pre * (1.0 - sig))
    mid[early:, :hidden_width] = grad_gate.astype(BF16)
    mid[early:, hidden_width : 2 * hidden_width] = (grad_hidden * act).astype(BF16)
    mid[early:, 2 * hidden_width :] = (weight * hidden).astype(BF16)
    for j in range(parts):
        columns = pl.ds(pl.multiple_of(place_ref[j] * depth, depth), depth)
        part = dot_nt(mid[early:, : 2 * hidden_width], weights[j][:, : 2 * hidden_width])
        tail[:, columns] = part[main * blocks :]
        part = part.astype(BF16)
        for i in range(blocks):
            backs[i][:, columns] = part[main * i : main * (i + 1)]
    row = lax.broadcasted_iota(jnp.int32, (main, LANES), 0)
    lane = lax.broadcasted_iota(jnp.int32, (main, LANES), 1)
    for i in range(blocks):
        for c in range(chunks):
            fold[c : c + 1, :] = tail[i : i + 1, LANES * c : LANES * (c + 1)]
        backs[i][:chunks, width:] = fold[...].astype(BF16)
        mine = jnp.where(row == lane, route[main * i : main * (i + 1)], 0.0)
        mine = jnp.sum(mine, axis=0, keepdims=True)
        mine = jnp.where(lane[0:1] == main, route[main * blocks + i : main * blocks + i + 1], mine)
        backs[i][chunks:, width:] = jnp.broadcast_to(mine, (main - chunks, LANES)).astype(BF16)


def unpack_sum(weight, block_refs, rows, fold):
    count = len(block_refs)
    main = block_refs[0].shape[0]
    width = rows.shape[1]
    chunks = width // LANES
    mains, tails = picks(weight, main)
    mains = mains[:count]
    pick = jnp.concatenate(mains + [tails, jnp.zeros_like(tails)], axis=0).astype(BF16)
    lane = lax.broadcasted_iota(jnp.int32, (1, LANES), 1)
    routes = []
    for j in range(count):
        rows[main * j : main * (j + 1), :] = block_refs[j][:, :width]
        fold[chunks * j : chunks * (j + 1), :] = block_refs[j][:chunks, width:].astype(F32)
        mine = block_refs[j][chunks:, width:].astype(F32)
        dense = dot(mine[:, :main].astype(BF16), mains[j].astype(BF16))[0:1, :]
        last = jnp.sum(jnp.where(lane == main, mine[0:1, :], 0.0), axis=1, keepdims=True)
        routes.append(dense + last * tails[j : j + 1, :])
    for c in range(chunks):
        tail = fold[pl.ds(c, count, stride=chunks), :]
        tail = jnp.concatenate([tail, jnp.zeros((16 - count, LANES), F32)], axis=0).astype(BF16)
        rows[main * count :, LANES * c : LANES * (c + 1)] = tail
    return dot_tn(pick, rows[...]), routes


def relay_sum_kernel(joint_ref, b0, b1, b2, b3, out_ref, rows, fold):
    tokens, width = out_ref.shape[0], rows.shape[1]
    weight = joint_ref[0:16, width:].astype(F32)[0:8, :tokens]
    summed, routes = unpack_sum(weight, (b0, b1, b2, b3), rows, fold)
    out_ref[:, :width] = summed.astype(BF16)
    out_ref[:, width:] = jnp.zeros((tokens, LANES), BF16)
    block = jnp.concatenate(routes + [jnp.zeros((12, tokens), F32)], axis=0).astype(BF16)
    out_ref[0:16, width : width + tokens] = block


def near_sum_kernel(w_ref, b0, b1, b2, b3, after_ref, grad_ref, route_ref, rows, fold):
    summed, routes = unpack_sum(w_ref[...], (b0, b1, b2, b3), rows, fold)
    grad_ref[...] = summed
    route_ref[...] = jnp.concatenate(routes + [jnp.zeros_like(route) for route in routes], axis=0)


def combine_kernel(peer_ref, named_ref, near_ref, near_route_ref, far_ref, grad_ref, route_ref):
    tokens, width = grad_ref.shape
    grad_ref[...] = (near_ref[...] + far_ref[:, :width].astype(F32)).astype(BF16)
    others = far_ref[0:16, width : width + tokens].astype(F32)
    named = named_ref[...]
    route = jnp.zeros(route_ref.shape, F32)
    for j in range(4):
        route = route + jnp.where(named == peer_ref[j], near_route_ref[j : j + 1, :], 0.0)
        route = route + jnp.where(named == peer_ref[4 + j], others[j : j + 1, :], 0.0)
    route_ref[...] = route.astype(BF16)


def fill(rows, mids, rows_a, rows_b, rows_c, mid_a, mid_b):
    count = rows_a.shape[0]
    rows[0:count, :] = rows_a
    rows[count : 2 * count, :] = rows_b
    rows[2 * count :, :] = rows_c
    mids[0 : 2 * count, :] = mid_a
    mids[2 * count :, :] = mid_b


def first_weight_kernel(rows_a, rows_b, near_ref, mid_ref, in_ref, out_ref, rows, mids):
    depth, hidden_width = out_ref.shape
    near, near_mid = near_ref[:, : 2 * depth], near_ref[:, 4 * depth :]
    fill(rows, mids, rows_a[...], rows_b[...], near, mid_ref[...], near_mid)
    in_ref[...] = dot_tn(rows[:, :depth], mids[:, : 2 * hidden_width])
    out_ref[...] = dot_tn(rows[:, depth:], mids[:, 2 * hidden_width :])


def second_weight_kernel(rows_a, rows_b, near_ref, mid_a, mid_b, in_part, out_part, *refs):
    in_ref, out_ref, rows, mids, in_held, out_held, sems = refs
    depth, hidden_width = out_part.shape
    span = slice(0, 2 * depth)
    fill(rows, mids, rows_a[:, span], rows_b[:, span], near_ref[:, 2 * depth : 4 * depth], mid_a[...], mid_b[...])
    copies = []
    step = depth // 4
    for m in range(4):
        at = slice(m * step, (m + 1) * step)
        lines = pl.ds(m * step, step)
        in_held[at, :] = in_part[at, :] + dot_tn(rows[:, at], mids[:, : 2 * hidden_width])
        copies.append(start(in_held.at[lines], in_ref.at[lines], sems.at[0, m]))
        other = slice(depth + m * step, depth + (m + 1) * step)
        out_held[at, :] = out_part[at, :] + dot_tn(rows[:, other], mids[:, 2 * hidden_width :])
        copies.append(start(out_held.at[lines], out_ref.at[lines], sems.at[1, m]))
    for copy in copies:
        copy.wait()


def call(kernel, outs, smem, vmem, either, scratch, flops, either_outs=0, aliases=None):
    on_vmem = pl.BlockSpec(memory_space=pltpu.VMEM)
    on_either = pl.BlockSpec(memory_space=pl.ANY)
    on_smem = pl.BlockSpec(memory_space=pltpu.SMEM)
    outs = [jax.ShapeDtypeStruct(shape, kind) for shape, kind in outs]
    moved = sum(a.size * a.dtype.itemsize for a in list(vmem) + outs[either_outs:])
    return pl.pallas_call(
        kernel,
        out_shape=tuple(outs),
        in_specs=[on_smem] * len(smem) + [on_vmem] * len(vmem) + [on_either] * len(either),
        out_specs=tuple([on_either] * either_outs + [on_vmem] * (len(outs) - either_outs)),
        scratch_shapes=scratch,
        compiler_params=pltpu.CompilerParams(vmem_limit_bytes=16 * 1024 * 1024),
        cost_estimate=pl.CostEstimate(flops=flops, bytes_accessed=moved, transcendentals=0),
        input_output_aliases=aliases or {},
    )(*smem, *vmem, *either)


def swap(value, axis, mask):
    return lax.ppermute(value, axis, [(i, i ^ mask) for i in range(lax.axis_size(axis))])


def on_device_packed(tokens, grad_out, route_expert, route_weight, gate_up_weight, down_weight):
    token_count, width = tokens.shape
    blocks, parts, half = 8, 4, 4
    hidden_width = down_weight.shape[2]
    depth = width // parts
    chunks = width // LANES
    main = block_rows(token_count, route_expert.shape[1], blocks) // 16 * 16
    rows = main * half + 16

    peers = lax.axis_index("expert") ^ jnp.arange(blocks, dtype=jnp.int32)
    places = lax.axis_index("dp") ^ jnp.arange(parts, dtype=jnp.int32)
    named = route_expert.T
    packed_shape = ((2 * main, width + LANES), BF16)
    back_shape = ((main, width + LANES), BF16)

    joint, dense = call(
        route_kernel,
        [((2 * token_count, width + LANES), BF16), ((blocks, token_count), F32)],
        [peers],
        [named, route_weight.T, tokens, grad_out],
        [],
        [],
        0,
    )
    far_joint = swap(joint, "expert", half)

    (weights,) = call(
        join_kernel,
        [((depth, 3 * hidden_width), BF16)],
        [],
        [gate_up_weight[0], down_weight[0]],
        [],
        [],
        0,
    )
    far_weights = swap(weights, "dp", 2)

    def pack(first, value, after):
        packed = call(
            functools.partial(pack_kernel, first),
            [packed_shape] * half,
            [],
            [value],
            after,
            [pltpu.VMEM(*packed_shape), pltpu.VMEM((chunks, LANES), F32), pltpu.SemaphoreType.DMA],
            4 * (half * main + 16) * token_count * width,
            1,
        )
        return [packed[0]] + [swap(packed[j], "expert", j) for j in range(1, half)]

    def sliced(there, others, after):
        return call(
            functools.partial(slice_kernel, len(there)),
            [
                ((rows, 2 * depth), BF16),
                ((rows, 2 * depth), BF16),
                ((rows, 4 * depth), BF16),
                ((rows, LANES), F32),
            ],
            [places],
            there,
            others + after,
            [
                pltpu.VMEM((2, half * chunks, LANES), F32),
                pltpu.VMEM((len(others), *packed_shape[0]), BF16),
                pltpu.SemaphoreType.DMA((len(others),)),
            ],
            0,
        )

    own = pack(half, joint, [])
    far = pack(0, far_joint, [*own[1:], far_weights])
    *own_slices, own_weight = sliced([], own, [far[0]])
    own_far = swap(own_slices[2], "dp", 2)
    (stacked,) = call(
        stack_kernel,
        [((2 * depth, 3 * hidden_width), BF16)],
        [],
        [weights, far_weights],
        [far[0]],
        [],
        0,
    )
    weight_parts = [stacked, swap(stacked, "dp", 1)]

    def middle(slices, weight, before, after):
        early = before[0].shape[0] if before else 0
        return call(
            functools.partial(main_kernel, early),
            [((early + rows, 3 * hidden_width), BF16)] + [back_shape] * half,
            [places],
            [weight, *weight_parts, *slices, *before],
            after,
            [pltpu.VMEM((16, width), F32), pltpu.VMEM((chunks, LANES), F32)],
            2 * rows * width * 5 * hidden_width,
        )

    own_mid, *near_back = middle(own_slices, own_weight, [], [])
    *far_slices, far_weight = sliced(far[1:], far[:1], [own_mid])
    far_far = swap(far_slices[2], "dp", 2)
    mid, *far_back = middle(far_slices, far_weight, [own_mid], [own_far])

    sum_scratch = [
        pltpu.VMEM((half * main + 16, width), BF16),
        pltpu.VMEM((half * chunks, LANES), F32),
    ]
    sum_flops = 2 * (half * main + 16) * width * token_count
    far_back = far_back[-1:] + [swap(far_back[j - 1], "expert", j) for j in range(1, half)]
    (partial,) = call(
        relay_sum_kernel,
        [((token_count, width + LANES), BF16)],
        [],
        [far_joint, *far_back],
        [],
        sum_scratch,
        sum_flops,
    )
    far_partial = swap(partial, "expert", half)
    near_back = near_back[:1] + [swap(near_back[j], "expert", j) for j in range(1, half)]

    mid_far = swap(mid, "dp", 2)
    (near,) = call(
        relay_kernel,
        [((2 * rows, 4 * depth + 3 * hidden_width), BF16)],
        [],
        [own_slices[1], own_far, far_slices[1], far_far, mid],
        [partial, near_back[1]],
        [],
        0,
    )
    near = swap(near, "dp", 1)
    weight_shapes = [((depth, 2 * hidden_width), F32), ((depth, hidden_width), F32)]
    weight_scratch = [pltpu.VMEM((4 * rows, 2 * depth), BF16), pltpu.VMEM((4 * rows, 3 * hidden_width), BF16)]
    weight_flops = 2 * 4 * rows * depth * 3 * hidden_width
    first = call(
        first_weight_kernel,
        weight_shapes,
        [],
        [own_slices[0], far_slices[0], near, mid],
        [],
        weight_scratch,
        weight_flops,
    )
    near_sum, near_route = call(
        near_sum_kernel,
        [((token_count, width), F32), ((blocks, token_count), F32)],
        [],
        [dense, *near_back],
        [first[1]],
        sum_scratch,
        sum_flops,
    )
    grad_tokens, grad_route = call(
        combine_kernel,
        [((token_count, width), BF16), (named.shape, BF16)],
        [peers],
        [named, near_sum, near_route, far_partial],
        [],
        [],
        0,
    )

    (mid_far,) = call(
        after_kernel,
        [(mid_far.shape, BF16)],
        [],
        [],
        [mid_far, first[1], far_partial, near_sum],
        [],
        0,
        1,
        {0: 0},
    )
    grad_gate_up, grad_down = call(
        second_weight_kernel,
        weight_shapes,
        [],
        [own_far, far_far, near, mid_far, swap(mid_far, "dp", 1), *first],
        [],
        weight_scratch
        + [
            pltpu.VMEM((depth, 2 * hidden_width), F32),
            pltpu.VMEM((depth, hidden_width), F32),
            pltpu.SemaphoreType.DMA((2, 4)),
        ],
        weight_flops,
        2,
    )
    return (grad_tokens, grad_route.T, grad_gate_up[None], grad_down[None])


def block_rows(token_count, route_count, expert_total):
    return min(token_count, (token_count * route_count + expert_total - 1) // expert_total + 1)


def to_local(rows, group_count, local_count, capacity):
    tail = rows.shape[2:]
    shaped = rows.reshape((group_count, local_count, capacity) + tail)
    shaped = jnp.swapaxes(shaped, 0, 1)
    return shaped.reshape((local_count, group_count * capacity) + tail)


def to_groups(rows, group_count, local_count, capacity):
    tail = rows.shape[2:]
    shaped = rows.reshape((local_count, group_count, capacity) + tail)
    shaped = jnp.swapaxes(shaped, 0, 1)
    return shaped.reshape((group_count, local_count * capacity) + tail)


def on_device_routed(tokens, grad_out, route_expert, route_weight, gate_up_weight, down_weight):
    token_count, model_width = tokens.shape
    route_count = route_expert.shape[1]
    group_count = lax.axis_size("expert")
    local_count = gate_up_weight.shape[0]
    hidden_width = down_weight.shape[2]
    expert_total = local_count * group_count
    capacity = min(token_count, (token_count * route_count + expert_total - 1) // expert_total + 1)
    slot_total = expert_total * capacity
    flat_expert = route_expert.reshape(-1)
    expert_ids = jnp.arange(expert_total, dtype=jnp.int32)
    onehot = (flat_expert[:, None] == expert_ids[None, :]).astype(jnp.int32)
    before = jnp.cumsum(onehot, axis=0) - onehot
    rank = jnp.sum(before * onehot, axis=1)
    slot_of = flat_expert * capacity + rank
    slot_ids = jnp.arange(slot_total, dtype=jnp.int32)
    placed = slot_ids[:, None] == slot_of[None, :]
    by_token = jnp.any(placed.reshape(slot_total, token_count, route_count), axis=2).astype(
        jnp.bfloat16
    )
    send_x = jnp.dot(by_token, tokens, preferred_element_type=jnp.float32).astype(jnp.bfloat16)
    send_dy = jnp.dot(by_token, grad_out, preferred_element_type=jnp.float32).astype(jnp.bfloat16)
    flat_weight = route_weight.reshape(-1).astype(jnp.float32)
    send_w = jnp.sum(jnp.where(placed, flat_weight[None, :], 0.0), axis=1).astype(jnp.bfloat16)
    recv_x, recv_dy, recv_w = (
        lax.all_to_all(
            send_x.reshape(group_count, local_count * capacity, model_width),
            "expert",
            split_axis=0,
            concat_axis=0,
            tiled=True,
        ),
        lax.all_to_all(
            send_dy.reshape(group_count, local_count * capacity, model_width),
            "expert",
            split_axis=0,
            concat_axis=0,
            tiled=True,
        ),
        lax.all_to_all(
            send_w.reshape(group_count, local_count * capacity),
            "expert",
            split_axis=0,
            concat_axis=0,
            tiled=True,
        ),
    )
    rows_x = to_local(recv_x, group_count, local_count, capacity)
    rows_dy = to_local(recv_dy, group_count, local_count, capacity)
    rows_w = to_local(recv_w, group_count, local_count, capacity)
    full_in, full_out = (
        lax.all_gather(gate_up_weight, "dp", axis=1, tiled=True),
        lax.all_gather(down_weight, "dp", axis=1, tiled=True),
    )
    pre = jnp.einsum("erd,edf->erf", rows_x, full_in, preferred_element_type=jnp.float32)
    gate_pre = pre[:, :, :hidden_width]
    up_pre = pre[:, :, hidden_width:]
    act = swish(gate_pre)
    hidden = (act * up_pre).astype(jnp.bfloat16)
    expert_out = jnp.einsum("erf,edf->erd", hidden, full_out, preferred_element_type=jnp.float32)
    route_grad = jnp.sum(rows_dy.astype(jnp.float32) * expert_out, axis=2).astype(jnp.bfloat16)
    scaled = (rows_w.astype(jnp.float32)[:, :, None] * rows_dy).astype(jnp.bfloat16)
    grad_hidden = jnp.einsum("erd,edf->erf", scaled, full_out, preferred_element_type=jnp.float32)
    sig = jax.nn.sigmoid(gate_pre)
    grad_gate = grad_hidden * up_pre * sig * (1.0 + gate_pre * (1.0 - sig))
    grad_up = grad_hidden * act
    grad_pre = jnp.concatenate([grad_gate, grad_up], axis=2).astype(jnp.bfloat16)
    rows_grad = jnp.einsum(
        "erf,edf->erd", grad_pre, full_in, preferred_element_type=jnp.float32
    ).astype(jnp.bfloat16)
    back_x, back_w = (
        lax.all_to_all(
            to_groups(rows_grad, group_count, local_count, capacity),
            "expert",
            split_axis=0,
            concat_axis=0,
            tiled=True,
        ),
        lax.all_to_all(
            to_groups(route_grad, group_count, local_count, capacity),
            "expert",
            split_axis=0,
            concat_axis=0,
            tiled=True,
        ),
    )
    back_x = back_x.reshape(slot_total, model_width)
    back_w = back_w.reshape(slot_total).astype(jnp.float32)
    grad_tokens = jnp.einsum(
        "st,sd->td", by_token, back_x, preferred_element_type=jnp.float32
    ).astype(jnp.bfloat16)
    grad_route = jnp.sum(jnp.where(placed, back_w[:, None], 0.0), axis=0)
    grad_route = grad_route.reshape(token_count, route_count).astype(jnp.bfloat16)
    all_x = lax.all_to_all(rows_x, "dp", split_axis=2, concat_axis=1, tiled=True)
    grad_gate_up = jnp.einsum(
        "erd,erf->edf",
        all_x,
        lax.all_gather(grad_pre, "dp", axis=1, tiled=True),
        preferred_element_type=jnp.float32,
    )
    summed = lax.psum_scatter(
        jnp.einsum("erd,erf->def", scaled, hidden, preferred_element_type=jnp.float32),
        "dp",
        scatter_dimension=0,
        tiled=True,
    )
    grad_down = jnp.swapaxes(summed, 0, 1)
    return (grad_tokens, grad_route, grad_gate_up, grad_down)


def packs(tokens, route_expert, down_weight):
    chunks = tokens.shape[1] // LANES
    capacity = block_rows(tokens.shape[0], route_expert.shape[1], lax.axis_size("expert"))
    return (
        lax.axis_size("expert") == 8
        and lax.axis_size("dp") == 4
        and down_weight.shape[0] == 1
        and capacity % 16 <= 1
        and chunks == 16
        and 2 * chunks <= capacity < LANES // 2
    )


def solution(mesh):
    def on_device(*arrays):
        if packs(arrays[0], arrays[2], arrays[5]):
            return on_device_packed(*arrays)
        return on_device_routed(*arrays)

    return jax.shard_map(
        on_device,
        mesh=mesh,
        in_specs=(
            P(("expert", "dp"), None),
            P(("expert", "dp"), None),
            P(("expert", "dp"), None),
            P(("expert", "dp"), None),
            P("expert", "dp", None),
            P("expert", "dp", None),
        ),
        out_specs=(
            P(("expert", "dp"), None),
            P(("expert", "dp"), None),
            P("expert", "dp", None),
            P("expert", "dp", None),
        ),
        check_vma=False,
    )
```

```python
import functools

import jax
import jax.numpy as jnp
from jax import lax
from jax.experimental import pallas as pl
from jax.experimental.pallas import tpu as pltpu
from jax.sharding import PartitionSpec as P

BF16 = jnp.bfloat16
F32 = jnp.float32
LANES = 128


def swish(value):
    return value * jax.nn.sigmoid(value)


def dot(a, b):
    return jnp.dot(a, b, preferred_element_type=F32)


def dot_nt(a, b):
    return lax.dot_general(a, b, (((1,), (1,)), ((), ())), preferred_element_type=F32)


def dot_tn(a, b):
    return lax.dot_general(a, b, (((0,), (0,)), ((), ())), preferred_element_type=F32)


def start(source, target, sem):
    copy = pltpu.make_async_copy(source, target, sem)
    copy.start()
    return copy


def picks(weight, main):
    token_count = weight.shape[1]
    routed = weight != 0.0
    first = lax.broadcasted_iota(jnp.int32, (token_count, token_count), 0)
    second = lax.broadcasted_iota(jnp.int32, (token_count, token_count), 1)
    upper = (first < second).astype(F32).astype(BF16)
    rank = dot(routed.astype(F32).astype(BF16), upper)
    rank = jnp.where(routed, rank, -1.0).astype(jnp.int32)
    slots = lax.broadcasted_iota(jnp.int32, (main, token_count), 0)
    mains = [(slots == rank[i : i + 1, :]).astype(F32) for i in range(weight.shape[0])]
    tails = (rank == main).astype(F32)
    return mains, tails


def route_kernel(peer_ref, named_ref, given_ref, x_ref, dy_ref, joint_ref, dense_ref):
    count, width = x_ref.shape
    named = named_ref[...]
    given = given_ref[...].astype(F32)
    experts = dense_ref.shape[0]
    lines = [
        jnp.sum(jnp.where(named == peer_ref[i], given, 0.0), axis=0, keepdims=True) for i in range(experts)
    ]
    dense = jnp.concatenate(lines, axis=0)
    dense_ref[...] = dense
    turned = jnp.concatenate(lines[experts // 2 :] + lines[: experts // 2] + [jnp.zeros_like(dense)], axis=0)
    joint_ref[0:count, :width] = x_ref[...]
    joint_ref[count:, :width] = dy_ref[...]
    joint_ref[:, width:] = jnp.zeros((2 * count, LANES), BF16)
    joint_ref[0:16, width : width + count] = turned.astype(BF16)


def join_kernel(in_ref, out_ref, joint_ref):
    width = in_ref.shape[1]
    joint_ref[:, :width] = in_ref[...]
    joint_ref[:, width:] = out_ref[...]


def stack_kernel(own_ref, far_ref, after_ref, stacked_ref):
    count = own_ref.shape[0]
    stacked_ref[0:count, :] = own_ref[...]
    stacked_ref[count:, :] = far_ref[...]


def after_kernel(*refs):
    pass


def relay_kernel(near_a, far_a, near_b, far_b, mid_ref, after_ref, joint_ref):
    count, width = near_a.shape
    for at, near, far in ((0, near_a, far_a), (count, near_b, far_b)):
        joint_ref[at : at + count, :width] = near[...]
        joint_ref[at : at + count, width : 2 * width] = far[:, width:]
    joint_ref[:, 2 * width :] = mid_ref[...]


def pack_kernel(first, joint_ref, *refs):
    count = 4
    fold = refs[-1]
    out_refs = refs[-1 - count : -1]
    tokens, width = joint_ref.shape[0] // 2, joint_ref.shape[1] - LANES
    chunks = width // LANES
    main = out_refs[0].shape[0] // 2
    weight = joint_ref[0:16, width:].astype(F32)[0:8, :tokens]
    mains, tails = picks(weight, main)
    mains = mains[first : first + count]
    pick = jnp.concatenate(mains + [tails, jnp.zeros_like(tails)], axis=0).astype(BF16)
    lane = lax.broadcasted_iota(jnp.int32, (main, LANES), 1)
    for at, base, low in ((0, 0, 0), (tokens, main, chunks)):
        rows = dot(pick, joint_ref[at : at + tokens, :width])
        for j in range(count):
            out_refs[j][base : base + main, :width] = rows[main * j : main * (j + 1)].astype(BF16)
            line = main * count + first + j
            for c in range(chunks):
                fold[c : c + 1, :] = rows[line : line + 1, LANES * c : LANES * (c + 1)]
            out_refs[j][low : low + chunks, width:] = fold[...].astype(BF16)
    for j in range(count):
        mine = weight[first + j : first + j + 1, :]
        column = jnp.sum(mains[j] * mine, axis=1, keepdims=True)
        last = jnp.sum(tails[first + j : first + j + 1, :] * mine, axis=1, keepdims=True)
        out_refs[j][main:, width:] = jnp.where(lane < LANES // 2, column, last).astype(BF16)


def slice_kernel(place_ref, *refs):
    blocks, parts = 4, 4
    in_refs, (keep_ref, near_ref, far_ref, weight_ref, fold) = refs[:blocks], refs[-5:]
    main = in_refs[0].shape[0] // 2
    depth = keep_ref.shape[1] // 2
    width = parts * depth
    chunks = width // LANES
    targets = [(keep_ref, 0), (near_ref, 0), (far_ref, 0), (far_ref, 2 * depth)]
    lane = lax.broadcasted_iota(jnp.int32, (1, LANES), 1)
    lasts = []
    for i in range(blocks):
        for j, (target, shift) in enumerate(targets):
            columns = pl.ds(pl.multiple_of(place_ref[j] * depth, depth), depth)
            for side in range(2):
                at = shift + side * depth
                target[main * i : main * (i + 1), at : at + depth] = in_refs[i][
                    side * main : (side + 1) * main, columns
                ]
        for side in range(2):
            fold[side, chunks * i : chunks * (i + 1), :] = in_refs[i][
                side * chunks : (side + 1) * chunks, width:
            ].astype(F32)
        weights = in_refs[i][main:, width:].astype(F32)
        weight_ref[main * i : main * (i + 1), :] = weights
        last = jnp.sum(jnp.where(lane == LANES - 1, weights[0:1, :], 0.0), axis=1, keepdims=True)
        lasts.append(jnp.broadcast_to(last, (1, LANES)))
    weight_ref[main * blocks :, :] = jnp.concatenate(lasts + [jnp.zeros((16 - blocks, LANES), F32)], axis=0)
    each = chunks // parts
    for j, (target, shift) in enumerate(targets):
        for side in range(2):
            for q in range(each):
                tail = fold[side, pl.ds(place_ref[j] * each + q, blocks, stride=chunks), :]
                tail = jnp.concatenate([tail, jnp.zeros((16 - blocks, LANES), F32)], axis=0).astype(BF16)
                at = shift + side * depth + q * LANES
                target[main * blocks :, at : at + LANES] = tail


def main_kernel(early, place_ref, w_ref, *refs):
    blocks, parts = 4, 4
    own_ref, other_ref = refs[:2]
    keep_ref, near_ref, far_ref = refs[2:5]
    mid, backs, (tail, fold) = refs[-3 - blocks], refs[-2 - blocks : -2], refs[-2:]
    depth = keep_ref.shape[1] // 2
    width = parts * depth
    hidden_width = mid.shape[1] // 3
    main = backs[0].shape[0]
    chunks = width // LANES
    total = keep_ref.shape[0]
    first, second = pl.ds(0, depth), pl.ds(depth, depth)
    weights = [own_ref.at[first], other_ref.at[first], own_ref.at[second], other_ref.at[second]]
    pre = jnp.zeros((total, 2 * hidden_width), F32)
    grad = jnp.zeros((total, hidden_width), F32)
    for j, (ref, shift) in enumerate([(keep_ref, 0), (near_ref, 0), (far_ref, 0), (far_ref, 2 * depth)]):
        pre += dot(ref[:, shift : shift + depth], weights[j][:, : 2 * hidden_width])
        grad += dot(ref[:, shift + depth : shift + 2 * depth], weights[j][:, 2 * hidden_width :])
    if early:
        mid[0:early, :] = refs[5][...]
    weight = w_ref[:, 0:1]
    gate_pre = pre[:, :hidden_width]
    up_pre = pre[:, hidden_width:]
    sig = jax.nn.sigmoid(gate_pre)
    act = gate_pre * sig
    hidden = (act * up_pre).astype(BF16).astype(F32)
    route = jnp.sum(hidden * grad, axis=1, keepdims=True)
    grad_hidden = weight * grad
    grad_gate = grad_hidden * up_pre * sig * (1.0 + gate_pre * (1.0 - sig))
    mid[early:, :hidden_width] = grad_gate.astype(BF16)
    mid[early:, hidden_width : 2 * hidden_width] = (grad_hidden * act).astype(BF16)
    mid[early:, 2 * hidden_width :] = (weight * hidden).astype(BF16)
    for j in range(parts):
        columns = pl.ds(pl.multiple_of(place_ref[j] * depth, depth), depth)
        part = dot_nt(mid[early:, : 2 * hidden_width], weights[j][:, : 2 * hidden_width])
        tail[:, columns] = part[main * blocks :]
        part = part.astype(BF16)
        for i in range(blocks):
            backs[i][:, columns] = part[main * i : main * (i + 1)]
    row = lax.broadcasted_iota(jnp.int32, (main, LANES), 0)
    lane = lax.broadcasted_iota(jnp.int32, (main, LANES), 1)
    for i in range(blocks):
        for c in range(chunks):
            fold[c : c + 1, :] = tail[i : i + 1, LANES * c : LANES * (c + 1)]
        backs[i][:chunks, width:] = fold[...].astype(BF16)
        mine = jnp.where(row == lane, route[main * i : main * (i + 1)], 0.0)
        mine = jnp.sum(mine, axis=0, keepdims=True)
        mine = jnp.where(lane[0:1] == main, route[main * blocks + i : main * blocks + i + 1], mine)
        backs[i][chunks:, width:] = jnp.broadcast_to(mine, (main - chunks, LANES)).astype(BF16)


def unpack_sum(weight, block_refs, rows, fold):
    count = len(block_refs)
    main = block_refs[0].shape[0]
    width = rows.shape[1]
    chunks = width // LANES
    mains, tails = picks(weight, main)
    mains = mains[:count]
    pick = jnp.concatenate(mains + [tails, jnp.zeros_like(tails)], axis=0).astype(BF16)
    lane = lax.broadcasted_iota(jnp.int32, (1, LANES), 1)
    routes = []
    for j in range(count):
        rows[main * j : main * (j + 1), :] = block_refs[j][:, :width]
        fold[chunks * j : chunks * (j + 1), :] = block_refs[j][:chunks, width:].astype(F32)
        mine = block_refs[j][chunks:, width:].astype(F32)
        dense = dot(mine[:, :main].astype(BF16), mains[j].astype(BF16))[0:1, :]
        last = jnp.sum(jnp.where(lane == main, mine[0:1, :], 0.0), axis=1, keepdims=True)
        routes.append(dense + last * tails[j : j + 1, :])
    for c in range(chunks):
        tail = fold[pl.ds(c, count, stride=chunks), :]
        tail = jnp.concatenate([tail, jnp.zeros((16 - count, LANES), F32)], axis=0).astype(BF16)
        rows[main * count :, LANES * c : LANES * (c + 1)] = tail
    return dot_tn(pick, rows[...]), routes


def relay_sum_kernel(joint_ref, b0, b1, b2, b3, out_ref, rows, fold):
    tokens, width = out_ref.shape[0], rows.shape[1]
    weight = joint_ref[0:16, width:].astype(F32)[0:8, :tokens]
    summed, routes = unpack_sum(weight, (b0, b1, b2, b3), rows, fold)
    out_ref[:, :width] = summed.astype(BF16)
    out_ref[:, width:] = jnp.zeros((tokens, LANES), BF16)
    block = jnp.concatenate(routes + [jnp.zeros((12, tokens), F32)], axis=0).astype(BF16)
    out_ref[0:16, width : width + tokens] = block


def near_sum_kernel(w_ref, b0, b1, b2, b3, after_ref, grad_ref, route_ref, rows, fold):
    summed, routes = unpack_sum(w_ref[...], (b0, b1, b2, b3), rows, fold)
    grad_ref[...] = summed
    route_ref[...] = jnp.concatenate(routes + [jnp.zeros_like(route) for route in routes], axis=0)


def combine_kernel(peer_ref, named_ref, near_ref, near_route_ref, far_ref, grad_ref, route_ref):
    tokens, width = grad_ref.shape
    grad_ref[...] = (near_ref[...] + far_ref[:, :width].astype(F32)).astype(BF16)
    others = far_ref[0:16, width : width + tokens].astype(F32)
    named = named_ref[...]
    route = jnp.zeros(route_ref.shape, F32)
    for j in range(4):
        route = route + jnp.where(named == peer_ref[j], near_route_ref[j : j + 1, :], 0.0)
        route = route + jnp.where(named == peer_ref[4 + j], others[j : j + 1, :], 0.0)
    route_ref[...] = route.astype(BF16)


def fill(rows, mids, rows_a, rows_b, rows_c, mid_a, mid_b):
    count = rows_a.shape[0]
    rows[0:count, :] = rows_a
    rows[count : 2 * count, :] = rows_b
    rows[2 * count :, :] = rows_c
    mids[0 : 2 * count, :] = mid_a
    mids[2 * count :, :] = mid_b


def first_weight_kernel(rows_a, rows_b, near_ref, mid_ref, in_ref, out_ref, rows, mids):
    depth, hidden_width = out_ref.shape
    near, near_mid = near_ref[:, : 2 * depth], near_ref[:, 4 * depth :]
    fill(rows, mids, rows_a[...], rows_b[...], near, mid_ref[...], near_mid)
    in_ref[...] = dot_tn(rows[:, :depth], mids[:, : 2 * hidden_width])
    out_ref[...] = dot_tn(rows[:, depth:], mids[:, 2 * hidden_width :])


def second_weight_kernel(rows_a, rows_b, near_ref, mid_a, mid_b, in_part, out_part, *refs):
    in_ref, out_ref, rows, mids, in_held, out_held, sems = refs
    depth, hidden_width = out_part.shape
    span = slice(0, 2 * depth)
    fill(rows, mids, rows_a[:, span], rows_b[:, span], near_ref[:, 2 * depth : 4 * depth], mid_a[...], mid_b[...])
    copies = []
    step = depth // 4
    for m in range(4):
        at = slice(m * step, (m + 1) * step)
        lines = pl.ds(m * step, step)
        in_held[at, :] = in_part[at, :] + dot_tn(rows[:, at], mids[:, : 2 * hidden_width])
        copies.append(start(in_held.at[lines], in_ref.at[lines], sems.at[0, m]))
        other = slice(depth + m * step, depth + (m + 1) * step)
        out_held[at, :] = out_part[at, :] + dot_tn(rows[:, other], mids[:, 2 * hidden_width :])
        copies.append(start(out_held.at[lines], out_ref.at[lines], sems.at[1, m]))
    for copy in copies:
        copy.wait()


def call(kernel, outs, smem, vmem, either, scratch, flops, either_outs=0, aliases=None):
    on_vmem = pl.BlockSpec(memory_space=pltpu.VMEM)
    on_either = pl.BlockSpec(memory_space=pl.ANY)
    on_smem = pl.BlockSpec(memory_space=pltpu.SMEM)
    outs = [jax.ShapeDtypeStruct(shape, kind) for shape, kind in outs]
    moved = sum(a.size * a.dtype.itemsize for a in list(vmem) + outs[either_outs:])
    return pl.pallas_call(
        kernel,
        out_shape=tuple(outs),
        in_specs=[on_smem] * len(smem) + [on_vmem] * len(vmem) + [on_either] * len(either),
        out_specs=tuple([on_either] * either_outs + [on_vmem] * (len(outs) - either_outs)),
        scratch_shapes=scratch,
        compiler_params=pltpu.CompilerParams(vmem_limit_bytes=16 * 1024 * 1024),
        cost_estimate=pl.CostEstimate(flops=flops, bytes_accessed=moved, transcendentals=0),
        input_output_aliases=aliases or {},
    )(*smem, *vmem, *either)


def swap(value, axis, mask):
    return lax.ppermute(value, axis, [(i, i ^ mask) for i in range(lax.axis_size(axis))])


def on_device_packed(tokens, grad_out, route_expert, route_weight, gate_up_weight, down_weight):
    token_count, width = tokens.shape
    blocks, parts, half = 8, 4, 4
    hidden_width = down_weight.shape[2]
    depth = width // parts
    chunks = width // LANES
    main = block_rows(token_count, route_expert.shape[1], blocks) // 16 * 16
    rows = main * half + 16

    peers = lax.axis_index("expert") ^ jnp.arange(blocks, dtype=jnp.int32)
    places = lax.axis_index("dp") ^ jnp.arange(parts, dtype=jnp.int32)
    named = route_expert.T
    packed_shape = ((2 * main, width + LANES), BF16)
    back_shape = ((main, width + LANES), BF16)

    joint, dense = call(
        route_kernel,
        [((2 * token_count, width + LANES), BF16), ((blocks, token_count), F32)],
        [peers],
        [named, route_weight.T, tokens, grad_out],
        [],
        [],
        0,
    )
    far_joint = swap(joint, "expert", half)

    (weights,) = call(
        join_kernel,
        [((depth, 3 * hidden_width), BF16)],
        [],
        [gate_up_weight[0], down_weight[0]],
        [],
        [],
        0,
    )
    far_weights = swap(weights, "dp", 2)

    def pack(first, value, after):
        packed = call(
            functools.partial(pack_kernel, first),
            [packed_shape] * half,
            [],
            [value],
            after,
            [pltpu.VMEM((chunks, LANES), F32)],
            4 * (half * main + 16) * token_count * width,
        )
        return [packed[0]] + [swap(packed[j], "expert", j) for j in range(1, half)]

    def sliced(packed, after):
        return call(
            slice_kernel,
            [
                ((rows, 2 * depth), BF16),
                ((rows, 2 * depth), BF16),
                ((rows, 4 * depth), BF16),
                ((rows, LANES), F32),
            ],
            [places],
            packed,
            after,
            [pltpu.VMEM((2, half * chunks, LANES), F32)],
            0,
        )

    own = pack(half, joint, [])
    *own_slices, own_weight = sliced(own, [far_joint])
    own_far = swap(own_slices[2], "dp", 2)
    far = pack(0, far_joint, [own_slices[0], far_weights])
    (stacked,) = call(
        stack_kernel,
        [((2 * depth, 3 * hidden_width), BF16)],
        [],
        [weights, far_weights],
        [far[0]],
        [],
        0,
    )
    weight_parts = [stacked, swap(stacked, "dp", 1)]

    def middle(slices, weight, before):
        early = before[0].shape[0] if before else 0
        return call(
            functools.partial(main_kernel, early),
            [((early + rows, 3 * hidden_width), BF16)] + [back_shape] * half,
            [places],
            [weight, *weight_parts, *slices, *before],
            [],
            [pltpu.VMEM((16, width), F32), pltpu.VMEM((chunks, LANES), F32)],
            2 * rows * width * 5 * hidden_width,
        )

    own_mid, *near_back = middle(own_slices, own_weight, [])
    near_back[1] = swap(near_back[1], "expert", 1)
    *far_slices, far_weight = sliced(far, [own_mid, near_back[1]])
    far_far = swap(far_slices[2], "dp", 2)
    mid, *far_back = middle(far_slices, far_weight, [own_mid])

    sum_scratch = [
        pltpu.VMEM((half * main + 16, width), BF16),
        pltpu.VMEM((half * chunks, LANES), F32),
    ]
    sum_flops = 2 * (half * main + 16) * width * token_count
    far_back = far_back[:1] + [swap(far_back[j], "expert", j) for j in range(1, half)]
    (partial,) = call(
        relay_sum_kernel,
        [((token_count, width + LANES), BF16)],
        [],
        [far_joint, *far_back],
        [],
        sum_scratch,
        sum_flops,
    )
    far_partial = swap(partial, "expert", half)

    mid_far = swap(mid, "dp", 2)
    (near,) = call(
        relay_kernel,
        [((2 * rows, 4 * depth + 3 * hidden_width), BF16)],
        [],
        [own_slices[1], own_far, far_slices[1], far_far, mid],
        [partial],
        [],
        0,
    )
    near = swap(near, "dp", 1)
    near_back = near_back[:2] + [swap(near_back[j], "expert", j) for j in range(2, half)]
    weight_shapes = [((depth, 2 * hidden_width), F32), ((depth, hidden_width), F32)]
    weight_scratch = [pltpu.VMEM((4 * rows, 2 * depth), BF16), pltpu.VMEM((4 * rows, 3 * hidden_width), BF16)]
    weight_flops = 2 * 4 * rows * depth * 3 * hidden_width
    first = call(
        first_weight_kernel,
        weight_shapes,
        [],
        [own_slices[0], far_slices[0], near, mid],
        [],
        weight_scratch,
        weight_flops,
    )
    near_sum, near_route = call(
        near_sum_kernel,
        [((token_count, width), F32), ((blocks, token_count), F32)],
        [],
        [dense, *near_back],
        [first[1]],
        sum_scratch,
        sum_flops,
    )
    grad_tokens, grad_route = call(
        combine_kernel,
        [((token_count, width), BF16), (named.shape, BF16)],
        [peers],
        [named, near_sum, near_route, far_partial],
        [],
        [],
        0,
    )

    (mid_far,) = call(
        after_kernel,
        [(mid_far.shape, BF16)],
        [],
        [],
        [mid_far, first[1], far_partial, near_sum],
        [],
        0,
        1,
        {0: 0},
    )
    grad_gate_up, grad_down = call(
        second_weight_kernel,
        weight_shapes,
        [],
        [own_far, far_far, near, mid_far, swap(mid_far, "dp", 1), *first],
        [],
        weight_scratch
        + [
            pltpu.VMEM((depth, 2 * hidden_width), F32),
            pltpu.VMEM((depth, hidden_width), F32),
            pltpu.SemaphoreType.DMA((2, 4)),
        ],
        weight_flops,
        2,
    )
    return (grad_tokens, grad_route.T, grad_gate_up[None], grad_down[None])


def block_rows(token_count, route_count, expert_total):
    return min(token_count, (token_count * route_count + expert_total - 1) // expert_total + 1)


def to_local(rows, group_count, local_count, capacity):
    tail = rows.shape[2:]
    shaped = rows.reshape((group_count, local_count, capacity) + tail)
    shaped = jnp.swapaxes(shaped, 0, 1)
    return shaped.reshape((local_count, group_count * capacity) + tail)


def to_groups(rows, group_count, local_count, capacity):
    tail = rows.shape[2:]
    shaped = rows.reshape((local_count, group_count, capacity) + tail)
    shaped = jnp.swapaxes(shaped, 0, 1)
    return shaped.reshape((group_count, local_count * capacity) + tail)


def on_device_routed(tokens, grad_out, route_expert, route_weight, gate_up_weight, down_weight):
    token_count, model_width = tokens.shape
    route_count = route_expert.shape[1]
    group_count = lax.axis_size("expert")
    local_count = gate_up_weight.shape[0]
    hidden_width = down_weight.shape[2]
    expert_total = local_count * group_count
    capacity = min(token_count, (token_count * route_count + expert_total - 1) // expert_total + 1)
    slot_total = expert_total * capacity
    flat_expert = route_expert.reshape(-1)
    expert_ids = jnp.arange(expert_total, dtype=jnp.int32)
    onehot = (flat_expert[:, None] == expert_ids[None, :]).astype(jnp.int32)
    before = jnp.cumsum(onehot, axis=0) - onehot
    rank = jnp.sum(before * onehot, axis=1)
    slot_of = flat_expert * capacity + rank
    slot_ids = jnp.arange(slot_total, dtype=jnp.int32)
    placed = slot_ids[:, None] == slot_of[None, :]
    by_token = jnp.any(placed.reshape(slot_total, token_count, route_count), axis=2).astype(
        jnp.bfloat16
    )
    send_x = jnp.dot(by_token, tokens, preferred_element_type=jnp.float32).astype(jnp.bfloat16)
    send_dy = jnp.dot(by_token, grad_out, preferred_element_type=jnp.float32).astype(jnp.bfloat16)
    flat_weight = route_weight.reshape(-1).astype(jnp.float32)
    send_w = jnp.sum(jnp.where(placed, flat_weight[None, :], 0.0), axis=1).astype(jnp.bfloat16)
    recv_x, recv_dy, recv_w = (
        lax.all_to_all(
            send_x.reshape(group_count, local_count * capacity, model_width),
            "expert",
            split_axis=0,
            concat_axis=0,
            tiled=True,
        ),
        lax.all_to_all(
            send_dy.reshape(group_count, local_count * capacity, model_width),
            "expert",
            split_axis=0,
            concat_axis=0,
            tiled=True,
        ),
        lax.all_to_all(
            send_w.reshape(group_count, local_count * capacity),
            "expert",
            split_axis=0,
            concat_axis=0,
            tiled=True,
        ),
    )
    rows_x = to_local(recv_x, group_count, local_count, capacity)
    rows_dy = to_local(recv_dy, group_count, local_count, capacity)
    rows_w = to_local(recv_w, group_count, local_count, capacity)
    full_in, full_out = (
        lax.all_gather(gate_up_weight, "dp", axis=1, tiled=True),
        lax.all_gather(down_weight, "dp", axis=1, tiled=True),
    )
    pre = jnp.einsum("erd,edf->erf", rows_x, full_in, preferred_element_type=jnp.float32)
    gate_pre = pre[:, :, :hidden_width]
    up_pre = pre[:, :, hidden_width:]
    act = swish(gate_pre)
    hidden = (act * up_pre).astype(jnp.bfloat16)
    expert_out = jnp.einsum("erf,edf->erd", hidden, full_out, preferred_element_type=jnp.float32)
    route_grad = jnp.sum(rows_dy.astype(jnp.float32) * expert_out, axis=2).astype(jnp.bfloat16)
    scaled = (rows_w.astype(jnp.float32)[:, :, None] * rows_dy).astype(jnp.bfloat16)
    grad_hidden = jnp.einsum("erd,edf->erf", scaled, full_out, preferred_element_type=jnp.float32)
    sig = jax.nn.sigmoid(gate_pre)
    grad_gate = grad_hidden * up_pre * sig * (1.0 + gate_pre * (1.0 - sig))
    grad_up = grad_hidden * act
    grad_pre = jnp.concatenate([grad_gate, grad_up], axis=2).astype(jnp.bfloat16)
    rows_grad = jnp.einsum(
        "erf,edf->erd", grad_pre, full_in, preferred_element_type=jnp.float32
    ).astype(jnp.bfloat16)
    back_x, back_w = (
        lax.all_to_all(
            to_groups(rows_grad, group_count, local_count, capacity),
            "expert",
            split_axis=0,
            concat_axis=0,
            tiled=True,
        ),
        lax.all_to_all(
            to_groups(route_grad, group_count, local_count, capacity),
            "expert",
            split_axis=0,
            concat_axis=0,
            tiled=True,
        ),
    )
    back_x = back_x.reshape(slot_total, model_width)
    back_w = back_w.reshape(slot_total).astype(jnp.float32)
    grad_tokens = jnp.einsum(
        "st,sd->td", by_token, back_x, preferred_element_type=jnp.float32
    ).astype(jnp.bfloat16)
    grad_route = jnp.sum(jnp.where(placed, back_w[:, None], 0.0), axis=0)
    grad_route = grad_route.reshape(token_count, route_count).astype(jnp.bfloat16)
    all_x = lax.all_to_all(rows_x, "dp", split_axis=2, concat_axis=1, tiled=True)
    grad_gate_up = jnp.einsum(
        "erd,erf->edf",
        all_x,
        lax.all_gather(grad_pre, "dp", axis=1, tiled=True),
        preferred_element_type=jnp.float32,
    )
    summed = lax.psum_scatter(
        jnp.einsum("erd,erf->def", scaled, hidden, preferred_element_type=jnp.float32),
        "dp",
        scatter_dimension=0,
        tiled=True,
    )
    grad_down = jnp.swapaxes(summed, 0, 1)
    return (grad_tokens, grad_route, grad_gate_up, grad_down)


def packs(tokens, route_expert, down_weight):
    chunks = tokens.shape[1] // LANES
    capacity = block_rows(tokens.shape[0], route_expert.shape[1], lax.axis_size("expert"))
    return (
        lax.axis_size("expert") == 8
        and lax.axis_size("dp") == 4
        and down_weight.shape[0] == 1
        and capacity % 16 <= 1
        and chunks == 16
        and 2 * chunks <= capacity < LANES // 2
    )


def solution(mesh):
    def on_device(*arrays):
        if packs(arrays[0], arrays[2], arrays[5]):
            return on_device_packed(*arrays)
        return on_device_routed(*arrays)

    return jax.shard_map(
        on_device,
        mesh=mesh,
        in_specs=(
            P(("expert", "dp"), None),
            P(("expert", "dp"), None),
            P(("expert", "dp"), None),
            P(("expert", "dp"), None),
            P("expert", "dp", None),
            P("expert", "dp", None),
        ),
        out_specs=(
            P(("expert", "dp"), None),
            P(("expert", "dp"), None),
            P("expert", "dp", None),
            P("expert", "dp", None),
        ),
        check_vma=False,
    )
```

```python
import functools

import jax
import jax.numpy as jnp
from jax import lax
from jax.experimental import pallas as pl
from jax.experimental.pallas import tpu as pltpu
from jax.sharding import PartitionSpec as P

BF16 = jnp.bfloat16
F32 = jnp.float32
LANES = 128


def swish(value):
    return value * jax.nn.sigmoid(value)


def dot(a, b):
    return jnp.dot(a, b, preferred_element_type=F32)


def dot_nt(a, b):
    return lax.dot_general(a, b, (((1,), (1,)), ((), ())), preferred_element_type=F32)


def dot_tn(a, b):
    return lax.dot_general(a, b, (((0,), (0,)), ((), ())), preferred_element_type=F32)


def start(source, target, sem):
    copy = pltpu.make_async_copy(source, target, sem)
    copy.start()
    return copy


def picks(weight, main):
    token_count = weight.shape[1]
    routed = weight != 0.0
    first = lax.broadcasted_iota(jnp.int32, (token_count, token_count), 0)
    second = lax.broadcasted_iota(jnp.int32, (token_count, token_count), 1)
    upper = (first < second).astype(F32).astype(BF16)
    rank = dot(routed.astype(F32).astype(BF16), upper)
    rank = jnp.where(routed, rank, -1.0).astype(jnp.int32)
    slots = lax.broadcasted_iota(jnp.int32, (main, token_count), 0)
    mains = [(slots == rank[i : i + 1, :]).astype(F32) for i in range(weight.shape[0])]
    tails = (rank == main).astype(F32)
    return mains, tails


def route_kernel(peer_ref, named_ref, given_ref, x_ref, dy_ref, joint_ref, dense_ref):
    count, width = x_ref.shape
    named = named_ref[...]
    given = given_ref[...].astype(F32)
    experts = dense_ref.shape[0]
    lines = [
        jnp.sum(jnp.where(named == peer_ref[i], given, 0.0), axis=0, keepdims=True) for i in range(experts)
    ]
    dense = jnp.concatenate(lines, axis=0)
    dense_ref[...] = dense
    turned = jnp.concatenate(lines[experts // 2 :] + lines[: experts // 2] + [jnp.zeros_like(dense)], axis=0)
    joint_ref[:, :width] = x_ref[...]
    joint_ref[:, width : 2 * width] = dy_ref[...]
    joint_ref[:, 2 * width :] = jnp.zeros((count, LANES), BF16)
    joint_ref[0:16, 2 * width : 2 * width + count] = turned.astype(BF16)


def stack_kernel(own_ref, far_ref, after_ref, stacked_ref):
    count = own_ref.shape[0]
    stacked_ref[0:count, :] = own_ref[...]
    stacked_ref[count:, :] = far_ref[...]


def after_kernel(*refs):
    pass


def relay_kernel(near_a, far_a, near_b, far_b, mid_ref, *refs):
    joint_ref = refs[-1]
    count, width = near_a.shape
    for at, near, far in ((0, near_a, far_a), (count, near_b, far_b)):
        joint_ref[at : at + count, :width] = near[...]
        joint_ref[at : at + count, width : 2 * width] = far[:, width:]
    joint_ref[:, 2 * width :] = mid_ref[...]


def pack_blocks(experts, joint_ref, out_refs, fold):
    count = len(experts)
    tokens, width = joint_ref.shape[0], out_refs[0].shape[1] - LANES
    chunks = width // LANES
    main = out_refs[0].shape[0] // 2
    weight = joint_ref[0:16, 2 * width :].astype(F32)[0:8, :tokens]
    mains, tails = picks(weight, main)
    pick = jnp.concatenate([mains[e] for e in experts] + [tails, jnp.zeros_like(tails)], axis=0).astype(BF16)
    lane = lax.broadcasted_iota(jnp.int32, (main, LANES), 1)
    for at, base, low in ((0, 0, 0), (width, main, chunks)):
        rows = dot(pick, joint_ref[:, at : at + width])
        for j, e in enumerate(experts):
            out_refs[j][base : base + main, :width] = rows[main * j : main * (j + 1)].astype(BF16)
            line = main * count + e
            for c in range(chunks):
                fold[c : c + 1, :] = rows[line : line + 1, LANES * c : LANES * (c + 1)]
            out_refs[j][low : low + chunks, width:] = fold[...].astype(BF16)
    for j, e in enumerate(experts):
        mine = weight[e : e + 1, :]
        column = jnp.sum(mains[e] * mine, axis=1, keepdims=True)
        last = jnp.sum(tails[e : e + 1, :] * mine, axis=1, keepdims=True)
        out_refs[j][main:, width:] = jnp.where(lane < LANES // 2, column, last).astype(BF16)


def pack_kernel(experts, joint_ref, *refs):
    pack_blocks(experts, joint_ref, refs[-1 - len(experts) : -1], refs[-1])


def slice_kernel(own, place_ref, *refs):
    blocks, parts = 4, 4
    keep_ref, near_ref, far_ref, weight_ref, fold, kept = refs[-6:]
    in_refs = list(refs[:blocks])
    if own:
        in_refs[0] = kept
        pack_blocks([own], refs[0], [kept], fold.at[0, pl.ds(0, 16)])
    main = in_refs[0].shape[0] // 2
    depth = keep_ref.shape[1] // 2
    width = parts * depth
    chunks = width // LANES
    targets = [(keep_ref, 0), (near_ref, 0), (far_ref, 0), (far_ref, 2 * depth)]
    lane = lax.broadcasted_iota(jnp.int32, (1, LANES), 1)
    lasts = []
    for i in range(blocks):
        for j, (target, shift) in enumerate(targets):
            columns = pl.ds(pl.multiple_of(place_ref[j] * depth, depth), depth)
            for side in range(2):
                at = shift + side * depth
                target[main * i : main * (i + 1), at : at + depth] = in_refs[i][
                    side * main : (side + 1) * main, columns
                ]
        for side in range(2):
            fold[side, chunks * i : chunks * (i + 1), :] = in_refs[i][
                side * chunks : (side + 1) * chunks, width:
            ].astype(F32)
        weights = in_refs[i][main:, width:].astype(F32)
        weight_ref[main * i : main * (i + 1), :] = weights
        last = jnp.sum(jnp.where(lane == LANES - 1, weights[0:1, :], 0.0), axis=1, keepdims=True)
        lasts.append(jnp.broadcast_to(last, (1, LANES)))
    weight_ref[main * blocks :, :] = jnp.concatenate(lasts + [jnp.zeros((16 - blocks, LANES), F32)], axis=0)
    each = chunks // parts
    for j, (target, shift) in enumerate(targets):
        for side in range(2):
            for q in range(each):
                tail = fold[side, pl.ds(place_ref[j] * each + q, blocks, stride=chunks), :]
                tail = jnp.concatenate([tail, jnp.zeros((16 - blocks, LANES), F32)], axis=0).astype(BF16)
                at = shift + side * depth + q * LANES
                target[main * blocks :, at : at + LANES] = tail


def main_kernel(early, place_ref, w_ref, *refs):
    blocks, parts = 4, 4
    own_ref, other_ref = refs[:2]
    keep_ref, near_ref, far_ref = refs[2:5]
    mid, backs, (tail, fold) = refs[-3 - blocks], refs[-2 - blocks : -2], refs[-2:]
    depth = keep_ref.shape[1] // 2
    width = parts * depth
    hidden_width = mid.shape[1] // 3
    main = backs[0].shape[0]
    chunks = width // LANES
    total = keep_ref.shape[0]
    first, second = pl.ds(0, depth), pl.ds(depth, depth)
    weights = [own_ref.at[first], other_ref.at[first], own_ref.at[second], other_ref.at[second]]
    pre = jnp.zeros((total, 2 * hidden_width), F32)
    grad = jnp.zeros((total, hidden_width), F32)
    for j, (ref, shift) in enumerate([(keep_ref, 0), (near_ref, 0), (far_ref, 0), (far_ref, 2 * depth)]):
        pre += dot(ref[:, shift : shift + depth], weights[j][:, : 2 * hidden_width])
        grad += dot(ref[:, shift + depth : shift + 2 * depth], weights[j][:, 2 * hidden_width :])
    if early:
        mid[0:early, :] = refs[5][...]
    weight = w_ref[:, 0:1]
    gate_pre = pre[:, :hidden_width]
    up_pre = pre[:, hidden_width:]
    sig = jax.nn.sigmoid(gate_pre)
    act = gate_pre * sig
    hidden = (act * up_pre).astype(BF16).astype(F32)
    route = jnp.sum(hidden * grad, axis=1, keepdims=True)
    grad_hidden = weight * grad
    grad_gate = grad_hidden * up_pre * sig * (1.0 + gate_pre * (1.0 - sig))
    mid[early:, :hidden_width] = grad_gate.astype(BF16)
    mid[early:, hidden_width : 2 * hidden_width] = (grad_hidden * act).astype(BF16)
    mid[early:, 2 * hidden_width :] = (weight * hidden).astype(BF16)
    for j in range(parts):
        columns = pl.ds(pl.multiple_of(place_ref[j] * depth, depth), depth)
        part = dot_nt(mid[early:, : 2 * hidden_width], weights[j][:, : 2 * hidden_width])
        tail[:, columns] = part[main * blocks :]
        part = part.astype(BF16)
        for i in range(blocks):
            backs[i][:, columns] = part[main * i : main * (i + 1)]
    row = lax.broadcasted_iota(jnp.int32, (main, LANES), 0)
    lane = lax.broadcasted_iota(jnp.int32, (main, LANES), 1)
    for i in range(blocks):
        for c in range(chunks):
            fold[c : c + 1, :] = tail[i : i + 1, LANES * c : LANES * (c + 1)]
        backs[i][:chunks, width:] = fold[...].astype(BF16)
        mine = jnp.where(row == lane, route[main * i : main * (i + 1)], 0.0)
        mine = jnp.sum(mine, axis=0, keepdims=True)
        mine = jnp.where(lane[0:1] == main, route[main * blocks + i : main * blocks + i + 1], mine)
        backs[i][chunks:, width:] = jnp.broadcast_to(mine, (main - chunks, LANES)).astype(BF16)


def unpack_sum(weight, block_refs, rows, fold):
    count = len(block_refs)
    main = block_refs[0].shape[0]
    width = rows.shape[1]
    chunks = width // LANES
    mains, tails = picks(weight, main)
    mains = mains[:count]
    pick = jnp.concatenate(mains + [tails, jnp.zeros_like(tails)], axis=0).astype(BF16)
    lane = lax.broadcasted_iota(jnp.int32, (1, LANES), 1)
    routes = []
    for j in range(count):
        rows[main * j : main * (j + 1), :] = block_refs[j][:, :width]
        fold[chunks * j : chunks * (j + 1), :] = block_refs[j][:chunks, width:].astype(F32)
        mine = block_refs[j][chunks:, width:].astype(F32)
        dense = dot(mine[:, :main].astype(BF16), mains[j].astype(BF16))[0:1, :]
        last = jnp.sum(jnp.where(lane == main, mine[0:1, :], 0.0), axis=1, keepdims=True)
        routes.append(dense + last * tails[j : j + 1, :])
    for c in range(chunks):
        tail = fold[pl.ds(c, count, stride=chunks), :]
        tail = jnp.concatenate([tail, jnp.zeros((16 - count, LANES), F32)], axis=0).astype(BF16)
        rows[main * count :, LANES * c : LANES * (c + 1)] = tail
    return dot_tn(pick, rows[...]), routes


def relay_sum_kernel(joint_ref, b0, b1, b2, b3, out_ref, rows, fold):
    tokens, width = joint_ref.shape[0], rows.shape[1]
    weight = joint_ref[0:16, 2 * width :].astype(F32)[0:8, :tokens]
    summed, routes = unpack_sum(weight, (b0, b1, b2, b3), rows, fold)
    lines = tokens // 2
    out_ref[:, :width] = summed[0:lines].astype(BF16)
    out_ref[:, width : 2 * width] = summed[lines:].astype(BF16)
    out_ref[:, 2 * width :] = jnp.zeros((lines, LANES), BF16)
    block = jnp.concatenate(routes + [jnp.zeros((12, tokens), F32)], axis=0).astype(BF16)
    out_ref[0:16, 2 * width : 2 * width + tokens] = block


def near_sum_kernel(w_ref, b0, b1, b2, b3, after_ref, grad_ref, route_ref, rows, fold):
    summed, routes = unpack_sum(w_ref[...], (b0, b1, b2, b3), rows, fold)
    grad_ref[...] = summed
    route_ref[...] = jnp.concatenate(routes + [jnp.zeros_like(route) for route in routes], axis=0)


def combine_kernel(peer_ref, named_ref, near_ref, near_route_ref, far_ref, grad_ref, route_ref):
    tokens, width = grad_ref.shape
    lines = tokens // 2
    for half in range(2):
        at, columns = slice(half * lines, (half + 1) * lines), slice(half * width, (half + 1) * width)
        grad_ref[at, :] = (near_ref[at, :] + far_ref[:, columns].astype(F32)).astype(BF16)
    others = far_ref[0:16, 2 * width : 2 * width + tokens].astype(F32)
    named = named_ref[...]
    route = jnp.zeros(route_ref.shape, F32)
    for j in range(4):
        route = route + jnp.where(named == peer_ref[j], near_route_ref[j : j + 1, :], 0.0)
        route = route + jnp.where(named == peer_ref[4 + j], others[j : j + 1, :], 0.0)
    route_ref[...] = route.astype(BF16)


def fill(rows, mids, rows_a, rows_b, rows_c, mid_a, mid_b):
    count = rows_a.shape[0]
    rows[0:count, :] = rows_a
    rows[count : 2 * count, :] = rows_b
    rows[2 * count :, :] = rows_c
    mids[0 : 2 * count, :] = mid_a
    mids[2 * count :, :] = mid_b


def first_weight_kernel(rows_a, rows_b, near_ref, mid_ref, in_ref, out_ref, rows, mids):
    depth, hidden_width = out_ref.shape
    near, near_mid = near_ref[:, : 2 * depth], near_ref[:, 4 * depth :]
    fill(rows, mids, rows_a[...], rows_b[...], near, mid_ref[...], near_mid)
    in_ref[...] = dot_tn(rows[:, :depth], mids[:, : 2 * hidden_width])
    out_ref[...] = dot_tn(rows[:, depth:], mids[:, 2 * hidden_width :])


def second_weight_kernel(rows_a, rows_b, mid_ref, in_part, out_part, in_ref, out_ref, rows):
    depth, hidden_width = out_ref.shape
    count = rows_a.shape[0]
    rows[0:count, :] = rows_a[:, : 2 * depth]
    rows[count:, :] = rows_b[:, : 2 * depth]
    in_ref[...] = in_part[...] + dot_tn(rows[:, :depth], mid_ref[:, : 2 * hidden_width])
    out_ref[...] = out_part[...] + dot_tn(rows[:, depth:], mid_ref[:, 2 * hidden_width :])


def last_weight_kernel(near_ref, mid_ref, in_part, out_part, in_ref, out_ref, in_held, out_held, sems):
    depth, hidden_width = out_part.shape
    copies = []
    step = depth // 4
    for m in range(4):
        at = slice(m * step, (m + 1) * step)
        lines = pl.ds(m * step, step)
        base = 2 * depth + m * step
        in_held[at, :] = in_part[at, :] + dot_tn(near_ref[:, base : base + step], mid_ref[:, : 2 * hidden_width])
        copies.append(start(in_held.at[lines], in_ref.at[lines], sems.at[0, m]))
        base += depth
        out_held[at, :] = out_part[at, :] + dot_tn(near_ref[:, base : base + step], mid_ref[:, 2 * hidden_width :])
        copies.append(start(out_held.at[lines], out_ref.at[lines], sems.at[1, m]))
    for copy in copies:
        copy.wait()


def call(kernel, outs, smem, vmem, either, scratch, flops, either_outs=0, aliases=None):
    on_vmem = pl.BlockSpec(memory_space=pltpu.VMEM)
    on_either = pl.BlockSpec(memory_space=pl.ANY)
    on_smem = pl.BlockSpec(memory_space=pltpu.SMEM)
    outs = [jax.ShapeDtypeStruct(shape, kind) for shape, kind in outs]
    moved = sum(a.size * a.dtype.itemsize for a in list(vmem) + outs[either_outs:])
    return pl.pallas_call(
        kernel,
        out_shape=tuple(outs),
        in_specs=[on_smem] * len(smem) + [on_vmem] * len(vmem) + [on_either] * len(either),
        out_specs=tuple([on_either] * either_outs + [on_vmem] * (len(outs) - either_outs)),
        scratch_shapes=scratch,
        compiler_params=pltpu.CompilerParams(vmem_limit_bytes=16 * 1024 * 1024),
        cost_estimate=pl.CostEstimate(flops=flops, bytes_accessed=moved, transcendentals=0),
        input_output_aliases=aliases or {},
    )(*smem, *vmem, *either)


def swap(value, axis, mask):
    return lax.ppermute(value, axis, [(i, i ^ mask) for i in range(lax.axis_size(axis))])


def on_device_packed(tokens, grad_out, route_expert, route_weight, gate_up_weight, down_weight):
    token_count, width = tokens.shape
    blocks, parts, half = 8, 4, 4
    hidden_width = down_weight.shape[2]
    depth = width // parts
    chunks = width // LANES
    main = block_rows(token_count, route_expert.shape[1], blocks) // 16 * 16
    rows = main * half + 16

    peers = lax.axis_index("expert") ^ jnp.arange(blocks, dtype=jnp.int32)
    places = lax.axis_index("dp") ^ jnp.arange(parts, dtype=jnp.int32)
    named = route_expert.T
    packed_shape = ((2 * main, width + LANES), BF16)
    back_shape = ((main, width + LANES), BF16)

    joint, dense = call(
        route_kernel,
        [((token_count, 2 * width + LANES), BF16), ((blocks, token_count), F32)],
        [peers],
        [named, route_weight.T, tokens, grad_out],
        [],
        [],
        0,
    )
    far_joint = swap(joint, "expert", half)

    weights = jnp.concatenate([gate_up_weight[0], down_weight[0]], axis=1)
    far_weights = swap(weights, "dp", 2)

    def pack(experts, value, after):
        return call(
            functools.partial(pack_kernel, experts),
            [packed_shape] * len(experts),
            [],
            [value],
            after,
            [pltpu.VMEM((chunks, LANES), F32)],
            4 * (len(experts) * main + 16) * token_count * width,
        )

    def sliced(own, packed, after):
        return call(
            functools.partial(slice_kernel, own),
            [
                ((rows, 2 * depth), BF16),
                ((rows, 2 * depth), BF16),
                ((rows, 4 * depth), BF16),
                ((rows, LANES), F32),
            ],
            [places],
            packed,
            after,
            [pltpu.VMEM((2, half * chunks, LANES), F32), pltpu.VMEM(*packed_shape)],
            0,
        )

    own = [swap(value, "expert", j + 1) for j, value in enumerate(pack(range(half + 1, blocks), joint, []))]
    *own_slices, own_weight = sliced(half, [joint, *own], [far_joint])
    own_far = swap(own_slices[2], "dp", 2)
    far = pack(range(half), far_joint, [own_slices[0], far_weights])
    far = [far[0]] + [swap(far[j], "expert", j) for j in range(1, half)]
    (stacked,) = call(
        stack_kernel,
        [((2 * depth, 3 * hidden_width), BF16)],
        [],
        [weights, far_weights],
        [far[0]],
        [],
        0,
    )
    weight_parts = [stacked, swap(stacked, "dp", 1)]

    def middle(slices, weight, before, after):
        early = before[0].shape[0] if before else 0
        return call(
            functools.partial(main_kernel, early),
            [((early + rows, 3 * hidden_width), BF16)] + [back_shape] * half,
            [places],
            [weight, *weight_parts, *slices, *before],
            after,
            [pltpu.VMEM((16, width), F32), pltpu.VMEM((chunks, LANES), F32)],
            2 * rows * width * 5 * hidden_width,
        )

    own_mid, *near_back = middle(own_slices, own_weight, [], [])
    near_back = near_back[:1] + [swap(near_back[j], "expert", j) for j in range(1, half)]
    *far_slices, far_weight = sliced(None, far, [own_mid, own_far])
    far_far = swap(far_slices[2], "dp", 2)
    mid, *far_back = middle(far_slices, far_weight, [own_mid], [])

    sum_scratch = [
        pltpu.VMEM((half * main + 16, width), BF16),
        pltpu.VMEM((half * chunks, LANES), F32),
    ]
    sum_flops = 2 * (half * main + 16) * width * token_count
    far_back = far_back[:1] + [swap(far_back[j], "expert", j) for j in range(1, half)]
    (partial,) = call(
        relay_sum_kernel,
        [((token_count // 2, 2 * width + LANES), BF16)],
        [],
        [far_joint, *far_back],
        [],
        sum_scratch,
        sum_flops,
    )
    far_partial = swap(partial, "expert", half)

    mid_far = swap(mid, "dp", 2)
    (near,) = call(
        relay_kernel,
        [((2 * rows, 4 * depth + 3 * hidden_width), BF16)],
        [],
        [own_slices[1], own_far, far_slices[1], far_far, mid],
        [partial, near_back[1]],
        [],
        0,
    )
    near = swap(near, "dp", 1)
    weight_shapes = [((depth, 2 * hidden_width), F32), ((depth, hidden_width), F32)]
    weight_scratch = [pltpu.VMEM((4 * rows, 2 * depth), BF16), pltpu.VMEM((4 * rows, 3 * hidden_width), BF16)]
    weight_flops = 2 * 4 * rows * depth * 3 * hidden_width
    first = call(
        first_weight_kernel,
        weight_shapes,
        [],
        [own_slices[0], far_slices[0], near, mid],
        [],
        weight_scratch,
        weight_flops,
    )
    near_sum, near_route = call(
        near_sum_kernel,
        [((token_count, width), F32), ((blocks, token_count), F32)],
        [],
        [dense, *near_back],
        [first[1]],
        sum_scratch,
        sum_flops,
    )
    grad_tokens, grad_route = call(
        combine_kernel,
        [((token_count, width), BF16), (named.shape, BF16)],
        [peers],
        [named, near_sum, near_route, far_partial],
        [],
        [],
        0,
    )

    (mid_far,) = call(
        after_kernel,
        [(mid_far.shape, BF16)],
        [],
        [],
        [mid_far, first[1], far_partial, near_sum],
        [],
        0,
        1,
        {0: 0},
    )
    second = call(
        second_weight_kernel,
        weight_shapes,
        [],
        [own_far, far_far, mid_far, *first],
        [],
        [pltpu.VMEM((2 * rows, 2 * depth), BF16)],
        weight_flops // 2,
    )
    grad_gate_up, grad_down = call(
        last_weight_kernel,
        weight_shapes,
        [],
        [near, swap(mid_far, "dp", 1), *second],
        [],
        [
            pltpu.VMEM((depth, 2 * hidden_width), F32),
            pltpu.VMEM((depth, hidden_width), F32),
            pltpu.SemaphoreType.DMA((2, 4)),
        ],
        weight_flops // 2,
        2,
    )
    return (grad_tokens, grad_route.T, grad_gate_up[None], grad_down[None])


def block_rows(token_count, route_count, expert_total):
    return min(token_count, (token_count * route_count + expert_total - 1) // expert_total + 1)


def to_local(rows, group_count, local_count, capacity):
    tail = rows.shape[2:]
    shaped = rows.reshape((group_count, local_count, capacity) + tail)
    shaped = jnp.swapaxes(shaped, 0, 1)
    return shaped.reshape((local_count, group_count * capacity) + tail)


def to_groups(rows, group_count, local_count, capacity):
    tail = rows.shape[2:]
    shaped = rows.reshape((local_count, group_count, capacity) + tail)
    shaped = jnp.swapaxes(shaped, 0, 1)
    return shaped.reshape((group_count, local_count * capacity) + tail)


def on_device_routed(tokens, grad_out, route_expert, route_weight, gate_up_weight, down_weight):
    token_count, model_width = tokens.shape
    route_count = route_expert.shape[1]
    group_count = lax.axis_size("expert")
    local_count = gate_up_weight.shape[0]
    hidden_width = down_weight.shape[2]
    expert_total = local_count * group_count
    capacity = min(token_count, (token_count * route_count + expert_total - 1) // expert_total + 1)
    slot_total = expert_total * capacity
    flat_expert = route_expert.reshape(-1)
    expert_ids = jnp.arange(expert_total, dtype=jnp.int32)
    onehot = (flat_expert[:, None] == expert_ids[None, :]).astype(jnp.int32)
    before = jnp.cumsum(onehot, axis=0) - onehot
    rank = jnp.sum(before * onehot, axis=1)
    slot_of = flat_expert * capacity + rank
    slot_ids = jnp.arange(slot_total, dtype=jnp.int32)
    placed = slot_ids[:, None] == slot_of[None, :]
    by_token = jnp.any(placed.reshape(slot_total, token_count, route_count), axis=2).astype(
        jnp.bfloat16
    )
    send_x = jnp.dot(by_token, tokens, preferred_element_type=jnp.float32).astype(jnp.bfloat16)
    send_dy = jnp.dot(by_token, grad_out, preferred_element_type=jnp.float32).astype(jnp.bfloat16)
    flat_weight = route_weight.reshape(-1).astype(jnp.float32)
    send_w = jnp.sum(jnp.where(placed, flat_weight[None, :], 0.0), axis=1).astype(jnp.bfloat16)
    recv_x, recv_dy, recv_w = (
        lax.all_to_all(
            send_x.reshape(group_count, local_count * capacity, model_width),
            "expert",
            split_axis=0,
            concat_axis=0,
            tiled=True,
        ),
        lax.all_to_all(
            send_dy.reshape(group_count, local_count * capacity, model_width),
            "expert",
            split_axis=0,
            concat_axis=0,
            tiled=True,
        ),
        lax.all_to_all(
            send_w.reshape(group_count, local_count * capacity),
            "expert",
            split_axis=0,
            concat_axis=0,
            tiled=True,
        ),
    )
    rows_x = to_local(recv_x, group_count, local_count, capacity)
    rows_dy = to_local(recv_dy, group_count, local_count, capacity)
    rows_w = to_local(recv_w, group_count, local_count, capacity)
    full_in, full_out = (
        lax.all_gather(gate_up_weight, "dp", axis=1, tiled=True),
        lax.all_gather(down_weight, "dp", axis=1, tiled=True),
    )
    pre = jnp.einsum("erd,edf->erf", rows_x, full_in, preferred_element_type=jnp.float32)
    gate_pre = pre[:, :, :hidden_width]
    up_pre = pre[:, :, hidden_width:]
    act = swish(gate_pre)
    hidden = (act * up_pre).astype(jnp.bfloat16)
    expert_out = jnp.einsum("erf,edf->erd", hidden, full_out, preferred_element_type=jnp.float32)
    route_grad = jnp.sum(rows_dy.astype(jnp.float32) * expert_out, axis=2).astype(jnp.bfloat16)
    scaled = (rows_w.astype(jnp.float32)[:, :, None] * rows_dy).astype(jnp.bfloat16)
    grad_hidden = jnp.einsum("erd,edf->erf", scaled, full_out, preferred_element_type=jnp.float32)
    sig = jax.nn.sigmoid(gate_pre)
    grad_gate = grad_hidden * up_pre * sig * (1.0 + gate_pre * (1.0 - sig))
    grad_up = grad_hidden * act
    grad_pre = jnp.concatenate([grad_gate, grad_up], axis=2).astype(jnp.bfloat16)
    rows_grad = jnp.einsum(
        "erf,edf->erd", grad_pre, full_in, preferred_element_type=jnp.float32
    ).astype(jnp.bfloat16)
    back_x, back_w = (
        lax.all_to_all(
            to_groups(rows_grad, group_count, local_count, capacity),
            "expert",
            split_axis=0,
            concat_axis=0,
            tiled=True,
        ),
        lax.all_to_all(
            to_groups(route_grad, group_count, local_count, capacity),
            "expert",
            split_axis=0,
            concat_axis=0,
            tiled=True,
        ),
    )
    back_x = back_x.reshape(slot_total, model_width)
    back_w = back_w.reshape(slot_total).astype(jnp.float32)
    grad_tokens = jnp.einsum(
        "st,sd->td", by_token, back_x, preferred_element_type=jnp.float32
    ).astype(jnp.bfloat16)
    grad_route = jnp.sum(jnp.where(placed, back_w[:, None], 0.0), axis=0)
    grad_route = grad_route.reshape(token_count, route_count).astype(jnp.bfloat16)
    all_x = lax.all_to_all(rows_x, "dp", split_axis=2, concat_axis=1, tiled=True)
    grad_gate_up = jnp.einsum(
        "erd,erf->edf",
        all_x,
        lax.all_gather(grad_pre, "dp", axis=1, tiled=True),
        preferred_element_type=jnp.float32,
    )
    summed = lax.psum_scatter(
        jnp.einsum("erd,erf->def", scaled, hidden, preferred_element_type=jnp.float32),
        "dp",
        scatter_dimension=0,
        tiled=True,
    )
    grad_down = jnp.swapaxes(summed, 0, 1)
    return (grad_tokens, grad_route, grad_gate_up, grad_down)


def packs(tokens, route_expert, down_weight):
    chunks = tokens.shape[1] // LANES
    capacity = block_rows(tokens.shape[0], route_expert.shape[1], lax.axis_size("expert"))
    return (
        lax.axis_size("expert") == 8
        and lax.axis_size("dp") == 4
        and down_weight.shape[0] == 1
        and capacity % 16 <= 1
        and chunks == 16
        and 2 * chunks <= capacity < LANES // 2
    )


def solution(mesh):
    def on_device(*arrays):
        if packs(arrays[0], arrays[2], arrays[5]):
            return on_device_packed(*arrays)
        return on_device_routed(*arrays)

    return jax.shard_map(
        on_device,
        mesh=mesh,
        in_specs=(
            P(("expert", "dp"), None),
            P(("expert", "dp"), None),
            P(("expert", "dp"), None),
            P(("expert", "dp"), None),
            P("expert", "dp", None),
            P("expert", "dp", None),
        ),
        out_specs=(
            P(("expert", "dp"), None),
            P(("expert", "dp"), None),
            P("expert", "dp", None),
            P("expert", "dp", None),
        ),
        check_vma=False,
    )
```

```python
import functools

import jax
import jax.numpy as jnp
from jax import lax
from jax.experimental import pallas as pl
from jax.experimental.pallas import tpu as pltpu
from jax.sharding import PartitionSpec as P

BF16 = jnp.bfloat16
F32 = jnp.float32
LANES = 128


def swish(value):
    return value * jax.nn.sigmoid(value)


def dot(a, b):
    return jnp.dot(a, b, preferred_element_type=F32)


def dot_nt(a, b):
    return lax.dot_general(a, b, (((1,), (1,)), ((), ())), preferred_element_type=F32)


def dot_tn(a, b):
    return lax.dot_general(a, b, (((0,), (0,)), ((), ())), preferred_element_type=F32)


def start(source, target, sem):
    copy = pltpu.make_async_copy(source, target, sem)
    copy.start()
    return copy


def picks(weight, main):
    token_count = weight.shape[1]
    routed = weight != 0.0
    first = lax.broadcasted_iota(jnp.int32, (token_count, token_count), 0)
    second = lax.broadcasted_iota(jnp.int32, (token_count, token_count), 1)
    upper = (first < second).astype(F32).astype(BF16)
    rank = dot(routed.astype(F32).astype(BF16), upper)
    rank = jnp.where(routed, rank, -1.0).astype(jnp.int32)
    slots = lax.broadcasted_iota(jnp.int32, (main, token_count), 0)
    mains = [(slots == rank[i : i + 1, :]).astype(F32) for i in range(weight.shape[0])]
    tails = (rank == main).astype(F32)
    return mains, tails


def route_kernel(peer_ref, named_ref, given_ref, x_ref, dy_ref, joint_ref, dense_ref):
    count, width = x_ref.shape
    named = named_ref[...]
    given = given_ref[...].astype(F32)
    experts = dense_ref.shape[0]
    lines = [
        jnp.sum(jnp.where(named == peer_ref[i], given, 0.0), axis=0, keepdims=True) for i in range(experts)
    ]
    dense = jnp.concatenate(lines, axis=0)
    dense_ref[...] = dense
    turned = jnp.concatenate(lines[experts // 2 :] + lines[: experts // 2] + [jnp.zeros_like(dense)], axis=0)
    joint_ref[:, :width] = x_ref[...]
    joint_ref[:, width : 2 * width] = dy_ref[...]
    joint_ref[:, 2 * width :] = jnp.zeros((count, LANES), BF16)
    joint_ref[0:16, 2 * width : 2 * width + count] = turned.astype(BF16)


def join_kernel(in_ref, out_ref, after_ref, *pieces):
    width = in_ref.shape[1]
    at = 0
    for piece in pieces:
        to = at + piece.shape[0]
        piece[:, :width] = in_ref[at:to, :]
        piece[:, width:] = out_ref[at:to, :]
        at = to


def stack_kernel(*refs):
    *pieces, after_ref, stacked_ref = refs
    at = 0
    for piece in pieces:
        stacked_ref[at : at + piece.shape[0], :] = piece[...]
        at += piece.shape[0]


def after_kernel(*refs):
    pass


def relay_kernel(near_a, far_a, near_b, far_b, mid_ref, *refs):
    joint_ref = refs[-1]
    count, width = near_a.shape
    for at, near, far in ((0, near_a, far_a), (count, near_b, far_b)):
        joint_ref[at : at + count, :width] = near[...]
        joint_ref[at : at + count, width : 2 * width] = far[:, width:]
    joint_ref[:, 2 * width :] = mid_ref[...]


def pack_blocks(experts, joint_ref, out_refs, fold):
    count = len(experts)
    tokens, width = joint_ref.shape[0], out_refs[0].shape[1] - LANES
    chunks = width // LANES
    main = out_refs[0].shape[0] // 2
    weight = joint_ref[0:16, 2 * width :].astype(F32)[0:8, :tokens]
    mains, tails = picks(weight, main)
    pick = jnp.concatenate([mains[e] for e in experts] + [tails, jnp.zeros_like(tails)], axis=0).astype(BF16)
    lane = lax.broadcasted_iota(jnp.int32, (main, LANES), 1)
    for at, base, low in ((0, 0, 0), (width, main, chunks)):
        rows = dot(pick, joint_ref[:, at : at + width])
        for j, e in enumerate(experts):
            out_refs[j][base : base + main, :width] = rows[main * j : main * (j + 1)].astype(BF16)
            line = main * count + e
            for c in range(chunks):
                fold[c : c + 1, :] = rows[line : line + 1, LANES * c : LANES * (c + 1)]
            out_refs[j][low : low + chunks, width:] = fold[...].astype(BF16)
    for j, e in enumerate(experts):
        mine = weight[e : e + 1, :]
        column = jnp.sum(mains[e] * mine, axis=1, keepdims=True)
        last = jnp.sum(tails[e : e + 1, :] * mine, axis=1, keepdims=True)
        out_refs[j][main:, width:] = jnp.where(lane < LANES // 2, column, last).astype(BF16)


def pack_all_kernel(experts, spot_ref, joint_ref, out_ref, fold):
    pack_blocks(experts, joint_ref, [out_ref.at[spot_ref[j]] for j in range(len(experts))], fold)


def pack_kernel(experts, joint_ref, *refs):
    pack_blocks(experts, joint_ref, refs[-1 - len(experts) : -1], refs[-1])


def slice_kernel(own, place_ref, *refs):
    blocks, parts = 4, 4
    keep_ref, near_ref, far_ref, weight_ref, fold = refs[-5:]
    in_refs = list(refs[:blocks])
    if own:
        in_refs = [refs[1].at[refs[0][i]] for i in range(blocks)]
    main = in_refs[0].shape[0] // 2
    depth = keep_ref.shape[1] // 2
    width = parts * depth
    chunks = width // LANES
    targets = [(keep_ref, 0), (near_ref, 0), (far_ref, 0), (far_ref, 2 * depth)]
    lane = lax.broadcasted_iota(jnp.int32, (1, LANES), 1)
    lasts = []
    for i in range(blocks):
        for j, (target, shift) in enumerate(targets):
            columns = pl.ds(pl.multiple_of(place_ref[j] * depth, depth), depth)
            for side in range(2):
                at = shift + side * depth
                target[main * i : main * (i + 1), at : at + depth] = in_refs[i][
                    side * main : (side + 1) * main, columns
                ]
        for side in range(2):
            fold[side, chunks * i : chunks * (i + 1), :] = in_refs[i][
                side * chunks : (side + 1) * chunks, width:
            ].astype(F32)
        weights = in_refs[i][main:, width:].astype(F32)
        weight_ref[main * i : main * (i + 1), :] = weights
        last = jnp.sum(jnp.where(lane == LANES - 1, weights[0:1, :], 0.0), axis=1, keepdims=True)
        lasts.append(jnp.broadcast_to(last, (1, LANES)))
    weight_ref[main * blocks :, :] = jnp.concatenate(lasts + [jnp.zeros((16 - blocks, LANES), F32)], axis=0)
    each = chunks // parts
    for j, (target, shift) in enumerate(targets):
        for side in range(2):
            for q in range(each):
                tail = fold[side, pl.ds(place_ref[j] * each + q, blocks, stride=chunks), :]
                tail = jnp.concatenate([tail, jnp.zeros((16 - blocks, LANES), F32)], axis=0).astype(BF16)
                at = shift + side * depth + q * LANES
                target[main * blocks :, at : at + LANES] = tail


def main_kernel(early, place_ref, w_ref, *refs):
    blocks, parts = 4, 4
    own_ref, other_ref = refs[:2]
    keep_ref, near_ref, far_ref = refs[2:5]
    mid, backs, (tail, fold) = refs[-3 - blocks], refs[-2 - blocks : -2], refs[-2:]
    depth = keep_ref.shape[1] // 2
    width = parts * depth
    hidden_width = mid.shape[1] // 3
    main = backs[0].shape[0]
    chunks = width // LANES
    total = keep_ref.shape[0]
    first, second = pl.ds(0, depth), pl.ds(depth, depth)
    weights = [own_ref.at[first], other_ref.at[first], own_ref.at[second], other_ref.at[second]]
    pre = jnp.zeros((total, 2 * hidden_width), F32)
    grad = jnp.zeros((total, hidden_width), F32)
    for j, (ref, shift) in enumerate([(keep_ref, 0), (near_ref, 0), (far_ref, 0), (far_ref, 2 * depth)]):
        pre += dot(ref[:, shift : shift + depth], weights[j][:, : 2 * hidden_width])
        grad += dot(ref[:, shift + depth : shift + 2 * depth], weights[j][:, 2 * hidden_width :])
    if early:
        mid[0:early, :] = refs[5][...]
    weight = w_ref[:, 0:1]
    gate_pre = pre[:, :hidden_width]
    up_pre = pre[:, hidden_width:]
    sig = jax.nn.sigmoid(gate_pre)
    act = gate_pre * sig
    hidden = (act * up_pre).astype(BF16).astype(F32)
    route = jnp.sum(hidden * grad, axis=1, keepdims=True)
    grad_hidden = weight * grad
    grad_gate = grad_hidden * up_pre * sig * (1.0 + gate_pre * (1.0 - sig))
    mid[early:, :hidden_width] = grad_gate.astype(BF16)
    mid[early:, hidden_width : 2 * hidden_width] = (grad_hidden * act).astype(BF16)
    mid[early:, 2 * hidden_width :] = (weight * hidden).astype(BF16)
    for j in range(parts):
        columns = pl.ds(pl.multiple_of(place_ref[j] * depth, depth), depth)
        part = dot_nt(mid[early:, : 2 * hidden_width], weights[j][:, : 2 * hidden_width])
        tail[:, columns] = part[main * blocks :]
        part = part.astype(BF16)
        for i in range(blocks):
            backs[i][:, columns] = part[main * i : main * (i + 1)]
    row = lax.broadcasted_iota(jnp.int32, (main, LANES), 0)
    lane = lax.broadcasted_iota(jnp.int32, (main, LANES), 1)
    for i in range(blocks):
        for c in range(chunks):
            fold[c : c + 1, :] = tail[i : i + 1, LANES * c : LANES * (c + 1)]
        backs[i][:chunks, width:] = fold[...].astype(BF16)
        mine = jnp.where(row == lane, route[main * i : main * (i + 1)], 0.0)
        mine = jnp.sum(mine, axis=0, keepdims=True)
        mine = jnp.where(lane[0:1] == main, route[main * blocks + i : main * blocks + i + 1], mine)
        backs[i][chunks:, width:] = jnp.broadcast_to(mine, (main - chunks, LANES)).astype(BF16)


def unpack_sum(weight, block_refs, rows, fold):
    count = len(block_refs)
    main = block_refs[0].shape[0]
    width = rows.shape[1]
    chunks = width // LANES
    mains, tails = picks(weight, main)
    mains = mains[:count]
    pick = jnp.concatenate(mains + [tails, jnp.zeros_like(tails)], axis=0).astype(BF16)
    lane = lax.broadcasted_iota(jnp.int32, (1, LANES), 1)
    routes = []
    for j in range(count):
        rows[main * j : main * (j + 1), :] = block_refs[j][:, :width]
        fold[chunks * j : chunks * (j + 1), :] = block_refs[j][:chunks, width:].astype(F32)
        mine = block_refs[j][chunks:, width:].astype(F32)
        dense = dot(mine[:, :main].astype(BF16), mains[j].astype(BF16))[0:1, :]
        last = jnp.sum(jnp.where(lane == main, mine[0:1, :], 0.0), axis=1, keepdims=True)
        routes.append(dense + last * tails[j : j + 1, :])
    for c in range(chunks):
        tail = fold[pl.ds(c, count, stride=chunks), :]
        tail = jnp.concatenate([tail, jnp.zeros((16 - count, LANES), F32)], axis=0).astype(BF16)
        rows[main * count :, LANES * c : LANES * (c + 1)] = tail
    return dot_tn(pick, rows[...]), routes


def relay_sum_kernel(joint_ref, b0, b1, b2, b3, out_ref, rows, fold):
    tokens, width = joint_ref.shape[0], rows.shape[1]
    weight = joint_ref[0:16, 2 * width :].astype(F32)[0:8, :tokens]
    summed, routes = unpack_sum(weight, (b0, b1, b2, b3), rows, fold)
    lines = tokens // 2
    out_ref[:, :width] = summed[0:lines].astype(BF16)
    out_ref[:, width : 2 * width] = summed[lines:].astype(BF16)
    out_ref[:, 2 * width :] = jnp.zeros((lines, LANES), BF16)
    block = jnp.concatenate(routes + [jnp.zeros((12, tokens), F32)], axis=0).astype(BF16)
    out_ref[0:16, 2 * width : 2 * width + tokens] = block


def near_sum_kernel(w_ref, b0, b1, b2, b3, after_ref, grad_ref, route_ref, rows, fold):
    summed, routes = unpack_sum(w_ref[...], (b0, b1, b2, b3), rows, fold)
    grad_ref[...] = summed
    route_ref[...] = jnp.concatenate(routes + [jnp.zeros_like(route) for route in routes], axis=0)


def combine_kernel(peer_ref, named_ref, near_ref, near_route_ref, far_ref, grad_ref, route_ref):
    tokens, width = grad_ref.shape
    lines = tokens // 2
    for half in range(2):
        at, columns = slice(half * lines, (half + 1) * lines), slice(half * width, (half + 1) * width)
        grad_ref[at, :] = (near_ref[at, :] + far_ref[:, columns].astype(F32)).astype(BF16)
    others = far_ref[0:16, 2 * width : 2 * width + tokens].astype(F32)
    named = named_ref[...]
    route = jnp.zeros(route_ref.shape, F32)
    for j in range(4):
        route = route + jnp.where(named == peer_ref[j], near_route_ref[j : j + 1, :], 0.0)
        route = route + jnp.where(named == peer_ref[4 + j], others[j : j + 1, :], 0.0)
    route_ref[...] = route.astype(BF16)


def fill(rows, mids, rows_a, rows_b, rows_c, mid_a, mid_b):
    count = rows_a.shape[0]
    rows[0:count, :] = rows_a
    rows[count : 2 * count, :] = rows_b
    rows[2 * count :, :] = rows_c
    mids[0 : 2 * count, :] = mid_a
    mids[2 * count :, :] = mid_b


def first_weight_kernel(rows_a, rows_b, near_ref, mid_ref, in_ref, out_ref, rows, mids):
    depth, hidden_width = out_ref.shape
    near, near_mid = near_ref[:, : 2 * depth], near_ref[:, 4 * depth :]
    fill(rows, mids, rows_a[...], rows_b[...], near, mid_ref[...], near_mid)
    in_ref[...] = dot_tn(rows[:, :depth], mids[:, : 2 * hidden_width])
    out_ref[...] = dot_tn(rows[:, depth:], mids[:, 2 * hidden_width :])


def second_weight_kernel(rows_a, rows_b, mid_ref, in_part, out_part, in_ref, out_ref, rows):
    depth, hidden_width = out_ref.shape
    count = rows_a.shape[0]
    rows[0:count, :] = rows_a[:, : 2 * depth]
    rows[count:, :] = rows_b[:, : 2 * depth]
    in_ref[...] = in_part[...] + dot_tn(rows[:, :depth], mid_ref[:, : 2 * hidden_width])
    out_ref[...] = out_part[...] + dot_tn(rows[:, depth:], mid_ref[:, 2 * hidden_width :])


def last_weight_kernel(near_ref, mid_ref, in_part, out_part, in_ref, out_ref, in_held, out_held, sems):
    depth, hidden_width = out_part.shape
    copies = []
    step = depth // 4
    for m in range(4):
        at = slice(m * step, (m + 1) * step)
        lines = pl.ds(m * step, step)
        base = 2 * depth + m * step
        in_held[at, :] = in_part[at, :] + dot_tn(near_ref[:, base : base + step], mid_ref[:, : 2 * hidden_width])
        copies.append(start(in_held.at[lines], in_ref.at[lines], sems.at[0, m]))
        base += depth
        out_held[at, :] = out_part[at, :] + dot_tn(near_ref[:, base : base + step], mid_ref[:, 2 * hidden_width :])
        copies.append(start(out_held.at[lines], out_ref.at[lines], sems.at[1, m]))
    for copy in copies:
        copy.wait()


def call(kernel, outs, smem, vmem, either, scratch, flops, either_outs=0, aliases=None):
    on_vmem = pl.BlockSpec(memory_space=pltpu.VMEM)
    on_either = pl.BlockSpec(memory_space=pl.ANY)
    on_smem = pl.BlockSpec(memory_space=pltpu.SMEM)
    outs = [jax.ShapeDtypeStruct(shape, kind) for shape, kind in outs]
    moved = sum(a.size * a.dtype.itemsize for a in list(vmem) + outs[either_outs:])
    return pl.pallas_call(
        kernel,
        out_shape=tuple(outs),
        in_specs=[on_smem] * len(smem) + [on_vmem] * len(vmem) + [on_either] * len(either),
        out_specs=tuple([on_either] * either_outs + [on_vmem] * (len(outs) - either_outs)),
        scratch_shapes=scratch,
        compiler_params=pltpu.CompilerParams(vmem_limit_bytes=16 * 1024 * 1024),
        cost_estimate=pl.CostEstimate(flops=flops, bytes_accessed=moved, transcendentals=0),
        input_output_aliases=aliases or {},
    )(*smem, *vmem, *either)


def swap(value, axis, mask):
    return lax.ppermute(value, axis, [(i, i ^ mask) for i in range(lax.axis_size(axis))])


def on_device_packed(tokens, grad_out, route_expert, route_weight, gate_up_weight, down_weight):
    token_count, width = tokens.shape
    blocks, parts, half = 8, 4, 4
    hidden_width = down_weight.shape[2]
    depth = width // parts
    chunks = width // LANES
    main = block_rows(token_count, route_expert.shape[1], blocks) // 16 * 16
    rows = main * half + 16

    peers = lax.axis_index("expert") ^ jnp.arange(blocks, dtype=jnp.int32)
    places = lax.axis_index("dp") ^ jnp.arange(parts, dtype=jnp.int32)
    named = route_expert.T
    packed_shape = ((2 * main, width + LANES), BF16)
    back_shape = ((main, width + LANES), BF16)

    joint, dense = call(
        route_kernel,
        [((token_count, 2 * width + LANES), BF16), ((blocks, token_count), F32)],
        [peers],
        [named, route_weight.T, tokens, grad_out],
        [],
        [],
        0,
    )
    far_joint = swap(joint, "expert", half)

    cuts = (0, 176, 352, depth)
    weights = call(
        join_kernel,
        [((high - low, 3 * hidden_width), BF16) for low, high in zip(cuts, cuts[1:])],
        [],
        [gate_up_weight[0], down_weight[0]],
        [dense],
        [],
        0,
    )
    far_weights = [swap(piece, "dp", 2) for piece in weights]

    def pack(experts, value, after):
        return call(
            functools.partial(pack_kernel, experts),
            [packed_shape] * len(experts),
            [],
            [value],
            after,
            [pltpu.VMEM((chunks, LANES), F32)],
            4 * (len(experts) * main + 16) * token_count * width,
        )

    def sliced(spots, packed, after):
        return call(
            functools.partial(slice_kernel, len(spots)),
            [
                ((rows, 2 * depth), BF16),
                ((rows, 2 * depth), BF16),
                ((rows, 4 * depth), BF16),
                ((rows, LANES), F32),
            ],
            [places, *spots],
            packed,
            after,
            [pltpu.VMEM((2, half * chunks, LANES), F32)],
            0,
        )

    spots = peers[:half] % half
    (packed,) = call(
        functools.partial(pack_all_kernel, range(half, blocks)),
        [((half, *packed_shape[0]), BF16)],
        [spots],
        [joint],
        [],
        [pltpu.VMEM((chunks, LANES), F32)],
        4 * (half * main + 16) * token_count * width,
    )
    own = lax.all_to_all(
        packed,
        "expert",
        split_axis=0,
        concat_axis=0,
        tiled=True,
        axis_index_groups=[list(range(half)), list(range(half, blocks))],
    )
    *own_slices, own_weight = sliced([spots], [own], [far_joint])
    own_far = swap(own_slices[2], "dp", 2)
    far = pack(range(half), far_joint, [own_slices[0], *far_weights])
    far = [far[0]] + [swap(far[j], "expert", j) for j in range(1, half)]
    (stacked,) = call(
        stack_kernel,
        [((2 * depth, 3 * hidden_width), BF16)],
        [],
        [*weights, *far_weights],
        [far[0]],
        [],
        0,
    )
    weight_parts = [stacked, swap(stacked, "dp", 1)]

    def middle(slices, weight, before, after):
        early = before[0].shape[0] if before else 0
        return call(
            functools.partial(main_kernel, early),
            [((early + rows, 3 * hidden_width), BF16)] + [back_shape] * half,
            [places],
            [weight, *weight_parts, *slices, *before],
            after,
            [pltpu.VMEM((16, width), F32), pltpu.VMEM((chunks, LANES), F32)],
            2 * rows * width * 5 * hidden_width,
        )

    own_mid, *near_back = middle(own_slices, own_weight, [], [])
    near_back = near_back[:1] + [swap(near_back[j], "expert", j) for j in range(1, half)]
    *far_slices, far_weight = sliced([], far, [own_mid, own_far])
    far_far = swap(far_slices[2], "dp", 2)
    mid, *far_back = middle(far_slices, far_weight, [own_mid], [])

    sum_scratch = [
        pltpu.VMEM((half * main + 16, width), BF16),
        pltpu.VMEM((half * chunks, LANES), F32),
    ]
    sum_flops = 2 * (half * main + 16) * width * token_count
    far_back = far_back[:1] + [swap(far_back[j], "expert", j) for j in range(1, half)]
    (partial,) = call(
        relay_sum_kernel,
        [((token_count // 2, 2 * width + LANES), BF16)],
        [],
        [far_joint, *far_back],
        [],
        sum_scratch,
        sum_flops,
    )
    far_partial = swap(partial, "expert", half)

    mid_far = swap(mid, "dp", 2)
    (near,) = call(
        relay_kernel,
        [((2 * rows, 4 * depth + 3 * hidden_width), BF16)],
        [],
        [own_slices[1], own_far, far_slices[1], far_far, mid],
        [partial, near_back[1]],
        [],
        0,
    )
    near = swap(near, "dp", 1)
    weight_shapes = [((depth, 2 * hidden_width), F32), ((depth, hidden_width), F32)]
    weight_scratch = [pltpu.VMEM((4 * rows, 2 * depth), BF16), pltpu.VMEM((4 * rows, 3 * hidden_width), BF16)]
    weight_flops = 2 * 4 * rows * depth * 3 * hidden_width
    first = call(
        first_weight_kernel,
        weight_shapes,
        [],
        [own_slices[0], far_slices[0], near, mid],
        [],
        weight_scratch,
        weight_flops,
    )
    near_sum, near_route = call(
        near_sum_kernel,
        [((token_count, width), F32), ((blocks, token_count), F32)],
        [],
        [dense, *near_back],
        [first[1]],
        sum_scratch,
        sum_flops,
    )
    grad_tokens, grad_route = call(
        combine_kernel,
        [((token_count, width), BF16), (named.shape, BF16)],
        [peers],
        [named, near_sum, near_route, far_partial],
        [],
        [],
        0,
    )

    (mid_far,) = call(
        after_kernel,
        [(mid_far.shape, BF16)],
        [],
        [],
        [mid_far, first[1], far_partial, near_sum],
        [],
        0,
        1,
        {0: 0},
    )
    second = call(
        second_weight_kernel,
        weight_shapes,
        [],
        [own_far, far_far, mid_far, *first],
        [],
        [pltpu.VMEM((2 * rows, 2 * depth), BF16)],
        weight_flops // 2,
    )
    grad_gate_up, grad_down = call(
        last_weight_kernel,
        weight_shapes,
        [],
        [near, swap(mid_far, "dp", 1), *second],
        [],
        [
            pltpu.VMEM((depth, 2 * hidden_width), F32),
            pltpu.VMEM((depth, hidden_width), F32),
            pltpu.SemaphoreType.DMA((2, 4)),
        ],
        weight_flops // 2,
        2,
    )
    return (grad_tokens, grad_route.T, grad_gate_up[None], grad_down[None])


def block_rows(token_count, route_count, expert_total):
    return min(token_count, (token_count * route_count + expert_total - 1) // expert_total + 1)


def to_local(rows, group_count, local_count, capacity):
    tail = rows.shape[2:]
    shaped = rows.reshape((group_count, local_count, capacity) + tail)
    shaped = jnp.swapaxes(shaped, 0, 1)
    return shaped.reshape((local_count, group_count * capacity) + tail)


def to_groups(rows, group_count, local_count, capacity):
    tail = rows.shape[2:]
    shaped = rows.reshape((local_count, group_count, capacity) + tail)
    shaped = jnp.swapaxes(shaped, 0, 1)
    return shaped.reshape((group_count, local_count * capacity) + tail)


def on_device_routed(tokens, grad_out, route_expert, route_weight, gate_up_weight, down_weight):
    token_count, model_width = tokens.shape
    route_count = route_expert.shape[1]
    group_count = lax.axis_size("expert")
    local_count = gate_up_weight.shape[0]
    hidden_width = down_weight.shape[2]
    expert_total = local_count * group_count
    capacity = min(token_count, (token_count * route_count + expert_total - 1) // expert_total + 1)
    slot_total = expert_total * capacity
    flat_expert = route_expert.reshape(-1)
    expert_ids = jnp.arange(expert_total, dtype=jnp.int32)
    onehot = (flat_expert[:, None] == expert_ids[None, :]).astype(jnp.int32)
    before = jnp.cumsum(onehot, axis=0) - onehot
    rank = jnp.sum(before * onehot, axis=1)
    slot_of = flat_expert * capacity + rank
    slot_ids = jnp.arange(slot_total, dtype=jnp.int32)
    placed = slot_ids[:, None] == slot_of[None, :]
    by_token = jnp.any(placed.reshape(slot_total, token_count, route_count), axis=2).astype(
        jnp.bfloat16
    )
    send_x = jnp.dot(by_token, tokens, preferred_element_type=jnp.float32).astype(jnp.bfloat16)
    send_dy = jnp.dot(by_token, grad_out, preferred_element_type=jnp.float32).astype(jnp.bfloat16)
    flat_weight = route_weight.reshape(-1).astype(jnp.float32)
    send_w = jnp.sum(jnp.where(placed, flat_weight[None, :], 0.0), axis=1).astype(jnp.bfloat16)
    recv_x, recv_dy, recv_w = (
        lax.all_to_all(
            send_x.reshape(group_count, local_count * capacity, model_width),
            "expert",
            split_axis=0,
            concat_axis=0,
            tiled=True,
        ),
        lax.all_to_all(
            send_dy.reshape(group_count, local_count * capacity, model_width),
            "expert",
            split_axis=0,
            concat_axis=0,
            tiled=True,
        ),
        lax.all_to_all(
            send_w.reshape(group_count, local_count * capacity),
            "expert",
            split_axis=0,
            concat_axis=0,
            tiled=True,
        ),
    )
    rows_x = to_local(recv_x, group_count, local_count, capacity)
    rows_dy = to_local(recv_dy, group_count, local_count, capacity)
    rows_w = to_local(recv_w, group_count, local_count, capacity)
    full_in, full_out = (
        lax.all_gather(gate_up_weight, "dp", axis=1, tiled=True),
        lax.all_gather(down_weight, "dp", axis=1, tiled=True),
    )
    pre = jnp.einsum("erd,edf->erf", rows_x, full_in, preferred_element_type=jnp.float32)
    gate_pre = pre[:, :, :hidden_width]
    up_pre = pre[:, :, hidden_width:]
    act = swish(gate_pre)
    hidden = (act * up_pre).astype(jnp.bfloat16)
    expert_out = jnp.einsum("erf,edf->erd", hidden, full_out, preferred_element_type=jnp.float32)
    route_grad = jnp.sum(rows_dy.astype(jnp.float32) * expert_out, axis=2).astype(jnp.bfloat16)
    scaled = (rows_w.astype(jnp.float32)[:, :, None] * rows_dy).astype(jnp.bfloat16)
    grad_hidden = jnp.einsum("erd,edf->erf", scaled, full_out, preferred_element_type=jnp.float32)
    sig = jax.nn.sigmoid(gate_pre)
    grad_gate = grad_hidden * up_pre * sig * (1.0 + gate_pre * (1.0 - sig))
    grad_up = grad_hidden * act
    grad_pre = jnp.concatenate([grad_gate, grad_up], axis=2).astype(jnp.bfloat16)
    rows_grad = jnp.einsum(
        "erf,edf->erd", grad_pre, full_in, preferred_element_type=jnp.float32
    ).astype(jnp.bfloat16)
    back_x, back_w = (
        lax.all_to_all(
            to_groups(rows_grad, group_count, local_count, capacity),
            "expert",
            split_axis=0,
            concat_axis=0,
            tiled=True,
        ),
        lax.all_to_all(
            to_groups(route_grad, group_count, local_count, capacity),
            "expert",
            split_axis=0,
            concat_axis=0,
            tiled=True,
        ),
    )
    back_x = back_x.reshape(slot_total, model_width)
    back_w = back_w.reshape(slot_total).astype(jnp.float32)
    grad_tokens = jnp.einsum(
        "st,sd->td", by_token, back_x, preferred_element_type=jnp.float32
    ).astype(jnp.bfloat16)
    grad_route = jnp.sum(jnp.where(placed, back_w[:, None], 0.0), axis=0)
    grad_route = grad_route.reshape(token_count, route_count).astype(jnp.bfloat16)
    all_x = lax.all_to_all(rows_x, "dp", split_axis=2, concat_axis=1, tiled=True)
    grad_gate_up = jnp.einsum(
        "erd,erf->edf",
        all_x,
        lax.all_gather(grad_pre, "dp", axis=1, tiled=True),
        preferred_element_type=jnp.float32,
    )
    summed = lax.psum_scatter(
        jnp.einsum("erd,erf->def", scaled, hidden, preferred_element_type=jnp.float32),
        "dp",
        scatter_dimension=0,
        tiled=True,
    )
    grad_down = jnp.swapaxes(summed, 0, 1)
    return (grad_tokens, grad_route, grad_gate_up, grad_down)


def packs(tokens, route_expert, down_weight):
    chunks = tokens.shape[1] // LANES
    capacity = block_rows(tokens.shape[0], route_expert.shape[1], lax.axis_size("expert"))
    return (
        lax.axis_size("expert") == 8
        and lax.axis_size("dp") == 4
        and down_weight.shape[0] == 1
        and capacity % 16 <= 1
        and chunks == 16
        and 2 * chunks <= capacity < LANES // 2
    )


def solution(mesh):
    def on_device(*arrays):
        if packs(arrays[0], arrays[2], arrays[5]):
            return on_device_packed(*arrays)
        return on_device_routed(*arrays)

    return jax.shard_map(
        on_device,
        mesh=mesh,
        in_specs=(
            P(("expert", "dp"), None),
            P(("expert", "dp"), None),
            P(("expert", "dp"), None),
            P(("expert", "dp"), None),
            P("expert", "dp", None),
            P("expert", "dp", None),
        ),
        out_specs=(
            P(("expert", "dp"), None),
            P(("expert", "dp"), None),
            P("expert", "dp", None),
            P("expert", "dp", None),
        ),
        check_vma=False,
    )
```

```python
import functools

import jax
import jax.numpy as jnp
from jax import lax
from jax.experimental import pallas as pl
from jax.experimental.pallas import tpu as pltpu
from jax.sharding import PartitionSpec as P

BF16 = jnp.bfloat16
F32 = jnp.float32
LANES = 128


def swish(value):
    return value * jax.nn.sigmoid(value)


def dot(a, b):
    return jnp.dot(a, b, preferred_element_type=F32)


def dot_nt(a, b):
    return lax.dot_general(a, b, (((1,), (1,)), ((), ())), preferred_element_type=F32)


def dot_tn(a, b):
    return lax.dot_general(a, b, (((0,), (0,)), ((), ())), preferred_element_type=F32)


def start(source, target, sem):
    copy = pltpu.make_async_copy(source, target, sem)
    copy.start()
    return copy


def picks(weight, main):
    token_count = weight.shape[1]
    routed = weight != 0.0
    first = lax.broadcasted_iota(jnp.int32, (token_count, token_count), 0)
    second = lax.broadcasted_iota(jnp.int32, (token_count, token_count), 1)
    upper = (first < second).astype(F32).astype(BF16)
    rank = dot(routed.astype(F32).astype(BF16), upper)
    rank = jnp.where(routed, rank, -1.0).astype(jnp.int32)
    slots = lax.broadcasted_iota(jnp.int32, (main, token_count), 0)
    mains = [(slots == rank[i : i + 1, :]).astype(F32) for i in range(weight.shape[0])]
    tails = (rank == main).astype(F32)
    return mains, tails


def route_kernel(peer_ref, named_ref, given_ref, x_ref, dy_ref, joint_ref, dense_ref):
    count, width = x_ref.shape
    named = named_ref[...]
    given = given_ref[...].astype(F32)
    experts = dense_ref.shape[0]
    lines = [
        jnp.sum(jnp.where(named == peer_ref[i], given, 0.0), axis=0, keepdims=True) for i in range(experts)
    ]
    dense = jnp.concatenate(lines, axis=0)
    dense_ref[...] = dense
    turned = jnp.concatenate(lines[experts // 2 :] + lines[: experts // 2] + [jnp.zeros_like(dense)], axis=0)
    joint_ref[:, :width] = x_ref[...]
    joint_ref[:, width : 2 * width] = dy_ref[...]
    joint_ref[:, 2 * width :] = jnp.zeros((count, LANES), BF16)
    joint_ref[0:16, 2 * width : 2 * width + count] = turned.astype(BF16)


def stack_kernel(own_ref, far_ref, after_ref, stacked_ref):
    count = own_ref.shape[0]
    stacked_ref[0:count, :] = own_ref[...]
    stacked_ref[count:, :] = far_ref[...]


def after_kernel(*refs):
    pass


def relay_kernel(near_a, far_a, near_b, far_b, mid_ref, *refs):
    joint_ref = refs[-1]
    count, width = near_a.shape
    for at, near, far in ((0, near_a, far_a), (count, near_b, far_b)):
        joint_ref[at : at + count, :width] = near[...]
        joint_ref[at : at + count, width : 2 * width] = far[:, width:]
    joint_ref[:, 2 * width :] = mid_ref[...]


def pack_blocks(experts, joint_ref, out_refs, fold):
    count = len(experts)
    tokens, width = joint_ref.shape[0], out_refs[0].shape[1] - LANES
    chunks = width // LANES
    main = out_refs[0].shape[0] // 2
    weight = joint_ref[0:16, 2 * width :].astype(F32)[0:8, :tokens]
    mains, tails = picks(weight, main)
    pick = jnp.concatenate([mains[e] for e in experts] + [tails, jnp.zeros_like(tails)], axis=0).astype(BF16)
    lane = lax.broadcasted_iota(jnp.int32, (main, LANES), 1)
    for at, base, low in ((0, 0, 0), (width, main, chunks)):
        rows = dot(pick, joint_ref[:, at : at + width])
        for j, e in enumerate(experts):
            out_refs[j][base : base + main, :width] = rows[main * j : main * (j + 1)].astype(BF16)
            line = main * count + e
            for c in range(chunks):
                fold[c : c + 1, :] = rows[line : line + 1, LANES * c : LANES * (c + 1)]
            out_refs[j][low : low + chunks, width:] = fold[...].astype(BF16)
    for j, e in enumerate(experts):
        mine = weight[e : e + 1, :]
        column = jnp.sum(mains[e] * mine, axis=1, keepdims=True)
        last = jnp.sum(tails[e : e + 1, :] * mine, axis=1, keepdims=True)
        out_refs[j][main:, width:] = jnp.where(lane < LANES // 2, column, last).astype(BF16)


def pack_kernel(experts, joint_ref, *refs):
    pack_blocks(experts, joint_ref, refs[-1 - len(experts) : -1], refs[-1])


def slice_kernel(own, place_ref, *refs):
    blocks, parts = 4, 4
    keep_ref, near_ref, far_ref, weight_ref, fold, kept = refs[-6:]
    in_refs = list(refs[:blocks])
    if own:
        in_refs[0] = kept
        pack_blocks([own], refs[0], [kept], fold.at[0, pl.ds(0, 16)])
    main = in_refs[0].shape[0] // 2
    depth = keep_ref.shape[1] // 2
    width = parts * depth
    chunks = width // LANES
    targets = [(keep_ref, 0), (near_ref, 0), (far_ref, 0), (far_ref, 2 * depth)]
    lane = lax.broadcasted_iota(jnp.int32, (1, LANES), 1)
    lasts = []
    for i in range(blocks):
        for j, (target, shift) in enumerate(targets):
            columns = pl.ds(pl.multiple_of(place_ref[j] * depth, depth), depth)
            for side in range(2):
                at = shift + side * depth
                target[main * i : main * (i + 1), at : at + depth] = in_refs[i][
                    side * main : (side + 1) * main, columns
                ]
        for side in range(2):
            fold[side, chunks * i : chunks * (i + 1), :] = in_refs[i][
                side * chunks : (side + 1) * chunks, width:
            ].astype(F32)
        weights = in_refs[i][main:, width:].astype(F32)
        weight_ref[main * i : main * (i + 1), :] = weights
        last = jnp.sum(jnp.where(lane == LANES - 1, weights[0:1, :], 0.0), axis=1, keepdims=True)
        lasts.append(jnp.broadcast_to(last, (1, LANES)))
    weight_ref[main * blocks :, :] = jnp.concatenate(lasts + [jnp.zeros((16 - blocks, LANES), F32)], axis=0)
    each = chunks // parts
    for j, (target, shift) in enumerate(targets):
        for side in range(2):
            for q in range(each):
                tail = fold[side, pl.ds(place_ref[j] * each + q, blocks, stride=chunks), :]
                tail = jnp.concatenate([tail, jnp.zeros((16 - blocks, LANES), F32)], axis=0).astype(BF16)
                at = shift + side * depth + q * LANES
                target[main * blocks :, at : at + LANES] = tail


def main_kernel(early, place_ref, w_ref, *refs):
    blocks, parts = 4, 4
    own_ref, other_ref = refs[:2]
    keep_ref, near_ref, far_ref = refs[2:5]
    mid, backs, (tail, fold) = refs[-3 - blocks], refs[-2 - blocks : -2], refs[-2:]
    depth = keep_ref.shape[1] // 2
    width = parts * depth
    hidden_width = mid.shape[1] // 3
    main = backs[0].shape[0]
    chunks = width // LANES
    total = keep_ref.shape[0]
    first, second = pl.ds(0, depth), pl.ds(depth, depth)
    weights = [own_ref.at[first], other_ref.at[first], own_ref.at[second], other_ref.at[second]]
    pre = jnp.zeros((total, 2 * hidden_width), F32)
    grad = jnp.zeros((total, hidden_width), F32)
    for j, (ref, shift) in enumerate([(keep_ref, 0), (near_ref, 0), (far_ref, 0), (far_ref, 2 * depth)]):
        pre += dot(ref[:, shift : shift + depth], weights[j][:, : 2 * hidden_width])
        grad += dot(ref[:, shift + depth : shift + 2 * depth], weights[j][:, 2 * hidden_width :])
    if early:
        mid[0:early, :] = refs[5][...]
    weight = w_ref[:, 0:1]
    gate_pre = pre[:, :hidden_width]
    up_pre = pre[:, hidden_width:]
    sig = jax.nn.sigmoid(gate_pre)
    act = gate_pre * sig
    hidden = (act * up_pre).astype(BF16).astype(F32)
    route = jnp.sum(hidden * grad, axis=1, keepdims=True)
    grad_hidden = weight * grad
    grad_gate = grad_hidden * up_pre * sig * (1.0 + gate_pre * (1.0 - sig))
    mid[early:, :hidden_width] = grad_gate.astype(BF16)
    mid[early:, hidden_width : 2 * hidden_width] = (grad_hidden * act).astype(BF16)
    mid[early:, 2 * hidden_width :] = (weight * hidden).astype(BF16)
    for j in range(parts):
        columns = pl.ds(pl.multiple_of(place_ref[j] * depth, depth), depth)
        part = dot_nt(mid[early:, : 2 * hidden_width], weights[j][:, : 2 * hidden_width])
        tail[:, columns] = part[main * blocks :]
        part = part.astype(BF16)
        for i in range(blocks):
            backs[i][:, columns] = part[main * i : main * (i + 1)]
    row = lax.broadcasted_iota(jnp.int32, (main, LANES), 0)
    lane = lax.broadcasted_iota(jnp.int32, (main, LANES), 1)
    for i in range(blocks):
        for c in range(chunks):
            fold[c : c + 1, :] = tail[i : i + 1, LANES * c : LANES * (c + 1)]
        backs[i][:chunks, width:] = fold[...].astype(BF16)
        mine = jnp.where(row == lane, route[main * i : main * (i + 1)], 0.0)
        mine = jnp.sum(mine, axis=0, keepdims=True)
        mine = jnp.where(lane[0:1] == main, route[main * blocks + i : main * blocks + i + 1], mine)
        backs[i][chunks:, width:] = jnp.broadcast_to(mine, (main - chunks, LANES)).astype(BF16)


def unpack_sum(weight, block_refs, rows, fold):
    count = len(block_refs)
    main = block_refs[0].shape[0]
    width = rows.shape[1]
    chunks = width // LANES
    mains, tails = picks(weight, main)
    mains = mains[:count]
    pick = jnp.concatenate(mains + [tails, jnp.zeros_like(tails)], axis=0).astype(BF16)
    lane = lax.broadcasted_iota(jnp.int32, (1, LANES), 1)
    routes = []
    for j in range(count):
        rows[main * j : main * (j + 1), :] = block_refs[j][:, :width]
        fold[chunks * j : chunks * (j + 1), :] = block_refs[j][:chunks, width:].astype(F32)
        mine = block_refs[j][chunks:, width:].astype(F32)
        dense = dot(mine[:, :main].astype(BF16), mains[j].astype(BF16))[0:1, :]
        last = jnp.sum(jnp.where(lane == main, mine[0:1, :], 0.0), axis=1, keepdims=True)
        routes.append(dense + last * tails[j : j + 1, :])
    for c in range(chunks):
        tail = fold[pl.ds(c, count, stride=chunks), :]
        tail = jnp.concatenate([tail, jnp.zeros((16 - count, LANES), F32)], axis=0).astype(BF16)
        rows[main * count :, LANES * c : LANES * (c + 1)] = tail
    return dot_tn(pick, rows[...]), routes


def relay_sum_kernel(joint_ref, b0, b1, b2, b3, out_ref, rows, fold):
    tokens, width = joint_ref.shape[0], rows.shape[1]
    weight = joint_ref[0:16, 2 * width :].astype(F32)[0:8, :tokens]
    summed, routes = unpack_sum(weight, (b0, b1, b2, b3), rows, fold)
    lines = tokens // 2
    out_ref[:, :width] = summed[0:lines].astype(BF16)
    out_ref[:, width : 2 * width] = summed[lines:].astype(BF16)
    out_ref[:, 2 * width :] = jnp.zeros((lines, LANES), BF16)
    block = jnp.concatenate(routes + [jnp.zeros((12, tokens), F32)], axis=0).astype(BF16)
    out_ref[0:16, 2 * width : 2 * width + tokens] = block


def combine_kernel(peer_ref, named_ref, w_ref, b0, b1, b2, b3, far_ref, *refs):
    grad_ref, route_ref, in_ref, out_ref, held, rows, fold, lines_ref, sem = refs[5:]
    tokens, width = held.shape
    summed, routes = unpack_sum(w_ref[...], (b0, b1, b2, b3), rows, fold)
    lines = tokens // 2
    for half in range(2):
        at, columns = slice(half * lines, (half + 1) * lines), slice(half * width, (half + 1) * width)
        held[at, :] = (summed[at, :] + far_ref[:, columns].astype(F32)).astype(BF16)
    copy = start(held, grad_ref, sem)
    others = far_ref[0:16, 2 * width : 2 * width + tokens].astype(F32)
    named = named_ref[...]
    route = jnp.zeros(route_ref.shape, F32)
    for j in range(4):
        route = route + jnp.where(named == peer_ref[j], routes[j], 0.0)
        route = route + jnp.where(named == peer_ref[4 + j], others[j : j + 1, :], 0.0)
    route_ref[...] = route.astype(BF16)
    second_weight_part(*refs[:5], in_ref, out_ref, lines_ref)
    copy.wait()


def fill(rows, mids, rows_a, rows_b, rows_c, mid_a, mid_b):
    count = rows_a.shape[0]
    rows[0:count, :] = rows_a
    rows[count : 2 * count, :] = rows_b
    rows[2 * count :, :] = rows_c
    mids[0 : 2 * count, :] = mid_a
    mids[2 * count :, :] = mid_b


def first_weight_kernel(rows_a, rows_b, near_ref, mid_ref, in_ref, out_ref, rows, mids):
    depth, hidden_width = out_ref.shape
    near, near_mid = near_ref[:, : 2 * depth], near_ref[:, 4 * depth :]
    fill(rows, mids, rows_a[...], rows_b[...], near, mid_ref[...], near_mid)
    in_ref[...] = dot_tn(rows[:, :depth], mids[:, : 2 * hidden_width])
    out_ref[...] = dot_tn(rows[:, depth:], mids[:, 2 * hidden_width :])


def second_weight_part(rows_a, rows_b, mid_ref, in_part, out_part, in_ref, out_ref, rows):
    depth, hidden_width = out_ref.shape
    count = rows_a.shape[0]
    rows[0:count, :] = rows_a[:, : 2 * depth]
    rows[count:, :] = rows_b[:, : 2 * depth]
    in_ref[...] = in_part[...] + dot_tn(rows[:, :depth], mid_ref[:, : 2 * hidden_width])
    out_ref[...] = out_part[...] + dot_tn(rows[:, depth:], mid_ref[:, 2 * hidden_width :])


def last_weight_kernel(near_ref, mid_ref, in_part, out_part, in_ref, out_ref, in_held, out_held, sems):
    depth, hidden_width = out_part.shape
    copies = []
    step = depth // 4
    for m in range(4):
        at = slice(m * step, (m + 1) * step)
        lines = pl.ds(m * step, step)
        base = 2 * depth + m * step
        in_held[at, :] = in_part[at, :] + dot_tn(near_ref[:, base : base + step], mid_ref[:, : 2 * hidden_width])
        copies.append(start(in_held.at[lines], in_ref.at[lines], sems.at[0, m]))
        base += depth
        out_held[at, :] = out_part[at, :] + dot_tn(near_ref[:, base : base + step], mid_ref[:, 2 * hidden_width :])
        copies.append(start(out_held.at[lines], out_ref.at[lines], sems.at[1, m]))
    for copy in copies:
        copy.wait()


def call(kernel, outs, smem, vmem, either, scratch, flops, either_outs=0, aliases=None):
    on_vmem = pl.BlockSpec(memory_space=pltpu.VMEM)
    on_either = pl.BlockSpec(memory_space=pl.ANY)
    on_smem = pl.BlockSpec(memory_space=pltpu.SMEM)
    outs = [jax.ShapeDtypeStruct(shape, kind) for shape, kind in outs]
    moved = sum(a.size * a.dtype.itemsize for a in list(vmem) + outs[either_outs:])
    return pl.pallas_call(
        kernel,
        out_shape=tuple(outs),
        in_specs=[on_smem] * len(smem) + [on_vmem] * len(vmem) + [on_either] * len(either),
        out_specs=tuple([on_either] * either_outs + [on_vmem] * (len(outs) - either_outs)),
        scratch_shapes=scratch,
        compiler_params=pltpu.CompilerParams(vmem_limit_bytes=16 * 1024 * 1024),
        cost_estimate=pl.CostEstimate(flops=flops, bytes_accessed=moved, transcendentals=0),
        input_output_aliases=aliases or {},
    )(*smem, *vmem, *either)


def swap(value, axis, mask):
    return lax.ppermute(value, axis, [(i, i ^ mask) for i in range(lax.axis_size(axis))])


def on_device_packed(tokens, grad_out, route_expert, route_weight, gate_up_weight, down_weight):
    token_count, width = tokens.shape
    blocks, parts, half = 8, 4, 4
    hidden_width = down_weight.shape[2]
    depth = width // parts
    chunks = width // LANES
    main = block_rows(token_count, route_expert.shape[1], blocks) // 16 * 16
    rows = main * half + 16

    peers = lax.axis_index("expert") ^ jnp.arange(blocks, dtype=jnp.int32)
    places = lax.axis_index("dp") ^ jnp.arange(parts, dtype=jnp.int32)
    named = route_expert.T
    packed_shape = ((2 * main, width + LANES), BF16)
    back_shape = ((main, width + LANES), BF16)

    joint, dense = call(
        route_kernel,
        [((token_count, 2 * width + LANES), BF16), ((blocks, token_count), F32)],
        [peers],
        [named, route_weight.T, tokens, grad_out],
        [],
        [],
        0,
    )
    far_joint = swap(joint, "expert", half)

    weights = jnp.concatenate([gate_up_weight[0], down_weight[0]], axis=1)
    far_weights = swap(weights, "dp", 2)

    def pack(experts, value, after):
        return call(
            functools.partial(pack_kernel, experts),
            [packed_shape] * len(experts),
            [],
            [value],
            after,
            [pltpu.VMEM((chunks, LANES), F32)],
            4 * (len(experts) * main + 16) * token_count * width,
        )

    def sliced(own, packed, after):
        return call(
            functools.partial(slice_kernel, own),
            [
                ((rows, 2 * depth), BF16),
                ((rows, 2 * depth), BF16),
                ((rows, 4 * depth), BF16),
                ((rows, LANES), F32),
            ],
            [places],
            packed,
            after,
            [pltpu.VMEM((2, half * chunks, LANES), F32), pltpu.VMEM(*packed_shape)],
            0,
        )

    own = [swap(value, "expert", j + 1) for j, value in enumerate(pack(range(half + 1, blocks), joint, []))]
    *own_slices, own_weight = sliced(half, [joint, *own], [far_joint])
    own_far = swap(own_slices[2], "dp", 2)
    far = pack(range(half), far_joint, [own_slices[0], far_weights])
    far = [far[0]] + [swap(far[j], "expert", j) for j in range(1, half)]
    (stacked,) = call(
        stack_kernel,
        [((2 * depth, 3 * hidden_width), BF16)],
        [],
        [weights, far_weights],
        [far[0]],
        [],
        0,
    )
    weight_parts = [stacked, swap(stacked, "dp", 1)]

    def middle(slices, weight, before, after):
        early = before[0].shape[0] if before else 0
        return call(
            functools.partial(main_kernel, early),
            [((early + rows, 3 * hidden_width), BF16)] + [back_shape] * half,
            [places],
            [weight, *weight_parts, *slices, *before],
            after,
            [pltpu.VMEM((16, width), F32), pltpu.VMEM((chunks, LANES), F32)],
            2 * rows * width * 5 * hidden_width,
        )

    own_mid, *near_back = middle(own_slices, own_weight, [], [])
    near_back = near_back[:1] + [swap(near_back[j], "expert", j) for j in range(1, half)]
    *far_slices, far_weight = sliced(None, far, [own_mid, own_far])
    far_far = swap(far_slices[2], "dp", 2)
    mid, *far_back = middle(far_slices, far_weight, [own_mid], [])

    sum_scratch = [
        pltpu.VMEM((half * main + 16, width), BF16),
        pltpu.VMEM((half * chunks, LANES), F32),
    ]
    sum_flops = 2 * (half * main + 16) * width * token_count
    far_back = far_back[:1] + [swap(far_back[j], "expert", j) for j in range(1, half)]
    (partial,) = call(
        relay_sum_kernel,
        [((token_count // 2, 2 * width + LANES), BF16)],
        [],
        [far_joint, *far_back],
        [],
        sum_scratch,
        sum_flops,
    )
    far_partial = swap(partial, "expert", half)

    mid_far = swap(mid, "dp", 2)
    (near,) = call(
        relay_kernel,
        [((2 * rows, 4 * depth + 3 * hidden_width), BF16)],
        [],
        [own_slices[1], own_far, far_slices[1], far_far, mid],
        [partial, near_back[1]],
        [],
        0,
    )
    near = swap(near, "dp", 1)
    weight_shapes = [((depth, 2 * hidden_width), F32), ((depth, hidden_width), F32)]
    weight_scratch = [pltpu.VMEM((4 * rows, 2 * depth), BF16), pltpu.VMEM((4 * rows, 3 * hidden_width), BF16)]
    weight_flops = 2 * 4 * rows * depth * 3 * hidden_width
    first = call(
        first_weight_kernel,
        weight_shapes,
        [],
        [own_slices[0], far_slices[0], near, mid],
        [],
        weight_scratch,
        weight_flops,
    )
    (mid_far,) = call(
        after_kernel,
        [(mid_far.shape, BF16)],
        [],
        [],
        [mid_far, first[1], far_partial, *near_back[2:]],
        [],
        0,
        1,
        {0: 0},
    )
    grad_tokens, grad_route, *second = call(
        combine_kernel,
        [((token_count, width), BF16), (named.shape, BF16), *weight_shapes],
        [peers],
        [named, dense, *near_back, far_partial, own_far, far_far, mid_far, *first],
        [],
        [
            pltpu.VMEM((token_count, width), BF16),
            *sum_scratch,
            pltpu.VMEM((2 * rows, 2 * depth), BF16),
            pltpu.SemaphoreType.DMA,
        ],
        sum_flops + weight_flops // 2,
        1,
    )
    grad_gate_up, grad_down = call(
        last_weight_kernel,
        weight_shapes,
        [],
        [near, swap(mid_far, "dp", 1), *second],
        [],
        [
            pltpu.VMEM((depth, 2 * hidden_width), F32),
            pltpu.VMEM((depth, hidden_width), F32),
            pltpu.SemaphoreType.DMA((2, 4)),
        ],
        weight_flops // 2,
        2,
    )
    return (grad_tokens, grad_route.T, grad_gate_up[None], grad_down[None])


def block_rows(token_count, route_count, expert_total):
    return min(token_count, (token_count * route_count + expert_total - 1) // expert_total + 1)


def to_local(rows, group_count, local_count, capacity):
    tail = rows.shape[2:]
    shaped = rows.reshape((group_count, local_count, capacity) + tail)
    shaped = jnp.swapaxes(shaped, 0, 1)
    return shaped.reshape((local_count, group_count * capacity) + tail)


def to_groups(rows, group_count, local_count, capacity):
    tail = rows.shape[2:]
    shaped = rows.reshape((local_count, group_count, capacity) + tail)
    shaped = jnp.swapaxes(shaped, 0, 1)
    return shaped.reshape((group_count, local_count * capacity) + tail)


def on_device_routed(tokens, grad_out, route_expert, route_weight, gate_up_weight, down_weight):
    token_count, model_width = tokens.shape
    route_count = route_expert.shape[1]
    group_count = lax.axis_size("expert")
    local_count = gate_up_weight.shape[0]
    hidden_width = down_weight.shape[2]
    expert_total = local_count * group_count
    capacity = min(token_count, (token_count * route_count + expert_total - 1) // expert_total + 1)
    slot_total = expert_total * capacity
    flat_expert = route_expert.reshape(-1)
    expert_ids = jnp.arange(expert_total, dtype=jnp.int32)
    onehot = (flat_expert[:, None] == expert_ids[None, :]).astype(jnp.int32)
    before = jnp.cumsum(onehot, axis=0) - onehot
    rank = jnp.sum(before * onehot, axis=1)
    slot_of = flat_expert * capacity + rank
    slot_ids = jnp.arange(slot_total, dtype=jnp.int32)
    placed = slot_ids[:, None] == slot_of[None, :]
    by_token = jnp.any(placed.reshape(slot_total, token_count, route_count), axis=2).astype(
        jnp.bfloat16
    )
    send_x = jnp.dot(by_token, tokens, preferred_element_type=jnp.float32).astype(jnp.bfloat16)
    send_dy = jnp.dot(by_token, grad_out, preferred_element_type=jnp.float32).astype(jnp.bfloat16)
    flat_weight = route_weight.reshape(-1).astype(jnp.float32)
    send_w = jnp.sum(jnp.where(placed, flat_weight[None, :], 0.0), axis=1).astype(jnp.bfloat16)
    recv_x, recv_dy, recv_w = (
        lax.all_to_all(
            send_x.reshape(group_count, local_count * capacity, model_width),
            "expert",
            split_axis=0,
            concat_axis=0,
            tiled=True,
        ),
        lax.all_to_all(
            send_dy.reshape(group_count, local_count * capacity, model_width),
            "expert",
            split_axis=0,
            concat_axis=0,
            tiled=True,
        ),
        lax.all_to_all(
            send_w.reshape(group_count, local_count * capacity),
            "expert",
            split_axis=0,
            concat_axis=0,
            tiled=True,
        ),
    )
    rows_x = to_local(recv_x, group_count, local_count, capacity)
    rows_dy = to_local(recv_dy, group_count, local_count, capacity)
    rows_w = to_local(recv_w, group_count, local_count, capacity)
    full_in, full_out = (
        lax.all_gather(gate_up_weight, "dp", axis=1, tiled=True),
        lax.all_gather(down_weight, "dp", axis=1, tiled=True),
    )
    pre = jnp.einsum("erd,edf->erf", rows_x, full_in, preferred_element_type=jnp.float32)
    gate_pre = pre[:, :, :hidden_width]
    up_pre = pre[:, :, hidden_width:]
    act = swish(gate_pre)
    hidden = (act * up_pre).astype(jnp.bfloat16)
    expert_out = jnp.einsum("erf,edf->erd", hidden, full_out, preferred_element_type=jnp.float32)
    route_grad = jnp.sum(rows_dy.astype(jnp.float32) * expert_out, axis=2).astype(jnp.bfloat16)
    scaled = (rows_w.astype(jnp.float32)[:, :, None] * rows_dy).astype(jnp.bfloat16)
    grad_hidden = jnp.einsum("erd,edf->erf", scaled, full_out, preferred_element_type=jnp.float32)
    sig = jax.nn.sigmoid(gate_pre)
    grad_gate = grad_hidden * up_pre * sig * (1.0 + gate_pre * (1.0 - sig))
    grad_up = grad_hidden * act
    grad_pre = jnp.concatenate([grad_gate, grad_up], axis=2).astype(jnp.bfloat16)
    rows_grad = jnp.einsum(
        "erf,edf->erd", grad_pre, full_in, preferred_element_type=jnp.float32
    ).astype(jnp.bfloat16)
    back_x, back_w = (
        lax.all_to_all(
            to_groups(rows_grad, group_count, local_count, capacity),
            "expert",
            split_axis=0,
            concat_axis=0,
            tiled=True,
        ),
        lax.all_to_all(
            to_groups(route_grad, group_count, local_count, capacity),
            "expert",
            split_axis=0,
            concat_axis=0,
            tiled=True,
        ),
    )
    back_x = back_x.reshape(slot_total, model_width)
    back_w = back_w.reshape(slot_total).astype(jnp.float32)
    grad_tokens = jnp.einsum(
        "st,sd->td", by_token, back_x, preferred_element_type=jnp.float32
    ).astype(jnp.bfloat16)
    grad_route = jnp.sum(jnp.where(placed, back_w[:, None], 0.0), axis=0)
    grad_route = grad_route.reshape(token_count, route_count).astype(jnp.bfloat16)
    all_x = lax.all_to_all(rows_x, "dp", split_axis=2, concat_axis=1, tiled=True)
    grad_gate_up = jnp.einsum(
        "erd,erf->edf",
        all_x,
        lax.all_gather(grad_pre, "dp", axis=1, tiled=True),
        preferred_element_type=jnp.float32,
    )
    summed = lax.psum_scatter(
        jnp.einsum("erd,erf->def", scaled, hidden, preferred_element_type=jnp.float32),
        "dp",
        scatter_dimension=0,
        tiled=True,
    )
    grad_down = jnp.swapaxes(summed, 0, 1)
    return (grad_tokens, grad_route, grad_gate_up, grad_down)


def packs(tokens, route_expert, down_weight):
    chunks = tokens.shape[1] // LANES
    capacity = block_rows(tokens.shape[0], route_expert.shape[1], lax.axis_size("expert"))
    return (
        lax.axis_size("expert") == 8
        and lax.axis_size("dp") == 4
        and down_weight.shape[0] == 1
        and capacity % 16 <= 1
        and chunks == 16
        and 2 * chunks <= capacity < LANES // 2
    )


def solution(mesh):
    def on_device(*arrays):
        if packs(arrays[0], arrays[2], arrays[5]):
            return on_device_packed(*arrays)
        return on_device_routed(*arrays)

    return jax.shard_map(
        on_device,
        mesh=mesh,
        in_specs=(
            P(("expert", "dp"), None),
            P(("expert", "dp"), None),
            P(("expert", "dp"), None),
            P(("expert", "dp"), None),
            P("expert", "dp", None),
            P("expert", "dp", None),
        ),
        out_specs=(
            P(("expert", "dp"), None),
            P(("expert", "dp"), None),
            P("expert", "dp", None),
            P("expert", "dp", None),
        ),
        check_vma=False,
    )
```

```python
import functools

import jax
import jax.numpy as jnp
from jax import lax
from jax.experimental import pallas as pl
from jax.experimental.pallas import tpu as pltpu
from jax.sharding import PartitionSpec as P

BF16 = jnp.bfloat16
F32 = jnp.float32
LANES = 128


def swish(value):
    return value * jax.nn.sigmoid(value)


def dot(a, b):
    return jnp.dot(a, b, preferred_element_type=F32)


def dot_nt(a, b):
    return lax.dot_general(a, b, (((1,), (1,)), ((), ())), preferred_element_type=F32)


def dot_tn(a, b):
    return lax.dot_general(a, b, (((0,), (0,)), ((), ())), preferred_element_type=F32)


def start(source, target, sem):
    copy = pltpu.make_async_copy(source, target, sem)
    copy.start()
    return copy


def picks(weight, main):
    token_count = weight.shape[1]
    routed = weight != 0.0
    first = lax.broadcasted_iota(jnp.int32, (token_count, token_count), 0)
    second = lax.broadcasted_iota(jnp.int32, (token_count, token_count), 1)
    upper = (first < second).astype(F32).astype(BF16)
    rank = dot(routed.astype(F32).astype(BF16), upper)
    rank = jnp.where(routed, rank, -1.0).astype(jnp.int32)
    slots = lax.broadcasted_iota(jnp.int32, (main, token_count), 0)
    mains = [(slots == rank[i : i + 1, :]).astype(F32) for i in range(weight.shape[0])]
    tails = (rank == main).astype(F32)
    return mains, tails


def route_kernel(peer_ref, named_ref, given_ref, x_ref, dy_ref, joint_ref, dense_ref):
    count, width = x_ref.shape
    named = named_ref[...]
    given = given_ref[...].astype(F32)
    experts = dense_ref.shape[0]
    lines = [
        jnp.sum(jnp.where(named == peer_ref[i], given, 0.0), axis=0, keepdims=True) for i in range(experts)
    ]
    dense = jnp.concatenate(lines, axis=0)
    dense_ref[...] = dense
    turned = jnp.concatenate(lines[experts // 2 :] + lines[: experts // 2] + [jnp.zeros_like(dense)], axis=0)
    joint_ref[:, :width] = x_ref[...]
    joint_ref[:, width : 2 * width] = dy_ref[...]
    joint_ref[:, 2 * width :] = jnp.zeros((count, LANES), BF16)
    joint_ref[0:16, 2 * width : 2 * width + count] = turned.astype(BF16)


def stack_kernel(own_ref, far_ref, after_ref, stacked_ref):
    count = own_ref.shape[0]
    stacked_ref[0:count, :] = own_ref[...]
    stacked_ref[count:, :] = far_ref[...]


def after_kernel(*refs):
    pass


def relay_kernel(near_a, far_a, near_b, far_b, mid_ref, *refs):
    joint_ref = refs[-1]
    count, width = near_a.shape
    for at, near, far in ((0, near_a, far_a), (count, near_b, far_b)):
        joint_ref[at : at + count, :width] = near[...]
        joint_ref[at : at + count, width : 2 * width] = far[:, width:]
    joint_ref[:, 2 * width :] = mid_ref[...]


def pack_blocks(experts, joint_ref, out_refs, fold):
    count = len(experts)
    tokens, width = joint_ref.shape[0], out_refs[0].shape[1] - LANES
    chunks = width // LANES
    main = out_refs[0].shape[0] // 2
    weight = joint_ref[0:16, 2 * width :].astype(F32)[0:8, :tokens]
    mains, tails = picks(weight, main)
    pick = jnp.concatenate([mains[e] for e in experts] + [tails, jnp.zeros_like(tails)], axis=0).astype(BF16)
    lane = lax.broadcasted_iota(jnp.int32, (main, LANES), 1)
    for at, base, low in ((0, 0, 0), (width, main, chunks)):
        rows = dot(pick, joint_ref[:, at : at + width])
        for j, e in enumerate(experts):
            out_refs[j][base : base + main, :width] = rows[main * j : main * (j + 1)].astype(BF16)
            line = main * count + e
            for c in range(chunks):
                fold[c : c + 1, :] = rows[line : line + 1, LANES * c : LANES * (c + 1)]
            out_refs[j][low : low + chunks, width:] = fold[...].astype(BF16)
    for j, e in enumerate(experts):
        mine = weight[e : e + 1, :]
        column = jnp.sum(mains[e] * mine, axis=1, keepdims=True)
        last = jnp.sum(tails[e : e + 1, :] * mine, axis=1, keepdims=True)
        out_refs[j][main:, width:] = jnp.where(lane < LANES // 2, column, last).astype(BF16)


def pack_kernel(experts, joint_ref, *refs):
    pack_blocks(experts, joint_ref, refs[-1 - len(experts) : -1], refs[-1])


def slice_kernel(own, place_ref, *refs):
    blocks, parts = 4, 4
    keep_ref, near_ref, far_ref, weight_ref, fold, kept = refs[-6:]
    in_refs = list(refs[:blocks])
    if own:
        in_refs[0] = kept
        pack_blocks([own], refs[0], [kept], fold.at[0, pl.ds(0, 16)])
    main = in_refs[0].shape[0] // 2
    depth = keep_ref.shape[1] // 2
    width = parts * depth
    chunks = width // LANES
    targets = [(keep_ref, 0), (near_ref, 0), (far_ref, 0), (far_ref, 2 * depth)]
    lane = lax.broadcasted_iota(jnp.int32, (1, LANES), 1)
    lasts = []
    for i in range(blocks):
        for j, (target, shift) in enumerate(targets):
            columns = pl.ds(pl.multiple_of(place_ref[j] * depth, depth), depth)
            for side in range(2):
                at = shift + side * depth
                target[main * i : main * (i + 1), at : at + depth] = in_refs[i][
                    side * main : (side + 1) * main, columns
                ]
        for side in range(2):
            fold[side, chunks * i : chunks * (i + 1), :] = in_refs[i][
                side * chunks : (side + 1) * chunks, width:
            ].astype(F32)
        weights = in_refs[i][main:, width:].astype(F32)
        weight_ref[main * i : main * (i + 1), :] = weights
        last = jnp.sum(jnp.where(lane == LANES - 1, weights[0:1, :], 0.0), axis=1, keepdims=True)
        lasts.append(jnp.broadcast_to(last, (1, LANES)))
    weight_ref[main * blocks :, :] = jnp.concatenate(lasts + [jnp.zeros((16 - blocks, LANES), F32)], axis=0)
    each = chunks // parts
    for j, (target, shift) in enumerate(targets):
        for side in range(2):
            for q in range(each):
                tail = fold[side, pl.ds(place_ref[j] * each + q, blocks, stride=chunks), :]
                tail = jnp.concatenate([tail, jnp.zeros((16 - blocks, LANES), F32)], axis=0).astype(BF16)
                at = shift + side * depth + q * LANES
                target[main * blocks :, at : at + LANES] = tail


def main_kernel(early, place_ref, w_ref, *refs):
    blocks, parts = 4, 4
    own_ref, other_ref = refs[:2]
    keep_ref, near_ref, far_ref = refs[2:5]
    mid, backs, (tail, fold) = refs[-3 - blocks], refs[-2 - blocks : -2], refs[-2:]
    depth = keep_ref.shape[1] // 2
    width = parts * depth
    hidden_width = mid.shape[1] // 3
    main = backs[0].shape[0]
    chunks = width // LANES
    total = keep_ref.shape[0]
    first, second = pl.ds(0, depth), pl.ds(depth, depth)
    weights = [own_ref.at[first], other_ref.at[first], own_ref.at[second], other_ref.at[second]]
    pre = jnp.zeros((total, 2 * hidden_width), F32)
    grad = jnp.zeros((total, hidden_width), F32)
    for j, (ref, shift) in enumerate([(keep_ref, 0), (near_ref, 0), (far_ref, 0), (far_ref, 2 * depth)]):
        pre += dot(ref[:, shift : shift + depth], weights[j][:, : 2 * hidden_width])
        grad += dot(ref[:, shift + depth : shift + 2 * depth], weights[j][:, 2 * hidden_width :])
    if early:
        mid[0:early, :] = refs[5][...]
    weight = w_ref[:, 0:1]
    gate_pre = pre[:, :hidden_width]
    up_pre = pre[:, hidden_width:]
    sig = jax.nn.sigmoid(gate_pre)
    act = gate_pre * sig
    hidden = (act * up_pre).astype(BF16).astype(F32)
    route = jnp.sum(hidden * grad, axis=1, keepdims=True)
    grad_hidden = weight * grad
    grad_gate = grad_hidden * up_pre * sig * (1.0 + gate_pre * (1.0 - sig))
    mid[early:, :hidden_width] = grad_gate.astype(BF16)
    mid[early:, hidden_width : 2 * hidden_width] = (grad_hidden * act).astype(BF16)
    mid[early:, 2 * hidden_width :] = (weight * hidden).astype(BF16)
    for j in range(parts):
        columns = pl.ds(pl.multiple_of(place_ref[j] * depth, depth), depth)
        part = dot_nt(mid[early:, : 2 * hidden_width], weights[j][:, : 2 * hidden_width])
        tail[:, columns] = part[main * blocks :]
        part = part.astype(BF16)
        for i in range(blocks):
            backs[i][:, columns] = part[main * i : main * (i + 1)]
    row = lax.broadcasted_iota(jnp.int32, (main, LANES), 0)
    lane = lax.broadcasted_iota(jnp.int32, (main, LANES), 1)
    for i in range(blocks):
        for c in range(chunks):
            fold[c : c + 1, :] = tail[i : i + 1, LANES * c : LANES * (c + 1)]
        backs[i][:chunks, width:] = fold[...].astype(BF16)
        mine = jnp.where(row == lane, route[main * i : main * (i + 1)], 0.0)
        mine = jnp.sum(mine, axis=0, keepdims=True)
        mine = jnp.where(lane[0:1] == main, route[main * blocks + i : main * blocks + i + 1], mine)
        backs[i][chunks:, width:] = jnp.broadcast_to(mine, (main - chunks, LANES)).astype(BF16)


def unpack_sum(weight, block_refs, rows, fold):
    count = len(block_refs)
    main = block_refs[0].shape[0]
    width = rows.shape[1]
    chunks = width // LANES
    mains, tails = picks(weight, main)
    mains = mains[:count]
    pick = jnp.concatenate(mains + [tails, jnp.zeros_like(tails)], axis=0).astype(BF16)
    lane = lax.broadcasted_iota(jnp.int32, (1, LANES), 1)
    routes = []
    for j in range(count):
        rows[main * j : main * (j + 1), :] = block_refs[j][:, :width]
        fold[chunks * j : chunks * (j + 1), :] = block_refs[j][:chunks, width:].astype(F32)
        mine = block_refs[j][chunks:, width:].astype(F32)
        dense = dot(mine[:, :main].astype(BF16), mains[j].astype(BF16))[0:1, :]
        last = jnp.sum(jnp.where(lane == main, mine[0:1, :], 0.0), axis=1, keepdims=True)
        routes.append(dense + last * tails[j : j + 1, :])
    for c in range(chunks):
        tail = fold[pl.ds(c, count, stride=chunks), :]
        tail = jnp.concatenate([tail, jnp.zeros((16 - count, LANES), F32)], axis=0).astype(BF16)
        rows[main * count :, LANES * c : LANES * (c + 1)] = tail
    return dot_tn(pick, rows[...]), routes


def relay_sum_kernel(joint_ref, b0, b1, b2, b3, out_ref, rows, fold):
    tokens, width = joint_ref.shape[0], rows.shape[1]
    weight = joint_ref[0:16, 2 * width :].astype(F32)[0:8, :tokens]
    summed, routes = unpack_sum(weight, (b0, b1, b2, b3), rows, fold)
    lines = tokens // 2
    out_ref[:, :width] = summed[0:lines].astype(BF16)
    out_ref[:, width : 2 * width] = summed[lines:].astype(BF16)
    out_ref[:, 2 * width :] = jnp.zeros((lines, LANES), BF16)
    block = jnp.concatenate(routes + [jnp.zeros((12, tokens), F32)], axis=0).astype(BF16)
    out_ref[0:16, 2 * width : 2 * width + tokens] = block


def combine_kernel(peer_ref, named_ref, w_ref, b0, b1, b2, b3, far_ref, *refs):
    grad_ref, route_ref, in_ref, out_ref, held, rows, fold, lines_ref, sem = refs[5:]
    tokens, width = held.shape
    summed, routes = unpack_sum(w_ref[...], (b0, b1, b2, b3), rows, fold)
    lines = tokens // 2
    for half in range(2):
        at, columns = slice(half * lines, (half + 1) * lines), slice(half * width, (half + 1) * width)
        held[at, :] = (summed[at, :] + far_ref[:, columns].astype(F32)).astype(BF16)
    copy = start(held, grad_ref, sem)
    others = far_ref[0:16, 2 * width : 2 * width + tokens].astype(F32)
    named = named_ref[...]
    route = jnp.zeros(route_ref.shape, F32)
    for j in range(4):
        route = route + jnp.where(named == peer_ref[j], routes[j], 0.0)
        route = route + jnp.where(named == peer_ref[4 + j], others[j : j + 1, :], 0.0)
    route_ref[...] = route.astype(BF16)
    second_weight_part(*refs[:5], in_ref, out_ref, lines_ref)
    copy.wait()


def fill(rows, mids, rows_a, rows_b, rows_c, mid_a, mid_b):
    count = rows_a.shape[0]
    rows[0:count, :] = rows_a
    rows[count : 2 * count, :] = rows_b
    rows[2 * count :, :] = rows_c
    mids[0 : 2 * count, :] = mid_a
    mids[2 * count :, :] = mid_b


def first_weight_kernel(rows_a, rows_b, near_ref, mid_ref, in_ref, out_ref, rows, mids):
    depth, hidden_width = out_ref.shape
    near, near_mid = near_ref[:, : 2 * depth], near_ref[:, 4 * depth :]
    fill(rows, mids, rows_a[...], rows_b[...], near, mid_ref[...], near_mid)
    in_ref[...] = dot_tn(rows[:, :depth], mids[:, : 2 * hidden_width])
    out_ref[...] = dot_tn(rows[:, depth:], mids[:, 2 * hidden_width :])


def second_weight_part(rows_a, rows_b, mid_ref, in_part, out_part, in_ref, out_ref, rows):
    depth, hidden_width = out_ref.shape
    count = rows_a.shape[0]
    rows[0:count, :] = rows_a[:, : 2 * depth]
    rows[count:, :] = rows_b[:, : 2 * depth]
    in_ref[...] = in_part[...] + dot_tn(rows[:, :depth], mid_ref[:, : 2 * hidden_width])
    out_ref[...] = out_part[...] + dot_tn(rows[:, depth:], mid_ref[:, 2 * hidden_width :])


def last_weight_kernel(near_ref, mid_ref, in_part, out_part, in_ref, out_ref, in_held, out_held, sems):
    depth, hidden_width = out_part.shape
    copies = []
    step = depth // 4
    for m in range(4):
        at = slice(m * step, (m + 1) * step)
        lines = pl.ds(m * step, step)
        base = 2 * depth + m * step
        in_held[at, :] = in_part[at, :] + dot_tn(near_ref[:, base : base + step], mid_ref[:, : 2 * hidden_width])
        copies.append(start(in_held.at[lines], in_ref.at[lines], sems.at[0, m]))
        base += depth
        out_held[at, :] = out_part[at, :] + dot_tn(near_ref[:, base : base + step], mid_ref[:, 2 * hidden_width :])
        copies.append(start(out_held.at[lines], out_ref.at[lines], sems.at[1, m]))
    for copy in copies:
        copy.wait()


def call(kernel, outs, smem, vmem, either, scratch, flops, either_outs=0, aliases=None):
    on_vmem = pl.BlockSpec(memory_space=pltpu.VMEM)
    on_either = pl.BlockSpec(memory_space=pl.ANY)
    on_smem = pl.BlockSpec(memory_space=pltpu.SMEM)
    outs = [jax.ShapeDtypeStruct(shape, kind) for shape, kind in outs]
    moved = sum(a.size * a.dtype.itemsize for a in list(vmem) + outs[either_outs:])
    return pl.pallas_call(
        kernel,
        out_shape=tuple(outs),
        in_specs=[on_smem] * len(smem) + [on_vmem] * len(vmem) + [on_either] * len(either),
        out_specs=tuple([on_either] * either_outs + [on_vmem] * (len(outs) - either_outs)),
        scratch_shapes=scratch,
        compiler_params=pltpu.CompilerParams(vmem_limit_bytes=16 * 1024 * 1024),
        cost_estimate=pl.CostEstimate(flops=flops, bytes_accessed=moved, transcendentals=0),
        input_output_aliases=aliases or {},
    )(*smem, *vmem, *either)


def swap(value, axis, mask):
    return lax.ppermute(value, axis, [(i, i ^ mask) for i in range(lax.axis_size(axis))])


def on_device_packed(tokens, grad_out, route_expert, route_weight, gate_up_weight, down_weight):
    token_count, width = tokens.shape
    blocks, parts, half = 8, 4, 4
    hidden_width = down_weight.shape[2]
    depth = width // parts
    chunks = width // LANES
    main = block_rows(token_count, route_expert.shape[1], blocks) // 16 * 16
    rows = main * half + 16

    peers = lax.axis_index("expert") ^ jnp.arange(blocks, dtype=jnp.int32)
    places = lax.axis_index("dp") ^ jnp.arange(parts, dtype=jnp.int32)
    named = route_expert.T
    packed_shape = ((2 * main, width + LANES), BF16)
    back_shape = ((main, width + LANES), BF16)

    joint, dense = call(
        route_kernel,
        [((token_count, 2 * width + LANES), BF16), ((blocks, token_count), F32)],
        [peers],
        [named, route_weight.T, tokens, grad_out],
        [],
        [],
        0,
    )
    far_joint = swap(joint, "expert", half)

    weights = jnp.concatenate([gate_up_weight[0], down_weight[0]], axis=1)
    far_weights = swap(weights, "dp", 2)

    def pack(experts, value, after):
        return call(
            functools.partial(pack_kernel, experts),
            [packed_shape] * len(experts),
            [],
            [value],
            after,
            [pltpu.VMEM((chunks, LANES), F32)],
            4 * (len(experts) * main + 16) * token_count * width,
        )

    def sliced(own, packed, after):
        return call(
            functools.partial(slice_kernel, own),
            [
                ((rows, 2 * depth), BF16),
                ((rows, 2 * depth), BF16),
                ((rows, 4 * depth), BF16),
                ((rows, LANES), F32),
            ],
            [places],
            packed,
            after,
            [pltpu.VMEM((2, half * chunks, LANES), F32), pltpu.VMEM(*packed_shape)],
            0,
        )

    own = [swap(value, "expert", j + 1) for j, value in enumerate(pack(range(half + 1, blocks), joint, []))]
    *own_slices, own_weight = sliced(half, [joint, *own], [far_joint])
    own_far = swap(own_slices[2], "dp", 2)
    far = pack(range(half), far_joint, [own_slices[0], far_weights])
    far = [far[0]] + [swap(far[j], "expert", j) for j in range(1, half)]
    (stacked,) = call(
        stack_kernel,
        [((2 * depth, 3 * hidden_width), BF16)],
        [],
        [weights, far_weights],
        [far[0]],
        [],
        0,
    )
    weight_parts = [stacked, swap(stacked, "dp", 1)]

    def middle(slices, weight, before, after):
        early = before[0].shape[0] if before else 0
        return call(
            functools.partial(main_kernel, early),
            [((early + rows, 3 * hidden_width), BF16)] + [back_shape] * half,
            [places],
            [weight, *weight_parts, *slices, *before],
            after,
            [pltpu.VMEM((16, width), F32), pltpu.VMEM((chunks, LANES), F32)],
            2 * rows * width * 5 * hidden_width,
        )

    own_mid, *near_back = middle(own_slices, own_weight, [], [])
    near_back = near_back[:1] + [swap(near_back[j], "expert", j) for j in range(1, half)]
    *far_slices, far_weight = sliced(None, far, [own_mid, own_far])
    far_far = swap(far_slices[2], "dp", 2)
    mid, *far_back = middle(far_slices, far_weight, [own_mid], [])

    sum_scratch = [
        pltpu.VMEM((half * main + 16, width), BF16),
        pltpu.VMEM((half * chunks, LANES), F32),
    ]
    sum_flops = 2 * (half * main + 16) * width * token_count
    far_back = far_back[:1] + [swap(far_back[j], "expert", j) for j in range(1, half)]
    (partial,) = call(
        relay_sum_kernel,
        [((token_count // 2, 2 * width + LANES), BF16)],
        [],
        [far_joint, *far_back],
        [],
        sum_scratch,
        sum_flops,
    )
    far_partial = swap(partial, "expert", half)

    mid_far = swap(mid, "dp", 2)
    (near,) = call(
        relay_kernel,
        [((2 * rows, 4 * depth + 3 * hidden_width), BF16)],
        [],
        [own_slices[1], own_far, far_slices[1], far_far, mid],
        [partial],
        [],
        0,
    )
    near = swap(near, "dp", 1)
    weight_shapes = [((depth, 2 * hidden_width), F32), ((depth, hidden_width), F32)]
    weight_scratch = [pltpu.VMEM((4 * rows, 2 * depth), BF16), pltpu.VMEM((4 * rows, 3 * hidden_width), BF16)]
    weight_flops = 2 * 4 * rows * depth * 3 * hidden_width
    first = call(
        first_weight_kernel,
        weight_shapes,
        [],
        [own_slices[0], far_slices[0], near, mid],
        [],
        weight_scratch,
        weight_flops,
    )
    (mid_far,) = call(
        after_kernel,
        [(mid_far.shape, BF16)],
        [],
        [],
        [mid_far, first[1], far_partial, *near_back[1:]],
        [],
        0,
        1,
        {0: 0},
    )
    grad_tokens, grad_route, *second = call(
        combine_kernel,
        [((token_count, width), BF16), (named.shape, BF16), *weight_shapes],
        [peers],
        [named, dense, *near_back, far_partial, own_far, far_far, mid_far, *first],
        [],
        [
            pltpu.VMEM((token_count, width), BF16),
            *sum_scratch,
            pltpu.VMEM((2 * rows, 2 * depth), BF16),
            pltpu.SemaphoreType.DMA,
        ],
        sum_flops + weight_flops // 2,
        1,
    )
    grad_gate_up, grad_down = call(
        last_weight_kernel,
        weight_shapes,
        [],
        [near, swap(mid_far, "dp", 1), *second],
        [],
        [
            pltpu.VMEM((depth, 2 * hidden_width), F32),
            pltpu.VMEM((depth, hidden_width), F32),
            pltpu.SemaphoreType.DMA((2, 4)),
        ],
        weight_flops // 2,
        2,
    )
    return (grad_tokens, grad_route.T, grad_gate_up[None], grad_down[None])


def block_rows(token_count, route_count, expert_total):
    return min(token_count, (token_count * route_count + expert_total - 1) // expert_total + 1)


def to_local(rows, group_count, local_count, capacity):
    tail = rows.shape[2:]
    shaped = rows.reshape((group_count, local_count, capacity) + tail)
    shaped = jnp.swapaxes(shaped, 0, 1)
    return shaped.reshape((local_count, group_count * capacity) + tail)


def to_groups(rows, group_count, local_count, capacity):
    tail = rows.shape[2:]
    shaped = rows.reshape((local_count, group_count, capacity) + tail)
    shaped = jnp.swapaxes(shaped, 0, 1)
    return shaped.reshape((group_count, local_count * capacity) + tail)


def on_device_routed(tokens, grad_out, route_expert, route_weight, gate_up_weight, down_weight):
    token_count, model_width = tokens.shape
    route_count = route_expert.shape[1]
    group_count = lax.axis_size("expert")
    local_count = gate_up_weight.shape[0]
    hidden_width = down_weight.shape[2]
    expert_total = local_count * group_count
    capacity = min(token_count, (token_count * route_count + expert_total - 1) // expert_total + 1)
    slot_total = expert_total * capacity
    flat_expert = route_expert.reshape(-1)
    expert_ids = jnp.arange(expert_total, dtype=jnp.int32)
    onehot = (flat_expert[:, None] == expert_ids[None, :]).astype(jnp.int32)
    before = jnp.cumsum(onehot, axis=0) - onehot
    rank = jnp.sum(before * onehot, axis=1)
    slot_of = flat_expert * capacity + rank
    slot_ids = jnp.arange(slot_total, dtype=jnp.int32)
    placed = slot_ids[:, None] == slot_of[None, :]
    by_token = jnp.any(placed.reshape(slot_total, token_count, route_count), axis=2).astype(
        jnp.bfloat16
    )
    send_x = jnp.dot(by_token, tokens, preferred_element_type=jnp.float32).astype(jnp.bfloat16)
    send_dy = jnp.dot(by_token, grad_out, preferred_element_type=jnp.float32).astype(jnp.bfloat16)
    flat_weight = route_weight.reshape(-1).astype(jnp.float32)
    send_w = jnp.sum(jnp.where(placed, flat_weight[None, :], 0.0), axis=1).astype(jnp.bfloat16)
    recv_x, recv_dy, recv_w = (
        lax.all_to_all(
            send_x.reshape(group_count, local_count * capacity, model_width),
            "expert",
            split_axis=0,
            concat_axis=0,
            tiled=True,
        ),
        lax.all_to_all(
            send_dy.reshape(group_count, local_count * capacity, model_width),
            "expert",
            split_axis=0,
            concat_axis=0,
            tiled=True,
        ),
        lax.all_to_all(
            send_w.reshape(group_count, local_count * capacity),
            "expert",
            split_axis=0,
            concat_axis=0,
            tiled=True,
        ),
    )
    rows_x = to_local(recv_x, group_count, local_count, capacity)
    rows_dy = to_local(recv_dy, group_count, local_count, capacity)
    rows_w = to_local(recv_w, group_count, local_count, capacity)
    full_in, full_out = (
        lax.all_gather(gate_up_weight, "dp", axis=1, tiled=True),
        lax.all_gather(down_weight, "dp", axis=1, tiled=True),
    )
    pre = jnp.einsum("erd,edf->erf", rows_x, full_in, preferred_element_type=jnp.float32)
    gate_pre = pre[:, :, :hidden_width]
    up_pre = pre[:, :, hidden_width:]
    act = swish(gate_pre)
    hidden = (act * up_pre).astype(jnp.bfloat16)
    expert_out = jnp.einsum("erf,edf->erd", hidden, full_out, preferred_element_type=jnp.float32)
    route_grad = jnp.sum(rows_dy.astype(jnp.float32) * expert_out, axis=2).astype(jnp.bfloat16)
    scaled = (rows_w.astype(jnp.float32)[:, :, None] * rows_dy).astype(jnp.bfloat16)
    grad_hidden = jnp.einsum("erd,edf->erf", scaled, full_out, preferred_element_type=jnp.float32)
    sig = jax.nn.sigmoid(gate_pre)
    grad_gate = grad_hidden * up_pre * sig * (1.0 + gate_pre * (1.0 - sig))
    grad_up = grad_hidden * act
    grad_pre = jnp.concatenate([grad_gate, grad_up], axis=2).astype(jnp.bfloat16)
    rows_grad = jnp.einsum(
        "erf,edf->erd", grad_pre, full_in, preferred_element_type=jnp.float32
    ).astype(jnp.bfloat16)
    back_x, back_w = (
        lax.all_to_all(
            to_groups(rows_grad, group_count, local_count, capacity),
            "expert",
            split_axis=0,
            concat_axis=0,
            tiled=True,
        ),
        lax.all_to_all(
            to_groups(route_grad, group_count, local_count, capacity),
            "expert",
            split_axis=0,
            concat_axis=0,
            tiled=True,
        ),
    )
    back_x = back_x.reshape(slot_total, model_width)
    back_w = back_w.reshape(slot_total).astype(jnp.float32)
    grad_tokens = jnp.einsum(
        "st,sd->td", by_token, back_x, preferred_element_type=jnp.float32
    ).astype(jnp.bfloat16)
    grad_route = jnp.sum(jnp.where(placed, back_w[:, None], 0.0), axis=0)
    grad_route = grad_route.reshape(token_count, route_count).astype(jnp.bfloat16)
    all_x = lax.all_to_all(rows_x, "dp", split_axis=2, concat_axis=1, tiled=True)
    grad_gate_up = jnp.einsum(
        "erd,erf->edf",
        all_x,
        lax.all_gather(grad_pre, "dp", axis=1, tiled=True),
        preferred_element_type=jnp.float32,
    )
    summed = lax.psum_scatter(
        jnp.einsum("erd,erf->def", scaled, hidden, preferred_element_type=jnp.float32),
        "dp",
        scatter_dimension=0,
        tiled=True,
    )
    grad_down = jnp.swapaxes(summed, 0, 1)
    return (grad_tokens, grad_route, grad_gate_up, grad_down)


def packs(tokens, route_expert, down_weight):
    chunks = tokens.shape[1] // LANES
    capacity = block_rows(tokens.shape[0], route_expert.shape[1], lax.axis_size("expert"))
    return (
        lax.axis_size("expert") == 8
        and lax.axis_size("dp") == 4
        and down_weight.shape[0] == 1
        and capacity % 16 <= 1
        and chunks == 16
        and 2 * chunks <= capacity < LANES // 2
    )


def solution(mesh):
    def on_device(*arrays):
        if packs(arrays[0], arrays[2], arrays[5]):
            return on_device_packed(*arrays)
        return on_device_routed(*arrays)

    return jax.shard_map(
        on_device,
        mesh=mesh,
        in_specs=(
            P(("expert", "dp"), None),
            P(("expert", "dp"), None),
            P(("expert", "dp"), None),
            P(("expert", "dp"), None),
            P("expert", "dp", None),
            P("expert", "dp", None),
        ),
        out_specs=(
            P(("expert", "dp"), None),
            P(("expert", "dp"), None),
            P("expert", "dp", None),
            P("expert", "dp", None),
        ),
        check_vma=False,
    )
```

```python
import functools

import jax
import jax.numpy as jnp
from jax import lax
from jax.experimental import pallas as pl
from jax.experimental.pallas import tpu as pltpu
from jax.sharding import PartitionSpec as P

BF16 = jnp.bfloat16
F32 = jnp.float32
LANES = 128


def swish(value):
    return value * jax.nn.sigmoid(value)


def dot(a, b):
    return jnp.dot(a, b, preferred_element_type=F32)


def dot_nt(a, b):
    return lax.dot_general(a, b, (((1,), (1,)), ((), ())), preferred_element_type=F32)


def dot_tn(a, b):
    return lax.dot_general(a, b, (((0,), (0,)), ((), ())), preferred_element_type=F32)


def start(source, target, sem):
    copy = pltpu.make_async_copy(source, target, sem)
    copy.start()
    return copy


def picks(weight, main):
    token_count = weight.shape[1]
    routed = weight != 0.0
    first = lax.broadcasted_iota(jnp.int32, (token_count, token_count), 0)
    second = lax.broadcasted_iota(jnp.int32, (token_count, token_count), 1)
    upper = (first < second).astype(F32).astype(BF16)
    rank = dot(routed.astype(F32).astype(BF16), upper)
    rank = jnp.where(routed, rank, -1.0).astype(jnp.int32)
    slots = lax.broadcasted_iota(jnp.int32, (main, token_count), 0)
    mains = [(slots == rank[i : i + 1, :]).astype(F32) for i in range(weight.shape[0])]
    tails = (rank == main).astype(F32)
    return mains, tails


def route_kernel(peer_ref, named_ref, given_ref, x_ref, dy_ref, joint_ref, dense_ref):
    count, width = x_ref.shape
    named = named_ref[...]
    given = given_ref[...].astype(F32)
    experts = dense_ref.shape[0]
    lines = [
        jnp.sum(jnp.where(named == peer_ref[i], given, 0.0), axis=0, keepdims=True) for i in range(experts)
    ]
    dense = jnp.concatenate(lines, axis=0)
    dense_ref[...] = dense
    turned = jnp.concatenate(lines[experts // 2 :] + lines[: experts // 2] + [jnp.zeros_like(dense)], axis=0)
    joint_ref[:, :width] = x_ref[...]
    joint_ref[:, width : 2 * width] = dy_ref[...]
    joint_ref[:, 2 * width :] = jnp.zeros((count, LANES), BF16)
    joint_ref[0:16, 2 * width : 2 * width + count] = turned.astype(BF16)


def stack_kernel(own_ref, far_ref, after_ref, stacked_ref):
    count = own_ref.shape[0]
    stacked_ref[0:count, :] = own_ref[...]
    stacked_ref[count:, :] = far_ref[...]


def after_kernel(*refs):
    pass


def relay_kernel(near_a, far_a, near_b, far_b, mid_ref, *refs):
    joint_ref = refs[-1]
    count, width = near_a.shape
    for at, near, far in ((0, near_a, far_a), (count, near_b, far_b)):
        joint_ref[at : at + count, :width] = near[...]
        joint_ref[at : at + count, width : 2 * width] = far[:, width:]
    joint_ref[:, 2 * width :] = mid_ref[...]


def pack_blocks(experts, joint_ref, out_refs, fold):
    count = len(experts)
    tokens, width = joint_ref.shape[0], out_refs[0].shape[1] - LANES
    chunks = width // LANES
    main = out_refs[0].shape[0] // 2
    weight = joint_ref[0:16, 2 * width :].astype(F32)[0:8, :tokens]
    mains, tails = picks(weight, main)
    pick = jnp.concatenate([mains[e] for e in experts] + [tails, jnp.zeros_like(tails)], axis=0).astype(BF16)
    lane = lax.broadcasted_iota(jnp.int32, (main, LANES), 1)
    for at, base, low in ((0, 0, 0), (width, main, chunks)):
        rows = dot(pick, joint_ref[:, at : at + width])
        for j, e in enumerate(experts):
            out_refs[j][base : base + main, :width] = rows[main * j : main * (j + 1)].astype(BF16)
            line = main * count + e
            for c in range(chunks):
                fold[c : c + 1, :] = rows[line : line + 1, LANES * c : LANES * (c + 1)]
            out_refs[j][low : low + chunks, width:] = fold[...].astype(BF16)
    for j, e in enumerate(experts):
        mine = weight[e : e + 1, :]
        column = jnp.sum(mains[e] * mine, axis=1, keepdims=True)
        last = jnp.sum(tails[e : e + 1, :] * mine, axis=1, keepdims=True)
        out_refs[j][main:, width:] = jnp.where(lane < LANES // 2, column, last).astype(BF16)


def pack_kernel(experts, joint_ref, *refs):
    pack_blocks(experts, joint_ref, refs[-1 - len(experts) : -1], refs[-1])


def slice_kernel(own, place_ref, *refs):
    blocks, parts = 4, 4
    keep_ref, near_ref, far_ref, weight_ref, fold, kept = refs[-6:]
    in_refs = list(refs[:blocks])
    if own:
        in_refs[0] = kept
        pack_blocks([own], refs[0], [kept], fold.at[0, pl.ds(0, 16)])
    main = in_refs[0].shape[0] // 2
    depth = keep_ref.shape[1] // 2
    width = parts * depth
    chunks = width // LANES
    targets = [(keep_ref, 0), (near_ref, 0), (far_ref, 0), (far_ref, 2 * depth)]
    lane = lax.broadcasted_iota(jnp.int32, (1, LANES), 1)
    lasts = []
    for i in range(blocks):
        for j, (target, shift) in enumerate(targets):
            columns = pl.ds(pl.multiple_of(place_ref[j] * depth, depth), depth)
            for side in range(2):
                at = shift + side * depth
                target[main * i : main * (i + 1), at : at + depth] = in_refs[i][
                    side * main : (side + 1) * main, columns
                ]
        for side in range(2):
            fold[side, chunks * i : chunks * (i + 1), :] = in_refs[i][
                side * chunks : (side + 1) * chunks, width:
            ].astype(F32)
        weights = in_refs[i][main:, width:].astype(F32)
        weight_ref[main * i : main * (i + 1), :] = weights
        last = jnp.sum(jnp.where(lane == LANES - 1, weights[0:1, :], 0.0), axis=1, keepdims=True)
        lasts.append(jnp.broadcast_to(last, (1, LANES)))
    weight_ref[main * blocks :, :] = jnp.concatenate(lasts + [jnp.zeros((16 - blocks, LANES), F32)], axis=0)
    each = chunks // parts
    for j, (target, shift) in enumerate(targets):
        for side in range(2):
            for q in range(each):
                tail = fold[side, pl.ds(place_ref[j] * each + q, blocks, stride=chunks), :]
                tail = jnp.concatenate([tail, jnp.zeros((16 - blocks, LANES), F32)], axis=0).astype(BF16)
                at = shift + side * depth + q * LANES
                target[main * blocks :, at : at + LANES] = tail


def main_kernel(early, place_ref, w_ref, *refs):
    blocks, parts = 4, 4
    own_ref, other_ref = refs[:2]
    keep_ref, near_ref, far_ref = refs[2:5]
    mid, backs, (tail, fold) = refs[-3 - blocks], refs[-2 - blocks : -2], refs[-2:]
    depth = keep_ref.shape[1] // 2
    width = parts * depth
    hidden_width = mid.shape[1] // 3
    main = backs[0].shape[0]
    chunks = width // LANES
    total = keep_ref.shape[0]
    first, second = pl.ds(0, depth), pl.ds(depth, depth)
    weights = [own_ref.at[first], other_ref.at[first], own_ref.at[second], other_ref.at[second]]
    pre = jnp.zeros((total, 2 * hidden_width), F32)
    grad = jnp.zeros((total, hidden_width), F32)
    for j, (ref, shift) in enumerate([(keep_ref, 0), (near_ref, 0), (far_ref, 0), (far_ref, 2 * depth)]):
        pre += dot(ref[:, shift : shift + depth], weights[j][:, : 2 * hidden_width])
        grad += dot(ref[:, shift + depth : shift + 2 * depth], weights[j][:, 2 * hidden_width :])
    if early:
        mid[0:early, :] = refs[5][...]
    weight = w_ref[:, 0:1]
    gate_pre = pre[:, :hidden_width]
    up_pre = pre[:, hidden_width:]
    sig = jax.nn.sigmoid(gate_pre)
    act = gate_pre * sig
    hidden = (act * up_pre).astype(BF16).astype(F32)
    route = jnp.sum(hidden * grad, axis=1, keepdims=True)
    grad_hidden = weight * grad
    grad_gate = grad_hidden * up_pre * sig * (1.0 + gate_pre * (1.0 - sig))
    mid[early:, :hidden_width] = grad_gate.astype(BF16)
    mid[early:, hidden_width : 2 * hidden_width] = (grad_hidden * act).astype(BF16)
    mid[early:, 2 * hidden_width :] = (weight * hidden).astype(BF16)
    for j in range(parts):
        columns = pl.ds(pl.multiple_of(place_ref[j] * depth, depth), depth)
        part = dot_nt(mid[early:, : 2 * hidden_width], weights[j][:, : 2 * hidden_width])
        tail[:, columns] = part[main * blocks :]
        part = part.astype(BF16)
        for i in range(blocks):
            backs[i][:, columns] = part[main * i : main * (i + 1)]
    row = lax.broadcasted_iota(jnp.int32, (main, LANES), 0)
    lane = lax.broadcasted_iota(jnp.int32, (main, LANES), 1)
    for i in range(blocks):
        for c in range(chunks):
            fold[c : c + 1, :] = tail[i : i + 1, LANES * c : LANES * (c + 1)]
        backs[i][:chunks, width:] = fold[...].astype(BF16)
        mine = jnp.where(row == lane, route[main * i : main * (i + 1)], 0.0)
        mine = jnp.sum(mine, axis=0, keepdims=True)
        mine = jnp.where(lane[0:1] == main, route[main * blocks + i : main * blocks + i + 1], mine)
        backs[i][chunks:, width:] = jnp.broadcast_to(mine, (main - chunks, LANES)).astype(BF16)


def unpack_sum(weight, block_refs, rows, fold, order=(0, 1, 2, 3)):
    count = len(block_refs)
    main = block_refs[0].shape[0]
    width = rows.shape[1]
    chunks = width // LANES
    mains, tails = picks(weight, main)
    mains = [mains[e] for e in order]
    tails = jnp.concatenate([tails[e : e + 1, :] for e in order] + [jnp.zeros((16 - count, tails.shape[1]), F32)], axis=0)
    pick = jnp.concatenate(mains + [tails], axis=0).astype(BF16)
    lane = lax.broadcasted_iota(jnp.int32, (1, LANES), 1)
    routes = {}
    for j in range(count):
        rows[main * j : main * (j + 1), :] = block_refs[j][:, :width]
        fold[chunks * j : chunks * (j + 1), :] = block_refs[j][:chunks, width:].astype(F32)
        mine = block_refs[j][chunks:, width:].astype(F32)
        dense = dot(mine[:, :main].astype(BF16), mains[j].astype(BF16))[0:1, :]
        last = jnp.sum(jnp.where(lane == main, mine[0:1, :], 0.0), axis=1, keepdims=True)
        routes[order[j]] = dense + last * tails[j : j + 1, :]
    for c in range(chunks):
        tail = fold[pl.ds(c, count, stride=chunks), :]
        tail = jnp.concatenate([tail, jnp.zeros((16 - count, LANES), F32)], axis=0).astype(BF16)
        rows[main * count :, LANES * c : LANES * (c + 1)] = tail
    return dot_tn(pick, rows[...]), [routes[e] for e in range(count)]


def relay_sum_kernel(joint_ref, b0, b3, b2, b1, out_ref, rows, fold):
    tokens, width = joint_ref.shape[0], rows.shape[1]
    weight = joint_ref[0:16, 2 * width :].astype(F32)[0:8, :tokens]
    summed, routes = unpack_sum(weight, (b0, b3, b2, b1), rows, fold, (0, 3, 2, 1))
    lines = tokens // 2
    out_ref[:, :width] = summed[0:lines].astype(BF16)
    out_ref[:, width : 2 * width] = summed[lines:].astype(BF16)
    out_ref[:, 2 * width :] = jnp.zeros((lines, LANES), BF16)
    block = jnp.concatenate(routes + [jnp.zeros((12, tokens), F32)], axis=0).astype(BF16)
    out_ref[0:16, 2 * width : 2 * width + tokens] = block


def combine_kernel(peer_ref, named_ref, w_ref, b0, b3, b2, b1, far_ref, *refs):
    grad_ref, route_ref, in_ref, out_ref, held, rows, fold, lines_ref, sem = refs[5:]
    tokens, width = held.shape
    summed, routes = unpack_sum(w_ref[...], (b0, b3, b2, b1), rows, fold, (0, 3, 2, 1))
    lines = tokens // 2
    for half in range(2):
        at, columns = slice(half * lines, (half + 1) * lines), slice(half * width, (half + 1) * width)
        held[at, :] = (summed[at, :] + far_ref[:, columns].astype(F32)).astype(BF16)
    copy = start(held, grad_ref, sem)
    others = far_ref[0:16, 2 * width : 2 * width + tokens].astype(F32)
    named = named_ref[...]
    route = jnp.zeros(route_ref.shape, F32)
    for j in range(4):
        route = route + jnp.where(named == peer_ref[j], routes[j], 0.0)
        route = route + jnp.where(named == peer_ref[4 + j], others[j : j + 1, :], 0.0)
    route_ref[...] = route.astype(BF16)
    second_weight_part(*refs[:5], in_ref, out_ref, lines_ref)
    copy.wait()


def fill(rows, mids, rows_a, rows_b, rows_c, mid_a, mid_b):
    count = rows_a.shape[0]
    rows[0:count, :] = rows_a
    rows[count : 2 * count, :] = rows_b
    rows[2 * count :, :] = rows_c
    mids[0 : 2 * count, :] = mid_a
    mids[2 * count :, :] = mid_b


def first_weight_kernel(rows_a, rows_b, near_ref, mid_ref, in_ref, out_ref, rows, mids):
    depth, hidden_width = out_ref.shape
    near, near_mid = near_ref[:, : 2 * depth], near_ref[:, 4 * depth :]
    fill(rows, mids, rows_a[...], rows_b[...], near, mid_ref[...], near_mid)
    in_ref[...] = dot_tn(rows[:, :depth], mids[:, : 2 * hidden_width])
    out_ref[...] = dot_tn(rows[:, depth:], mids[:, 2 * hidden_width :])


def second_weight_part(rows_a, rows_b, mid_ref, in_part, out_part, in_ref, out_ref, rows):
    depth, hidden_width = out_ref.shape
    count = rows_a.shape[0]
    rows[0:count, :] = rows_a[:, : 2 * depth]
    rows[count:, :] = rows_b[:, : 2 * depth]
    in_ref[...] = in_part[...] + dot_tn(rows[:, :depth], mid_ref[:, : 2 * hidden_width])
    out_ref[...] = out_part[...] + dot_tn(rows[:, depth:], mid_ref[:, 2 * hidden_width :])


def last_weight_kernel(near_ref, mid_ref, in_part, out_part, in_ref, out_ref, in_held, out_held, sems):
    depth, hidden_width = out_part.shape
    copies = []
    step = depth // 4
    for m in range(4):
        at = slice(m * step, (m + 1) * step)
        lines = pl.ds(m * step, step)
        base = 2 * depth + m * step
        in_held[at, :] = in_part[at, :] + dot_tn(near_ref[:, base : base + step], mid_ref[:, : 2 * hidden_width])
        copies.append(start(in_held.at[lines], in_ref.at[lines], sems.at[0, m]))
        base += depth
        out_held[at, :] = out_part[at, :] + dot_tn(near_ref[:, base : base + step], mid_ref[:, 2 * hidden_width :])
        copies.append(start(out_held.at[lines], out_ref.at[lines], sems.at[1, m]))
    for copy in copies:
        copy.wait()


def call(kernel, outs, smem, vmem, either, scratch, flops, either_outs=0, aliases=None):
    on_vmem = pl.BlockSpec(memory_space=pltpu.VMEM)
    on_either = pl.BlockSpec(memory_space=pl.ANY)
    on_smem = pl.BlockSpec(memory_space=pltpu.SMEM)
    outs = [jax.ShapeDtypeStruct(shape, kind) for shape, kind in outs]
    moved = sum(a.size * a.dtype.itemsize for a in list(vmem) + outs[either_outs:])
    return pl.pallas_call(
        kernel,
        out_shape=tuple(outs),
        in_specs=[on_smem] * len(smem) + [on_vmem] * len(vmem) + [on_either] * len(either),
        out_specs=tuple([on_either] * either_outs + [on_vmem] * (len(outs) - either_outs)),
        scratch_shapes=scratch,
        compiler_params=pltpu.CompilerParams(vmem_limit_bytes=16 * 1024 * 1024),
        cost_estimate=pl.CostEstimate(flops=flops, bytes_accessed=moved, transcendentals=0),
        input_output_aliases=aliases or {},
    )(*smem, *vmem, *either)


def swap(value, axis, mask):
    return lax.ppermute(value, axis, [(i, i ^ mask) for i in range(lax.axis_size(axis))])


def on_device_packed(tokens, grad_out, route_expert, route_weight, gate_up_weight, down_weight):
    token_count, width = tokens.shape
    blocks, parts, half = 8, 4, 4
    hidden_width = down_weight.shape[2]
    depth = width // parts
    chunks = width // LANES
    main = block_rows(token_count, route_expert.shape[1], blocks) // 16 * 16
    rows = main * half + 16

    peers = lax.axis_index("expert") ^ jnp.arange(blocks, dtype=jnp.int32)
    places = lax.axis_index("dp") ^ jnp.arange(parts, dtype=jnp.int32)
    named = route_expert.T
    packed_shape = ((2 * main, width + LANES), BF16)
    back_shape = ((main, width + LANES), BF16)

    joint, dense = call(
        route_kernel,
        [((token_count, 2 * width + LANES), BF16), ((blocks, token_count), F32)],
        [peers],
        [named, route_weight.T, tokens, grad_out],
        [],
        [],
        0,
    )
    far_joint = swap(joint, "expert", half)

    weights = jnp.concatenate([gate_up_weight[0], down_weight[0]], axis=1)
    far_weights = swap(weights, "dp", 2)

    def pack(experts, value, after):
        return call(
            functools.partial(pack_kernel, experts),
            [packed_shape] * len(experts),
            [],
            [value],
            after,
            [pltpu.VMEM((chunks, LANES), F32)],
            4 * (len(experts) * main + 16) * token_count * width,
        )

    def sliced(own, packed, after):
        return call(
            functools.partial(slice_kernel, own),
            [
                ((rows, 2 * depth), BF16),
                ((rows, 2 * depth), BF16),
                ((rows, 4 * depth), BF16),
                ((rows, LANES), F32),
            ],
            [places],
            packed,
            after,
            [pltpu.VMEM((2, half * chunks, LANES), F32), pltpu.VMEM(*packed_shape)],
            0,
        )

    own = [swap(value, "expert", j + 1) for j, value in enumerate(pack(range(half + 1, blocks), joint, []))]
    *own_slices, own_weight = sliced(half, [joint, *own], [far_joint])
    own_far = swap(own_slices[2], "dp", 2)
    far = pack(range(half), far_joint, [own_slices[0], far_weights])
    far = [far[0]] + [swap(far[j], "expert", j) for j in range(1, half)]
    (stacked,) = call(
        stack_kernel,
        [((2 * depth, 3 * hidden_width), BF16)],
        [],
        [weights, far_weights],
        [far[0]],
        [],
        0,
    )
    weight_parts = [stacked, swap(stacked, "dp", 1)]

    def middle(slices, weight, before, after):
        early = before[0].shape[0] if before else 0
        return call(
            functools.partial(main_kernel, early),
            [((early + rows, 3 * hidden_width), BF16)] + [back_shape] * half,
            [places],
            [weight, *weight_parts, *slices, *before],
            after,
            [pltpu.VMEM((16, width), F32), pltpu.VMEM((chunks, LANES), F32)],
            2 * rows * width * 5 * hidden_width,
        )

    own_mid, *near_back = middle(own_slices, own_weight, [], [])
    near_back = near_back[:1] + [swap(near_back[j], "expert", j) for j in range(1, half)]
    *far_slices, far_weight = sliced(None, far, [own_mid, own_far])
    far_far = swap(far_slices[2], "dp", 2)
    mid, *far_back = middle(far_slices, far_weight, [own_mid], [])

    sum_scratch = [
        pltpu.VMEM((half * main + 16, width), BF16),
        pltpu.VMEM((half * chunks, LANES), F32),
    ]
    sum_flops = 2 * (half * main + 16) * width * token_count
    far_back = far_back[:1] + [swap(far_back[j], "expert", j) for j in range(1, half)]
    (partial,) = call(
        relay_sum_kernel,
        [((token_count // 2, 2 * width + LANES), BF16)],
        [],
        [far_joint, far_back[0], *far_back[:0:-1]],
        [],
        sum_scratch,
        sum_flops,
    )
    far_partial = swap(partial, "expert", half)

    mid_far = swap(mid, "dp", 2)
    (near,) = call(
        relay_kernel,
        [((2 * rows, 4 * depth + 3 * hidden_width), BF16)],
        [],
        [own_slices[1], own_far, far_slices[1], far_far, mid],
        [partial],
        [],
        0,
    )
    near = swap(near, "dp", 1)
    weight_shapes = [((depth, 2 * hidden_width), F32), ((depth, hidden_width), F32)]
    weight_scratch = [pltpu.VMEM((4 * rows, 2 * depth), BF16), pltpu.VMEM((4 * rows, 3 * hidden_width), BF16)]
    weight_flops = 2 * 4 * rows * depth * 3 * hidden_width
    first = call(
        first_weight_kernel,
        weight_shapes,
        [],
        [own_slices[0], far_slices[0], near, mid],
        [],
        weight_scratch,
        weight_flops,
    )
    (mid_far,) = call(
        after_kernel,
        [(mid_far.shape, BF16)],
        [],
        [],
        [mid_far, first[1], far_partial, *near_back[:0:-1]],
        [],
        0,
        1,
        {0: 0},
    )
    grad_tokens, grad_route, *second = call(
        combine_kernel,
        [((token_count, width), BF16), (named.shape, BF16), *weight_shapes],
        [peers],
        [named, dense, near_back[0], *near_back[:0:-1], far_partial, own_far, far_far, mid_far, *first],
        [],
        [
            pltpu.VMEM((token_count, width), BF16),
            *sum_scratch,
            pltpu.VMEM((2 * rows, 2 * depth), BF16),
            pltpu.SemaphoreType.DMA,
        ],
        sum_flops + weight_flops // 2,
        1,
    )
    grad_gate_up, grad_down = call(
        last_weight_kernel,
        weight_shapes,
        [],
        [near, swap(mid_far, "dp", 1), *second],
        [],
        [
            pltpu.VMEM((depth, 2 * hidden_width), F32),
            pltpu.VMEM((depth, hidden_width), F32),
            pltpu.SemaphoreType.DMA((2, 4)),
        ],
        weight_flops // 2,
        2,
    )
    return (grad_tokens, grad_route.T, grad_gate_up[None], grad_down[None])


def block_rows(token_count, route_count, expert_total):
    return min(token_count, (token_count * route_count + expert_total - 1) // expert_total + 1)


def to_local(rows, group_count, local_count, capacity):
    tail = rows.shape[2:]
    shaped = rows.reshape((group_count, local_count, capacity) + tail)
    shaped = jnp.swapaxes(shaped, 0, 1)
    return shaped.reshape((local_count, group_count * capacity) + tail)


def to_groups(rows, group_count, local_count, capacity):
    tail = rows.shape[2:]
    shaped = rows.reshape((local_count, group_count, capacity) + tail)
    shaped = jnp.swapaxes(shaped, 0, 1)
    return shaped.reshape((group_count, local_count * capacity) + tail)


def on_device_routed(tokens, grad_out, route_expert, route_weight, gate_up_weight, down_weight):
    token_count, model_width = tokens.shape
    route_count = route_expert.shape[1]
    group_count = lax.axis_size("expert")
    local_count = gate_up_weight.shape[0]
    hidden_width = down_weight.shape[2]
    expert_total = local_count * group_count
    capacity = min(token_count, (token_count * route_count + expert_total - 1) // expert_total + 1)
    slot_total = expert_total * capacity
    flat_expert = route_expert.reshape(-1)
    expert_ids = jnp.arange(expert_total, dtype=jnp.int32)
    onehot = (flat_expert[:, None] == expert_ids[None, :]).astype(jnp.int32)
    before = jnp.cumsum(onehot, axis=0) - onehot
    rank = jnp.sum(before * onehot, axis=1)
    slot_of = flat_expert * capacity + rank
    slot_ids = jnp.arange(slot_total, dtype=jnp.int32)
    placed = slot_ids[:, None] == slot_of[None, :]
    by_token = jnp.any(placed.reshape(slot_total, token_count, route_count), axis=2).astype(
        jnp.bfloat16
    )
    send_x = jnp.dot(by_token, tokens, preferred_element_type=jnp.float32).astype(jnp.bfloat16)
    send_dy = jnp.dot(by_token, grad_out, preferred_element_type=jnp.float32).astype(jnp.bfloat16)
    flat_weight = route_weight.reshape(-1).astype(jnp.float32)
    send_w = jnp.sum(jnp.where(placed, flat_weight[None, :], 0.0), axis=1).astype(jnp.bfloat16)
    recv_x, recv_dy, recv_w = (
        lax.all_to_all(
            send_x.reshape(group_count, local_count * capacity, model_width),
            "expert",
            split_axis=0,
            concat_axis=0,
            tiled=True,
        ),
        lax.all_to_all(
            send_dy.reshape(group_count, local_count * capacity, model_width),
            "expert",
            split_axis=0,
            concat_axis=0,
            tiled=True,
        ),
        lax.all_to_all(
            send_w.reshape(group_count, local_count * capacity),
            "expert",
            split_axis=0,
            concat_axis=0,
            tiled=True,
        ),
    )
    rows_x = to_local(recv_x, group_count, local_count, capacity)
    rows_dy = to_local(recv_dy, group_count, local_count, capacity)
    rows_w = to_local(recv_w, group_count, local_count, capacity)
    full_in, full_out = (
        lax.all_gather(gate_up_weight, "dp", axis=1, tiled=True),
        lax.all_gather(down_weight, "dp", axis=1, tiled=True),
    )
    pre = jnp.einsum("erd,edf->erf", rows_x, full_in, preferred_element_type=jnp.float32)
    gate_pre = pre[:, :, :hidden_width]
    up_pre = pre[:, :, hidden_width:]
    act = swish(gate_pre)
    hidden = (act * up_pre).astype(jnp.bfloat16)
    expert_out = jnp.einsum("erf,edf->erd", hidden, full_out, preferred_element_type=jnp.float32)
    route_grad = jnp.sum(rows_dy.astype(jnp.float32) * expert_out, axis=2).astype(jnp.bfloat16)
    scaled = (rows_w.astype(jnp.float32)[:, :, None] * rows_dy).astype(jnp.bfloat16)
    grad_hidden = jnp.einsum("erd,edf->erf", scaled, full_out, preferred_element_type=jnp.float32)
    sig = jax.nn.sigmoid(gate_pre)
    grad_gate = grad_hidden * up_pre * sig * (1.0 + gate_pre * (1.0 - sig))
    grad_up = grad_hidden * act
    grad_pre = jnp.concatenate([grad_gate, grad_up], axis=2).astype(jnp.bfloat16)
    rows_grad = jnp.einsum(
        "erf,edf->erd", grad_pre, full_in, preferred_element_type=jnp.float32
    ).astype(jnp.bfloat16)
    back_x, back_w = (
        lax.all_to_all(
            to_groups(rows_grad, group_count, local_count, capacity),
            "expert",
            split_axis=0,
            concat_axis=0,
            tiled=True,
        ),
        lax.all_to_all(
            to_groups(route_grad, group_count, local_count, capacity),
            "expert",
            split_axis=0,
            concat_axis=0,
            tiled=True,
        ),
    )
    back_x = back_x.reshape(slot_total, model_width)
    back_w = back_w.reshape(slot_total).astype(jnp.float32)
    grad_tokens = jnp.einsum(
        "st,sd->td", by_token, back_x, preferred_element_type=jnp.float32
    ).astype(jnp.bfloat16)
    grad_route = jnp.sum(jnp.where(placed, back_w[:, None], 0.0), axis=0)
    grad_route = grad_route.reshape(token_count, route_count).astype(jnp.bfloat16)
    all_x = lax.all_to_all(rows_x, "dp", split_axis=2, concat_axis=1, tiled=True)
    grad_gate_up = jnp.einsum(
        "erd,erf->edf",
        all_x,
        lax.all_gather(grad_pre, "dp", axis=1, tiled=True),
        preferred_element_type=jnp.float32,
    )
    summed = lax.psum_scatter(
        jnp.einsum("erd,erf->def", scaled, hidden, preferred_element_type=jnp.float32),
        "dp",
        scatter_dimension=0,
        tiled=True,
    )
    grad_down = jnp.swapaxes(summed, 0, 1)
    return (grad_tokens, grad_route, grad_gate_up, grad_down)


def packs(tokens, route_expert, down_weight):
    chunks = tokens.shape[1] // LANES
    capacity = block_rows(tokens.shape[0], route_expert.shape[1], lax.axis_size("expert"))
    return (
        lax.axis_size("expert") == 8
        and lax.axis_size("dp") == 4
        and down_weight.shape[0] == 1
        and capacity % 16 <= 1
        and chunks == 16
        and 2 * chunks <= capacity < LANES // 2
    )


def solution(mesh):
    def on_device(*arrays):
        if packs(arrays[0], arrays[2], arrays[5]):
            return on_device_packed(*arrays)
        return on_device_routed(*arrays)

    return jax.shard_map(
        on_device,
        mesh=mesh,
        in_specs=(
            P(("expert", "dp"), None),
            P(("expert", "dp"), None),
            P(("expert", "dp"), None),
            P(("expert", "dp"), None),
            P("expert", "dp", None),
            P("expert", "dp", None),
        ),
        out_specs=(
            P(("expert", "dp"), None),
            P(("expert", "dp"), None),
            P("expert", "dp", None),
            P("expert", "dp", None),
        ),
        check_vma=False,
    )
```

```python
import functools

import jax
import jax.numpy as jnp
from jax import lax
from jax.experimental import pallas as pl
from jax.experimental.pallas import tpu as pltpu
from jax.sharding import PartitionSpec as P

BF16 = jnp.bfloat16
F32 = jnp.float32
LANES = 128


def swish(value):
    return value * jax.nn.sigmoid(value)


def dot(a, b):
    return jnp.dot(a, b, preferred_element_type=F32)


def dot_nt(a, b):
    return lax.dot_general(a, b, (((1,), (1,)), ((), ())), preferred_element_type=F32)


def dot_tn(a, b):
    return lax.dot_general(a, b, (((0,), (0,)), ((), ())), preferred_element_type=F32)


def start(source, target, sem):
    copy = pltpu.make_async_copy(source, target, sem)
    copy.start()
    return copy


def picks(weight, main):
    token_count = weight.shape[1]
    routed = weight != 0.0
    first = lax.broadcasted_iota(jnp.int32, (token_count, token_count), 0)
    second = lax.broadcasted_iota(jnp.int32, (token_count, token_count), 1)
    upper = (first < second).astype(F32).astype(BF16)
    rank = dot(routed.astype(F32).astype(BF16), upper)
    rank = jnp.where(routed, rank, -1.0).astype(jnp.int32)
    slots = lax.broadcasted_iota(jnp.int32, (main, token_count), 0)
    mains = [(slots == rank[i : i + 1, :]).astype(F32) for i in range(weight.shape[0])]
    tails = (rank == main).astype(F32)
    return mains, tails


def route_kernel(peer_ref, named_ref, given_ref, x_ref, dy_ref, joint_ref, dense_ref):
    count, width = x_ref.shape
    named = named_ref[...]
    given = given_ref[...].astype(F32)
    experts = dense_ref.shape[0]
    lines = [
        jnp.sum(jnp.where(named == peer_ref[i], given, 0.0), axis=0, keepdims=True) for i in range(experts)
    ]
    dense = jnp.concatenate(lines, axis=0)
    dense_ref[...] = dense
    turned = jnp.concatenate(lines[experts // 2 :] + lines[: experts // 2] + [jnp.zeros_like(dense)], axis=0)
    joint_ref[:, :width] = x_ref[...]
    joint_ref[:, width : 2 * width] = dy_ref[...]
    joint_ref[:, 2 * width :] = jnp.zeros((count, LANES), BF16)
    joint_ref[0:16, 2 * width : 2 * width + count] = turned.astype(BF16)


def stack_kernel(own_ref, far_ref, after_ref, stacked_ref):
    count = own_ref.shape[0]
    stacked_ref[0:count, :] = own_ref[...]
    stacked_ref[count:, :] = far_ref[...]


def after_kernel(*refs):
    pass


def relay_kernel(near_a, far_a, near_b, far_b, mid_ref, *refs):
    joint_ref = refs[-1]
    count, width = near_a.shape
    for at, near, far in ((0, near_a, far_a), (count, near_b, far_b)):
        joint_ref[at : at + count, :width] = near[...]
        joint_ref[at : at + count, width : 2 * width] = far[:, width:]
    joint_ref[:, 2 * width :] = mid_ref[...]


def pack_blocks(experts, joint_ref, out_refs, fold):
    count = len(experts)
    tokens, width = joint_ref.shape[0], out_refs[0].shape[1] - LANES
    chunks = width // LANES
    main = out_refs[0].shape[0] // 2
    weight = joint_ref[0:16, 2 * width :].astype(F32)[0:8, :tokens]
    mains, tails = picks(weight, main)
    pick = jnp.concatenate([mains[e] for e in experts] + [tails, jnp.zeros_like(tails)], axis=0).astype(BF16)
    lane = lax.broadcasted_iota(jnp.int32, (main, LANES), 1)
    for at, base, low in ((0, 0, 0), (width, main, chunks)):
        rows = dot(pick, joint_ref[:, at : at + width])
        for j, e in enumerate(experts):
            out_refs[j][base : base + main, :width] = rows[main * j : main * (j + 1)].astype(BF16)
            line = main * count + e
            for c in range(chunks):
                fold[c : c + 1, :] = rows[line : line + 1, LANES * c : LANES * (c + 1)]
            out_refs[j][low : low + chunks, width:] = fold[...].astype(BF16)
    for j, e in enumerate(experts):
        mine = weight[e : e + 1, :]
        column = jnp.sum(mains[e] * mine, axis=1, keepdims=True)
        last = jnp.sum(tails[e : e + 1, :] * mine, axis=1, keepdims=True)
        out_refs[j][main:, width:] = jnp.where(lane < LANES // 2, column, last).astype(BF16)


def pack_kernel(experts, joint_ref, *refs):
    pack_blocks(experts, joint_ref, refs[-1 - len(experts) : -1], refs[-1])


def slice_kernel(own, place_ref, *refs):
    blocks, parts = 4, 4
    keep_ref, near_ref, far_ref, weight_ref, fold, kept = refs[-6:]
    in_refs = list(refs[:blocks])
    if own:
        in_refs[0] = kept
        pack_blocks([own], refs[0], [kept], fold.at[0, pl.ds(0, 16)])
    main = in_refs[0].shape[0] // 2
    depth = keep_ref.shape[1] // 2
    width = parts * depth
    chunks = width // LANES
    targets = [(keep_ref, 0), (near_ref, 0), (far_ref, 0), (far_ref, 2 * depth)]
    lane = lax.broadcasted_iota(jnp.int32, (1, LANES), 1)
    lasts = []
    for i in range(blocks):
        for j, (target, shift) in enumerate(targets):
            columns = pl.ds(pl.multiple_of(place_ref[j] * depth, depth), depth)
            for side in range(2):
                at = shift + side * depth
                target[main * i : main * (i + 1), at : at + depth] = in_refs[i][
                    side * main : (side + 1) * main, columns
                ]
        for side in range(2):
            fold[side, chunks * i : chunks * (i + 1), :] = in_refs[i][
                side * chunks : (side + 1) * chunks, width:
            ].astype(F32)
        weights = in_refs[i][main:, width:].astype(F32)
        weight_ref[main * i : main * (i + 1), :] = weights
        last = jnp.sum(jnp.where(lane == LANES - 1, weights[0:1, :], 0.0), axis=1, keepdims=True)
        lasts.append(jnp.broadcast_to(last, (1, LANES)))
    weight_ref[main * blocks :, :] = jnp.concatenate(lasts + [jnp.zeros((16 - blocks, LANES), F32)], axis=0)
    each = chunks // parts
    for j, (target, shift) in enumerate(targets):
        for side in range(2):
            for q in range(each):
                tail = fold[side, pl.ds(place_ref[j] * each + q, blocks, stride=chunks), :]
                tail = jnp.concatenate([tail, jnp.zeros((16 - blocks, LANES), F32)], axis=0).astype(BF16)
                at = shift + side * depth + q * LANES
                target[main * blocks :, at : at + LANES] = tail


def main_kernel(early, place_ref, w_ref, *refs):
    blocks, parts = 4, 4
    own_ref, other_ref = refs[:2]
    keep_ref, near_ref, far_ref = refs[2:5]
    mid, backs, (tail, fold) = refs[-3 - blocks], refs[-2 - blocks : -2], refs[-2:]
    depth = keep_ref.shape[1] // 2
    width = parts * depth
    hidden_width = mid.shape[1] // 3
    main = backs[0].shape[0]
    chunks = width // LANES
    total = keep_ref.shape[0]
    first, second = pl.ds(0, depth), pl.ds(depth, depth)
    weights = [own_ref.at[first], other_ref.at[first], own_ref.at[second], other_ref.at[second]]
    pre = jnp.zeros((total, 2 * hidden_width), F32)
    grad = jnp.zeros((total, hidden_width), F32)
    for j, (ref, shift) in enumerate([(keep_ref, 0), (near_ref, 0), (far_ref, 0), (far_ref, 2 * depth)]):
        pre += dot(ref[:, shift : shift + depth], weights[j][:, : 2 * hidden_width])
        grad += dot(ref[:, shift + depth : shift + 2 * depth], weights[j][:, 2 * hidden_width :])
    if early:
        mid[0:early, :] = refs[5][...]
    weight = w_ref[:, 0:1]
    gate_pre = pre[:, :hidden_width]
    up_pre = pre[:, hidden_width:]
    sig = jax.nn.sigmoid(gate_pre)
    act = gate_pre * sig
    hidden = (act * up_pre).astype(BF16).astype(F32)
    route = jnp.sum(hidden * grad, axis=1, keepdims=True)
    grad_hidden = weight * grad
    grad_gate = grad_hidden * up_pre * sig * (1.0 + gate_pre * (1.0 - sig))
    mid[early:, :hidden_width] = grad_gate.astype(BF16)
    mid[early:, hidden_width : 2 * hidden_width] = (grad_hidden * act).astype(BF16)
    mid[early:, 2 * hidden_width :] = (weight * hidden).astype(BF16)
    for j in range(parts):
        columns = pl.ds(pl.multiple_of(place_ref[j] * depth, depth), depth)
        part = dot_nt(mid[early:, : 2 * hidden_width], weights[j][:, : 2 * hidden_width])
        tail[:, columns] = part[main * blocks :]
        part = part.astype(BF16)
        for i in range(blocks):
            backs[i][:, columns] = part[main * i : main * (i + 1)]
    row = lax.broadcasted_iota(jnp.int32, (main, LANES), 0)
    lane = lax.broadcasted_iota(jnp.int32, (main, LANES), 1)
    for i in range(blocks):
        for c in range(chunks):
            fold[c : c + 1, :] = tail[i : i + 1, LANES * c : LANES * (c + 1)]
        backs[i][:chunks, width:] = fold[...].astype(BF16)
        mine = jnp.where(row == lane, route[main * i : main * (i + 1)], 0.0)
        mine = jnp.sum(mine, axis=0, keepdims=True)
        mine = jnp.where(lane[0:1] == main, route[main * blocks + i : main * blocks + i + 1], mine)
        backs[i][chunks:, width:] = jnp.broadcast_to(mine, (main - chunks, LANES)).astype(BF16)


def unpack_sum(weight, block_refs, rows, fold, order=(0, 1, 2, 3)):
    count = len(block_refs)
    main = block_refs[0].shape[0]
    width = rows.shape[1]
    chunks = width // LANES
    mains, tails = picks(weight, main)
    mains = [mains[e] for e in order]
    tails = jnp.concatenate([tails[e : e + 1, :] for e in order] + [jnp.zeros((16 - count, tails.shape[1]), F32)], axis=0)
    pick = jnp.concatenate(mains + [tails], axis=0).astype(BF16)
    lane = lax.broadcasted_iota(jnp.int32, (1, LANES), 1)
    routes = {}
    for j in range(count):
        rows[main * j : main * (j + 1), :] = block_refs[j][:, :width]
        fold[chunks * j : chunks * (j + 1), :] = block_refs[j][:chunks, width:].astype(F32)
        mine = block_refs[j][chunks:, width:].astype(F32)
        dense = dot(mine[:, :main].astype(BF16), mains[j].astype(BF16))[0:1, :]
        last = jnp.sum(jnp.where(lane == main, mine[0:1, :], 0.0), axis=1, keepdims=True)
        routes[order[j]] = dense + last * tails[j : j + 1, :]
    for c in range(chunks):
        tail = fold[pl.ds(c, count, stride=chunks), :]
        tail = jnp.concatenate([tail, jnp.zeros((16 - count, LANES), F32)], axis=0).astype(BF16)
        rows[main * count :, LANES * c : LANES * (c + 1)] = tail
    return dot_tn(pick, rows[...]), [routes[e] for e in range(count)]


def relay_sum_kernel(joint_ref, b0, b3, b2, b1, out_ref, rows, fold):
    tokens, width = joint_ref.shape[0], rows.shape[1]
    weight = joint_ref[0:16, 2 * width :].astype(F32)[0:8, :tokens]
    summed, routes = unpack_sum(weight, (b0, b3, b2, b1), rows, fold, (0, 3, 2, 1))
    lines = tokens // 2
    out_ref[:, :width] = summed[0:lines].astype(BF16)
    out_ref[:, width : 2 * width] = summed[lines:].astype(BF16)
    out_ref[:, 2 * width :] = jnp.zeros((lines, LANES), BF16)
    block = jnp.concatenate(routes + [jnp.zeros((12, tokens), F32)], axis=0).astype(BF16)
    out_ref[0:16, 2 * width : 2 * width + tokens] = block


def combine_kernel(peer_ref, named_ref, w_ref, b0, b3, b2, b1, far_ref, *refs):
    grad_ref, route_ref, in_ref, out_ref, held, rows, fold, lines_ref, sem = refs[5:]
    tokens, width = held.shape
    summed, routes = unpack_sum(w_ref[...], (b0, b3, b2, b1), rows, fold, (0, 3, 2, 1))
    lines = tokens // 2
    for half in range(2):
        at, columns = slice(half * lines, (half + 1) * lines), slice(half * width, (half + 1) * width)
        held[at, :] = (summed[at, :] + far_ref[:, columns].astype(F32)).astype(BF16)
    copy = start(held, grad_ref, sem)
    others = far_ref[0:16, 2 * width : 2 * width + tokens].astype(F32)
    named = named_ref[...]
    route = jnp.zeros(route_ref.shape, F32)
    for j in range(4):
        route = route + jnp.where(named == peer_ref[j], routes[j], 0.0)
        route = route + jnp.where(named == peer_ref[4 + j], others[j : j + 1, :], 0.0)
    route_ref[...] = route.astype(BF16)
    second_weight_part(*refs[:5], in_ref, out_ref, lines_ref)
    copy.wait()


def fill(rows, mids, rows_a, rows_b, rows_c, mid_a, mid_b):
    count = rows_a.shape[0]
    rows[0:count, :] = rows_a
    rows[count : 2 * count, :] = rows_b
    rows[2 * count :, :] = rows_c
    mids[0 : 2 * count, :] = mid_a
    mids[2 * count :, :] = mid_b


def first_weight_kernel(rows_a, rows_b, near_ref, mid_ref, in_ref, out_ref, rows, mids):
    depth, hidden_width = out_ref.shape
    near, near_mid = near_ref[:, : 2 * depth], near_ref[:, 4 * depth :]
    fill(rows, mids, rows_a[...], rows_b[...], near, mid_ref[...], near_mid)
    in_ref[...] = dot_tn(rows[:, :depth], mids[:, : 2 * hidden_width])
    out_ref[...] = dot_tn(rows[:, depth:], mids[:, 2 * hidden_width :])


def second_weight_part(rows_a, rows_b, mid_ref, in_part, out_part, in_ref, out_ref, rows):
    depth, hidden_width = out_ref.shape
    count = rows_a.shape[0]
    rows[0:count, :] = rows_a[:, : 2 * depth]
    rows[count:, :] = rows_b[:, : 2 * depth]
    in_ref[...] = in_part[...] + dot_tn(rows[:, :depth], mid_ref[:, : 2 * hidden_width])
    out_ref[...] = out_part[...] + dot_tn(rows[:, depth:], mid_ref[:, 2 * hidden_width :])


def last_weight_kernel(near_ref, mid_ref, in_part, out_part, in_ref, out_ref, in_held, out_held, sems):
    depth, hidden_width = out_part.shape
    copies = []
    step = depth // 4
    for m in range(4):
        at = slice(m * step, (m + 1) * step)
        lines = pl.ds(m * step, step)
        base = 2 * depth + m * step
        in_held[at, :] = in_part[at, :] + dot_tn(near_ref[:, base : base + step], mid_ref[:, : 2 * hidden_width])
        copies.append(start(in_held.at[lines], in_ref.at[lines], sems.at[0, m]))
        base += depth
        out_held[at, :] = out_part[at, :] + dot_tn(near_ref[:, base : base + step], mid_ref[:, 2 * hidden_width :])
        copies.append(start(out_held.at[lines], out_ref.at[lines], sems.at[1, m]))
    for copy in copies:
        copy.wait()


def call(kernel, outs, smem, vmem, either, scratch, flops, either_outs=0, aliases=None):
    on_vmem = pl.BlockSpec(memory_space=pltpu.VMEM)
    on_either = pl.BlockSpec(memory_space=pl.ANY)
    on_smem = pl.BlockSpec(memory_space=pltpu.SMEM)
    outs = [jax.ShapeDtypeStruct(shape, kind) for shape, kind in outs]
    moved = sum(a.size * a.dtype.itemsize for a in list(vmem) + outs[either_outs:])
    return pl.pallas_call(
        kernel,
        out_shape=tuple(outs),
        in_specs=[on_smem] * len(smem) + [on_vmem] * len(vmem) + [on_either] * len(either),
        out_specs=tuple([on_either] * either_outs + [on_vmem] * (len(outs) - either_outs)),
        scratch_shapes=scratch,
        compiler_params=pltpu.CompilerParams(vmem_limit_bytes=16 * 1024 * 1024),
        cost_estimate=pl.CostEstimate(flops=flops, bytes_accessed=moved, transcendentals=0),
        input_output_aliases=aliases or {},
    )(*smem, *vmem, *either)


def swap(value, axis, mask):
    return lax.ppermute(value, axis, [(i, i ^ mask) for i in range(lax.axis_size(axis))])


def on_device_packed(tokens, grad_out, route_expert, route_weight, gate_up_weight, down_weight):
    token_count, width = tokens.shape
    blocks, parts, half = 8, 4, 4
    hidden_width = down_weight.shape[2]
    depth = width // parts
    chunks = width // LANES
    main = block_rows(token_count, route_expert.shape[1], blocks) // 16 * 16
    rows = main * half + 16

    peers = lax.axis_index("expert") ^ jnp.arange(blocks, dtype=jnp.int32)
    places = lax.axis_index("dp") ^ jnp.arange(parts, dtype=jnp.int32)
    named = route_expert.T
    packed_shape = ((2 * main, width + LANES), BF16)
    back_shape = ((main, width + LANES), BF16)

    joint, dense = call(
        route_kernel,
        [((token_count, 2 * width + LANES), BF16), ((blocks, token_count), F32)],
        [peers],
        [named, route_weight.T, tokens, grad_out],
        [],
        [],
        0,
    )
    far_joint = swap(joint, "expert", half)

    weights = jnp.concatenate([gate_up_weight[0], down_weight[0]], axis=1)
    far_weights = swap(weights, "dp", 2)

    def pack(experts, value, after):
        return call(
            functools.partial(pack_kernel, experts),
            [packed_shape] * len(experts),
            [],
            [value],
            after,
            [pltpu.VMEM((chunks, LANES), F32)],
            4 * (len(experts) * main + 16) * token_count * width,
        )

    def sliced(own, packed, after):
        return call(
            functools.partial(slice_kernel, own),
            [
                ((rows, 2 * depth), BF16),
                ((rows, 2 * depth), BF16),
                ((rows, 4 * depth), BF16),
                ((rows, LANES), F32),
            ],
            [places],
            packed,
            after,
            [pltpu.VMEM((2, half * chunks, LANES), F32), pltpu.VMEM(*packed_shape)],
            0,
        )

    own = [swap(value, "expert", j + 1) for j, value in enumerate(pack(range(half + 1, blocks), joint, []))]
    *own_slices, own_weight = sliced(half, [joint, *own[::-1]], [far_joint])
    own_far = swap(own_slices[2], "dp", 2)
    far = pack(range(half), far_joint, [own_slices[0], far_weights])
    far = [far[0]] + [swap(far[j], "expert", j) for j in range(1, half)]
    (stacked,) = call(
        stack_kernel,
        [((2 * depth, 3 * hidden_width), BF16)],
        [],
        [weights, far_weights],
        [far[0]],
        [],
        0,
    )
    weight_parts = [stacked, swap(stacked, "dp", 1)]

    def middle(slices, weight, before, after):
        early = before[0].shape[0] if before else 0
        return call(
            functools.partial(main_kernel, early),
            [((early + rows, 3 * hidden_width), BF16)] + [back_shape] * half,
            [places],
            [weight, *weight_parts, *slices, *before],
            after,
            [pltpu.VMEM((16, width), F32), pltpu.VMEM((chunks, LANES), F32)],
            2 * rows * width * 5 * hidden_width,
        )

    own_mid, *near_back = middle(own_slices, own_weight, [], [])
    near_back = [near_back[0], *near_back[:0:-1]]
    near_back = near_back[:1] + [swap(near_back[j], "expert", j) for j in range(1, half)]
    *far_slices, far_weight = sliced(None, [far[0], *far[:0:-1]], [own_mid, own_far])
    far_far = swap(far_slices[2], "dp", 2)
    mid, *far_back = middle(far_slices, far_weight, [own_mid], [])

    sum_scratch = [
        pltpu.VMEM((half * main + 16, width), BF16),
        pltpu.VMEM((half * chunks, LANES), F32),
    ]
    sum_flops = 2 * (half * main + 16) * width * token_count
    far_back = [far_back[0], *far_back[:0:-1]]
    far_back = far_back[:1] + [swap(far_back[j], "expert", j) for j in range(1, half)]
    (partial,) = call(
        relay_sum_kernel,
        [((token_count // 2, 2 * width + LANES), BF16)],
        [],
        [far_joint, far_back[0], *far_back[:0:-1]],
        [],
        sum_scratch,
        sum_flops,
    )
    far_partial = swap(partial, "expert", half)

    mid_far = swap(mid, "dp", 2)
    (near,) = call(
        relay_kernel,
        [((2 * rows, 4 * depth + 3 * hidden_width), BF16)],
        [],
        [own_slices[1], own_far, far_slices[1], far_far, mid],
        [partial],
        [],
        0,
    )
    near = swap(near, "dp", 1)
    weight_shapes = [((depth, 2 * hidden_width), F32), ((depth, hidden_width), F32)]
    weight_scratch = [pltpu.VMEM((4 * rows, 2 * depth), BF16), pltpu.VMEM((4 * rows, 3 * hidden_width), BF16)]
    weight_flops = 2 * 4 * rows * depth * 3 * hidden_width
    first = call(
        first_weight_kernel,
        weight_shapes,
        [],
        [own_slices[0], far_slices[0], near, mid],
        [],
        weight_scratch,
        weight_flops,
    )
    (mid_far,) = call(
        after_kernel,
        [(mid_far.shape, BF16)],
        [],
        [],
        [mid_far, first[1], far_partial, *near_back[:0:-1]],
        [],
        0,
        1,
        {0: 0},
    )
    grad_tokens, grad_route, *second = call(
        combine_kernel,
        [((token_count, width), BF16), (named.shape, BF16), *weight_shapes],
        [peers],
        [named, dense, near_back[0], *near_back[:0:-1], far_partial, own_far, far_far, mid_far, *first],
        [],
        [
            pltpu.VMEM((token_count, width), BF16),
            *sum_scratch,
            pltpu.VMEM((2 * rows, 2 * depth), BF16),
            pltpu.SemaphoreType.DMA,
        ],
        sum_flops + weight_flops // 2,
        1,
    )
    grad_gate_up, grad_down = call(
        last_weight_kernel,
        weight_shapes,
        [],
        [near, swap(mid_far, "dp", 1), *second],
        [],
        [
            pltpu.VMEM((depth, 2 * hidden_width), F32),
            pltpu.VMEM((depth, hidden_width), F32),
            pltpu.SemaphoreType.DMA((2, 4)),
        ],
        weight_flops // 2,
        2,
    )
    return (grad_tokens, grad_route.T, grad_gate_up[None], grad_down[None])


def block_rows(token_count, route_count, expert_total):
    return min(token_count, (token_count * route_count + expert_total - 1) // expert_total + 1)


def to_local(rows, group_count, local_count, capacity):
    tail = rows.shape[2:]
    shaped = rows.reshape((group_count, local_count, capacity) + tail)
    shaped = jnp.swapaxes(shaped, 0, 1)
    return shaped.reshape((local_count, group_count * capacity) + tail)


def to_groups(rows, group_count, local_count, capacity):
    tail = rows.shape[2:]
    shaped = rows.reshape((local_count, group_count, capacity) + tail)
    shaped = jnp.swapaxes(shaped, 0, 1)
    return shaped.reshape((group_count, local_count * capacity) + tail)


def on_device_routed(tokens, grad_out, route_expert, route_weight, gate_up_weight, down_weight):
    token_count, model_width = tokens.shape
    route_count = route_expert.shape[1]
    group_count = lax.axis_size("expert")
    local_count = gate_up_weight.shape[0]
    hidden_width = down_weight.shape[2]
    expert_total = local_count * group_count
    capacity = min(token_count, (token_count * route_count + expert_total - 1) // expert_total + 1)
    slot_total = expert_total * capacity
    flat_expert = route_expert.reshape(-1)
    expert_ids = jnp.arange(expert_total, dtype=jnp.int32)
    onehot = (flat_expert[:, None] == expert_ids[None, :]).astype(jnp.int32)
    before = jnp.cumsum(onehot, axis=0) - onehot
    rank = jnp.sum(before * onehot, axis=1)
    slot_of = flat_expert * capacity + rank
    slot_ids = jnp.arange(slot_total, dtype=jnp.int32)
    placed = slot_ids[:, None] == slot_of[None, :]
    by_token = jnp.any(placed.reshape(slot_total, token_count, route_count), axis=2).astype(
        jnp.bfloat16
    )
    send_x = jnp.dot(by_token, tokens, preferred_element_type=jnp.float32).astype(jnp.bfloat16)
    send_dy = jnp.dot(by_token, grad_out, preferred_element_type=jnp.float32).astype(jnp.bfloat16)
    flat_weight = route_weight.reshape(-1).astype(jnp.float32)
    send_w = jnp.sum(jnp.where(placed, flat_weight[None, :], 0.0), axis=1).astype(jnp.bfloat16)
    recv_x, recv_dy, recv_w = (
        lax.all_to_all(
            send_x.reshape(group_count, local_count * capacity, model_width),
            "expert",
            split_axis=0,
            concat_axis=0,
            tiled=True,
        ),
        lax.all_to_all(
            send_dy.reshape(group_count, local_count * capacity, model_width),
            "expert",
            split_axis=0,
            concat_axis=0,
            tiled=True,
        ),
        lax.all_to_all(
            send_w.reshape(group_count, local_count * capacity),
            "expert",
            split_axis=0,
            concat_axis=0,
            tiled=True,
        ),
    )
    rows_x = to_local(recv_x, group_count, local_count, capacity)
    rows_dy = to_local(recv_dy, group_count, local_count, capacity)
    rows_w = to_local(recv_w, group_count, local_count, capacity)
    full_in, full_out = (
        lax.all_gather(gate_up_weight, "dp", axis=1, tiled=True),
        lax.all_gather(down_weight, "dp", axis=1, tiled=True),
    )
    pre = jnp.einsum("erd,edf->erf", rows_x, full_in, preferred_element_type=jnp.float32)
    gate_pre = pre[:, :, :hidden_width]
    up_pre = pre[:, :, hidden_width:]
    act = swish(gate_pre)
    hidden = (act * up_pre).astype(jnp.bfloat16)
    expert_out = jnp.einsum("erf,edf->erd", hidden, full_out, preferred_element_type=jnp.float32)
    route_grad = jnp.sum(rows_dy.astype(jnp.float32) * expert_out, axis=2).astype(jnp.bfloat16)
    scaled = (rows_w.astype(jnp.float32)[:, :, None] * rows_dy).astype(jnp.bfloat16)
    grad_hidden = jnp.einsum("erd,edf->erf", scaled, full_out, preferred_element_type=jnp.float32)
    sig = jax.nn.sigmoid(gate_pre)
    grad_gate = grad_hidden * up_pre * sig * (1.0 + gate_pre * (1.0 - sig))
    grad_up = grad_hidden * act
    grad_pre = jnp.concatenate([grad_gate, grad_up], axis=2).astype(jnp.bfloat16)
    rows_grad = jnp.einsum(
        "erf,edf->erd", grad_pre, full_in, preferred_element_type=jnp.float32
    ).astype(jnp.bfloat16)
    back_x, back_w = (
        lax.all_to_all(
            to_groups(rows_grad, group_count, local_count, capacity),
            "expert",
            split_axis=0,
            concat_axis=0,
            tiled=True,
        ),
        lax.all_to_all(
            to_groups(route_grad, group_count, local_count, capacity),
            "expert",
            split_axis=0,
            concat_axis=0,
            tiled=True,
        ),
    )
    back_x = back_x.reshape(slot_total, model_width)
    back_w = back_w.reshape(slot_total).astype(jnp.float32)
    grad_tokens = jnp.einsum(
        "st,sd->td", by_token, back_x, preferred_element_type=jnp.float32
    ).astype(jnp.bfloat16)
    grad_route = jnp.sum(jnp.where(placed, back_w[:, None], 0.0), axis=0)
    grad_route = grad_route.reshape(token_count, route_count).astype(jnp.bfloat16)
    all_x = lax.all_to_all(rows_x, "dp", split_axis=2, concat_axis=1, tiled=True)
    grad_gate_up = jnp.einsum(
        "erd,erf->edf",
        all_x,
        lax.all_gather(grad_pre, "dp", axis=1, tiled=True),
        preferred_element_type=jnp.float32,
    )
    summed = lax.psum_scatter(
        jnp.einsum("erd,erf->def", scaled, hidden, preferred_element_type=jnp.float32),
        "dp",
        scatter_dimension=0,
        tiled=True,
    )
    grad_down = jnp.swapaxes(summed, 0, 1)
    return (grad_tokens, grad_route, grad_gate_up, grad_down)


def packs(tokens, route_expert, down_weight):
    chunks = tokens.shape[1] // LANES
    capacity = block_rows(tokens.shape[0], route_expert.shape[1], lax.axis_size("expert"))
    return (
        lax.axis_size("expert") == 8
        and lax.axis_size("dp") == 4
        and down_weight.shape[0] == 1
        and capacity % 16 <= 1
        and chunks == 16
        and 2 * chunks <= capacity < LANES // 2
    )


def solution(mesh):
    def on_device(*arrays):
        if packs(arrays[0], arrays[2], arrays[5]):
            return on_device_packed(*arrays)
        return on_device_routed(*arrays)

    return jax.shard_map(
        on_device,
        mesh=mesh,
        in_specs=(
            P(("expert", "dp"), None),
            P(("expert", "dp"), None),
            P(("expert", "dp"), None),
            P(("expert", "dp"), None),
            P("expert", "dp", None),
            P("expert", "dp", None),
        ),
        out_specs=(
            P(("expert", "dp"), None),
            P(("expert", "dp"), None),
            P("expert", "dp", None),
            P("expert", "dp", None),
        ),
        check_vma=False,
    )
```

```python
import functools

import jax
import jax.numpy as jnp
from jax import lax
from jax.experimental import pallas as pl
from jax.experimental.pallas import tpu as pltpu
from jax.sharding import PartitionSpec as P

BF16 = jnp.bfloat16
F32 = jnp.float32
LANES = 128


def swish(value):
    return value * jax.nn.sigmoid(value)


def dot(a, b):
    return jnp.dot(a, b, preferred_element_type=F32)


def dot_nt(a, b):
    return lax.dot_general(a, b, (((1,), (1,)), ((), ())), preferred_element_type=F32)


def dot_tn(a, b):
    return lax.dot_general(a, b, (((0,), (0,)), ((), ())), preferred_element_type=F32)


def start(source, target, sem):
    copy = pltpu.make_async_copy(source, target, sem)
    copy.start()
    return copy


def picks(weight, main):
    token_count = weight.shape[1]
    routed = weight != 0.0
    first = lax.broadcasted_iota(jnp.int32, (token_count, token_count), 0)
    second = lax.broadcasted_iota(jnp.int32, (token_count, token_count), 1)
    upper = (first < second).astype(F32).astype(BF16)
    rank = dot(routed.astype(F32).astype(BF16), upper)
    rank = jnp.where(routed, rank, -1.0).astype(jnp.int32)
    slots = lax.broadcasted_iota(jnp.int32, (main, token_count), 0)
    mains = [(slots == rank[i : i + 1, :]).astype(F32) for i in range(weight.shape[0])]
    tails = (rank == main).astype(F32)
    return mains, tails


def route_kernel(peer_ref, named_ref, given_ref, x_ref, dy_ref, joint_ref, dense_ref):
    count, width = x_ref.shape
    named = named_ref[...]
    given = given_ref[...].astype(F32)
    experts = dense_ref.shape[0]
    lines = [
        jnp.sum(jnp.where(named == peer_ref[i], given, 0.0), axis=0, keepdims=True) for i in range(experts)
    ]
    dense = jnp.concatenate(lines, axis=0)
    dense_ref[...] = dense
    turned = jnp.concatenate(lines[experts // 2 :] + lines[: experts // 2] + [jnp.zeros_like(dense)], axis=0)
    joint_ref[:, :width] = x_ref[...]
    joint_ref[:, width : 2 * width] = dy_ref[...]
    joint_ref[:, 2 * width :] = jnp.zeros((count, LANES), BF16)
    joint_ref[0:16, 2 * width : 2 * width + count] = turned.astype(BF16)


def stack_kernel(own_ref, far_ref, after_ref, stacked_ref):
    count = own_ref.shape[0]
    stacked_ref[0:count, :] = own_ref[...]
    stacked_ref[count:, :] = far_ref[...]


def after_kernel(*refs):
    pass


def relay_kernel(near_a, far_a, near_b, far_b, mid_ref, *refs):
    joint_ref = refs[-1]
    count, width = near_a.shape
    for at, near, far in ((0, near_a, far_a), (count, near_b, far_b)):
        joint_ref[at : at + count, :width] = near[...]
        joint_ref[at : at + count, width : 2 * width] = far[:, width:]
    joint_ref[:, 2 * width :] = mid_ref[...]


def pack_blocks(experts, joint_ref, out_refs, fold):
    count = len(experts)
    tokens, width = joint_ref.shape[0], out_refs[0].shape[1] - LANES
    chunks = width // LANES
    main = out_refs[0].shape[0] // 2
    weight = joint_ref[0:16, 2 * width :].astype(F32)[0:8, :tokens]
    mains, tails = picks(weight, main)
    pick = jnp.concatenate([mains[e] for e in experts] + [tails, jnp.zeros_like(tails)], axis=0).astype(BF16)
    lane = lax.broadcasted_iota(jnp.int32, (main, LANES), 1)
    for at, base, low in ((0, 0, 0), (width, main, chunks)):
        rows = dot(pick, joint_ref[:, at : at + width])
        for j, e in enumerate(experts):
            out_refs[j][base : base + main, :width] = rows[main * j : main * (j + 1)].astype(BF16)
            line = main * count + e
            for c in range(chunks):
                fold[c : c + 1, :] = rows[line : line + 1, LANES * c : LANES * (c + 1)]
            out_refs[j][low : low + chunks, width:] = fold[...].astype(BF16)
    for j, e in enumerate(experts):
        mine = weight[e : e + 1, :]
        column = jnp.sum(mains[e] * mine, axis=1, keepdims=True)
        last = jnp.sum(tails[e : e + 1, :] * mine, axis=1, keepdims=True)
        out_refs[j][main:, width:] = jnp.where(lane < LANES // 2, column, last).astype(BF16)


def pack_kernel(experts, joint_ref, *refs):
    pack_blocks(experts, joint_ref, refs[-1 - len(experts) : -1], refs[-1])


def slice_kernel(own, place_ref, *refs):
    blocks, parts = 4, 4
    keep_ref, near_ref, far_ref, weight_ref, fold, kept = refs[-6:]
    in_refs = list(refs[:blocks])
    if own:
        in_refs[0] = kept
        pack_blocks([own], refs[0], [kept], fold.at[0, pl.ds(0, 16)])
    main = in_refs[0].shape[0] // 2
    depth = keep_ref.shape[1] // 2
    width = parts * depth
    chunks = width // LANES
    targets = [(keep_ref, 0), (near_ref, 0), (far_ref, 0), (far_ref, 2 * depth)]
    lane = lax.broadcasted_iota(jnp.int32, (1, LANES), 1)
    lasts = []
    for i in range(blocks):
        for j, (target, shift) in enumerate(targets):
            columns = pl.ds(pl.multiple_of(place_ref[j] * depth, depth), depth)
            for side in range(2):
                at = shift + side * depth
                target[main * i : main * (i + 1), at : at + depth] = in_refs[i][
                    side * main : (side + 1) * main, columns
                ]
        for side in range(2):
            fold[side, chunks * i : chunks * (i + 1), :] = in_refs[i][
                side * chunks : (side + 1) * chunks, width:
            ].astype(F32)
        weights = in_refs[i][main:, width:].astype(F32)
        weight_ref[main * i : main * (i + 1), :] = weights
        last = jnp.sum(jnp.where(lane == LANES - 1, weights[0:1, :], 0.0), axis=1, keepdims=True)
        lasts.append(jnp.broadcast_to(last, (1, LANES)))
    weight_ref[main * blocks :, :] = jnp.concatenate(lasts + [jnp.zeros((16 - blocks, LANES), F32)], axis=0)
    each = chunks // parts
    for j, (target, shift) in enumerate(targets):
        for side in range(2):
            for q in range(each):
                tail = fold[side, pl.ds(place_ref[j] * each + q, blocks, stride=chunks), :]
                tail = jnp.concatenate([tail, jnp.zeros((16 - blocks, LANES), F32)], axis=0).astype(BF16)
                at = shift + side * depth + q * LANES
                target[main * blocks :, at : at + LANES] = tail


def main_kernel(early, place_ref, w_ref, *refs):
    blocks, parts = 4, 4
    own_ref, other_ref = refs[:2]
    keep_ref, near_ref, far_ref = refs[2:5]
    mid, backs, (tail, fold) = refs[-3 - blocks], refs[-2 - blocks : -2], refs[-2:]
    depth = keep_ref.shape[1] // 2
    width = parts * depth
    hidden_width = mid.shape[1] // 3
    main = backs[0].shape[0]
    chunks = width // LANES
    total = keep_ref.shape[0]
    first, second = pl.ds(0, depth), pl.ds(depth, depth)
    weights = [own_ref.at[first], other_ref.at[first], own_ref.at[second], other_ref.at[second]]
    pre = jnp.zeros((total, 2 * hidden_width), F32)
    grad = jnp.zeros((total, hidden_width), F32)
    for j, (ref, shift) in enumerate([(keep_ref, 0), (near_ref, 0), (far_ref, 0), (far_ref, 2 * depth)]):
        pre += dot(ref[:, shift : shift + depth], weights[j][:, : 2 * hidden_width])
        grad += dot(ref[:, shift + depth : shift + 2 * depth], weights[j][:, 2 * hidden_width :])
    if early:
        mid[0:early, :] = refs[5][...]
    weight = w_ref[:, 0:1]
    gate_pre = pre[:, :hidden_width]
    up_pre = pre[:, hidden_width:]
    sig = jax.nn.sigmoid(gate_pre)
    act = gate_pre * sig
    hidden = (act * up_pre).astype(BF16).astype(F32)
    route = jnp.sum(hidden * grad, axis=1, keepdims=True)
    grad_hidden = weight * grad
    grad_gate = grad_hidden * up_pre * sig * (1.0 + gate_pre * (1.0 - sig))
    mid[early:, :hidden_width] = grad_gate.astype(BF16)
    mid[early:, hidden_width : 2 * hidden_width] = (grad_hidden * act).astype(BF16)
    mid[early:, 2 * hidden_width :] = (weight * hidden).astype(BF16)
    for j in range(parts):
        columns = pl.ds(pl.multiple_of(place_ref[j] * depth, depth), depth)
        part = dot_nt(mid[early:, : 2 * hidden_width], weights[j][:, : 2 * hidden_width])
        tail[:, columns] = part[main * blocks :]
        part = part.astype(BF16)
        for i in range(blocks):
            backs[i][:, columns] = part[main * i : main * (i + 1)]
    row = lax.broadcasted_iota(jnp.int32, (main, LANES), 0)
    lane = lax.broadcasted_iota(jnp.int32, (main, LANES), 1)
    for i in range(blocks):
        for c in range(chunks):
            fold[c : c + 1, :] = tail[i : i + 1, LANES * c : LANES * (c + 1)]
        backs[i][:chunks, width:] = fold[...].astype(BF16)
        mine = jnp.where(row == lane, route[main * i : main * (i + 1)], 0.0)
        mine = jnp.sum(mine, axis=0, keepdims=True)
        mine = jnp.where(lane[0:1] == main, route[main * blocks + i : main * blocks + i + 1], mine)
        backs[i][chunks:, width:] = jnp.broadcast_to(mine, (main - chunks, LANES)).astype(BF16)


def unpack_sum(weight, block_refs, rows, fold, order=(0, 1, 2, 3)):
    count = len(block_refs)
    main = block_refs[0].shape[0]
    width = rows.shape[1]
    chunks = width // LANES
    mains, tails = picks(weight, main)
    mains = [mains[e] for e in order]
    tails = jnp.concatenate([tails[e : e + 1, :] for e in order] + [jnp.zeros((16 - count, tails.shape[1]), F32)], axis=0)
    pick = jnp.concatenate(mains + [tails], axis=0).astype(BF16)
    lane = lax.broadcasted_iota(jnp.int32, (1, LANES), 1)
    routes = {}
    for j in range(count):
        rows[main * j : main * (j + 1), :] = block_refs[j][:, :width]
        fold[chunks * j : chunks * (j + 1), :] = block_refs[j][:chunks, width:].astype(F32)
        mine = block_refs[j][chunks:, width:].astype(F32)
        dense = dot(mine[:, :main].astype(BF16), mains[j].astype(BF16))[0:1, :]
        last = jnp.sum(jnp.where(lane == main, mine[0:1, :], 0.0), axis=1, keepdims=True)
        routes[order[j]] = dense + last * tails[j : j + 1, :]
    for c in range(chunks):
        tail = fold[pl.ds(c, count, stride=chunks), :]
        tail = jnp.concatenate([tail, jnp.zeros((16 - count, LANES), F32)], axis=0).astype(BF16)
        rows[main * count :, LANES * c : LANES * (c + 1)] = tail
    return dot_tn(pick, rows[...]), [routes[e] for e in range(count)]


def relay_sum_kernel(joint_ref, b0, b3, b2, b1, out_ref, rows, fold):
    tokens, width = joint_ref.shape[0], rows.shape[1]
    weight = joint_ref[0:16, 2 * width :].astype(F32)[0:8, :tokens]
    summed, routes = unpack_sum(weight, (b0, b3, b2, b1), rows, fold, (0, 3, 2, 1))
    lines = tokens // 2
    out_ref[:, :width] = summed[0:lines].astype(BF16)
    out_ref[:, width : 2 * width] = summed[lines:].astype(BF16)
    out_ref[:, 2 * width :] = jnp.zeros((lines, LANES), BF16)
    block = jnp.concatenate(routes + [jnp.zeros((12, tokens), F32)], axis=0).astype(BF16)
    out_ref[0:16, 2 * width : 2 * width + tokens] = block


def combine_kernel(peer_ref, named_ref, w_ref, b0, b3, b2, b1, far_ref, *refs):
    grad_ref, route_ref, in_ref, out_ref, held, rows, fold, lines_ref, sem = refs[5:]
    tokens, width = held.shape
    summed, routes = unpack_sum(w_ref[...], (b0, b3, b2, b1), rows, fold, (0, 3, 2, 1))
    lines = tokens // 2
    for half in range(2):
        at, columns = slice(half * lines, (half + 1) * lines), slice(half * width, (half + 1) * width)
        held[at, :] = (summed[at, :] + far_ref[:, columns].astype(F32)).astype(BF16)
    copy = start(held, grad_ref, sem)
    others = far_ref[0:16, 2 * width : 2 * width + tokens].astype(F32)
    named = named_ref[...]
    route = jnp.zeros(route_ref.shape, F32)
    for j in range(4):
        route = route + jnp.where(named == peer_ref[j], routes[j], 0.0)
        route = route + jnp.where(named == peer_ref[4 + j], others[j : j + 1, :], 0.0)
    route_ref[...] = route.astype(BF16)
    second_weight_part(*refs[:5], in_ref, out_ref, lines_ref)
    copy.wait()


def fill(rows, mids, rows_a, rows_b, rows_c, mid_a, mid_b):
    count = rows_a.shape[0]
    rows[0:count, :] = rows_a
    rows[count : 2 * count, :] = rows_b
    rows[2 * count :, :] = rows_c
    mids[0 : 2 * count, :] = mid_a
    mids[2 * count :, :] = mid_b


def first_weight_kernel(rows_a, rows_b, near_ref, mid_ref, in_ref, out_ref, rows, mids):
    depth, hidden_width = out_ref.shape
    near, near_mid = near_ref[:, : 2 * depth], near_ref[:, 4 * depth :]
    fill(rows, mids, rows_a[...], rows_b[...], near, mid_ref[...], near_mid)
    in_ref[...] = dot_tn(rows[:, :depth], mids[:, : 2 * hidden_width])
    out_ref[...] = dot_tn(rows[:, depth:], mids[:, 2 * hidden_width :])


def second_weight_part(rows_a, rows_b, mid_ref, in_part, out_part, in_ref, out_ref, rows):
    depth, hidden_width = out_ref.shape
    count = rows_a.shape[0]
    rows[0:count, :] = rows_a[:, : 2 * depth]
    rows[count:, :] = rows_b[:, : 2 * depth]
    in_ref[...] = in_part[...] + dot_tn(rows[:, :depth], mid_ref[:, : 2 * hidden_width])
    out_ref[...] = out_part[...] + dot_tn(rows[:, depth:], mid_ref[:, 2 * hidden_width :])


def last_weight_kernel(near_ref, mid_ref, in_part, out_part, in_ref, out_ref, in_held, out_held, sems):
    depth, hidden_width = out_part.shape
    copies = []
    step = depth // 4
    for m in range(4):
        at = slice(m * step, (m + 1) * step)
        lines = pl.ds(m * step, step)
        base = 2 * depth + m * step
        in_held[at, :] = in_part[at, :] + dot_tn(near_ref[:, base : base + step], mid_ref[:, : 2 * hidden_width])
        copies.append(start(in_held.at[lines], in_ref.at[lines], sems.at[0, m]))
        base += depth
        out_held[at, :] = out_part[at, :] + dot_tn(near_ref[:, base : base + step], mid_ref[:, 2 * hidden_width :])
        copies.append(start(out_held.at[lines], out_ref.at[lines], sems.at[1, m]))
    for copy in copies:
        copy.wait()


def call(kernel, outs, smem, vmem, either, scratch, flops, either_outs=0, aliases=None):
    on_vmem = pl.BlockSpec(memory_space=pltpu.VMEM)
    on_either = pl.BlockSpec(memory_space=pl.ANY)
    on_smem = pl.BlockSpec(memory_space=pltpu.SMEM)
    outs = [jax.ShapeDtypeStruct(shape, kind) for shape, kind in outs]
    moved = sum(a.size * a.dtype.itemsize for a in list(vmem) + outs[either_outs:])
    return pl.pallas_call(
        kernel,
        out_shape=tuple(outs),
        in_specs=[on_smem] * len(smem) + [on_vmem] * len(vmem) + [on_either] * len(either),
        out_specs=tuple([on_either] * either_outs + [on_vmem] * (len(outs) - either_outs)),
        scratch_shapes=scratch,
        compiler_params=pltpu.CompilerParams(vmem_limit_bytes=16 * 1024 * 1024),
        cost_estimate=pl.CostEstimate(flops=flops, bytes_accessed=moved, transcendentals=0),
        input_output_aliases=aliases or {},
    )(*smem, *vmem, *either)


def swap(value, axis, mask):
    return lax.ppermute(value, axis, [(i, i ^ mask) for i in range(lax.axis_size(axis))])


def on_device_packed(tokens, grad_out, route_expert, route_weight, gate_up_weight, down_weight):
    token_count, width = tokens.shape
    blocks, parts, half = 8, 4, 4
    hidden_width = down_weight.shape[2]
    depth = width // parts
    chunks = width // LANES
    main = block_rows(token_count, route_expert.shape[1], blocks) // 16 * 16
    rows = main * half + 16

    peers = lax.axis_index("expert") ^ jnp.arange(blocks, dtype=jnp.int32)
    places = lax.axis_index("dp") ^ jnp.arange(parts, dtype=jnp.int32)
    named = route_expert.T
    packed_shape = ((2 * main, width + LANES), BF16)
    back_shape = ((main, width + LANES), BF16)

    joint, dense = call(
        route_kernel,
        [((token_count, 2 * width + LANES), BF16), ((blocks, token_count), F32)],
        [peers],
        [named, route_weight.T, tokens, grad_out],
        [],
        [],
        0,
    )
    far_joint = swap(joint, "expert", half)

    weights = jnp.concatenate([gate_up_weight[0], down_weight[0]], axis=1)
    far_weights = swap(weights, "dp", 2)

    def pack(experts, value, after):
        return call(
            functools.partial(pack_kernel, experts),
            [packed_shape] * len(experts),
            [],
            [value],
            after,
            [pltpu.VMEM((chunks, LANES), F32)],
            4 * (len(experts) * main + 16) * token_count * width,
        )

    def sliced(own, packed, after):
        return call(
            functools.partial(slice_kernel, own),
            [
                ((rows, 2 * depth), BF16),
                ((rows, 2 * depth), BF16),
                ((rows, 4 * depth), BF16),
                ((rows, LANES), F32),
            ],
            [places],
            packed,
            after,
            [pltpu.VMEM((2, half * chunks, LANES), F32), pltpu.VMEM(*packed_shape)],
            0,
        )

    own = [swap(value, "expert", j + 1) for j, value in enumerate(pack(range(half + 1, blocks), joint, []))]
    (kept,) = pack([half], joint, [own[2]])
    *own_slices, own_weight = sliced(None, [kept, *own[::-1]], [far_joint])
    own_far = swap(own_slices[2], "dp", 2)
    far = pack(range(half), far_joint, [own_slices[0], far_weights])
    far = [far[0]] + [swap(far[j], "expert", j) for j in range(1, half)]
    (stacked,) = call(
        stack_kernel,
        [((2 * depth, 3 * hidden_width), BF16)],
        [],
        [weights, far_weights],
        [far[0]],
        [],
        0,
    )
    weight_parts = [stacked, swap(stacked, "dp", 1)]

    def middle(slices, weight, before, after):
        early = before[0].shape[0] if before else 0
        return call(
            functools.partial(main_kernel, early),
            [((early + rows, 3 * hidden_width), BF16)] + [back_shape] * half,
            [places],
            [weight, *weight_parts, *slices, *before],
            after,
            [pltpu.VMEM((16, width), F32), pltpu.VMEM((chunks, LANES), F32)],
            2 * rows * width * 5 * hidden_width,
        )

    own_mid, *near_back = middle(own_slices, own_weight, [], [])
    near_back = [near_back[0], *near_back[:0:-1]]
    near_back = near_back[:1] + [swap(near_back[j], "expert", j) for j in range(1, half)]
    *far_slices, far_weight = sliced(None, [far[0], *far[:0:-1]], [own_mid, own_far])
    far_far = swap(far_slices[2], "dp", 2)
    mid, *far_back = middle(far_slices, far_weight, [own_mid], [])

    sum_scratch = [
        pltpu.VMEM((half * main + 16, width), BF16),
        pltpu.VMEM((half * chunks, LANES), F32),
    ]
    sum_flops = 2 * (half * main + 16) * width * token_count
    far_back = [far_back[0], *far_back[:0:-1]]
    far_back = far_back[:1] + [swap(far_back[j], "expert", j) for j in range(1, half)]
    (partial,) = call(
        relay_sum_kernel,
        [((token_count // 2, 2 * width + LANES), BF16)],
        [],
        [far_joint, far_back[0], *far_back[:0:-1]],
        [],
        sum_scratch,
        sum_flops,
    )
    far_partial = swap(partial, "expert", half)

    mid_far = swap(mid, "dp", 2)
    (near,) = call(
        relay_kernel,
        [((2 * rows, 4 * depth + 3 * hidden_width), BF16)],
        [],
        [own_slices[1], own_far, far_slices[1], far_far, mid],
        [partial],
        [],
        0,
    )
    near = swap(near, "dp", 1)
    weight_shapes = [((depth, 2 * hidden_width), F32), ((depth, hidden_width), F32)]
    weight_scratch = [pltpu.VMEM((4 * rows, 2 * depth), BF16), pltpu.VMEM((4 * rows, 3 * hidden_width), BF16)]
    weight_flops = 2 * 4 * rows * depth * 3 * hidden_width
    first = call(
        first_weight_kernel,
        weight_shapes,
        [],
        [own_slices[0], far_slices[0], near, mid],
        [],
        weight_scratch,
        weight_flops,
    )
    (mid_far,) = call(
        after_kernel,
        [(mid_far.shape, BF16)],
        [],
        [],
        [mid_far, first[1], far_partial, *near_back[:0:-1]],
        [],
        0,
        1,
        {0: 0},
    )
    grad_tokens, grad_route, *second = call(
        combine_kernel,
        [((token_count, width), BF16), (named.shape, BF16), *weight_shapes],
        [peers],
        [named, dense, near_back[0], *near_back[:0:-1], far_partial, own_far, far_far, mid_far, *first],
        [],
        [
            pltpu.VMEM((token_count, width), BF16),
            *sum_scratch,
            pltpu.VMEM((2 * rows, 2 * depth), BF16),
            pltpu.SemaphoreType.DMA,
        ],
        sum_flops + weight_flops // 2,
        1,
    )
    grad_gate_up, grad_down = call(
        last_weight_kernel,
        weight_shapes,
        [],
        [near, swap(mid_far, "dp", 1), *second],
        [],
        [
            pltpu.VMEM((depth, 2 * hidden_width), F32),
            pltpu.VMEM((depth, hidden_width), F32),
            pltpu.SemaphoreType.DMA((2, 4)),
        ],
        weight_flops // 2,
        2,
    )
    return (grad_tokens, grad_route.T, grad_gate_up[None], grad_down[None])


def block_rows(token_count, route_count, expert_total):
    return min(token_count, (token_count * route_count + expert_total - 1) // expert_total + 1)


def to_local(rows, group_count, local_count, capacity):
    tail = rows.shape[2:]
    shaped = rows.reshape((group_count, local_count, capacity) + tail)
    shaped = jnp.swapaxes(shaped, 0, 1)
    return shaped.reshape((local_count, group_count * capacity) + tail)


def to_groups(rows, group_count, local_count, capacity):
    tail = rows.shape[2:]
    shaped = rows.reshape((local_count, group_count, capacity) + tail)
    shaped = jnp.swapaxes(shaped, 0, 1)
    return shaped.reshape((group_count, local_count * capacity) + tail)


def on_device_routed(tokens, grad_out, route_expert, route_weight, gate_up_weight, down_weight):
    token_count, model_width = tokens.shape
    route_count = route_expert.shape[1]
    group_count = lax.axis_size("expert")
    local_count = gate_up_weight.shape[0]
    hidden_width = down_weight.shape[2]
    expert_total = local_count * group_count
    capacity = min(token_count, (token_count * route_count + expert_total - 1) // expert_total + 1)
    slot_total = expert_total * capacity
    flat_expert = route_expert.reshape(-1)
    expert_ids = jnp.arange(expert_total, dtype=jnp.int32)
    onehot = (flat_expert[:, None] == expert_ids[None, :]).astype(jnp.int32)
    before = jnp.cumsum(onehot, axis=0) - onehot
    rank = jnp.sum(before * onehot, axis=1)
    slot_of = flat_expert * capacity + rank
    slot_ids = jnp.arange(slot_total, dtype=jnp.int32)
    placed = slot_ids[:, None] == slot_of[None, :]
    by_token = jnp.any(placed.reshape(slot_total, token_count, route_count), axis=2).astype(
        jnp.bfloat16
    )
    send_x = jnp.dot(by_token, tokens, preferred_element_type=jnp.float32).astype(jnp.bfloat16)
    send_dy = jnp.dot(by_token, grad_out, preferred_element_type=jnp.float32).astype(jnp.bfloat16)
    flat_weight = route_weight.reshape(-1).astype(jnp.float32)
    send_w = jnp.sum(jnp.where(placed, flat_weight[None, :], 0.0), axis=1).astype(jnp.bfloat16)
    recv_x, recv_dy, recv_w = (
        lax.all_to_all(
            send_x.reshape(group_count, local_count * capacity, model_width),
            "expert",
            split_axis=0,
            concat_axis=0,
            tiled=True,
        ),
        lax.all_to_all(
            send_dy.reshape(group_count, local_count * capacity, model_width),
            "expert",
            split_axis=0,
            concat_axis=0,
            tiled=True,
        ),
        lax.all_to_all(
            send_w.reshape(group_count, local_count * capacity),
            "expert",
            split_axis=0,
            concat_axis=0,
            tiled=True,
        ),
    )
    rows_x = to_local(recv_x, group_count, local_count, capacity)
    rows_dy = to_local(recv_dy, group_count, local_count, capacity)
    rows_w = to_local(recv_w, group_count, local_count, capacity)
    full_in, full_out = (
        lax.all_gather(gate_up_weight, "dp", axis=1, tiled=True),
        lax.all_gather(down_weight, "dp", axis=1, tiled=True),
    )
    pre = jnp.einsum("erd,edf->erf", rows_x, full_in, preferred_element_type=jnp.float32)
    gate_pre = pre[:, :, :hidden_width]
    up_pre = pre[:, :, hidden_width:]
    act = swish(gate_pre)
    hidden = (act * up_pre).astype(jnp.bfloat16)
    expert_out = jnp.einsum("erf,edf->erd", hidden, full_out, preferred_element_type=jnp.float32)
    route_grad = jnp.sum(rows_dy.astype(jnp.float32) * expert_out, axis=2).astype(jnp.bfloat16)
    scaled = (rows_w.astype(jnp.float32)[:, :, None] * rows_dy).astype(jnp.bfloat16)
    grad_hidden = jnp.einsum("erd,edf->erf", scaled, full_out, preferred_element_type=jnp.float32)
    sig = jax.nn.sigmoid(gate_pre)
    grad_gate = grad_hidden * up_pre * sig * (1.0 + gate_pre * (1.0 - sig))
    grad_up = grad_hidden * act
    grad_pre = jnp.concatenate([grad_gate, grad_up], axis=2).astype(jnp.bfloat16)
    rows_grad = jnp.einsum(
        "erf,edf->erd", grad_pre, full_in, preferred_element_type=jnp.float32
    ).astype(jnp.bfloat16)
    back_x, back_w = (
        lax.all_to_all(
            to_groups(rows_grad, group_count, local_count, capacity),
            "expert",
            split_axis=0,
            concat_axis=0,
            tiled=True,
        ),
        lax.all_to_all(
            to_groups(route_grad, group_count, local_count, capacity),
            "expert",
            split_axis=0,
            concat_axis=0,
            tiled=True,
        ),
    )
    back_x = back_x.reshape(slot_total, model_width)
    back_w = back_w.reshape(slot_total).astype(jnp.float32)
    grad_tokens = jnp.einsum(
        "st,sd->td", by_token, back_x, preferred_element_type=jnp.float32
    ).astype(jnp.bfloat16)
    grad_route = jnp.sum(jnp.where(placed, back_w[:, None], 0.0), axis=0)
    grad_route = grad_route.reshape(token_count, route_count).astype(jnp.bfloat16)
    all_x = lax.all_to_all(rows_x, "dp", split_axis=2, concat_axis=1, tiled=True)
    grad_gate_up = jnp.einsum(
        "erd,erf->edf",
        all_x,
        lax.all_gather(grad_pre, "dp", axis=1, tiled=True),
        preferred_element_type=jnp.float32,
    )
    summed = lax.psum_scatter(
        jnp.einsum("erd,erf->def", scaled, hidden, preferred_element_type=jnp.float32),
        "dp",
        scatter_dimension=0,
        tiled=True,
    )
    grad_down = jnp.swapaxes(summed, 0, 1)
    return (grad_tokens, grad_route, grad_gate_up, grad_down)


def packs(tokens, route_expert, down_weight):
    chunks = tokens.shape[1] // LANES
    capacity = block_rows(tokens.shape[0], route_expert.shape[1], lax.axis_size("expert"))
    return (
        lax.axis_size("expert") == 8
        and lax.axis_size("dp") == 4
        and down_weight.shape[0] == 1
        and capacity % 16 <= 1
        and chunks == 16
        and 2 * chunks <= capacity < LANES // 2
    )


def solution(mesh):
    def on_device(*arrays):
        if packs(arrays[0], arrays[2], arrays[5]):
            return on_device_packed(*arrays)
        return on_device_routed(*arrays)

    return jax.shard_map(
        on_device,
        mesh=mesh,
        in_specs=(
            P(("expert", "dp"), None),
            P(("expert", "dp"), None),
            P(("expert", "dp"), None),
            P(("expert", "dp"), None),
            P("expert", "dp", None),
            P("expert", "dp", None),
        ),
        out_specs=(
            P(("expert", "dp"), None),
            P(("expert", "dp"), None),
            P("expert", "dp", None),
            P("expert", "dp", None),
        ),
        check_vma=False,
    )
```

```python
import functools

import jax
import jax.numpy as jnp
from jax import lax
from jax.experimental import pallas as pl
from jax.experimental.pallas import tpu as pltpu
from jax.sharding import PartitionSpec as P

BF16 = jnp.bfloat16
F32 = jnp.float32
LANES = 128


def swish(value):
    return value * jax.nn.sigmoid(value)


def dot(a, b):
    return jnp.dot(a, b, preferred_element_type=F32)


def dot_nt(a, b):
    return lax.dot_general(a, b, (((1,), (1,)), ((), ())), preferred_element_type=F32)


def dot_tn(a, b):
    return lax.dot_general(a, b, (((0,), (0,)), ((), ())), preferred_element_type=F32)


def start(source, target, sem):
    copy = pltpu.make_async_copy(source, target, sem)
    copy.start()
    return copy


def picks(weight, main):
    token_count = weight.shape[1]
    routed = weight != 0.0
    first = lax.broadcasted_iota(jnp.int32, (token_count, token_count), 0)
    second = lax.broadcasted_iota(jnp.int32, (token_count, token_count), 1)
    upper = (first < second).astype(F32).astype(BF16)
    rank = dot(routed.astype(F32).astype(BF16), upper)
    rank = jnp.where(routed, rank, -1.0).astype(jnp.int32)
    slots = lax.broadcasted_iota(jnp.int32, (main, token_count), 0)
    mains = [(slots == rank[i : i + 1, :]).astype(F32) for i in range(weight.shape[0])]
    tails = (rank == main).astype(F32)
    return mains, tails


def route_kernel(peer_ref, named_ref, given_ref, x_ref, dy_ref, joint_ref, dense_ref):
    count, width = x_ref.shape
    named = named_ref[...]
    given = given_ref[...].astype(F32)
    experts = dense_ref.shape[0]
    lines = [
        jnp.sum(jnp.where(named == peer_ref[i], given, 0.0), axis=0, keepdims=True) for i in range(experts)
    ]
    dense = jnp.concatenate(lines, axis=0)
    dense_ref[...] = dense
    turned = jnp.concatenate(lines[experts // 2 :] + lines[: experts // 2] + [jnp.zeros_like(dense)], axis=0)
    joint_ref[:, :width] = x_ref[...]
    joint_ref[:, width : 2 * width] = dy_ref[...]
    joint_ref[:, 2 * width :] = jnp.zeros((count, LANES), BF16)
    joint_ref[0:16, 2 * width : 2 * width + count] = turned.astype(BF16)


def stack_kernel(own_ref, far_ref, after_ref, stacked_ref):
    count = own_ref.shape[0]
    stacked_ref[0:count, :] = own_ref[...]
    stacked_ref[count:, :] = far_ref[...]


def after_kernel(*refs):
    pass


def relay_kernel(near_a, far_a, near_b, far_b, mid_ref, *refs):
    joint_ref = refs[-1]
    count, width = near_a.shape
    for at, near, far in ((0, near_a, far_a), (count, near_b, far_b)):
        joint_ref[at : at + count, :width] = near[...]
        joint_ref[at : at + count, width : 2 * width] = far[:, width:]
    joint_ref[:, 2 * width :] = mid_ref[...]


def pack_blocks(experts, joint_ref, out_refs, fold):
    count = len(experts)
    tokens, width = joint_ref.shape[0], out_refs[0].shape[1] - LANES
    chunks = width // LANES
    main = out_refs[0].shape[0] // 2
    weight = joint_ref[0:16, 2 * width :].astype(F32)[0:8, :tokens]
    mains, tails = picks(weight, main)
    pick = jnp.concatenate([mains[e] for e in experts] + [tails, jnp.zeros_like(tails)], axis=0).astype(BF16)
    lane = lax.broadcasted_iota(jnp.int32, (main, LANES), 1)
    for at, base, low in ((0, 0, 0), (width, main, chunks)):
        rows = dot(pick, joint_ref[:, at : at + width])
        for j, e in enumerate(experts):
            out_refs[j][base : base + main, :width] = rows[main * j : main * (j + 1)].astype(BF16)
            line = main * count + e
            for c in range(chunks):
                fold[c : c + 1, :] = rows[line : line + 1, LANES * c : LANES * (c + 1)]
            out_refs[j][low : low + chunks, width:] = fold[...].astype(BF16)
    for j, e in enumerate(experts):
        mine = weight[e : e + 1, :]
        column = jnp.sum(mains[e] * mine, axis=1, keepdims=True)
        last = jnp.sum(tails[e : e + 1, :] * mine, axis=1, keepdims=True)
        out_refs[j][main:, width:] = jnp.where(lane < LANES // 2, column, last).astype(BF16)


def pack_kernel(experts, joint_ref, *refs):
    pack_blocks(experts, joint_ref, refs[-1 - len(experts) : -1], refs[-1])


def slice_kernel(place_ref, *refs):
    blocks, parts = 4, 4
    keep_ref, near_ref, far_ref, weight_ref, fold = refs[-5:]
    in_refs = refs[:blocks]
    main = in_refs[0].shape[0] // 2
    depth = keep_ref.shape[1] // 2
    width = parts * depth
    chunks = width // LANES
    targets = [(keep_ref, 0), (near_ref, 0), (far_ref, 0), (far_ref, 2 * depth)]
    lane = lax.broadcasted_iota(jnp.int32, (1, LANES), 1)
    lasts = []
    for i in range(blocks):
        for j, (target, shift) in enumerate(targets):
            columns = pl.ds(pl.multiple_of(place_ref[j] * depth, depth), depth)
            for side in range(2):
                at = shift + side * depth
                target[main * i : main * (i + 1), at : at + depth] = in_refs[i][
                    side * main : (side + 1) * main, columns
                ]
        for side in range(2):
            fold[side, chunks * i : chunks * (i + 1), :] = in_refs[i][
                side * chunks : (side + 1) * chunks, width:
            ].astype(F32)
        weights = in_refs[i][main:, width:].astype(F32)
        weight_ref[main * i : main * (i + 1), :] = weights
        last = jnp.sum(jnp.where(lane == LANES - 1, weights[0:1, :], 0.0), axis=1, keepdims=True)
        lasts.append(jnp.broadcast_to(last, (1, LANES)))
    weight_ref[main * blocks :, :] = jnp.concatenate(lasts + [jnp.zeros((16 - blocks, LANES), F32)], axis=0)
    each = chunks // parts
    for j, (target, shift) in enumerate(targets):
        for side in range(2):
            for q in range(each):
                tail = fold[side, pl.ds(place_ref[j] * each + q, blocks, stride=chunks), :]
                tail = jnp.concatenate([tail, jnp.zeros((16 - blocks, LANES), F32)], axis=0).astype(BF16)
                at = shift + side * depth + q * LANES
                target[main * blocks :, at : at + LANES] = tail


def main_kernel(early, place_ref, w_ref, *refs):
    blocks, parts = 4, 4
    own_ref, other_ref = refs[:2]
    keep_ref, near_ref, far_ref = refs[2:5]
    mid, backs, (tail, fold) = refs[-3 - blocks], refs[-2 - blocks : -2], refs[-2:]
    depth = keep_ref.shape[1] // 2
    width = parts * depth
    hidden_width = mid.shape[1] // 3
    main = backs[0].shape[0]
    chunks = width // LANES
    total = keep_ref.shape[0]
    first, second = pl.ds(0, depth), pl.ds(depth, depth)
    weights = [own_ref.at[first], other_ref.at[first], own_ref.at[second], other_ref.at[second]]
    pre = jnp.zeros((total, 2 * hidden_width), F32)
    grad = jnp.zeros((total, hidden_width), F32)
    for j, (ref, shift) in enumerate([(keep_ref, 0), (near_ref, 0), (far_ref, 0), (far_ref, 2 * depth)]):
        pre += dot(ref[:, shift : shift + depth], weights[j][:, : 2 * hidden_width])
        grad += dot(ref[:, shift + depth : shift + 2 * depth], weights[j][:, 2 * hidden_width :])
    if early:
        mid[0:early, :] = refs[5][...]
    weight = w_ref[:, 0:1]
    gate_pre = pre[:, :hidden_width]
    up_pre = pre[:, hidden_width:]
    sig = jax.nn.sigmoid(gate_pre)
    act = gate_pre * sig
    hidden = (act * up_pre).astype(BF16).astype(F32)
    route = jnp.sum(hidden * grad, axis=1, keepdims=True)
    grad_hidden = weight * grad
    grad_gate = grad_hidden * up_pre * sig * (1.0 + gate_pre * (1.0 - sig))
    mid[early:, :hidden_width] = grad_gate.astype(BF16)
    mid[early:, hidden_width : 2 * hidden_width] = (grad_hidden * act).astype(BF16)
    mid[early:, 2 * hidden_width :] = (weight * hidden).astype(BF16)
    for j in range(parts):
        columns = pl.ds(pl.multiple_of(place_ref[j] * depth, depth), depth)
        part = dot_nt(mid[early:, : 2 * hidden_width], weights[j][:, : 2 * hidden_width])
        tail[:, columns] = part[main * blocks :]
        part = part.astype(BF16)
        for i in range(blocks):
            backs[i][:, columns] = part[main * i : main * (i + 1)]
    row = lax.broadcasted_iota(jnp.int32, (main, LANES), 0)
    lane = lax.broadcasted_iota(jnp.int32, (main, LANES), 1)
    for i in range(blocks):
        for c in range(chunks):
            fold[c : c + 1, :] = tail[i : i + 1, LANES * c : LANES * (c + 1)]
        backs[i][:chunks, width:] = fold[...].astype(BF16)
        mine = jnp.where(row == lane, route[main * i : main * (i + 1)], 0.0)
        mine = jnp.sum(mine, axis=0, keepdims=True)
        mine = jnp.where(lane[0:1] == main, route[main * blocks + i : main * blocks + i + 1], mine)
        backs[i][chunks:, width:] = jnp.broadcast_to(mine, (main - chunks, LANES)).astype(BF16)


def unpack_sum(weight, block_refs, rows, fold, order=(0, 1, 2, 3)):
    count = len(block_refs)
    main = block_refs[0].shape[0]
    width = rows.shape[1]
    chunks = width // LANES
    mains, tails = picks(weight, main)
    mains = [mains[e] for e in order]
    tails = jnp.concatenate([tails[e : e + 1, :] for e in order] + [jnp.zeros((16 - count, tails.shape[1]), F32)], axis=0)
    pick = jnp.concatenate(mains + [tails], axis=0).astype(BF16)
    lane = lax.broadcasted_iota(jnp.int32, (1, LANES), 1)
    routes = {}
    for j in range(count):
        rows[main * j : main * (j + 1), :] = block_refs[j][:, :width]
        fold[chunks * j : chunks * (j + 1), :] = block_refs[j][:chunks, width:].astype(F32)
        mine = block_refs[j][chunks:, width:].astype(F32)
        dense = dot(mine[:, :main].astype(BF16), mains[j].astype(BF16))[0:1, :]
        last = jnp.sum(jnp.where(lane == main, mine[0:1, :], 0.0), axis=1, keepdims=True)
        routes[order[j]] = dense + last * tails[j : j + 1, :]
    for c in range(chunks):
        tail = fold[pl.ds(c, count, stride=chunks), :]
        tail = jnp.concatenate([tail, jnp.zeros((16 - count, LANES), F32)], axis=0).astype(BF16)
        rows[main * count :, LANES * c : LANES * (c + 1)] = tail
    return dot_tn(pick, rows[...]), [routes[e] for e in range(count)]


def relay_sum_kernel(joint_ref, b0, b3, b2, b1, out_ref, rows, fold):
    tokens, width = joint_ref.shape[0], rows.shape[1]
    weight = joint_ref[0:16, 2 * width :].astype(F32)[0:8, :tokens]
    summed, routes = unpack_sum(weight, (b0, b3, b2, b1), rows, fold, (0, 3, 2, 1))
    lines = tokens // 2
    out_ref[:, :width] = summed[0:lines].astype(BF16)
    out_ref[:, width : 2 * width] = summed[lines:].astype(BF16)
    out_ref[:, 2 * width :] = jnp.zeros((lines, LANES), BF16)
    block = jnp.concatenate(routes + [jnp.zeros((12, tokens), F32)], axis=0).astype(BF16)
    out_ref[0:16, 2 * width : 2 * width + tokens] = block


def combine_kernel(peer_ref, named_ref, w_ref, b0, b3, b2, b1, far_ref, *refs):
    grad_ref, route_ref, in_ref, out_ref, held, rows, fold, lines_ref, sem = refs[5:]
    tokens, width = held.shape
    summed, routes = unpack_sum(w_ref[...], (b0, b3, b2, b1), rows, fold, (0, 3, 2, 1))
    lines = tokens // 2
    for half in range(2):
        at, columns = slice(half * lines, (half + 1) * lines), slice(half * width, (half + 1) * width)
        held[at, :] = (summed[at, :] + far_ref[:, columns].astype(F32)).astype(BF16)
    copy = start(held, grad_ref, sem)
    others = far_ref[0:16, 2 * width : 2 * width + tokens].astype(F32)
    named = named_ref[...]
    route = jnp.zeros(route_ref.shape, F32)
    for j in range(4):
        route = route + jnp.where(named == peer_ref[j], routes[j], 0.0)
        route = route + jnp.where(named == peer_ref[4 + j], others[j : j + 1, :], 0.0)
    route_ref[...] = route.astype(BF16)
    second_weight_part(*refs[:5], in_ref, out_ref, lines_ref)
    copy.wait()


def fill(rows, mids, rows_a, rows_b, rows_c, mid_a, mid_b):
    count = rows_a.shape[0]
    rows[0:count, :] = rows_a
    rows[count : 2 * count, :] = rows_b
    rows[2 * count :, :] = rows_c
    mids[0 : 2 * count, :] = mid_a
    mids[2 * count :, :] = mid_b


def first_weight_kernel(rows_a, rows_b, near_ref, mid_ref, in_ref, out_ref, rows, mids):
    depth, hidden_width = out_ref.shape
    near, near_mid = near_ref[:, : 2 * depth], near_ref[:, 4 * depth :]
    fill(rows, mids, rows_a[...], rows_b[...], near, mid_ref[...], near_mid)
    in_ref[...] = dot_tn(rows[:, :depth], mids[:, : 2 * hidden_width])
    out_ref[...] = dot_tn(rows[:, depth:], mids[:, 2 * hidden_width :])


def second_weight_part(rows_a, rows_b, mid_ref, in_part, out_part, in_ref, out_ref, rows):
    depth, hidden_width = out_ref.shape
    count = rows_a.shape[0]
    rows[0:count, :] = rows_a[:, : 2 * depth]
    rows[count:, :] = rows_b[:, : 2 * depth]
    in_ref[...] = in_part[...] + dot_tn(rows[:, :depth], mid_ref[:, : 2 * hidden_width])
    out_ref[...] = out_part[...] + dot_tn(rows[:, depth:], mid_ref[:, 2 * hidden_width :])


def last_weight_kernel(near_ref, mid_ref, in_part, out_part, in_ref, out_ref, in_held, out_held, sems):
    depth, hidden_width = out_part.shape
    copies = []
    step = depth // 4
    for m in range(4):
        at = slice(m * step, (m + 1) * step)
        lines = pl.ds(m * step, step)
        base = 2 * depth + m * step
        in_held[at, :] = in_part[at, :] + dot_tn(near_ref[:, base : base + step], mid_ref[:, : 2 * hidden_width])
        copies.append(start(in_held.at[lines], in_ref.at[lines], sems.at[0, m]))
        base += depth
        out_held[at, :] = out_part[at, :] + dot_tn(near_ref[:, base : base + step], mid_ref[:, 2 * hidden_width :])
        copies.append(start(out_held.at[lines], out_ref.at[lines], sems.at[1, m]))
    for copy in copies:
        copy.wait()


def call(kernel, outs, smem, vmem, either, scratch, flops, either_outs=0, aliases=None):
    on_vmem = pl.BlockSpec(memory_space=pltpu.VMEM)
    on_either = pl.BlockSpec(memory_space=pl.ANY)
    on_smem = pl.BlockSpec(memory_space=pltpu.SMEM)
    outs = [jax.ShapeDtypeStruct(shape, kind) for shape, kind in outs]
    moved = sum(a.size * a.dtype.itemsize for a in list(vmem) + outs[either_outs:])
    return pl.pallas_call(
        kernel,
        out_shape=tuple(outs),
        in_specs=[on_smem] * len(smem) + [on_vmem] * len(vmem) + [on_either] * len(either),
        out_specs=tuple([on_either] * either_outs + [on_vmem] * (len(outs) - either_outs)),
        scratch_shapes=scratch,
        compiler_params=pltpu.CompilerParams(vmem_limit_bytes=16 * 1024 * 1024),
        cost_estimate=pl.CostEstimate(flops=flops, bytes_accessed=moved, transcendentals=0),
        input_output_aliases=aliases or {},
    )(*smem, *vmem, *either)


def swap(value, axis, mask):
    return lax.ppermute(value, axis, [(i, i ^ mask) for i in range(lax.axis_size(axis))])


def on_device_packed(tokens, grad_out, route_expert, route_weight, gate_up_weight, down_weight):
    token_count, width = tokens.shape
    blocks, parts, half = 8, 4, 4
    hidden_width = down_weight.shape[2]
    depth = width // parts
    chunks = width // LANES
    main = block_rows(token_count, route_expert.shape[1], blocks) // 16 * 16
    rows = main * half + 16

    peers = lax.axis_index("expert") ^ jnp.arange(blocks, dtype=jnp.int32)
    places = lax.axis_index("dp") ^ jnp.arange(parts, dtype=jnp.int32)
    named = route_expert.T
    packed_shape = ((2 * main, width + LANES), BF16)
    back_shape = ((main, width + LANES), BF16)

    joint, dense = call(
        route_kernel,
        [((token_count, 2 * width + LANES), BF16), ((blocks, token_count), F32)],
        [peers],
        [named, route_weight.T, tokens, grad_out],
        [],
        [],
        0,
    )
    far_joint = swap(joint, "expert", half)

    weights = jnp.concatenate([gate_up_weight[0], down_weight[0]], axis=1)
    far_weights = swap(weights, "dp", 2)

    def pack(experts, value, after):
        return call(
            functools.partial(pack_kernel, experts),
            [packed_shape] * len(experts),
            [],
            [value],
            after,
            [pltpu.VMEM((chunks, LANES), F32)],
            4 * (len(experts) * main + 16) * token_count * width,
        )

    def sliced(packed, after):
        return call(
            slice_kernel,
            [
                ((rows, 2 * depth), BF16),
                ((rows, 2 * depth), BF16),
                ((rows, 4 * depth), BF16),
                ((rows, LANES), F32),
            ],
            [places],
            packed,
            after,
            [pltpu.VMEM((2, (half + 1) * chunks, LANES), F32)],
            0,
        )

    own = [swap(value, "expert", j + 1) for j, value in enumerate(pack(range(half + 1, blocks), joint, []))]
    (kept,) = pack([half], joint, [own[2]])
    *own_slices, own_weight = sliced([kept, *own[::-1]], [far_joint])
    own_far = swap(own_slices[2], "dp", 2)
    far = pack(range(half), far_joint, [own_slices[0], far_weights])
    far = [far[0]] + [swap(far[j], "expert", j) for j in range(1, half)]
    (stacked,) = call(
        stack_kernel,
        [((2 * depth, 3 * hidden_width), BF16)],
        [],
        [weights, far_weights],
        [far[0]],
        [],
        0,
    )
    weight_parts = [stacked, swap(stacked, "dp", 1)]

    def middle(slices, weight, before, after):
        early = before[0].shape[0] if before else 0
        return call(
            functools.partial(main_kernel, early),
            [((early + rows, 3 * hidden_width), BF16)] + [back_shape] * half,
            [places],
            [weight, *weight_parts, *slices, *before],
            after,
            [pltpu.VMEM((16, width), F32), pltpu.VMEM((chunks, LANES), F32)],
            2 * rows * width * 5 * hidden_width,
        )

    own_mid, *near_back = middle(own_slices, own_weight, [], [])
    near_back = [near_back[0], *near_back[:0:-1]]
    near_back = near_back[:1] + [swap(near_back[j], "expert", j) for j in range(1, half)]
    *far_slices, far_weight = sliced([far[0], *far[:0:-1]], [own_mid, own_far])
    far_far = swap(far_slices[2], "dp", 2)
    mid, *far_back = middle(far_slices, far_weight, [own_mid], [])

    sum_scratch = [
        pltpu.VMEM((half * main + 16, width), BF16),
        pltpu.VMEM(((half + 1) * chunks, LANES), F32),
    ]
    sum_flops = 2 * (half * main + 16) * width * token_count
    far_back = [far_back[0], *far_back[:0:-1]]
    far_back = far_back[:1] + [swap(far_back[j], "expert", j) for j in range(1, half)]
    (partial,) = call(
        relay_sum_kernel,
        [((token_count // 2, 2 * width + LANES), BF16)],
        [],
        [far_joint, far_back[0], *far_back[:0:-1]],
        [],
        sum_scratch,
        sum_flops,
    )
    far_partial = swap(partial, "expert", half)

    mid_far = swap(mid, "dp", 2)
    (near,) = call(
        relay_kernel,
        [((2 * rows, 4 * depth + 3 * hidden_width), BF16)],
        [],
        [own_slices[1], own_far, far_slices[1], far_far, mid],
        [partial],
        [],
        0,
    )
    near = swap(near, "dp", 1)
    weight_shapes = [((depth, 2 * hidden_width), F32), ((depth, hidden_width), F32)]
    weight_scratch = [pltpu.VMEM((4 * rows, 2 * depth), BF16), pltpu.VMEM((4 * rows, 3 * hidden_width), BF16)]
    weight_flops = 2 * 4 * rows * depth * 3 * hidden_width
    first = call(
        first_weight_kernel,
        weight_shapes,
        [],
        [own_slices[0], far_slices[0], near, mid],
        [],
        weight_scratch,
        weight_flops,
    )
    (mid_far,) = call(
        after_kernel,
        [(mid_far.shape, BF16)],
        [],
        [],
        [mid_far, first[1], far_partial, *near_back[:0:-1]],
        [],
        0,
        1,
        {0: 0},
    )
    grad_tokens, grad_route, *second = call(
        combine_kernel,
        [((token_count, width), BF16), (named.shape, BF16), *weight_shapes],
        [peers],
        [named, dense, near_back[0], *near_back[:0:-1], far_partial, own_far, far_far, mid_far, *first],
        [],
        [
            pltpu.VMEM((token_count, width), BF16),
            *sum_scratch,
            pltpu.VMEM((2 * rows, 2 * depth), BF16),
            pltpu.SemaphoreType.DMA,
        ],
        sum_flops + weight_flops // 2,
        1,
    )
    grad_gate_up, grad_down = call(
        last_weight_kernel,
        weight_shapes,
        [],
        [near, swap(mid_far, "dp", 1), *second],
        [],
        [
            pltpu.VMEM((depth, 2 * hidden_width), F32),
            pltpu.VMEM((depth, hidden_width), F32),
            pltpu.SemaphoreType.DMA((2, 4)),
        ],
        weight_flops // 2,
        2,
    )
    return (grad_tokens, grad_route.T, grad_gate_up[None], grad_down[None])


def block_rows(token_count, route_count, expert_total):
    return min(token_count, (token_count * route_count + expert_total - 1) // expert_total + 1)


def to_local(rows, group_count, local_count, capacity):
    tail = rows.shape[2:]
    shaped = rows.reshape((group_count, local_count, capacity) + tail)
    shaped = jnp.swapaxes(shaped, 0, 1)
    return shaped.reshape((local_count, group_count * capacity) + tail)


def to_groups(rows, group_count, local_count, capacity):
    tail = rows.shape[2:]
    shaped = rows.reshape((local_count, group_count, capacity) + tail)
    shaped = jnp.swapaxes(shaped, 0, 1)
    return shaped.reshape((group_count, local_count * capacity) + tail)


def on_device_routed(tokens, grad_out, route_expert, route_weight, gate_up_weight, down_weight):
    token_count, model_width = tokens.shape
    route_count = route_expert.shape[1]
    group_count = lax.axis_size("expert")
    local_count = gate_up_weight.shape[0]
    hidden_width = down_weight.shape[2]
    expert_total = local_count * group_count
    capacity = min(token_count, (token_count * route_count + expert_total - 1) // expert_total + 1)
    slot_total = expert_total * capacity
    flat_expert = route_expert.reshape(-1)
    expert_ids = jnp.arange(expert_total, dtype=jnp.int32)
    onehot = (flat_expert[:, None] == expert_ids[None, :]).astype(jnp.int32)
    before = jnp.cumsum(onehot, axis=0) - onehot
    rank = jnp.sum(before * onehot, axis=1)
    slot_of = flat_expert * capacity + rank
    slot_ids = jnp.arange(slot_total, dtype=jnp.int32)
    placed = slot_ids[:, None] == slot_of[None, :]
    by_token = jnp.any(placed.reshape(slot_total, token_count, route_count), axis=2).astype(
        jnp.bfloat16
    )
    send_x = jnp.dot(by_token, tokens, preferred_element_type=jnp.float32).astype(jnp.bfloat16)
    send_dy = jnp.dot(by_token, grad_out, preferred_element_type=jnp.float32).astype(jnp.bfloat16)
    flat_weight = route_weight.reshape(-1).astype(jnp.float32)
    send_w = jnp.sum(jnp.where(placed, flat_weight[None, :], 0.0), axis=1).astype(jnp.bfloat16)
    recv_x, recv_dy, recv_w = (
        lax.all_to_all(
            send_x.reshape(group_count, local_count * capacity, model_width),
            "expert",
            split_axis=0,
            concat_axis=0,
            tiled=True,
        ),
        lax.all_to_all(
            send_dy.reshape(group_count, local_count * capacity, model_width),
            "expert",
            split_axis=0,
            concat_axis=0,
            tiled=True,
        ),
        lax.all_to_all(
            send_w.reshape(group_count, local_count * capacity),
            "expert",
            split_axis=0,
            concat_axis=0,
            tiled=True,
        ),
    )
    rows_x = to_local(recv_x, group_count, local_count, capacity)
    rows_dy = to_local(recv_dy, group_count, local_count, capacity)
    rows_w = to_local(recv_w, group_count, local_count, capacity)
    full_in, full_out = (
        lax.all_gather(gate_up_weight, "dp", axis=1, tiled=True),
        lax.all_gather(down_weight, "dp", axis=1, tiled=True),
    )
    pre = jnp.einsum("erd,edf->erf", rows_x, full_in, preferred_element_type=jnp.float32)
    gate_pre = pre[:, :, :hidden_width]
    up_pre = pre[:, :, hidden_width:]
    act = swish(gate_pre)
    hidden = (act * up_pre).astype(jnp.bfloat16)
    expert_out = jnp.einsum("erf,edf->erd", hidden, full_out, preferred_element_type=jnp.float32)
    route_grad = jnp.sum(rows_dy.astype(jnp.float32) * expert_out, axis=2).astype(jnp.bfloat16)
    scaled = (rows_w.astype(jnp.float32)[:, :, None] * rows_dy).astype(jnp.bfloat16)
    grad_hidden = jnp.einsum("erd,edf->erf", scaled, full_out, preferred_element_type=jnp.float32)
    sig = jax.nn.sigmoid(gate_pre)
    grad_gate = grad_hidden * up_pre * sig * (1.0 + gate_pre * (1.0 - sig))
    grad_up = grad_hidden * act
    grad_pre = jnp.concatenate([grad_gate, grad_up], axis=2).astype(jnp.bfloat16)
    rows_grad = jnp.einsum(
        "erf,edf->erd", grad_pre, full_in, preferred_element_type=jnp.float32
    ).astype(jnp.bfloat16)
    back_x, back_w = (
        lax.all_to_all(
            to_groups(rows_grad, group_count, local_count, capacity),
            "expert",
            split_axis=0,
            concat_axis=0,
            tiled=True,
        ),
        lax.all_to_all(
            to_groups(route_grad, group_count, local_count, capacity),
            "expert",
            split_axis=0,
            concat_axis=0,
            tiled=True,
        ),
    )
    back_x = back_x.reshape(slot_total, model_width)
    back_w = back_w.reshape(slot_total).astype(jnp.float32)
    grad_tokens = jnp.einsum(
        "st,sd->td", by_token, back_x, preferred_element_type=jnp.float32
    ).astype(jnp.bfloat16)
    grad_route = jnp.sum(jnp.where(placed, back_w[:, None], 0.0), axis=0)
    grad_route = grad_route.reshape(token_count, route_count).astype(jnp.bfloat16)
    all_x = lax.all_to_all(rows_x, "dp", split_axis=2, concat_axis=1, tiled=True)
    grad_gate_up = jnp.einsum(
        "erd,erf->edf",
        all_x,
        lax.all_gather(grad_pre, "dp", axis=1, tiled=True),
        preferred_element_type=jnp.float32,
    )
    summed = lax.psum_scatter(
        jnp.einsum("erd,erf->def", scaled, hidden, preferred_element_type=jnp.float32),
        "dp",
        scatter_dimension=0,
        tiled=True,
    )
    grad_down = jnp.swapaxes(summed, 0, 1)
    return (grad_tokens, grad_route, grad_gate_up, grad_down)


def packs(tokens, route_expert, down_weight):
    chunks = tokens.shape[1] // LANES
    capacity = block_rows(tokens.shape[0], route_expert.shape[1], lax.axis_size("expert"))
    return (
        lax.axis_size("expert") == 8
        and lax.axis_size("dp") == 4
        and down_weight.shape[0] == 1
        and capacity % 16 <= 1
        and chunks == 16
        and 2 * chunks <= capacity < LANES // 2
    )


def solution(mesh):
    def on_device(*arrays):
        if packs(arrays[0], arrays[2], arrays[5]):
            return on_device_packed(*arrays)
        return on_device_routed(*arrays)

    return jax.shard_map(
        on_device,
        mesh=mesh,
        in_specs=(
            P(("expert", "dp"), None),
            P(("expert", "dp"), None),
            P(("expert", "dp"), None),
            P(("expert", "dp"), None),
            P("expert", "dp", None),
            P("expert", "dp", None),
        ),
        out_specs=(
            P(("expert", "dp"), None),
            P(("expert", "dp"), None),
            P("expert", "dp", None),
            P("expert", "dp", None),
        ),
        check_vma=False,
    )
```

```python
import functools

import jax
import jax.numpy as jnp
from jax import lax
from jax.experimental import pallas as pl
from jax.experimental.pallas import tpu as pltpu
from jax.sharding import PartitionSpec as P

BF16 = jnp.bfloat16
F32 = jnp.float32
LANES = 128


def swish(value):
    return value * jax.nn.sigmoid(value)


def dot(a, b):
    return jnp.dot(a, b, preferred_element_type=F32)


def dot_nt(a, b):
    return lax.dot_general(a, b, (((1,), (1,)), ((), ())), preferred_element_type=F32)


def dot_tn(a, b):
    return lax.dot_general(a, b, (((0,), (0,)), ((), ())), preferred_element_type=F32)


def start(source, target, sem):
    copy = pltpu.make_async_copy(source, target, sem)
    copy.start()
    return copy


def picks(weight, main):
    token_count = weight.shape[1]
    routed = weight != 0.0
    first = lax.broadcasted_iota(jnp.int32, (token_count, token_count), 0)
    second = lax.broadcasted_iota(jnp.int32, (token_count, token_count), 1)
    upper = (first < second).astype(F32).astype(BF16)
    rank = dot(routed.astype(F32).astype(BF16), upper)
    rank = jnp.where(routed, rank, -1.0).astype(jnp.int32)
    slots = lax.broadcasted_iota(jnp.int32, (main, token_count), 0)
    mains = [(slots == rank[i : i + 1, :]).astype(F32) for i in range(weight.shape[0])]
    tails = (rank == main).astype(F32)
    return mains, tails


def route_kernel(peer_ref, named_ref, given_ref, x_ref, dy_ref, joint_ref, dense_ref):
    count, width = x_ref.shape
    named = named_ref[...]
    given = given_ref[...].astype(F32)
    experts = dense_ref.shape[0]
    lines = [
        jnp.sum(jnp.where(named == peer_ref[i], given, 0.0), axis=0, keepdims=True) for i in range(experts)
    ]
    dense = jnp.concatenate(lines, axis=0)
    dense_ref[...] = dense
    turned = jnp.concatenate(lines[experts // 2 :] + lines[: experts // 2] + [jnp.zeros_like(dense)], axis=0)
    joint_ref[:, :width] = x_ref[...]
    joint_ref[:, width : 2 * width] = dy_ref[...]
    joint_ref[:, 2 * width :] = jnp.zeros((count, LANES), BF16)
    joint_ref[0:16, 2 * width : 2 * width + count] = turned.astype(BF16)


def stack_kernel(own_ref, far_ref, after_ref, stacked_ref):
    count = own_ref.shape[0]
    stacked_ref[0:count, :] = own_ref[...]
    stacked_ref[count:, :] = far_ref[...]


def after_kernel(*refs):
    pass


def relay_kernel(near_a, far_a, near_b, far_b, mid_ref, *refs):
    joint_ref = refs[-1]
    count, width = near_a.shape
    for at, near, far in ((0, near_a, far_a), (count, near_b, far_b)):
        joint_ref[at : at + count, :width] = near[...]
        joint_ref[at : at + count, width : 2 * width] = far[:, width:]
    joint_ref[:, 2 * width :] = mid_ref[...]


def pack_blocks(experts, joint_ref, out_refs, fold):
    count = len(experts)
    tokens, width = joint_ref.shape[0], out_refs[0].shape[1] - LANES
    chunks = width // LANES
    main = out_refs[0].shape[0] // 2
    weight = joint_ref[0:16, 2 * width :].astype(F32)[0:8, :tokens]
    mains, tails = picks(weight, main)
    pick = jnp.concatenate([mains[e] for e in experts] + [tails, jnp.zeros_like(tails)], axis=0).astype(BF16)
    lane = lax.broadcasted_iota(jnp.int32, (main, LANES), 1)
    for at, base, low in ((0, 0, 0), (width, main, chunks)):
        rows = dot(pick, joint_ref[:, at : at + width])
        for j, e in enumerate(experts):
            out_refs[j][base : base + main, :width] = rows[main * j : main * (j + 1)].astype(BF16)
            line = main * count + e
            for c in range(chunks):
                fold[c : c + 1, :] = rows[line : line + 1, LANES * c : LANES * (c + 1)]
            out_refs[j][low : low + chunks, width:] = fold[...].astype(BF16)
    for j, e in enumerate(experts):
        mine = weight[e : e + 1, :]
        column = jnp.sum(mains[e] * mine, axis=1, keepdims=True)
        last = jnp.sum(tails[e : e + 1, :] * mine, axis=1, keepdims=True)
        out_refs[j][main:, width:] = jnp.where(lane < LANES // 2, column, last).astype(BF16)


def pack_kernel(experts, joint_ref, *refs):
    pack_blocks(experts, joint_ref, refs[-1 - len(experts) : -1], refs[-1])


def keep_kernel(expert, joint_ref, block_ref, kept_ref, held_ref, fold):
    pack_blocks([expert], joint_ref, [kept_ref], fold)
    held_ref[...] = block_ref[...]


def slice_kernel(place_ref, *refs):
    blocks, parts = 4, 4
    keep_ref, near_ref, far_ref, weight_ref, fold = refs[-5:]
    in_refs = refs[:blocks]
    main = in_refs[0].shape[0] // 2
    depth = keep_ref.shape[1] // 2
    width = parts * depth
    chunks = width // LANES
    targets = [(keep_ref, 0), (near_ref, 0), (far_ref, 0), (far_ref, 2 * depth)]
    lane = lax.broadcasted_iota(jnp.int32, (1, LANES), 1)
    lasts = []
    for i in range(blocks):
        for j, (target, shift) in enumerate(targets):
            columns = pl.ds(pl.multiple_of(place_ref[j] * depth, depth), depth)
            for side in range(2):
                at = shift + side * depth
                target[main * i : main * (i + 1), at : at + depth] = in_refs[i][
                    side * main : (side + 1) * main, columns
                ]
        for side in range(2):
            fold[side, chunks * i : chunks * (i + 1), :] = in_refs[i][
                side * chunks : (side + 1) * chunks, width:
            ].astype(F32)
        weights = in_refs[i][main:, width:].astype(F32)
        weight_ref[main * i : main * (i + 1), :] = weights
        last = jnp.sum(jnp.where(lane == LANES - 1, weights[0:1, :], 0.0), axis=1, keepdims=True)
        lasts.append(jnp.broadcast_to(last, (1, LANES)))
    weight_ref[main * blocks :, :] = jnp.concatenate(lasts + [jnp.zeros((16 - blocks, LANES), F32)], axis=0)
    each = chunks // parts
    for j, (target, shift) in enumerate(targets):
        for side in range(2):
            for q in range(each):
                tail = fold[side, pl.ds(place_ref[j] * each + q, blocks, stride=chunks), :]
                tail = jnp.concatenate([tail, jnp.zeros((16 - blocks, LANES), F32)], axis=0).astype(BF16)
                at = shift + side * depth + q * LANES
                target[main * blocks :, at : at + LANES] = tail


def main_kernel(early, place_ref, w_ref, *refs):
    blocks, parts = 4, 4
    own_ref, other_ref = refs[:2]
    keep_ref, near_ref, far_ref = refs[2:5]
    mid, backs, (tail, fold) = refs[-3 - blocks], refs[-2 - blocks : -2], refs[-2:]
    depth = keep_ref.shape[1] // 2
    width = parts * depth
    hidden_width = mid.shape[1] // 3
    main = backs[0].shape[0]
    chunks = width // LANES
    total = keep_ref.shape[0]
    first, second = pl.ds(0, depth), pl.ds(depth, depth)
    weights = [own_ref.at[first], other_ref.at[first], own_ref.at[second], other_ref.at[second]]
    pre = jnp.zeros((total, 2 * hidden_width), F32)
    grad = jnp.zeros((total, hidden_width), F32)
    for j, (ref, shift) in enumerate([(keep_ref, 0), (near_ref, 0), (far_ref, 0), (far_ref, 2 * depth)]):
        pre += dot(ref[:, shift : shift + depth], weights[j][:, : 2 * hidden_width])
        grad += dot(ref[:, shift + depth : shift + 2 * depth], weights[j][:, 2 * hidden_width :])
    if early:
        mid[0:early, :] = refs[5][...]
    weight = w_ref[:, 0:1]
    gate_pre = pre[:, :hidden_width]
    up_pre = pre[:, hidden_width:]
    sig = jax.nn.sigmoid(gate_pre)
    act = gate_pre * sig
    hidden = (act * up_pre).astype(BF16).astype(F32)
    route = jnp.sum(hidden * grad, axis=1, keepdims=True)
    grad_hidden = weight * grad
    grad_gate = grad_hidden * up_pre * sig * (1.0 + gate_pre * (1.0 - sig))
    mid[early:, :hidden_width] = grad_gate.astype(BF16)
    mid[early:, hidden_width : 2 * hidden_width] = (grad_hidden * act).astype(BF16)
    mid[early:, 2 * hidden_width :] = (weight * hidden).astype(BF16)
    for j in range(parts):
        columns = pl.ds(pl.multiple_of(place_ref[j] * depth, depth), depth)
        part = dot_nt(mid[early:, : 2 * hidden_width], weights[j][:, : 2 * hidden_width])
        tail[:, columns] = part[main * blocks :]
        part = part.astype(BF16)
        for i in range(blocks):
            backs[i][:, columns] = part[main * i : main * (i + 1)]
    row = lax.broadcasted_iota(jnp.int32, (main, LANES), 0)
    lane = lax.broadcasted_iota(jnp.int32, (main, LANES), 1)
    for i in range(blocks):
        for c in range(chunks):
            fold[c : c + 1, :] = tail[i : i + 1, LANES * c : LANES * (c + 1)]
        backs[i][:chunks, width:] = fold[...].astype(BF16)
        mine = jnp.where(row == lane, route[main * i : main * (i + 1)], 0.0)
        mine = jnp.sum(mine, axis=0, keepdims=True)
        mine = jnp.where(lane[0:1] == main, route[main * blocks + i : main * blocks + i + 1], mine)
        backs[i][chunks:, width:] = jnp.broadcast_to(mine, (main - chunks, LANES)).astype(BF16)


def unpack_sum(weight, block_refs, rows, fold, order=(0, 1, 2, 3)):
    count = len(block_refs)
    main = block_refs[0].shape[0]
    width = rows.shape[1]
    chunks = width // LANES
    mains, tails = picks(weight, main)
    mains = [mains[e] for e in order]
    tails = jnp.concatenate([tails[e : e + 1, :] for e in order] + [jnp.zeros((16 - count, tails.shape[1]), F32)], axis=0)
    pick = jnp.concatenate(mains + [tails], axis=0).astype(BF16)
    lane = lax.broadcasted_iota(jnp.int32, (1, LANES), 1)
    routes = {}
    for j in range(count):
        rows[main * j : main * (j + 1), :] = block_refs[j][:, :width]
        fold[chunks * j : chunks * (j + 1), :] = block_refs[j][:chunks, width:].astype(F32)
        mine = block_refs[j][chunks:, width:].astype(F32)
        dense = dot(mine[:, :main].astype(BF16), mains[j].astype(BF16))[0:1, :]
        last = jnp.sum(jnp.where(lane == main, mine[0:1, :], 0.0), axis=1, keepdims=True)
        routes[order[j]] = dense + last * tails[j : j + 1, :]
    for c in range(chunks):
        tail = fold[pl.ds(c, count, stride=chunks), :]
        tail = jnp.concatenate([tail, jnp.zeros((16 - count, LANES), F32)], axis=0).astype(BF16)
        rows[main * count :, LANES * c : LANES * (c + 1)] = tail
    return dot_tn(pick, rows[...]), [routes[e] for e in range(count)]


def relay_sum_kernel(joint_ref, b0, b3, b2, b1, out_ref, rows, fold):
    tokens, width = joint_ref.shape[0], rows.shape[1]
    weight = joint_ref[0:16, 2 * width :].astype(F32)[0:8, :tokens]
    summed, routes = unpack_sum(weight, (b0, b3, b2, b1), rows, fold, (0, 3, 2, 1))
    lines = tokens // 2
    out_ref[:, :width] = summed[0:lines].astype(BF16)
    out_ref[:, width : 2 * width] = summed[lines:].astype(BF16)
    out_ref[:, 2 * width :] = jnp.zeros((lines, LANES), BF16)
    block = jnp.concatenate(routes + [jnp.zeros((12, tokens), F32)], axis=0).astype(BF16)
    out_ref[0:16, 2 * width : 2 * width + tokens] = block


def combine_kernel(peer_ref, named_ref, w_ref, b0, b3, b2, b1, far_ref, *refs):
    grad_ref, route_ref, in_ref, out_ref, held, rows, fold, lines_ref, sem = refs[5:]
    tokens, width = held.shape
    summed, routes = unpack_sum(w_ref[...], (b0, b3, b2, b1), rows, fold, (0, 3, 2, 1))
    lines = tokens // 2
    for half in range(2):
        at, columns = slice(half * lines, (half + 1) * lines), slice(half * width, (half + 1) * width)
        held[at, :] = (summed[at, :] + far_ref[:, columns].astype(F32)).astype(BF16)
    copy = start(held, grad_ref, sem)
    others = far_ref[0:16, 2 * width : 2 * width + tokens].astype(F32)
    named = named_ref[...]
    route = jnp.zeros(route_ref.shape, F32)
    for j in range(4):
        route = route + jnp.where(named == peer_ref[j], routes[j], 0.0)
        route = route + jnp.where(named == peer_ref[4 + j], others[j : j + 1, :], 0.0)
    route_ref[...] = route.astype(BF16)
    second_weight_part(*refs[:5], in_ref, out_ref, lines_ref)
    copy.wait()


def fill(rows, mids, rows_a, rows_b, rows_c, mid_a, mid_b):
    count = rows_a.shape[0]
    rows[0:count, :] = rows_a
    rows[count : 2 * count, :] = rows_b
    rows[2 * count :, :] = rows_c
    mids[0 : 2 * count, :] = mid_a
    mids[2 * count :, :] = mid_b


def first_weight_kernel(rows_a, rows_b, near_ref, mid_ref, in_ref, out_ref, rows, mids):
    depth, hidden_width = out_ref.shape
    near, near_mid = near_ref[:, : 2 * depth], near_ref[:, 4 * depth :]
    fill(rows, mids, rows_a[...], rows_b[...], near, mid_ref[...], near_mid)
    in_ref[...] = dot_tn(rows[:, :depth], mids[:, : 2 * hidden_width])
    out_ref[...] = dot_tn(rows[:, depth:], mids[:, 2 * hidden_width :])


def second_weight_part(rows_a, rows_b, mid_ref, in_part, out_part, in_ref, out_ref, rows):
    depth, hidden_width = out_ref.shape
    count = rows_a.shape[0]
    rows[0:count, :] = rows_a[:, : 2 * depth]
    rows[count:, :] = rows_b[:, : 2 * depth]
    in_ref[...] = in_part[...] + dot_tn(rows[:, :depth], mid_ref[:, : 2 * hidden_width])
    out_ref[...] = out_part[...] + dot_tn(rows[:, depth:], mid_ref[:, 2 * hidden_width :])


def last_weight_kernel(near_ref, mid_ref, in_part, out_part, in_ref, out_ref, in_held, out_held, sems):
    depth, hidden_width = out_part.shape
    copies = []
    step = depth // 4
    for m in range(4):
        at = slice(m * step, (m + 1) * step)
        lines = pl.ds(m * step, step)
        base = 2 * depth + m * step
        in_held[at, :] = in_part[at, :] + dot_tn(near_ref[:, base : base + step], mid_ref[:, : 2 * hidden_width])
        copies.append(start(in_held.at[lines], in_ref.at[lines], sems.at[0, m]))
        base += depth
        out_held[at, :] = out_part[at, :] + dot_tn(near_ref[:, base : base + step], mid_ref[:, 2 * hidden_width :])
        copies.append(start(out_held.at[lines], out_ref.at[lines], sems.at[1, m]))
    for copy in copies:
        copy.wait()


def call(kernel, outs, smem, vmem, either, scratch, flops, either_outs=0, aliases=None):
    on_vmem = pl.BlockSpec(memory_space=pltpu.VMEM)
    on_either = pl.BlockSpec(memory_space=pl.ANY)
    on_smem = pl.BlockSpec(memory_space=pltpu.SMEM)
    outs = [jax.ShapeDtypeStruct(shape, kind) for shape, kind in outs]
    moved = sum(a.size * a.dtype.itemsize for a in list(vmem) + outs[either_outs:])
    return pl.pallas_call(
        kernel,
        out_shape=tuple(outs),
        in_specs=[on_smem] * len(smem) + [on_vmem] * len(vmem) + [on_either] * len(either),
        out_specs=tuple([on_either] * either_outs + [on_vmem] * (len(outs) - either_outs)),
        scratch_shapes=scratch,
        compiler_params=pltpu.CompilerParams(vmem_limit_bytes=16 * 1024 * 1024),
        cost_estimate=pl.CostEstimate(flops=flops, bytes_accessed=moved, transcendentals=0),
        input_output_aliases=aliases or {},
    )(*smem, *vmem, *either)


def swap(value, axis, mask):
    return lax.ppermute(value, axis, [(i, i ^ mask) for i in range(lax.axis_size(axis))])


def on_device_packed(tokens, grad_out, route_expert, route_weight, gate_up_weight, down_weight):
    token_count, width = tokens.shape
    blocks, parts, half = 8, 4, 4
    hidden_width = down_weight.shape[2]
    depth = width // parts
    chunks = width // LANES
    main = block_rows(token_count, route_expert.shape[1], blocks) // 16 * 16
    rows = main * half + 16

    peers = lax.axis_index("expert") ^ jnp.arange(blocks, dtype=jnp.int32)
    places = lax.axis_index("dp") ^ jnp.arange(parts, dtype=jnp.int32)
    named = route_expert.T
    packed_shape = ((2 * main, width + LANES), BF16)
    back_shape = ((main, width + LANES), BF16)

    joint, dense = call(
        route_kernel,
        [((token_count, 2 * width + LANES), BF16), ((blocks, token_count), F32)],
        [peers],
        [named, route_weight.T, tokens, grad_out],
        [],
        [],
        0,
    )
    far_joint = swap(joint, "expert", half)

    weights = jnp.concatenate([gate_up_weight[0], down_weight[0]], axis=1)
    far_weights = swap(weights, "dp", 2)

    def pack(experts, value, after):
        return call(
            functools.partial(pack_kernel, experts),
            [packed_shape] * len(experts),
            [],
            [value],
            after,
            [pltpu.VMEM((chunks, LANES), F32)],
            4 * (len(experts) * main + 16) * token_count * width,
        )

    def sliced(packed, after):
        return call(
            slice_kernel,
            [
                ((rows, 2 * depth), BF16),
                ((rows, 2 * depth), BF16),
                ((rows, 4 * depth), BF16),
                ((rows, LANES), F32),
            ],
            [places],
            packed,
            after,
            [pltpu.VMEM((2, (half + 1) * chunks, LANES), F32)],
            0,
        )

    own = [swap(value, "expert", j + 1) for j, value in enumerate(pack(range(half + 1, blocks), joint, []))]
    kept, own[2] = call(
        functools.partial(keep_kernel, half),
        [packed_shape] * 2,
        [],
        [joint, own[2]],
        [],
        [pltpu.VMEM((chunks, LANES), F32)],
        4 * (main + 16) * token_count * width,
    )
    *own_slices, own_weight = sliced([kept, *own[::-1]], [far_joint])
    own_far = swap(own_slices[2], "dp", 2)
    far = pack(range(half), far_joint, [own_slices[0], far_weights])
    far = [far[0]] + [swap(far[j], "expert", j) for j in range(1, half)]
    (stacked,) = call(
        stack_kernel,
        [((2 * depth, 3 * hidden_width), BF16)],
        [],
        [weights, far_weights],
        [far[0]],
        [],
        0,
    )
    weight_parts = [stacked, swap(stacked, "dp", 1)]

    def middle(slices, weight, before, after):
        early = before[0].shape[0] if before else 0
        return call(
            functools.partial(main_kernel, early),
            [((early + rows, 3 * hidden_width), BF16)] + [back_shape] * half,
            [places],
            [weight, *weight_parts, *slices, *before],
            after,
            [pltpu.VMEM((16, width), F32), pltpu.VMEM((chunks, LANES), F32)],
            2 * rows * width * 5 * hidden_width,
        )

    own_mid, *near_back = middle(own_slices, own_weight, [], [])
    near_back = [near_back[0], *near_back[:0:-1]]
    near_back = near_back[:1] + [swap(near_back[j], "expert", j) for j in range(1, half)]
    *far_slices, far_weight = sliced([far[0], *far[:0:-1]], [own_mid, own_far])
    far_far = swap(far_slices[2], "dp", 2)
    mid, *far_back = middle(far_slices, far_weight, [own_mid], [])

    sum_scratch = [
        pltpu.VMEM((half * main + 16, width), BF16),
        pltpu.VMEM(((half + 1) * chunks, LANES), F32),
    ]
    sum_flops = 2 * (half * main + 16) * width * token_count
    far_back = [far_back[0], *far_back[:0:-1]]
    far_back = far_back[:1] + [swap(far_back[j], "expert", j) for j in range(1, half)]
    (partial,) = call(
        relay_sum_kernel,
        [((token_count // 2, 2 * width + LANES), BF16)],
        [],
        [far_joint, far_back[0], *far_back[:0:-1]],
        [],
        sum_scratch,
        sum_flops,
    )
    far_partial = swap(partial, "expert", half)

    mid_far = swap(mid, "dp", 2)
    (near,) = call(
        relay_kernel,
        [((2 * rows, 4 * depth + 3 * hidden_width), BF16)],
        [],
        [own_slices[1], own_far, far_slices[1], far_far, mid],
        [partial],
        [],
        0,
    )
    near = swap(near, "dp", 1)
    weight_shapes = [((depth, 2 * hidden_width), F32), ((depth, hidden_width), F32)]
    weight_scratch = [pltpu.VMEM((4 * rows, 2 * depth), BF16), pltpu.VMEM((4 * rows, 3 * hidden_width), BF16)]
    weight_flops = 2 * 4 * rows * depth * 3 * hidden_width
    first = call(
        first_weight_kernel,
        weight_shapes,
        [],
        [own_slices[0], far_slices[0], near, mid],
        [],
        weight_scratch,
        weight_flops,
    )
    (mid_far,) = call(
        after_kernel,
        [(mid_far.shape, BF16)],
        [],
        [],
        [mid_far, first[1], far_partial, *near_back[:0:-1]],
        [],
        0,
        1,
        {0: 0},
    )
    grad_tokens, grad_route, *second = call(
        combine_kernel,
        [((token_count, width), BF16), (named.shape, BF16), *weight_shapes],
        [peers],
        [named, dense, near_back[0], *near_back[:0:-1], far_partial, own_far, far_far, mid_far, *first],
        [],
        [
            pltpu.VMEM((token_count, width), BF16),
            *sum_scratch,
            pltpu.VMEM((2 * rows, 2 * depth), BF16),
            pltpu.SemaphoreType.DMA,
        ],
        sum_flops + weight_flops // 2,
        1,
    )
    grad_gate_up, grad_down = call(
        last_weight_kernel,
        weight_shapes,
        [],
        [near, swap(mid_far, "dp", 1), *second],
        [],
        [
            pltpu.VMEM((depth, 2 * hidden_width), F32),
            pltpu.VMEM((depth, hidden_width), F32),
            pltpu.SemaphoreType.DMA((2, 4)),
        ],
        weight_flops // 2,
        2,
    )
    return (grad_tokens, grad_route.T, grad_gate_up[None], grad_down[None])


def block_rows(token_count, route_count, expert_total):
    return min(token_count, (token_count * route_count + expert_total - 1) // expert_total + 1)


def to_local(rows, group_count, local_count, capacity):
    tail = rows.shape[2:]
    shaped = rows.reshape((group_count, local_count, capacity) + tail)
    shaped = jnp.swapaxes(shaped, 0, 1)
    return shaped.reshape((local_count, group_count * capacity) + tail)


def to_groups(rows, group_count, local_count, capacity):
    tail = rows.shape[2:]
    shaped = rows.reshape((local_count, group_count, capacity) + tail)
    shaped = jnp.swapaxes(shaped, 0, 1)
    return shaped.reshape((group_count, local_count * capacity) + tail)


def on_device_routed(tokens, grad_out, route_expert, route_weight, gate_up_weight, down_weight):
    token_count, model_width = tokens.shape
    route_count = route_expert.shape[1]
    group_count = lax.axis_size("expert")
    local_count = gate_up_weight.shape[0]
    hidden_width = down_weight.shape[2]
    expert_total = local_count * group_count
    capacity = min(token_count, (token_count * route_count + expert_total - 1) // expert_total + 1)
    slot_total = expert_total * capacity
    flat_expert = route_expert.reshape(-1)
    expert_ids = jnp.arange(expert_total, dtype=jnp.int32)
    onehot = (flat_expert[:, None] == expert_ids[None, :]).astype(jnp.int32)
    before = jnp.cumsum(onehot, axis=0) - onehot
    rank = jnp.sum(before * onehot, axis=1)
    slot_of = flat_expert * capacity + rank
    slot_ids = jnp.arange(slot_total, dtype=jnp.int32)
    placed = slot_ids[:, None] == slot_of[None, :]
    by_token = jnp.any(placed.reshape(slot_total, token_count, route_count), axis=2).astype(
        jnp.bfloat16
    )
    send_x = jnp.dot(by_token, tokens, preferred_element_type=jnp.float32).astype(jnp.bfloat16)
    send_dy = jnp.dot(by_token, grad_out, preferred_element_type=jnp.float32).astype(jnp.bfloat16)
    flat_weight = route_weight.reshape(-1).astype(jnp.float32)
    send_w = jnp.sum(jnp.where(placed, flat_weight[None, :], 0.0), axis=1).astype(jnp.bfloat16)
    recv_x, recv_dy, recv_w = (
        lax.all_to_all(
            send_x.reshape(group_count, local_count * capacity, model_width),
            "expert",
            split_axis=0,
            concat_axis=0,
            tiled=True,
        ),
        lax.all_to_all(
            send_dy.reshape(group_count, local_count * capacity, model_width),
            "expert",
            split_axis=0,
            concat_axis=0,
            tiled=True,
        ),
        lax.all_to_all(
            send_w.reshape(group_count, local_count * capacity),
            "expert",
            split_axis=0,
            concat_axis=0,
            tiled=True,
        ),
    )
    rows_x = to_local(recv_x, group_count, local_count, capacity)
    rows_dy = to_local(recv_dy, group_count, local_count, capacity)
    rows_w = to_local(recv_w, group_count, local_count, capacity)
    full_in, full_out = (
        lax.all_gather(gate_up_weight, "dp", axis=1, tiled=True),
        lax.all_gather(down_weight, "dp", axis=1, tiled=True),
    )
    pre = jnp.einsum("erd,edf->erf", rows_x, full_in, preferred_element_type=jnp.float32)
    gate_pre = pre[:, :, :hidden_width]
    up_pre = pre[:, :, hidden_width:]
    act = swish(gate_pre)
    hidden = (act * up_pre).astype(jnp.bfloat16)
    expert_out = jnp.einsum("erf,edf->erd", hidden, full_out, preferred_element_type=jnp.float32)
    route_grad = jnp.sum(rows_dy.astype(jnp.float32) * expert_out, axis=2).astype(jnp.bfloat16)
    scaled = (rows_w.astype(jnp.float32)[:, :, None] * rows_dy).astype(jnp.bfloat16)
    grad_hidden = jnp.einsum("erd,edf->erf", scaled, full_out, preferred_element_type=jnp.float32)
    sig = jax.nn.sigmoid(gate_pre)
    grad_gate = grad_hidden * up_pre * sig * (1.0 + gate_pre * (1.0 - sig))
    grad_up = grad_hidden * act
    grad_pre = jnp.concatenate([grad_gate, grad_up], axis=2).astype(jnp.bfloat16)
    rows_grad = jnp.einsum(
        "erf,edf->erd", grad_pre, full_in, preferred_element_type=jnp.float32
    ).astype(jnp.bfloat16)
    back_x, back_w = (
        lax.all_to_all(
            to_groups(rows_grad, group_count, local_count, capacity),
            "expert",
            split_axis=0,
            concat_axis=0,
            tiled=True,
        ),
        lax.all_to_all(
            to_groups(route_grad, group_count, local_count, capacity),
            "expert",
            split_axis=0,
            concat_axis=0,
            tiled=True,
        ),
    )
    back_x = back_x.reshape(slot_total, model_width)
    back_w = back_w.reshape(slot_total).astype(jnp.float32)
    grad_tokens = jnp.einsum(
        "st,sd->td", by_token, back_x, preferred_element_type=jnp.float32
    ).astype(jnp.bfloat16)
    grad_route = jnp.sum(jnp.where(placed, back_w[:, None], 0.0), axis=0)
    grad_route = grad_route.reshape(token_count, route_count).astype(jnp.bfloat16)
    all_x = lax.all_to_all(rows_x, "dp", split_axis=2, concat_axis=1, tiled=True)
    grad_gate_up = jnp.einsum(
        "erd,erf->edf",
        all_x,
        lax.all_gather(grad_pre, "dp", axis=1, tiled=True),
        preferred_element_type=jnp.float32,
    )
    summed = lax.psum_scatter(
        jnp.einsum("erd,erf->def", scaled, hidden, preferred_element_type=jnp.float32),
        "dp",
        scatter_dimension=0,
        tiled=True,
    )
    grad_down = jnp.swapaxes(summed, 0, 1)
    return (grad_tokens, grad_route, grad_gate_up, grad_down)


def packs(tokens, route_expert, down_weight):
    chunks = tokens.shape[1] // LANES
    capacity = block_rows(tokens.shape[0], route_expert.shape[1], lax.axis_size("expert"))
    return (
        lax.axis_size("expert") == 8
        and lax.axis_size("dp") == 4
        and down_weight.shape[0] == 1
        and capacity % 16 <= 1
        and chunks == 16
        and 2 * chunks <= capacity < LANES // 2
    )


def solution(mesh):
    def on_device(*arrays):
        if packs(arrays[0], arrays[2], arrays[5]):
            return on_device_packed(*arrays)
        return on_device_routed(*arrays)

    return jax.shard_map(
        on_device,
        mesh=mesh,
        in_specs=(
            P(("expert", "dp"), None),
            P(("expert", "dp"), None),
            P(("expert", "dp"), None),
            P(("expert", "dp"), None),
            P("expert", "dp", None),
            P("expert", "dp", None),
        ),
        out_specs=(
            P(("expert", "dp"), None),
            P(("expert", "dp"), None),
            P("expert", "dp", None),
            P("expert", "dp", None),
        ),
        check_vma=False,
    )
```
